32 devices in a mesh: section: 4 (over y, x), tile: 8 (over z, core).
Axes of the slice: x: 2, y: 2, z: 4, core: 2. Of those that a mesh axis runs over, the one named last changes fastest.
Arguments:
- bricks: bfloat16 [128, 39304], P('tile'), may hold values from -6 to 6
- sends: int32 [4, 8, 8, 2], P('section', 'tile'), may hold values from 0 to 15
- cells: int32 [4, 8, 3, 40960], P('section', 'tile'), may hold values from 0 to 32
- fracs: float32 [4, 8, 3, 40960], P('section', 'tile'), may hold values from 0 to 1
- sample_order: int32 [4, 8, 160, 256], P('section', 'tile'), may hold values from 0 to 255, each once within a row
- pending: bfloat16 [4, 4, 64, 256], P('section', None, 'tile'), may hold values from -6 to 6
- w_in: bfloat16 [9, 32, 4], replicated, may hold values from -1 to 1
- w_mid: bfloat16 [9, 32, 32], replicated, may hold values from -0.375 to 0.375
- w_down: bfloat16 [9, 112, 32], replicated, may hold values from -0.375 to 0.375
- w_deep: bfloat16 [9, 112, 112], replicated, may hold values from -0.1875 to 0.1875
- w_up: bfloat16 [9, 32, 144], replicated, may hold values from -0.15625 to 0.15625
- w_out: bfloat16 [9, 3, 32], replicated, may hold values from -0.375 to 0.375
Outputs:
- handoff: bfloat16 [4, 4, 64, 256], P('section', None, 'tile')
- denoised: bfloat16 [4, 3, 64, 256], P('section', None, 'tile')
The draws below stay inside these ranges and needn't reach their ends.
Inputs may be any that keep to these rules, and one draw needn't show every extreme that they name: `sample_order`: each block of 256 names every number below 256 once.
All inputs are finite; a program needn't handle non-finite values.
Results may differ from the reference program's by a relative error of at most 0.012.
Values may be sent and summed in bfloat16 or wider, within the bound.
No kernel may reach another device: no remote copies, remote signals or barrier semaphores. Data moves between devices by JAX's collectives and lax.ppermute only.
A program may use at most 128 MiB of HBM per device.

```python
import math
import jax
import jax.numpy as jnp
import numpy as np
from jax import lax

EDGE = 34
BR_DEV = 16
CAP = 2
TH = 8
WID = 256
NSP = 4
NRAY = 8
NOS = 2
GCH = 4
C1 = 32
C2 = 112
OUTC = 3
CELLS = 39304
BRICKS = 128
SAMP = 40960
ROWS = 64
N_SECTION = 4
N_TILE = 8


def touch_ends(values, stream_key, least, largest):
    index_at = [jax.random.randint(jax.random.fold_in(stream_key, axis), (), 0, length) for axis, length in enumerate(values.shape)]
    main_axis = values.shape.index(max(values.shape))
    next_to = index_at[:main_axis] + [(index_at[main_axis] + 1) % values.shape[main_axis]] + index_at[main_axis + 1:]
    return values.at[tuple(index_at)].set(least).at[tuple(next_to)].set(largest)


def level_of(stream_key, shape, split, smallest, top_value):
    level, own = 1.0, jax.random.fold_in(stream_key, 6)
    for position, blocks in split:
        steps = jnp.exp(jax.random.uniform(jax.random.fold_in(own, position), (blocks,), jnp.float32, smallest / len(split), top_value / len(split)))
        level = level * jnp.repeat(steps, shape[position] // blocks).reshape([-1 if axis == position else 1 for axis in range(len(shape))])
    return level


def rank_table(number_of, slope):
    loads = [(1 << 20) // math.isqrt(standing ** slope) + 1 for standing in range(1, number_of + 1)]
    deviation = 1 + sum(loads) // (1 << 30)
    return np.cumsum(np.array([max(1, weight // deviation) for weight in loads]))


def ranked(key, extent, number_of, slope):
    table = rank_table(number_of, slope)
    lot = jax.random.randint(jax.random.fold_in(key, 1), extent, 0, int(table[number_of - 1]))
    rank = jnp.searchsorted(jnp.asarray(table, jnp.int32), lot, side="right")
    return jax.random.permutation(jax.random.fold_in(key, 2), number_of)[rank].astype(jnp.int32)


def normal_values(rng, dims, scale, limit, split=(), kind=jnp.bfloat16):
    result = jax.random.normal(rng, dims, jnp.float32) * scale
    if len(split) > 0:
        result = level_of(rng, dims, split, -0.22, 0.18) * result
    return jnp.clip(result, min=-limit, max=limit).astype(kind)


def setup_inputs(seed: int = 0) -> dict:
    streams_of = jax.random.split(jax.random.key(seed), 13)
    return {
        "bricks": normal_values(streams_of[0], (BRICKS, CELLS), 1.0, 6.0, ((0, 8),)),
        "sends": touch_ends(ranked(streams_of[1], (N_SECTION, N_TILE, N_TILE, CAP), BR_DEV, 2), jax.random.fold_in(streams_of[1], 3), 0, BR_DEV - 1).astype(jnp.int32),
        "cells": touch_ends(jax.random.randint(streams_of[2], (N_SECTION, N_TILE, 3, SAMP), 0, EDGE - 1), jax.random.fold_in(streams_of[2], 1), 0, (EDGE - 1) - 1).astype(jnp.int32),
        "fracs": jnp.clip(1.0 * jax.random.uniform(streams_of[3], (N_SECTION, N_TILE, 3, SAMP), jnp.float32) ** level_of(streams_of[3], (N_SECTION, N_TILE, 3, SAMP), ((0, 4), (1, 8)), -0.2, 0.2), 0.0, 1.0),
        "sample_order": jax.vmap(lambda own: jax.random.permutation(own, WID))(jax.random.split(streams_of[4], N_SECTION * N_TILE * (SAMP // WID))).reshape((N_SECTION, N_TILE, SAMP // WID, WID)).astype(jnp.int32),
        "pending": normal_values(streams_of[5], (N_SECTION, GCH, ROWS, WID), 1.0, 6.0, ((0, 4), (2, 8))),
        "w_in": normal_values(streams_of[6], (9, C1, GCH), (9 * GCH) ** -0.5, 1.0),
        "w_mid": normal_values(streams_of[7], (9, C1, C1), (9 * C1) ** -0.5, 0.375),
        "w_down": normal_values(streams_of[8], (9, C2, C1), (9 * C1) ** -0.5, 0.375),
        "w_deep": normal_values(streams_of[9], (9, C2, C2), (9 * C2) ** -0.5, 0.1875),
        "w_up": normal_values(streams_of[10], (9, C1, C1 + C2), (9 * (C1 + C2)) ** -0.5, 0.15625),
        "w_out": normal_values(streams_of[11], (9, OUTC, C1), (9 * C1) ** -0.5, 0.375),
    }


SHARP = 2.0


def axis_weights(index, frac):
    places = jnp.arange(EDGE, dtype=jnp.int32)
    lower = (places == index[..., None]).astype(jnp.float32)
    upper = (places == index[..., None] + 1).astype(jnp.float32)
    return lower * (1.0 - frac[..., None]) + upper * frac[..., None]


def spread_weights(index, frac, places):
    lower = (places == index[..., None]).astype(jnp.float32)
    upper = (places == index[..., None] + 1).astype(jnp.float32)
    return lower * (1.0 - frac[..., None]) + upper * frac[..., None]


def trilinear(slabs, cell_part, frac_part):
    groups = cell_part.shape[1]
    flat_places = jnp.arange(EDGE * EDGE, dtype=jnp.int32)
    row_place = flat_places // EDGE
    col_place = flat_places % EDGE
    weight_x = spread_weights(cell_part[0], frac_part[0], row_place)
    weight_y = spread_weights(cell_part[1], frac_part[1], col_place)
    weight_z = axis_weights(cell_part[2], frac_part[2])
    plane = (weight_x * weight_y).astype(jnp.bfloat16)
    cube = slabs.reshape(groups, EDGE, EDGE * EDGE)
    rows_out = jnp.einsum("gsq,gzq->gsz", plane.astype(jnp.float32), cube.astype(jnp.float32))
    return jnp.sum(rows_out * weight_z, axis=-1)


def group_size(slots, per_slot):
    width = min(slots, max(1, 4096 // per_slot))
    while slots % width:
        width -= 1
    return width


def sample_values(received, cell_all, frac_all):
    slots = received.shape[0]
    per_slot = cell_all.shape[1] // slots
    width = group_size(slots, per_slot)
    cell_grid = cell_all.reshape(3, slots, per_slot)
    frac_grid = frac_all.reshape(3, slots, per_slot)

    def one_group(number):
        start = number * width
        slabs = lax.dynamic_slice_in_dim(received, start, width, 0)
        cell_part = lax.dynamic_slice_in_dim(cell_grid, start, width, 1)
        frac_part = lax.dynamic_slice_in_dim(frac_grid, start, width, 1)
        return trilinear(slabs, cell_part, frac_part)

    found = lax.map(one_group, jnp.arange(slots // width, dtype=jnp.int32))
    return found.reshape(-1)


def gbuffer(values, order, height, width):
    base = jnp.arange(order.shape[0], dtype=jnp.int32)[:, None] * order.shape[1]
    flat_order = (order + base).reshape(-1).astype(jnp.int32)
    ray = jnp.take(values, flat_order).reshape(NSP + NRAY * NOS, height, width)
    alpha = jax.nn.sigmoid(SHARP * ray)
    remain = jnp.ones((height, width), jnp.float32)
    shade = jnp.zeros((height, width), jnp.float32)
    depth = jnp.zeros((height, width), jnp.float32)
    for step in range(NSP):
        weight = remain * alpha[step]
        shade = shade + weight * ray[step]
        depth = depth + weight * ((step + 1) / NSP)
        remain = remain * (1.0 - alpha[step])
    opacity = 1.0 - remain
    passing = (1.0 - alpha[NSP:]).reshape(NRAY, NOS, height, width)
    occlusion = jnp.mean(jnp.prod(passing, axis=1), axis=0)
    return jnp.stack([shade, opacity, depth, occlusion], axis=0).astype(jnp.bfloat16)


def conv_rows(padded, weight):
    height = padded.shape[1] - 2
    width = padded.shape[2]
    wide = jnp.pad(padded, ((0, 0), (0, 0), (1, 1)))
    total = jnp.zeros((weight.shape[1], height, width), jnp.float32)
    for row_tap in range(3):
        for col_tap in range(3):
            total = total + jnp.einsum("oc,crw->orw", weight[3 * row_tap + col_tap].astype(jnp.float32), wide[:, row_tap:row_tap + height, col_tap:col_tap + width].astype(jnp.float32))
    return total


def same_conv(field, weight):
    return conv_rows(jnp.pad(field, ((0, 0), (1, 1), (0, 0))), weight)


def pooling(field):
    chans, height, width = field.shape
    return field.astype(jnp.float32).reshape(chans, height // 2, 2, width // 2, 2).mean(axis=(2, 4)).astype(jnp.bfloat16)


def reference(bricks, sends, cells, fracs, sample_order, pending, w_in, w_mid, w_down, w_deep, w_up, w_out):
    n_section, n_tile = sends.shape[0], sends.shape[1]

    def render_one(flat):
        section_now = flat // n_tile
        tile_now = flat % n_tile
        picks = sends[section_now, :, tile_now, :]
        global_ids = (jnp.arange(n_tile, dtype=jnp.int32)[:, None] * BR_DEV + picks).reshape(-1).astype(jnp.int32)
        received = jnp.take(bricks, global_ids, axis=0)
        values = sample_values(received, cells[section_now, tile_now], fracs[section_now, tile_now])
        return gbuffer(values, sample_order[section_now, tile_now], TH, WID)

    blocks = lax.map(render_one, jnp.arange(n_section * n_tile, dtype=jnp.int32))
    rendered = blocks.reshape(n_section, n_tile, GCH, TH, WID).transpose(0, 2, 1, 3, 4).reshape(n_section, GCH, n_tile * TH, WID)
    handoff = jnp.roll(rendered, 1, axis=0)

    def denoise(field):
        first = jax.nn.silu(same_conv(field, w_in)).astype(jnp.bfloat16)
        second = jax.nn.silu(same_conv(first, w_mid)).astype(jnp.bfloat16)
        pooled = pooling(second)
        third = jax.nn.silu(same_conv(pooled, w_down)).astype(jnp.bfloat16)
        fourth = jax.nn.silu(same_conv(third, w_deep)).astype(jnp.bfloat16)
        raised = jnp.repeat(jnp.repeat(fourth, 2, axis=1), 2, axis=2)
        joined = jnp.concatenate([second, raised], axis=0)
        fifth = jax.nn.silu(same_conv(joined, w_up)).astype(jnp.bfloat16)
        return same_conv(fifth, w_out).astype(jnp.bfloat16)

    denoised = lax.map(denoise, pending)
    return handoff, denoised
```

```python
import functools

import jax
import jax.numpy as jnp
from jax import lax
from jax.experimental import pallas as pl
from jax.experimental.pallas import tpu as pltpu
from jax.sharding import PartitionSpec as P

EDGE = 34
NSP = 4
NRAY = 8
NOS = 2
LANES = 128
BLOCK = 256
STRIDE = 6
WINDOWS = 6
MAIN = 32
TAIL = 16
BRICK_ROWS = WINDOWS * MAIN + TAIL
KDIM = 256

F32 = jnp.float32
BF16 = jnp.bfloat16
VMEM_LIMIT = 48 * 1024 * 1024


def params():
    return pltpu.CompilerParams(vmem_limit_bytes=VMEM_LIMIT)


def vmem():
    return pl.BlockSpec(memory_space=pltpu.VMEM)


def smem():
    return pl.BlockSpec(memory_space=pltpu.SMEM)


def positions_kernel(cells_ref, fracs_ref, out_ref):
    owners, rows, _ = out_ref.shape
    blocks = rows // 6
    span = blocks * BLOCK

    def one_owner(owner, carry):
        for block in range(blocks):
            start = pl.multiple_of(owner * span + block * BLOCK, BLOCK)
            place = (
                cells_ref[0, 0, :, pl.ds(start, BLOCK)].astype(F32)
                + fracs_ref[0, 0, :, pl.ds(start, BLOCK)]
            )
            for axis in range(3):
                for half in range(2):
                    row = axis * 2 * blocks + half * blocks + block
                    out_ref[owner, row : row + 1, :] = place[
                        axis : axis + 1, half * LANES : (half + 1) * LANES
                    ]
        return carry

    lax.fori_loop(0, owners, one_owner, 0)


def positions(cells, fracs, owners):
    samples = cells.shape[3]
    rows = 3 * samples // owners // LANES
    return pl.pallas_call(
        positions_kernel,
        out_shape=jax.ShapeDtypeStruct((owners, rows, LANES), F32),
        in_specs=[vmem(), vmem()],
        out_specs=vmem(),
        compiler_params=params(),
        cost_estimate=pl.CostEstimate(
            flops=3 * samples, bytes_accessed=36 * samples, transcendentals=0
        ),
        name="positions",
    )(cells, fracs)


def windows_kernel(cube_ref, out_ref, wide, tail):
    count = cube_ref.shape[0]
    plane = EDGE * EDGE
    wide[...] = jnp.zeros_like(wide)
    wide[:, :EDGE, :plane] = cube_ref[...]
    column = lax.broadcasted_iota(jnp.int32, (1, KDIM), 1)
    main = (column // MAIN) * EDGE + column % MAIN
    rest = column - 7 * MAIN
    last = (rest % 8) * EDGE + MAIN + rest // 8
    source = jnp.where(column < 7 * MAIN, main, last)
    unused = (column >= 7 * MAIN) & ((rest % 8 == 7) | (rest >= TAIL))
    source = jnp.where(unused, -(1 << 20), source)
    for window in range(WINDOWS):
        first = window * STRIDE * EDGE
        low = first // LANES * LANES
        length = min(3 * LANES, wide.shape[2] - low)
        place = lax.broadcasted_iota(jnp.int32, (length, KDIM), 0)
        pick = jnp.where(place == source + (first - low), 1.0, 0.0).astype(BF16)
        found = jnp.dot(
            wide[:, :, low : low + length].reshape(-1, length),
            pick,
            preferred_element_type=F32,
        )
        found = found.reshape(count, 48, KDIM)
        out_ref[:, window * MAIN : (window + 1) * MAIN, :] = found[:, :MAIN, :].astype(BF16)
        tail[:, window : window + 1, :] = found[:, MAIN : MAIN + 1, :]
        tail[:, 8 + window : 9 + window, :] = found[:, MAIN + 1 : MAIN + 2, :]
    for row in (6, 7, 14, 15):
        tail[:, row : row + 1, :] = jnp.zeros((count, 1, KDIM), F32)
    out_ref[:, WINDOWS * MAIN :, :] = tail[...].astype(BF16)


def windows_of(bricks):
    count = bricks.shape[0]
    cube = bricks.reshape(count, EDGE, EDGE * EDGE)
    return pl.pallas_call(
        windows_kernel,
        out_shape=jax.ShapeDtypeStruct((count, BRICK_ROWS, KDIM), BF16),
        in_specs=[vmem()],
        out_specs=vmem(),
        scratch_shapes=[
            pltpu.VMEM((count, 48, 10 * LANES), BF16),
            pltpu.VMEM((count, TAIL, KDIM), F32),
        ],
        compiler_params=params(),
        cost_estimate=pl.CostEstimate(
            flops=2 * count * 48 * 384 * KDIM * WINDOWS, bytes_accessed=4 * 1024 * 1024,
            transcendentals=0,
        ),
        name="brick_windows",
    )(cube)


def hat(distance):
    return jnp.maximum(1.0 - jnp.abs(distance), 0.0)


def blend(brick, px, py, pz):
    width = px.shape[1]
    places = lax.broadcasted_iota(jnp.int32, (MAIN, width), 0).astype(F32)
    eight = lax.broadcasted_iota(jnp.int32, (8, width), 0).astype(F32)
    weight_y = hat(places - py)
    weight_z = hat(places - pz)
    window = jnp.clip(jnp.floor(px * (1.0 / STRIDE)), 0.0, WINDOWS - 1.0)
    weight_x = hat(eight - (px - STRIDE * window))
    parts = [(weight_y * weight_x[i : i + 1]).astype(BF16) for i in range(STRIDE + 1)]
    parts.append((weight_x * hat(MAIN - py)).astype(BF16))
    parts.append((weight_x * hat(MAIN + 1 - py)).astype(BF16))
    parts.append(jnp.zeros((TAIL, width), BF16))
    plane = jnp.concatenate(parts, axis=0)
    found = jnp.dot(brick, plane, preferred_element_type=F32)
    chosen = found[:MAIN]
    for other in range(1, WINDOWS):
        chosen = jnp.where(
            window == float(other), found[other * MAIN : (other + 1) * MAIN], chosen
        )
    total = (chosen * weight_z).reshape(MAIN // 8, 8, width).sum(axis=0)
    base = WINDOWS * MAIN
    edges = found[base : base + 8] * hat(MAIN - pz) + found[base + 8 :] * hat(MAIN + 1 - pz)
    total = total + jnp.where(eight == window, edges, 0.0)
    return jnp.sum(total, axis=0, keepdims=True)


def samples_kernel(picks_ref, brick_ref, place_ref, out_ref):
    owners, rows, _ = place_ref.shape
    cap = picks_ref.shape[3]
    blocks = rows // 6
    per_slot = blocks // cap

    def one_slot(slot, carry):
        renderer = slot // cap
        piece = slot % cap
        brick = brick_ref[picks_ref[0, 0, renderer, piece]]
        for step in range(per_slot):
            row = piece * per_slot + step

            def line(axis):
                both = [
                    place_ref[renderer, pl.ds((2 * axis + half) * blocks + row, 1), :]
                    for half in range(2)
                ]
                return jnp.concatenate(both, axis=1)

            value = blend(brick, line(0), line(1), line(2))
            for half in range(2):
                out_ref[renderer, pl.ds(half * blocks + row, 1), :] = value[
                    :, half * LANES : (half + 1) * LANES
                ]
        return carry

    lax.fori_loop(0, owners * cap, one_slot, 0)


def sample_values(picks, windows, places):
    owners, rows, _ = places.shape
    samples = owners * rows * LANES // 3
    return pl.pallas_call(
        samples_kernel,
        out_shape=jax.ShapeDtypeStruct((owners, rows // 3, LANES), F32),
        in_specs=[smem(), vmem(), vmem()],
        out_specs=vmem(),
        compiler_params=params(),
        cost_estimate=pl.CostEstimate(
            flops=2 * samples * KDIM * BRICK_ROWS, bytes_accessed=3 * 1024 * 1024,
            transcendentals=0,
        ),
        name="sample_values",
    )(picks, windows, places)


def gbuffer_kernel(value_ref, order_ref, out_ref, low, high):
    groups, rows, _ = value_ref.shape
    blocks = rows // 2
    for group in range(groups):
        low[group * blocks : (group + 1) * blocks, :] = value_ref[group, :blocks, :]
        high[group * blocks : (group + 1) * blocks, :] = value_ref[group, blocks:, :]
    height = out_ref.shape[2]

    def ray_of(number):
        rows_now = slice(number * height, (number + 1) * height)
        first, second = low[rows_now, :], high[rows_now, :]
        parts = []
        for half in range(2):
            order = order_ref[0, 0, rows_now, half * LANES : (half + 1) * LANES]
            inner = order & (LANES - 1)
            parts.append(
                jnp.where(
                    order < LANES,
                    jnp.take_along_axis(first, inner, axis=1, mode="promise_in_bounds"),
                    jnp.take_along_axis(second, inner, axis=1, mode="promise_in_bounds"),
                )
            )
        return jnp.concatenate(parts, axis=1)

    remain = 1.0
    shade = 0.0
    depth = 0.0
    for step in range(NSP):
        ray = ray_of(step)
        half_tanh = 0.5 * jnp.tanh(ray)
        weight = remain * (0.5 + half_tanh)
        shade = shade + weight * ray
        depth = depth + weight * ((step + 1) / NSP)
        remain = remain * (0.5 - half_tanh)
    occlusion = 0.0
    for ray_number in range(NRAY):
        passing = 1.0
        for step in range(NOS):
            ray = ray_of(NSP + ray_number * NOS + step)
            passing = passing * (0.5 - 0.5 * jnp.tanh(ray))
        occlusion = occlusion + passing
    out_ref[0, 0] = shade.astype(BF16)
    out_ref[0, 1] = (1.0 - remain).astype(BF16)
    out_ref[0, 2] = depth.astype(BF16)
    out_ref[0, 3] = (occlusion * (1.0 / NRAY)).astype(BF16)


def gbuffer(values, order, height, width):
    total = order.shape[2]
    return pl.pallas_call(
        gbuffer_kernel,
        out_shape=jax.ShapeDtypeStruct((1, 4, height, width), BF16),
        in_specs=[vmem(), vmem()],
        out_specs=vmem(),
        scratch_shapes=[pltpu.VMEM((total, LANES), F32), pltpu.VMEM((total, LANES), F32)],
        compiler_params=params(),
        cost_estimate=pl.CostEstimate(
            flops=20 * total * BLOCK, bytes_accessed=8 * total * BLOCK, transcendentals=0
        ),
        name="gbuffer",
    )(values, order)


def silu(field):
    half = 0.5 * field
    return half + half * jnp.tanh(half)


def conv_line(source, row, weight_ref, out_chans):
    chans = weight_ref.shape[2]
    total = None
    for tap in range(3):
        weight = weight_ref[3 * tap : 3 * tap + 3].reshape(3 * out_chans, chans)
        part = jnp.dot(weight, source[row + tap], preferred_element_type=F32)
        total = part if total is None else total + part
    width = total.shape[1]
    left, middle, right = (total[i * out_chans : (i + 1) * out_chans] for i in range(3))
    lane = lax.broadcasted_iota(jnp.int32, (1, width), 1)
    from_left = jnp.where(lane == 0, 0.0, pltpu.roll(left, 1, 1))
    from_right = jnp.where(lane == width - 1, 0.0, pltpu.roll(right, width - 1, 1))
    return middle + from_left + from_right


def unet_kernel(
    where_ref, x_ref, w_in, w_mid, w_down, w_deep, w_up, w_out, out_ref,
    first, second, pooled, third, fourth, joined, fifth, final,
):
    height = out_ref.shape[2]
    half_height = height // 2
    width = out_ref.shape[3]
    above = jnp.where(where_ref[0] > 0, 1.0, 0.0)
    below = jnp.where(where_ref[0] < where_ref[1] - 1, 1.0, 0.0)

    def inside(row, low, high):
        return jnp.where(row < low, above, jnp.where(row >= high, below, 1.0))

    def layer(source, weight_ref, target, low, high):
        chans = target.shape[1]

        def step(row, carry):
            line = silu(conv_line(source, row, weight_ref, chans))
            target[row] = (line * inside(row, low, high)).astype(BF16)
            return carry

        lax.fori_loop(0, target.shape[0], step, 0, unroll=2)

    layer(x_ref, w_in, first, height - 1, 2 * height - 1)
    layer(first, w_mid, second, height - 2, 2 * height - 2)

    place = lax.broadcasted_iota(jnp.int32, (width, width // 2), 0) // 2
    target = lax.broadcasted_iota(jnp.int32, (width, width // 2), 1)
    shrink = jnp.where(place == target, 0.25, 0.0).astype(BF16)
    count, chans = second.shape[0], second.shape[1]
    pairs = jnp.dot(
        second[...].reshape(count * chans, width), shrink, preferred_element_type=F32
    ).reshape(count // 2, 2, chans, width // 2)
    pooled[...] = (pairs[:, 0] + pairs[:, 1]).astype(BF16)

    layer(pooled, w_down, third, half_height - 2, 2 * half_height - 2)
    layer(third, w_deep, fourth, half_height - 3, 2 * half_height - 3)

    place = lax.broadcasted_iota(jnp.int32, (width // 2, width), 0)
    target = lax.broadcasted_iota(jnp.int32, (width // 2, width), 1) // 2
    spread = jnp.where(place == target, 1.0, 0.0).astype(BF16)
    deep = fourth.shape[1]
    for row in range(fourth.shape[0]):
        wide = jnp.dot(fourth[row], spread, preferred_element_type=F32).astype(BF16)
        for half in range(2):
            joined[2 * row + half, chans:, :] = wide
            joined[2 * row + half, :chans, :] = second[2 * row + half + 4]

    layer(joined, w_up, fifth, 1, height + 1)

    colours = out_ref.shape[1]
    for row in range(height):
        line = conv_line(fifth, row, w_out, w_out.shape[1])
        for colour in range(colours):
            final[colour, row : row + 1, :] = line[colour : colour + 1, :]
    out_ref[0] = final[...].astype(BF16)


def unet(where, field, w_in, w_mid, w_down, w_deep, w_up, w_out, colours):
    height = field.shape[0] // 3
    half = height // 2
    width = field.shape[2]
    one, two = w_mid.shape[1], w_deep.shape[1]
    return pl.pallas_call(
        unet_kernel,
        out_shape=jax.ShapeDtypeStruct((1, colours, height, width), BF16),
        in_specs=[smem()] + [vmem()] * 7,
        out_specs=vmem(),
        scratch_shapes=[
            pltpu.VMEM((3 * height - 2, one, width), BF16),
            pltpu.VMEM((3 * height - 4, one, width), BF16),
            pltpu.VMEM((3 * half - 2, one, width // 2), BF16),
            pltpu.VMEM((3 * half - 4, two, width // 2), BF16),
            pltpu.VMEM((3 * half - 6, two, width // 2), BF16),
            pltpu.VMEM((height + 4, one + two, width), BF16),
            pltpu.VMEM((height + 2, one, width), BF16),
            pltpu.VMEM((colours, height, width), F32),
        ],
        compiler_params=params(),
        cost_estimate=pl.CostEstimate(
            flops=3_000_000_000, bytes_accessed=2 * 1024 * 1024, transcendentals=500_000
        ),
        name="unet",
    )(where, field, w_in, w_mid, w_down, w_deep, w_up, w_out)


def on_device(
    bricks, sends, cells, fracs, sample_order, pending, w_in, w_mid, w_down, w_deep, w_up, w_out
):
    n_tile = lax.axis_size("tile")
    tile = lax.axis_index("tile")
    n_section = lax.axis_size("section")
    cap = sends.shape[3]
    height = pending.shape[2]
    width = pending.shape[3]
    samples = cells.shape[3]
    slots = n_tile * cap
    per_slot = samples // slots
    padded = -(-per_slot // BLOCK) * BLOCK

    def fill(part):
        if padded == per_slot:
            return part
        part = part.reshape(1, 1, 3, slots, per_slot)
        part = jnp.pad(part, ((0, 0),) * 4 + ((0, padded - per_slot),))
        return part.reshape(1, 1, 3, slots * padded)

    def trim(found):
        if padded == per_slot:
            return found
        rows = found.shape[1] // 2
        flat = found.reshape(n_tile, 2, rows, LANES).transpose(0, 2, 1, 3)
        flat = flat.reshape(slots, padded)[:, :per_slot]
        flat = flat.reshape(1, samples // BLOCK, 2, LANES).transpose(0, 2, 1, 3)
        return flat.reshape(1, samples // LANES, LANES)

    down = [(i, i + 1) for i in range(n_tile - 1)]
    up = [(i + 1, i) for i in range(n_tile - 1)]
    over = lax.ppermute(pending, "tile", down)
    under = lax.ppermute(pending, "tile", up)
    places = positions(fill(cells), fill(fracs), n_tile)
    arrived = lax.all_to_all(places, "tile", split_axis=0, concat_axis=0, tiled=True)

    windows = windows_of(bricks)
    field = jnp.concatenate([over[0], pending[0], under[0]], axis=1).transpose(1, 0, 2)
    field = jnp.pad(field, ((0, 0), (0, 16 - field.shape[1]), (0, 0)))
    colours = w_out.shape[1]
    where = jnp.stack([tile, jnp.int32(n_tile)]).astype(jnp.int32)
    denoised = unet(
        where,
        field,
        jnp.pad(w_in, ((0, 0), (0, 0), (0, 16 - w_in.shape[2]))),
        w_mid,
        w_down,
        w_deep,
        w_up,
        jnp.pad(w_out, ((0, 0), (0, 16 - colours), (0, 0))),
        colours,
    )

    found = sample_values(sends, windows, arrived)
    values = lax.all_to_all(found, "tile", split_axis=0, concat_axis=0, tiled=True)
    rendered = gbuffer(trim(values), sample_order, height, width)
    ring = [(i, (i + 1) % n_section) for i in range(n_section)]
    handoff = lax.ppermute(rendered, "section", ring)
    return (handoff, denoised)


def solution(mesh):
    in_specs = (
        P("tile", None),
        P("section", "tile", None, None),
        P("section", "tile", None, None),
        P("section", "tile", None, None),
        P("section", "tile", None, None),
        P("section", None, "tile", None),
        P(),
        P(),
        P(),
        P(),
        P(),
        P(),
    )
    out_specs = (P("section", None, "tile", None), P("section", None, "tile", None))
    return jax.shard_map(
        on_device, mesh=mesh, in_specs=in_specs, out_specs=out_specs, check_vma=False
    )
```

```python
import functools

import jax
import jax.numpy as jnp
from jax import lax
from jax.experimental import pallas as pl
from jax.experimental.pallas import tpu as pltpu
from jax.sharding import PartitionSpec as P

EDGE = 34
NSP = 4
NRAY = 8
NOS = 2
LANES = 128
BLOCK = 256
STRIDE = 6
WINDOWS = 6
MAIN = 32
TAIL = 16
BRICK_ROWS = WINDOWS * MAIN + TAIL
KDIM = 256

F32 = jnp.float32
BF16 = jnp.bfloat16
VMEM_LIMIT = 48 * 1024 * 1024


def params():
    return pltpu.CompilerParams(vmem_limit_bytes=VMEM_LIMIT)


def vmem():
    return pl.BlockSpec(memory_space=pltpu.VMEM)


def smem():
    return pl.BlockSpec(memory_space=pltpu.SMEM)


def positions_kernel(cells_ref, fracs_ref, out_ref):
    owners, rows, _ = out_ref.shape
    lines = rows // 3
    for axis in range(3):
        place = cells_ref[axis].astype(F32) + fracs_ref[axis]
        out_ref[:, axis * lines : (axis + 1) * lines, :] = place.reshape(owners, lines, LANES)


def positions(cells, fracs, owners):
    lines = cells.shape[1]
    return pl.pallas_call(
        positions_kernel,
        out_shape=jax.ShapeDtypeStruct((owners, 3 * lines // owners, LANES), F32),
        in_specs=[vmem(), vmem()],
        out_specs=vmem(),
        compiler_params=params(),
        cost_estimate=pl.CostEstimate(
            flops=3 * lines * LANES, bytes_accessed=36 * lines * LANES, transcendentals=0
        ),
        name="positions",
    )(cells, fracs)


def windows_kernel(cube_ref, out_ref, wide, tail):
    count = cube_ref.shape[0]
    plane = EDGE * EDGE
    wide[...] = jnp.zeros_like(wide)
    wide[:, :EDGE, :plane] = cube_ref[...]
    column = lax.broadcasted_iota(jnp.int32, (1, KDIM), 1)
    main = (column // MAIN) * EDGE + column % MAIN
    rest = column - 7 * MAIN
    last = (rest % 8) * EDGE + MAIN + rest // 8
    source = jnp.where(column < 7 * MAIN, main, last)
    unused = (column >= 7 * MAIN) & ((rest % 8 == 7) | (rest >= TAIL))
    source = jnp.where(unused, -(1 << 20), source)
    for window in range(WINDOWS):
        first = window * STRIDE * EDGE
        low = first // LANES * LANES
        length = min(3 * LANES, wide.shape[2] - low)
        place = lax.broadcasted_iota(jnp.int32, (length, KDIM), 0)
        pick = jnp.where(place == source + (first - low), 1.0, 0.0).astype(BF16)
        found = jnp.dot(
            wide[:, :, low : low + length].reshape(-1, length),
            pick,
            preferred_element_type=F32,
        )
        found = found.reshape(count, 48, KDIM)
        out_ref[:, window * MAIN : (window + 1) * MAIN, :] = found[:, :MAIN, :].astype(BF16)
        tail[:, window : window + 1, :] = found[:, MAIN : MAIN + 1, :]
        tail[:, 8 + window : 9 + window, :] = found[:, MAIN + 1 : MAIN + 2, :]
    for row in (6, 7, 14, 15):
        tail[:, row : row + 1, :] = jnp.zeros((count, 1, KDIM), F32)
    out_ref[:, WINDOWS * MAIN :, :] = tail[...].astype(BF16)


def windows_of(bricks):
    count = bricks.shape[0]
    cube = bricks.reshape(count, EDGE, EDGE * EDGE)
    return pl.pallas_call(
        windows_kernel,
        out_shape=jax.ShapeDtypeStruct((count, BRICK_ROWS, KDIM), BF16),
        in_specs=[vmem()],
        out_specs=vmem(),
        scratch_shapes=[
            pltpu.VMEM((count, 48, 10 * LANES), BF16),
            pltpu.VMEM((count, TAIL, KDIM), F32),
        ],
        compiler_params=params(),
        cost_estimate=pl.CostEstimate(
            flops=2 * count * 48 * 384 * KDIM * WINDOWS, bytes_accessed=4 * 1024 * 1024,
            transcendentals=0,
        ),
        name="brick_windows",
    )(cube)


def hat(distance):
    return jnp.maximum(1.0 - jnp.abs(distance), 0.0)


def blend(brick, px, py, pz):
    width = px.shape[1]
    places = lax.broadcasted_iota(jnp.int32, (MAIN, width), 0).astype(F32)
    eight = lax.broadcasted_iota(jnp.int32, (8, width), 0).astype(F32)
    weight_y = hat(places - py)
    weight_z = hat(places - pz)
    window = jnp.clip(jnp.floor(px * (1.0 / STRIDE)), 0.0, WINDOWS - 1.0)
    weight_x = hat(eight - (px - STRIDE * window))
    parts = [(weight_y * weight_x[i : i + 1]).astype(BF16) for i in range(STRIDE + 1)]
    parts.append((weight_x * hat(MAIN - py)).astype(BF16))
    parts.append((weight_x * hat(MAIN + 1 - py)).astype(BF16))
    parts.append(jnp.zeros((TAIL, width), BF16))
    plane = jnp.concatenate(parts, axis=0)
    found = jnp.dot(brick, plane, preferred_element_type=F32)
    chosen = found[:MAIN]
    for other in range(1, WINDOWS):
        chosen = jnp.where(
            window == float(other), found[other * MAIN : (other + 1) * MAIN], chosen
        )
    total = (chosen * weight_z).reshape(MAIN // 8, 8, width).sum(axis=0)
    base = WINDOWS * MAIN
    edges = found[base : base + 8] * hat(MAIN - pz) + found[base + 8 :] * hat(MAIN + 1 - pz)
    total = total + jnp.where(eight == window, edges, 0.0)
    return jnp.sum(total, axis=0, keepdims=True)


def samples_kernel(picks_ref, brick_ref, place_ref, after_ref, out_ref, values):
    owners, rows, _ = place_ref.shape
    cap = picks_ref.shape[3]
    lines = rows // 3
    per_slot = lines // 2 // cap

    def one_slot(slot, carry):
        renderer = slot // cap
        piece = slot % cap
        brick = brick_ref[picks_ref[0, 0, renderer, piece]]
        for step in range(per_slot):
            row = 2 * (piece * per_slot + step)

            def line(axis):
                both = [
                    place_ref[renderer, pl.ds(axis * lines + row + half, 1), :]
                    for half in range(2)
                ]
                return jnp.concatenate(both, axis=1)

            value = blend(brick, line(0), line(1), line(2))
            for half in range(2):
                values[renderer, pl.ds(row + half, 1), :] = value[
                    :, half * LANES : (half + 1) * LANES
                ]
        return carry

    lax.fori_loop(0, owners * cap, one_slot, 0)
    out_ref[...] = values[...].astype(BF16)


def sample_values(picks, windows, places, after):
    owners, rows, _ = places.shape
    samples = owners * rows * LANES // 3
    shape = (owners, rows // 3, LANES)
    return pl.pallas_call(
        samples_kernel,
        out_shape=jax.ShapeDtypeStruct(shape, BF16),
        in_specs=[smem(), vmem(), vmem(), pl.BlockSpec(memory_space=pltpu.HBM)],
        out_specs=vmem(),
        scratch_shapes=[pltpu.VMEM(shape, F32)],
        compiler_params=params(),
        cost_estimate=pl.CostEstimate(
            flops=2 * samples * KDIM * BRICK_ROWS, bytes_accessed=3 * 1024 * 1024,
            transcendentals=0,
        ),
        name="sample_values",
    )(picks, windows, places, after)


def gbuffer_kernel(value_ref, order_ref, out_ref, values):
    values[...] = value_ref[...].astype(F32).reshape(values.shape)
    height = out_ref.shape[2]

    def ray_of(number):
        rows_now = slice(number * height, (number + 1) * height)
        first, second = (
            values[pl.ds(2 * number * height + half, height, stride=2), :] for half in range(2)
        )
        parts = []
        for half in range(2):
            order = order_ref[0, 0, rows_now, half * LANES : (half + 1) * LANES]
            inner = order & (LANES - 1)
            parts.append(
                jnp.where(
                    order < LANES,
                    jnp.take_along_axis(first, inner, axis=1, mode="promise_in_bounds"),
                    jnp.take_along_axis(second, inner, axis=1, mode="promise_in_bounds"),
                )
            )
        return jnp.concatenate(parts, axis=1)

    remain = 1.0
    shade = 0.0
    depth = 0.0
    for step in range(NSP):
        ray = ray_of(step)
        half_tanh = 0.5 * jnp.tanh(ray)
        weight = remain * (0.5 + half_tanh)
        shade = shade + weight * ray
        depth = depth + weight * ((step + 1) / NSP)
        remain = remain * (0.5 - half_tanh)
    occlusion = 0.0
    for ray_number in range(NRAY):
        passing = 1.0
        for step in range(NOS):
            ray = ray_of(NSP + ray_number * NOS + step)
            passing = passing * (0.5 - 0.5 * jnp.tanh(ray))
        occlusion = occlusion + passing
    out_ref[0, 0] = shade.astype(BF16)
    out_ref[0, 1] = (1.0 - remain).astype(BF16)
    out_ref[0, 2] = depth.astype(BF16)
    out_ref[0, 3] = (occlusion * (1.0 / NRAY)).astype(BF16)


def gbuffer(values, order, height, width):
    total = order.shape[2]
    return pl.pallas_call(
        gbuffer_kernel,
        out_shape=jax.ShapeDtypeStruct((1, 4, height, width), BF16),
        in_specs=[vmem(), vmem()],
        out_specs=vmem(),
        scratch_shapes=[pltpu.VMEM((2 * total, LANES), F32)],
        compiler_params=params(),
        cost_estimate=pl.CostEstimate(
            flops=20 * total * BLOCK, bytes_accessed=8 * total * BLOCK, transcendentals=0
        ),
        name="gbuffer",
    )(values, order)


def silu(field):
    half = 0.5 * field
    return half + half * jnp.tanh(half)


def conv_line(source, row, weight_ref, out_chans):
    chans = weight_ref.shape[2]
    total = None
    for tap in range(3):
        weight = weight_ref[3 * tap : 3 * tap + 3].reshape(3 * out_chans, chans)
        part = jnp.dot(weight, source[row + tap], preferred_element_type=F32)
        total = part if total is None else total + part
    width = total.shape[1]
    left, middle, right = (total[i * out_chans : (i + 1) * out_chans] for i in range(3))
    lane = lax.broadcasted_iota(jnp.int32, (1, width), 1)
    from_left = jnp.where(lane == 0, 0.0, pltpu.roll(left, 1, 1))
    from_right = jnp.where(lane == width - 1, 0.0, pltpu.roll(right, width - 1, 1))
    return middle + from_left + from_right


def unet_kernel(
    where_ref, x_ref, w_in, w_mid, w_down, w_deep, w_up, w_out, out_ref,
    first, second, pooled, third, fourth, joined, fifth, final,
):
    height = out_ref.shape[2]
    half_height = height // 2
    width = out_ref.shape[3]
    above = jnp.where(where_ref[0] > 0, 1.0, 0.0)
    below = jnp.where(where_ref[0] < where_ref[1] - 1, 1.0, 0.0)

    def inside(row, low, high):
        return jnp.where(row < low, above, jnp.where(row >= high, below, 1.0))

    def layer(source, weight_ref, target, low, high):
        chans = target.shape[1]

        def step(row, carry):
            line = silu(conv_line(source, row, weight_ref, chans))
            target[row] = (line * inside(row, low, high)).astype(BF16)
            return carry

        lax.fori_loop(0, target.shape[0], step, 0, unroll=2)

    layer(x_ref, w_in, first, height - 1, 2 * height - 1)
    layer(first, w_mid, second, height - 2, 2 * height - 2)

    place = lax.broadcasted_iota(jnp.int32, (width, width // 2), 0) // 2
    target = lax.broadcasted_iota(jnp.int32, (width, width // 2), 1)
    shrink = jnp.where(place == target, 0.25, 0.0).astype(BF16)
    count, chans = second.shape[0], second.shape[1]
    pairs = jnp.dot(
        second[...].reshape(count * chans, width), shrink, preferred_element_type=F32
    ).reshape(count // 2, 2, chans, width // 2)
    pooled[...] = (pairs[:, 0] + pairs[:, 1]).astype(BF16)

    layer(pooled, w_down, third, half_height - 2, 2 * half_height - 2)
    layer(third, w_deep, fourth, half_height - 3, 2 * half_height - 3)

    place = lax.broadcasted_iota(jnp.int32, (width // 2, width), 0)
    target = lax.broadcasted_iota(jnp.int32, (width // 2, width), 1) // 2
    spread = jnp.where(place == target, 1.0, 0.0).astype(BF16)
    deep = fourth.shape[1]
    for row in range(fourth.shape[0]):
        wide = jnp.dot(fourth[row], spread, preferred_element_type=F32).astype(BF16)
        for half in range(2):
            joined[2 * row + half, chans:, :] = wide
            joined[2 * row + half, :chans, :] = second[2 * row + half + 4]

    layer(joined, w_up, fifth, 1, height + 1)

    colours = out_ref.shape[1]
    for row in range(height):
        line = conv_line(fifth, row, w_out, w_out.shape[1])
        for colour in range(colours):
            final[colour, row : row + 1, :] = line[colour : colour + 1, :]
    out_ref[0] = final[...].astype(BF16)


def unet(where, field, w_in, w_mid, w_down, w_deep, w_up, w_out, colours):
    height = field.shape[0] // 3
    half = height // 2
    width = field.shape[2]
    one, two = w_mid.shape[1], w_deep.shape[1]
    return pl.pallas_call(
        unet_kernel,
        out_shape=jax.ShapeDtypeStruct((1, colours, height, width), BF16),
        in_specs=[smem()] + [vmem()] * 7,
        out_specs=vmem(),
        scratch_shapes=[
            pltpu.VMEM((3 * height - 2, one, width), BF16),
            pltpu.VMEM((3 * height - 4, one, width), BF16),
            pltpu.VMEM((3 * half - 2, one, width // 2), BF16),
            pltpu.VMEM((3 * half - 4, two, width // 2), BF16),
            pltpu.VMEM((3 * half - 6, two, width // 2), BF16),
            pltpu.VMEM((height + 4, one + two, width), BF16),
            pltpu.VMEM((height + 2, one, width), BF16),
            pltpu.VMEM((colours, height, width), F32),
        ],
        compiler_params=params(),
        cost_estimate=pl.CostEstimate(
            flops=3_000_000_000, bytes_accessed=2 * 1024 * 1024, transcendentals=500_000
        ),
        name="unet",
    )(where, field, w_in, w_mid, w_down, w_deep, w_up, w_out)


def on_device(
    bricks, sends, cells, fracs, sample_order, pending, w_in, w_mid, w_down, w_deep, w_up, w_out
):
    n_tile = lax.axis_size("tile")
    tile = lax.axis_index("tile")
    n_section = lax.axis_size("section")
    cap = sends.shape[3]
    height = pending.shape[2]
    width = pending.shape[3]
    samples = cells.shape[3]
    slots = n_tile * cap
    per_slot = samples // slots
    padded = -(-per_slot // BLOCK) * BLOCK

    def fill(part):
        if padded != per_slot:
            part = part.reshape(3, slots, per_slot)
            part = jnp.pad(part, ((0, 0), (0, 0), (0, padded - per_slot)))
        return part.reshape(3, slots * padded // LANES, LANES)

    def trim(found):
        if padded == per_slot:
            return found
        return found.reshape(slots, padded)[:, :per_slot].reshape(1, samples // LANES, LANES)

    down = [(i, i + 1) for i in range(n_tile - 1)]
    up = [(i + 1, i) for i in range(n_tile - 1)]
    over = lax.ppermute(pending, "tile", down)
    under = lax.ppermute(pending, "tile", up)
    places = positions(fill(cells), fill(fracs), n_tile)
    arrived = lax.all_to_all(places, "tile", split_axis=0, concat_axis=0, tiled=True)

    windows = windows_of(bricks)
    field = jnp.concatenate([over[0], pending[0], under[0]], axis=1).transpose(1, 0, 2)
    field = jnp.pad(field, ((0, 0), (0, 16 - field.shape[1]), (0, 0)))
    colours = w_out.shape[1]
    where = jnp.stack([tile, jnp.int32(n_tile)]).astype(jnp.int32)
    denoised = unet(
        where,
        field,
        jnp.pad(w_in, ((0, 0), (0, 0), (0, 16 - w_in.shape[2]))),
        w_mid,
        w_down,
        w_deep,
        w_up,
        jnp.pad(w_out, ((0, 0), (0, 16 - colours), (0, 0))),
        colours,
    )

    found = sample_values(sends, windows, arrived, denoised)
    values = lax.all_to_all(found, "tile", split_axis=0, concat_axis=0, tiled=True)
    rendered = gbuffer(trim(values), sample_order, height, width)
    ring = [(i, (i + 1) % n_section) for i in range(n_section)]
    handoff = lax.ppermute(rendered, "section", ring)
    return (handoff, denoised)


def solution(mesh):
    in_specs = (
        P("tile", None),
        P("section", "tile", None, None),
        P("section", "tile", None, None),
        P("section", "tile", None, None),
        P("section", "tile", None, None),
        P("section", None, "tile", None),
        P(),
        P(),
        P(),
        P(),
        P(),
        P(),
    )
    out_specs = (P("section", None, "tile", None), P("section", None, "tile", None))
    return jax.shard_map(
        on_device, mesh=mesh, in_specs=in_specs, out_specs=out_specs, check_vma=False
    )
```

```python
import functools

import jax
import jax.numpy as jnp
from jax import lax
from jax.experimental import pallas as pl
from jax.experimental.pallas import tpu as pltpu
from jax.sharding import PartitionSpec as P

EDGE = 34
NSP = 4
NRAY = 8
NOS = 2
LANES = 128
BLOCK = 256
STRIDE = 6
WINDOWS = 6
MAIN = 32
TAIL = 16
BRICK_ROWS = WINDOWS * MAIN + TAIL
KDIM = 256

F32 = jnp.float32
BF16 = jnp.bfloat16
MIB = 1024 * 1024


def params(mib):
    return pltpu.CompilerParams(vmem_limit_bytes=mib * MIB)


def vmem():
    return pl.BlockSpec(memory_space=pltpu.VMEM)


def smem():
    return pl.BlockSpec(memory_space=pltpu.SMEM)


def positions_kernel(cells_ref, fracs_ref, out_ref, cells, fracs, arrivals):
    owners, rows, _ = out_ref.shape
    lines = rows // 3
    copies = []
    for axis in range(3):
        for number, (source, target) in enumerate(((cells_ref, cells), (fracs_ref, fracs))):
            copy = pltpu.make_async_copy(
                source.at[axis], target.at[axis], arrivals.at[2 * axis + number]
            )
            copy.start()
            copies.append(copy)
    for axis in range(3):
        copies[2 * axis].wait()
        copies[2 * axis + 1].wait()
        place = cells[axis].astype(F32) + fracs[axis]
        out_ref[:, axis * lines : (axis + 1) * lines, :] = place.reshape(owners, lines, LANES)


def positions(cells, fracs, owners):
    lines = cells.shape[1]
    return pl.pallas_call(
        positions_kernel,
        out_shape=jax.ShapeDtypeStruct((owners, 3 * lines // owners, LANES), F32),
        in_specs=[pl.BlockSpec(memory_space=pltpu.HBM)] * 2,
        out_specs=vmem(),
        scratch_shapes=[
            pltpu.VMEM(cells.shape, jnp.int32),
            pltpu.VMEM(fracs.shape, F32),
            pltpu.SemaphoreType.DMA((6,)),
        ],
        compiler_params=params(12),
        cost_estimate=pl.CostEstimate(
            flops=3 * lines * LANES, bytes_accessed=36 * lines * LANES, transcendentals=0
        ),
        name="positions",
    )(cells, fracs)


def windows_kernel(cube_ref, out_ref, wide, tail):
    count = cube_ref.shape[0]
    plane = EDGE * EDGE
    wide[...] = jnp.zeros_like(wide)
    wide[:, :EDGE, :plane] = cube_ref[...]
    column = lax.broadcasted_iota(jnp.int32, (1, KDIM), 1)
    main = (column // MAIN) * EDGE + column % MAIN
    rest = column - 7 * MAIN
    last = (rest % 8) * EDGE + MAIN + rest // 8
    source = jnp.where(column < 7 * MAIN, main, last)
    unused = (column >= 7 * MAIN) & ((rest % 8 == 7) | (rest >= TAIL))
    source = jnp.where(unused, -(1 << 20), source)
    for window in range(WINDOWS):
        first = window * STRIDE * EDGE
        low = first // LANES * LANES
        length = min(3 * LANES, wide.shape[2] - low)
        place = lax.broadcasted_iota(jnp.int32, (length, KDIM), 0)
        pick = jnp.where(place == source + (first - low), 1.0, 0.0).astype(BF16)
        found = jnp.dot(
            wide[:, :, low : low + length].reshape(-1, length),
            pick,
            preferred_element_type=F32,
        )
        found = found.reshape(count, 48, KDIM)
        out_ref[:, window * MAIN : (window + 1) * MAIN, :] = found[:, :MAIN, :].astype(BF16)
        tail[:, window : window + 1, :] = found[:, MAIN : MAIN + 1, :]
        tail[:, 8 + window : 9 + window, :] = found[:, MAIN + 1 : MAIN + 2, :]
    for row in (6, 7, 14, 15):
        tail[:, row : row + 1, :] = jnp.zeros((count, 1, KDIM), F32)
    out_ref[:, WINDOWS * MAIN :, :] = tail[...].astype(BF16)


def windows_of(bricks):
    count = bricks.shape[0]
    cube = bricks.reshape(count, EDGE, EDGE * EDGE)
    return pl.pallas_call(
        windows_kernel,
        out_shape=jax.ShapeDtypeStruct((count, BRICK_ROWS, KDIM), BF16),
        in_specs=[vmem()],
        out_specs=vmem(),
        scratch_shapes=[
            pltpu.VMEM((count, 48, 10 * LANES), BF16),
            pltpu.VMEM((count, TAIL, KDIM), F32),
        ],
        compiler_params=params(16),
        cost_estimate=pl.CostEstimate(
            flops=2 * count * 48 * 384 * KDIM * WINDOWS, bytes_accessed=4 * 1024 * 1024,
            transcendentals=0,
        ),
        name="brick_windows",
    )(cube)


def hat(distance):
    return jnp.maximum(1.0 - jnp.abs(distance), 0.0)


def blend(brick, px, py, pz):
    width = px.shape[1]
    places = lax.broadcasted_iota(jnp.int32, (MAIN, width), 0).astype(F32)
    eight = lax.broadcasted_iota(jnp.int32, (8, width), 0).astype(F32)
    places_low = places.astype(BF16)

    def tile(line):
        return jnp.broadcast_to(line, (TAIL, width)).astype(BF16)

    cell_y = jnp.floor(py)
    frac_y = py - cell_y
    both = MAIN // TAIL
    lower = jnp.concatenate([tile(cell_y)] * both, axis=0)
    low_share = jnp.concatenate([tile(1.0 - frac_y)] * both, axis=0)
    high_share = jnp.concatenate([tile(frac_y)] * both, axis=0)
    nothing = jnp.zeros((MAIN, width), BF16)
    offset = places_low - lower
    weight_y = jnp.where(
        offset == 0, low_share, jnp.where(offset == 1, high_share, nothing)
    )
    weight_z = hat(places - pz)
    window = jnp.clip(jnp.floor(px * (1.0 / STRIDE)), 0.0, WINDOWS - 1.0)
    weight_x = hat(eight - (px - STRIDE * window))
    parts = []
    for i in range(STRIDE + 1):
        share = tile(weight_x[i : i + 1])
        parts.append(weight_y * jnp.concatenate([share] * both, axis=0))
    parts.append(
        jnp.concatenate(
            [weight_x * hat(MAIN - py), weight_x * hat(MAIN + 1 - py)], axis=0
        ).astype(BF16)
    )
    parts.append(jnp.zeros((TAIL, width), BF16))
    plane = jnp.concatenate(parts, axis=0)
    found = jnp.dot(brick, plane, preferred_element_type=F32)
    chosen = found[:MAIN]
    for other in range(1, WINDOWS):
        chosen = jnp.where(
            window == float(other), found[other * MAIN : (other + 1) * MAIN], chosen
        )
    total = (chosen * weight_z).reshape(MAIN // 8, 8, width).sum(axis=0)
    base = WINDOWS * MAIN
    edges = found[base : base + 8] * hat(MAIN - pz) + found[base + 8 :] * hat(MAIN + 1 - pz)
    total = total + jnp.where(eight == window, edges, 0.0)
    return jnp.sum(total, axis=0, keepdims=True)


def samples_kernel(picks_ref, brick_ref, place_ref, after_ref, out_ref, values):
    owners, rows, _ = place_ref.shape
    cap = picks_ref.shape[3]
    lines = rows // 3
    per_slot = lines // 2 // cap

    def one_slot(slot, carry):
        renderer = slot // cap
        piece = slot % cap
        brick = brick_ref[picks_ref[0, 0, renderer, piece]]
        for step in range(per_slot):
            row = 2 * (piece * per_slot + step)

            def line(axis):
                both = [
                    place_ref[renderer, pl.ds(axis * lines + row + half, 1), :]
                    for half in range(2)
                ]
                return jnp.concatenate(both, axis=1)

            value = blend(brick, line(0), line(1), line(2))
            for half in range(2):
                values[renderer, pl.ds(row + half, 1), :] = value[
                    :, half * LANES : (half + 1) * LANES
                ]
        return carry

    lax.fori_loop(0, owners * cap, one_slot, 0)
    out_ref[...] = values[...].astype(BF16)


def sample_values(picks, windows, places, after):
    owners, rows, _ = places.shape
    samples = owners * rows * LANES // 3
    shape = (owners, rows // 3, LANES)
    return pl.pallas_call(
        samples_kernel,
        out_shape=jax.ShapeDtypeStruct(shape, BF16),
        in_specs=[smem(), vmem(), vmem(), vmem()],
        out_specs=vmem(),
        scratch_shapes=[pltpu.VMEM(shape, F32)],
        compiler_params=params(16),
        cost_estimate=pl.CostEstimate(
            flops=2 * samples * KDIM * BRICK_ROWS, bytes_accessed=3 * 1024 * 1024,
            transcendentals=0,
        ),
        name="sample_values",
    )(picks, windows, places, after)


def gbuffer_kernel(value_ref, order_ref, out_ref, values):
    values[...] = value_ref[...].astype(F32).reshape(values.shape)
    height = out_ref.shape[2]

    def ray_of(number):
        rows_now = slice(number * height, (number + 1) * height)
        first, second = (
            values[pl.ds(2 * number * height + half, height, stride=2), :] for half in range(2)
        )
        parts = []
        for half in range(2):
            order = order_ref[0, 0, rows_now, half * LANES : (half + 1) * LANES]
            inner = order & (LANES - 1)
            parts.append(
                jnp.where(
                    order < LANES,
                    jnp.take_along_axis(first, inner, axis=1, mode="promise_in_bounds"),
                    jnp.take_along_axis(second, inner, axis=1, mode="promise_in_bounds"),
                )
            )
        return jnp.concatenate(parts, axis=1)

    remain = 1.0
    shade = 0.0
    depth = 0.0
    for step in range(NSP):
        ray = ray_of(step)
        half_tanh = 0.5 * jnp.tanh(ray)
        weight = remain * (0.5 + half_tanh)
        shade = shade + weight * ray
        depth = depth + weight * ((step + 1) / NSP)
        remain = remain * (0.5 - half_tanh)
    occlusion = 0.0
    for ray_number in range(NRAY):
        passing = 1.0
        for step in range(NOS):
            ray = ray_of(NSP + ray_number * NOS + step)
            passing = passing * (0.5 - 0.5 * jnp.tanh(ray))
        occlusion = occlusion + passing
    out_ref[0, 0] = shade.astype(BF16)
    out_ref[0, 1] = (1.0 - remain).astype(BF16)
    out_ref[0, 2] = depth.astype(BF16)
    out_ref[0, 3] = (occlusion * (1.0 / NRAY)).astype(BF16)


def gbuffer(values, order, height, width):
    total = order.shape[2]
    return pl.pallas_call(
        gbuffer_kernel,
        out_shape=jax.ShapeDtypeStruct((1, 4, height, width), BF16),
        in_specs=[vmem(), vmem()],
        out_specs=vmem(),
        scratch_shapes=[pltpu.VMEM((2 * total, LANES), F32)],
        compiler_params=params(16),
        cost_estimate=pl.CostEstimate(
            flops=20 * total * BLOCK, bytes_accessed=8 * total * BLOCK, transcendentals=0
        ),
        name="gbuffer",
    )(values, order)


def silu(field):
    half = 0.5 * field
    return half + half * jnp.tanh(half)


def shifted(rows, steps):
    lane = lax.broadcasted_iota(jnp.int32, (1, LANES), 1)
    edge = lane == (0 if steps == 1 else LANES - 1)
    moved = []
    for row in rows:
        tiles = [row[:, i : i + LANES] for i in range(0, row.shape[1], LANES)]
        tiles = [pltpu.roll(tile, steps % LANES, 1) for tile in tiles]
        for i, tile in enumerate(tiles):
            source = i - steps
            fill = tiles[source] if 0 <= source < len(tiles) else 0.0
            moved.append(jnp.where(edge, fill, tile))
    return jnp.concatenate(moved, axis=1)


def across(total, chans, row_width):
    left, middle, right = (total[i * chans : (i + 1) * chans] for i in range(3))

    def rows_of(part):
        return [part[:, i : i + row_width] for i in range(0, part.shape[1], row_width)]

    return middle + shifted(rows_of(left), 1) + shifted(rows_of(right), -1)


def taps(weight_ref, tap):
    _, out_chans, chans = weight_ref.shape
    return weight_ref[3 * tap : 3 * tap + 3].reshape(3 * out_chans, chans)


def beside(weight_ref):
    return jnp.concatenate([taps(weight_ref, tap) for tap in range(3)], axis=1)


def unet_kernel(
    where_ref, x_ref, w_in, w_mid, w_down, w_deep, w_up, w_out, out_ref, token_ref,
    first, second, pooled, third, fourth, joined, fifth, final,
):
    height = out_ref.shape[2]
    half_height = height // 2
    width = out_ref.shape[3]
    half_width = width // 2
    token_ref[...] = jnp.zeros_like(token_ref)
    above = jnp.where(where_ref[0] > 0, 1.0, 0.0)
    below = jnp.where(where_ref[0] < where_ref[1] - 1, 1.0, 0.0)

    def inside(row, low, high):
        return jnp.where(row < low, above, jnp.where(row >= high, below, 1.0))

    def full_layer(weight, source, target, low, high, unroll):
        chans = target.shape[1]
        depth = weight.shape[1]

        def step(row, carry):
            lines = source[pl.ds(row, 3)].reshape(depth, width)
            line = across(jnp.dot(weight, lines, preferred_element_type=F32), chans, width)
            target[row] = (silu(line) * inside(row, low, high)).astype(BF16)
            return carry

        lax.fori_loop(0, target.shape[0], step, 0, unroll=unroll)

    full_layer(beside(w_in), x_ref, first, height - 1, 2 * height - 1, first.shape[0] // 2)
    full_layer(beside(w_mid), first, second, height - 2, 2 * height - 2, second.shape[0] // 2)

    place = lax.broadcasted_iota(jnp.int32, (width, half_width), 0) // 2
    target = lax.broadcasted_iota(jnp.int32, (width, half_width), 1)
    shrink = jnp.where(place == target, 0.25, 0.0).astype(BF16)
    count, chans = second.shape[0], second.shape[1]
    pairs = jnp.dot(
        second[...].reshape(count * chans, width), shrink, preferred_element_type=F32
    ).reshape(count // 2, 2, chans, half_width)
    pooled[...] = (pairs[:, 0] + pairs[:, 1]).astype(BF16)

    def half_pair(source, row, tap):
        return jnp.concatenate([source[row + tap], source[row + tap + 1]], axis=1)

    def half_layer(product, target, low, high):
        chans = target.shape[1]
        for row in range(0, target.shape[0], 2):
            both = silu(across(product(row), chans, half_width))
            for now in range(2):
                line = both[:, now * half_width : (now + 1) * half_width]
                if row + now < low or row + now >= high:
                    line = line * inside(row + now, low, high)
                target[row + now] = line.astype(BF16)

    weight_down = beside(w_down)

    def down_product(row):
        lines = jnp.concatenate([half_pair(pooled, row, tap) for tap in range(3)], axis=0)
        return jnp.dot(weight_down, lines, preferred_element_type=F32)

    def deep_product(row):
        total = None
        for tap in range(3):
            part = jnp.dot(
                taps(w_deep, tap), half_pair(third, row, tap), preferred_element_type=F32
            )
            total = part if total is None else total + part
        return total

    half_layer(down_product, third, half_height - 2, 2 * half_height - 2)
    half_layer(deep_product, fourth, half_height - 3, 2 * half_height - 3)

    place = lax.broadcasted_iota(jnp.int32, (half_width, width), 0)
    target = lax.broadcasted_iota(jnp.int32, (half_width, width), 1) // 2
    spread = jnp.where(place == target, 1.0, 0.0).astype(BF16)
    deep = fourth.shape[1]
    wide = jnp.dot(
        fourth[...].reshape(-1, half_width), spread, preferred_element_type=F32
    ).astype(BF16).reshape(fourth.shape[0], deep, width)
    for row in range(2 * fourth.shape[0]):
        joined[row, chans:, :] = wide[row // 2]
        joined[row, :chans, :] = second[row + 4]

    def up_step(row, carry):
        total = None
        for tap in range(3):
            part = jnp.dot(taps(w_up, tap), joined[row + tap], preferred_element_type=F32)
            total = part if total is None else total + part
        line = silu(across(total, chans, width))
        fifth[row] = (line * inside(row, 1, height + 1)).astype(BF16)
        return carry

    lax.fori_loop(0, fifth.shape[0], up_step, 0, unroll=fifth.shape[0] // 2)

    colours = out_ref.shape[1]
    weight_out = beside(w_out)
    for row in range(height):
        lines = fifth[row : row + 3].reshape(3 * chans, width)
        total = jnp.dot(weight_out, lines, preferred_element_type=F32)
        line = across(total, w_out.shape[1], width)
        for colour in range(colours):
            final[colour, row : row + 1, :] = line[colour : colour + 1, :]
    out_ref[0] = final[...].astype(BF16)


def unet(where, field, w_in, w_mid, w_down, w_deep, w_up, w_out, colours):
    height = field.shape[0] // 3
    half = height // 2
    width = field.shape[2]
    one, two = w_mid.shape[1], w_deep.shape[1]
    return pl.pallas_call(
        unet_kernel,
        out_shape=(
            jax.ShapeDtypeStruct((1, colours, height, width), BF16),
            jax.ShapeDtypeStruct((8, LANES), F32),
        ),
        in_specs=[smem()] + [vmem()] * 7,
        out_specs=(vmem(), vmem()),
        scratch_shapes=[
            pltpu.VMEM((3 * height - 2, one, width), BF16),
            pltpu.VMEM((3 * height - 4, one, width), BF16),
            pltpu.VMEM((3 * half - 2, one, width // 2), BF16),
            pltpu.VMEM((3 * half - 4, two, width // 2), BF16),
            pltpu.VMEM((3 * half - 6, two, width // 2), BF16),
            pltpu.VMEM((height + 4, one + two, width), BF16),
            pltpu.VMEM((height + 2, one, width), BF16),
            pltpu.VMEM((colours, height, width), F32),
        ],
        compiler_params=params(20),
        cost_estimate=pl.CostEstimate(
            flops=3_000_000_000, bytes_accessed=2 * 1024 * 1024, transcendentals=500_000
        ),
        name="unet",
    )(where, field, w_in, w_mid, w_down, w_deep, w_up, w_out)


def on_device(
    bricks, sends, cells, fracs, sample_order, pending, w_in, w_mid, w_down, w_deep, w_up, w_out
):
    n_tile = lax.axis_size("tile")
    tile = lax.axis_index("tile")
    n_section = lax.axis_size("section")
    cap = sends.shape[3]
    height = pending.shape[2]
    width = pending.shape[3]
    samples = cells.shape[3]
    slots = n_tile * cap
    per_slot = samples // slots
    padded = -(-per_slot // BLOCK) * BLOCK

    def fill(part):
        if padded != per_slot:
            part = part.reshape(3, slots, per_slot)
            part = jnp.pad(part, ((0, 0), (0, 0), (0, padded - per_slot)))
        return part.reshape(3, slots * padded // LANES, LANES)

    def trim(found):
        if padded == per_slot:
            return found
        return found.reshape(slots, padded)[:, :per_slot].reshape(1, samples // LANES, LANES)

    down = [(i, i + 1) for i in range(n_tile - 1)]
    up = [(i + 1, i) for i in range(n_tile - 1)]
    over = lax.ppermute(pending, "tile", down)
    under = lax.ppermute(pending, "tile", up)
    places = positions(fill(cells), fill(fracs), n_tile)
    arrived = lax.all_to_all(places, "tile", split_axis=0, concat_axis=0, tiled=True)

    windows = windows_of(bricks)
    field = jnp.concatenate([over[0], pending[0], under[0]], axis=1).transpose(1, 0, 2)
    field = jnp.pad(field, ((0, 0), (0, 16 - field.shape[1]), (0, 0)))
    colours = w_out.shape[1]
    where = jnp.stack([tile, jnp.int32(n_tile)]).astype(jnp.int32)
    denoised, token = unet(
        where,
        field,
        jnp.pad(w_in, ((0, 0), (0, 0), (0, 16 - w_in.shape[2]))),
        w_mid,
        w_down,
        w_deep,
        w_up,
        jnp.pad(w_out, ((0, 0), (0, 16 - colours), (0, 0))),
        colours,
    )

    found = sample_values(sends, windows, arrived, token)
    values = lax.all_to_all(found, "tile", split_axis=0, concat_axis=0, tiled=True)
    rendered = gbuffer(trim(values), sample_order, height, width)
    ring = [(i, (i + 1) % n_section) for i in range(n_section)]
    handoff = lax.ppermute(rendered, "section", ring)
    return (handoff, denoised)


def solution(mesh):
    in_specs = (
        P("tile", None),
        P("section", "tile", None, None),
        P("section", "tile", None, None),
        P("section", "tile", None, None),
        P("section", "tile", None, None),
        P("section", None, "tile", None),
        P(),
        P(),
        P(),
        P(),
        P(),
        P(),
    )
    out_specs = (P("section", None, "tile", None), P("section", None, "tile", None))
    return jax.shard_map(
        on_device, mesh=mesh, in_specs=in_specs, out_specs=out_specs, check_vma=False
    )
```

```python
import functools

import jax
import jax.numpy as jnp
from jax import lax
from jax.experimental import pallas as pl
from jax.experimental.pallas import tpu as pltpu
from jax.sharding import PartitionSpec as P

EDGE = 34
NSP = 4
NRAY = 8
NOS = 2
LANES = 128
BLOCK = 256
STRIDE = 6
WINDOWS = 6
MAIN = 32
TAIL = 16
BRICK_ROWS = WINDOWS * MAIN + TAIL
KDIM = 256
RING = 8

F32 = jnp.float32
BF16 = jnp.bfloat16
MIB = 1024 * 1024


def params(mib):
    return pltpu.CompilerParams(vmem_limit_bytes=mib * MIB)


def vmem():
    return pl.BlockSpec(memory_space=pltpu.VMEM)


def smem():
    return pl.BlockSpec(memory_space=pltpu.SMEM)


def positions_kernel(cells_ref, fracs_ref, out_ref, cells, fracs, arrivals):
    owners, rows, _ = out_ref.shape
    lines = rows // 3
    copies = []
    for axis in range(3):
        for number, (source, target) in enumerate(((cells_ref, cells), (fracs_ref, fracs))):
            copy = pltpu.make_async_copy(
                source.at[axis], target.at[axis], arrivals.at[2 * axis + number]
            )
            copy.start()
            copies.append(copy)
    for axis in range(3):
        copies[2 * axis].wait()
        copies[2 * axis + 1].wait()
        place = cells[axis].astype(F32) + fracs[axis]
        out_ref[:, axis * lines : (axis + 1) * lines, :] = place.reshape(owners, lines, LANES)


def positions(cells, fracs, owners):
    lines = cells.shape[1]
    return pl.pallas_call(
        positions_kernel,
        out_shape=jax.ShapeDtypeStruct((owners, 3 * lines // owners, LANES), F32),
        in_specs=[pl.BlockSpec(memory_space=pltpu.HBM)] * 2,
        out_specs=vmem(),
        scratch_shapes=[
            pltpu.VMEM(cells.shape, jnp.int32),
            pltpu.VMEM(fracs.shape, F32),
            pltpu.SemaphoreType.DMA((6,)),
        ],
        compiler_params=params(60),
        cost_estimate=pl.CostEstimate(
            flops=3 * lines * LANES, bytes_accessed=36 * lines * LANES, transcendentals=0
        ),
        name="positions",
    )(cells, fracs)


def windows_kernel(cube_ref, out_ref, wide, found_all, tail, departures):
    count = cube_ref.shape[0]
    plane = EDGE * EDGE
    wide[...] = jnp.zeros_like(wide)
    wide[:, :EDGE, :plane] = cube_ref[...]
    column = lax.broadcasted_iota(jnp.int32, (1, KDIM), 1)
    main = (column // MAIN) * EDGE + column % MAIN
    rest = column - 7 * MAIN
    last = (rest % 8) * EDGE + MAIN + rest // 8
    source = jnp.where(column < 7 * MAIN, main, last)
    unused = (column >= 7 * MAIN) & ((rest % 8 == 7) | (rest >= TAIL))
    source = jnp.where(unused, -(1 << 20), source)
    copies = []

    def send(start, size):
        rows = pl.ds(start, size)
        copy = pltpu.make_async_copy(
            found_all.at[:, rows], out_ref.at[:, rows], departures.at[len(copies)]
        )
        copy.start()
        copies.append(copy)

    for window in range(WINDOWS):
        first = window * STRIDE * EDGE
        low = first // LANES * LANES
        length = min(3 * LANES, wide.shape[2] - low)
        place = lax.broadcasted_iota(jnp.int32, (length, KDIM), 0)
        pick = jnp.where(place == source + (first - low), 1.0, 0.0).astype(BF16)
        found = jnp.dot(
            wide[:, :, low : low + length].reshape(-1, length),
            pick,
            preferred_element_type=F32,
        )
        found = found.reshape(count, 48, KDIM)
        found_all[:, window * MAIN : (window + 1) * MAIN, :] = found[:, :MAIN, :].astype(BF16)
        tail[:, window : window + 1, :] = found[:, MAIN : MAIN + 1, :]
        tail[:, 8 + window : 9 + window, :] = found[:, MAIN + 1 : MAIN + 2, :]
        send(window * MAIN, MAIN)
    for row in (6, 7, 14, 15):
        tail[:, row : row + 1, :] = jnp.zeros((count, 1, KDIM), F32)
    found_all[:, WINDOWS * MAIN :, :] = tail[...].astype(BF16)
    send(WINDOWS * MAIN, TAIL)
    for copy in copies:
        copy.wait()


def windows_of(bricks):
    count = bricks.shape[0]
    cube = bricks.reshape(count, EDGE, EDGE * EDGE)
    shape = (count, BRICK_ROWS, KDIM)
    return pl.pallas_call(
        windows_kernel,
        out_shape=jax.ShapeDtypeStruct(shape, BF16),
        in_specs=[vmem()],
        out_specs=pl.BlockSpec(memory_space=pltpu.HBM),
        scratch_shapes=[
            pltpu.VMEM((count, 48, 10 * LANES), BF16),
            pltpu.VMEM(shape, BF16),
            pltpu.VMEM((count, TAIL, KDIM), F32),
            pltpu.SemaphoreType.DMA((WINDOWS + 1,)),
        ],
        compiler_params=params(60),
        cost_estimate=pl.CostEstimate(
            flops=2 * count * 48 * 384 * KDIM * WINDOWS, bytes_accessed=4 * MIB,
            transcendentals=0,
        ),
        name="brick_windows",
    )(cube)


def hat(distance):
    return jnp.maximum(1.0 - jnp.abs(distance), 0.0)


def blend(brick, px, py, pz):
    width = px.shape[1]
    places = lax.broadcasted_iota(jnp.int32, (MAIN, width), 0).astype(F32)
    eight = lax.broadcasted_iota(jnp.int32, (8, width), 0).astype(F32)
    places_low = places.astype(BF16)

    def tile(line):
        return jnp.broadcast_to(line, (TAIL, width)).astype(BF16)

    cell_y = jnp.floor(py)
    frac_y = py - cell_y
    both = MAIN // TAIL
    lower = jnp.concatenate([tile(cell_y)] * both, axis=0)
    low_share = jnp.concatenate([tile(1.0 - frac_y)] * both, axis=0)
    high_share = jnp.concatenate([tile(frac_y)] * both, axis=0)
    nothing = jnp.zeros((MAIN, width), BF16)
    offset = places_low - lower
    weight_y = jnp.where(
        offset == 0, low_share, jnp.where(offset == 1, high_share, nothing)
    )
    weight_z = hat(places - pz)
    window = jnp.clip(jnp.floor(px * (1.0 / STRIDE)), 0.0, WINDOWS - 1.0)
    weight_x = hat(eight - (px - STRIDE * window))
    parts = []
    for i in range(STRIDE + 1):
        share = tile(weight_x[i : i + 1])
        parts.append(weight_y * jnp.concatenate([share] * both, axis=0))
    parts.append(
        jnp.concatenate(
            [weight_x * hat(MAIN - py), weight_x * hat(MAIN + 1 - py)], axis=0
        ).astype(BF16)
    )
    parts.append(jnp.zeros((TAIL, width), BF16))
    plane = jnp.concatenate(parts, axis=0)
    found = jnp.dot(brick, plane, preferred_element_type=F32)
    chosen = found[:MAIN]
    for other in range(1, WINDOWS):
        chosen = jnp.where(
            window == float(other), found[other * MAIN : (other + 1) * MAIN], chosen
        )
    total = (chosen * weight_z).reshape(MAIN // 8, 8, width).sum(axis=0)
    base = WINDOWS * MAIN
    edges = found[base : base + 8] * hat(MAIN - pz) + found[base + 8 :] * hat(MAIN + 1 - pz)
    total = total + jnp.where(eight == window, edges, 0.0)
    return jnp.sum(total, axis=0, keepdims=True)


def samples_kernel(
    picks_ref, brick_ref, place_ref, after_ref, out_ref, values, ring, arrivals
):
    owners, rows, _ = place_ref.shape
    cap = picks_ref.shape[0]
    slots = owners * cap
    lines = rows // 3
    per_slot = lines // 2 // cap

    def fetch(slot):
        held = slot % RING
        return pltpu.make_async_copy(
            brick_ref.at[picks_ref[slot % cap, slot // cap]], ring.at[held], arrivals.at[held]
        )

    for slot in range(RING):
        fetch(slot).start()

    def one_slot(slot, carry):
        renderer = slot // cap
        piece = slot % cap
        held = slot % RING
        fetch(slot).wait()
        brick = ring[held]
        for step in range(per_slot):
            row = 2 * (piece * per_slot + step)

            def line(axis):
                both = [
                    place_ref[renderer, pl.ds(axis * lines + row + half, 1), :]
                    for half in range(2)
                ]
                return jnp.concatenate(both, axis=1)

            value = blend(brick, line(0), line(1), line(2))
            for half in range(2):
                values[renderer, pl.ds(row + half, 1), :] = value[
                    :, half * LANES : (half + 1) * LANES
                ]

        @pl.when(slot + RING < slots)
        def _():
            fetch(slot + RING).start()

        return carry

    lax.fori_loop(0, slots, one_slot, 0)
    out_ref[...] = values[...].astype(BF16)


def sample_values(picks, windows, places, after):
    owners, rows, _ = places.shape
    samples = owners * rows * LANES // 3
    shape = (owners, rows // 3, LANES)
    return pl.pallas_call(
        samples_kernel,
        out_shape=jax.ShapeDtypeStruct(shape, BF16),
        in_specs=[smem(), pl.BlockSpec(memory_space=pltpu.HBM), vmem(), vmem()],
        out_specs=vmem(),
        scratch_shapes=[
            pltpu.VMEM(shape, F32),
            pltpu.VMEM((RING, BRICK_ROWS, KDIM), BF16),
            pltpu.SemaphoreType.DMA((RING,)),
        ],
        compiler_params=params(60),
        cost_estimate=pl.CostEstimate(
            flops=2 * samples * KDIM * BRICK_ROWS, bytes_accessed=3 * MIB,
            transcendentals=0,
        ),
        name="sample_values",
    )(picks, windows, places, after)


def gbuffer_kernel(value_ref, order_ref, out_ref, values):
    values[...] = value_ref[...].astype(F32).reshape(values.shape)
    height = out_ref.shape[2]

    def ray_of(number):
        rows_now = slice(number * height, (number + 1) * height)
        first, second = (
            values[pl.ds(2 * number * height + half, height, stride=2), :] for half in range(2)
        )
        parts = []
        for half in range(2):
            order = order_ref[0, 0, rows_now, half * LANES : (half + 1) * LANES]
            inner = order & (LANES - 1)
            parts.append(
                jnp.where(
                    order < LANES,
                    jnp.take_along_axis(first, inner, axis=1, mode="promise_in_bounds"),
                    jnp.take_along_axis(second, inner, axis=1, mode="promise_in_bounds"),
                )
            )
        return jnp.concatenate(parts, axis=1)

    remain = 1.0
    shade = 0.0
    depth = 0.0
    for step in range(NSP):
        ray = ray_of(step)
        half_tanh = 0.5 * jnp.tanh(ray)
        weight = remain * (0.5 + half_tanh)
        shade = shade + weight * ray
        depth = depth + weight * ((step + 1) / NSP)
        remain = remain * (0.5 - half_tanh)
    occlusion = 0.0
    for ray_number in range(NRAY):
        passing = 1.0
        for step in range(NOS):
            ray = ray_of(NSP + ray_number * NOS + step)
            passing = passing * (0.5 - 0.5 * jnp.tanh(ray))
        occlusion = occlusion + passing
    out_ref[0, 0] = shade.astype(BF16)
    out_ref[0, 1] = (1.0 - remain).astype(BF16)
    out_ref[0, 2] = depth.astype(BF16)
    out_ref[0, 3] = (occlusion * (1.0 / NRAY)).astype(BF16)


def gbuffer(values, order, height, width):
    total = order.shape[2]
    return pl.pallas_call(
        gbuffer_kernel,
        out_shape=jax.ShapeDtypeStruct((1, 4, height, width), BF16),
        in_specs=[vmem(), vmem()],
        out_specs=vmem(),
        scratch_shapes=[pltpu.VMEM((2 * total, LANES), F32)],
        compiler_params=params(16),
        cost_estimate=pl.CostEstimate(
            flops=20 * total * BLOCK, bytes_accessed=8 * total * BLOCK, transcendentals=0
        ),
        name="gbuffer",
    )(values, order)


def silu(field):
    half = 0.5 * field
    return half + half * jnp.tanh(half)


def shifted(rows, steps):
    lane = lax.broadcasted_iota(jnp.int32, (1, LANES), 1)
    edge = lane == (0 if steps == 1 else LANES - 1)
    moved = []
    for row in rows:
        tiles = [row[:, i : i + LANES] for i in range(0, row.shape[1], LANES)]
        tiles = [pltpu.roll(tile, steps % LANES, 1) for tile in tiles]
        for i, tile in enumerate(tiles):
            source = i - steps
            fill = tiles[source] if 0 <= source < len(tiles) else 0.0
            moved.append(jnp.where(edge, fill, tile))
    return jnp.concatenate(moved, axis=1)


def across(total, chans, row_width):
    left, middle, right = (total[i * chans : (i + 1) * chans] for i in range(3))

    def rows_of(part):
        return [part[:, i : i + row_width] for i in range(0, part.shape[1], row_width)]

    return middle + shifted(rows_of(left), 1) + shifted(rows_of(right), -1)


def taps(weight_ref, tap):
    _, out_chans, chans = weight_ref.shape
    return weight_ref[3 * tap : 3 * tap + 3].reshape(3 * out_chans, chans)


def beside(weight_ref):
    return jnp.concatenate([taps(weight_ref, tap) for tap in range(3)], axis=1)


def unet_kernel(
    where_ref, band_ref, w_in, w_mid, w_down, w_deep, w_up, w_out, out_ref, token_ref,
    x_ref, first, second, pooled, third, fourth, joined, fifth, final,
):
    height = out_ref.shape[2]
    half_height = height // 2
    width = out_ref.shape[3]
    half_width = width // 2
    token_ref[...] = jnp.zeros_like(token_ref)
    above = jnp.where(where_ref[0] > 0, 1.0, 0.0)
    below = jnp.where(where_ref[0] < where_ref[1] - 1, 1.0, 0.0)

    def inside(row, low, high):
        return jnp.where(row < low, above, jnp.where(row >= high, below, 1.0))

    def full_layer(weight, source, target, low, high, unroll):
        chans = target.shape[1]
        depth = weight.shape[1]

        def step(row, carry):
            lines = source[pl.ds(row, 3)].reshape(depth, width)
            line = across(jnp.dot(weight, lines, preferred_element_type=F32), chans, width)
            target[row] = (silu(line) * inside(row, low, high)).astype(BF16)
            return carry

        lax.fori_loop(0, target.shape[0], step, 0, unroll=unroll)

    tile = where_ref[0]
    last = where_ref[1] - 1
    inputs = band_ref.shape[1]
    x_ref[...] = jnp.zeros_like(x_ref)
    for part in range(3):
        neighbour = jnp.clip(tile + part - 1, 0, last)
        share = (above, 1.0, below)[part]
        lines = band_ref[pl.ds(neighbour * height, height)].astype(F32) * share
        x_ref[part * height : (part + 1) * height, :inputs, :] = lines.astype(BF16)

    full_layer(beside(w_in), x_ref, first, height - 1, 2 * height - 1, first.shape[0] // 2)
    full_layer(beside(w_mid), first, second, height - 2, 2 * height - 2, second.shape[0] // 2)

    place = lax.broadcasted_iota(jnp.int32, (width, half_width), 0) // 2
    target = lax.broadcasted_iota(jnp.int32, (width, half_width), 1)
    shrink = jnp.where(place == target, 0.25, 0.0).astype(BF16)
    count, chans = second.shape[0], second.shape[1]
    pairs = jnp.dot(
        second[...].reshape(count * chans, width), shrink, preferred_element_type=F32
    ).reshape(count // 2, 2, chans, half_width)
    pooled[...] = (pairs[:, 0] + pairs[:, 1]).astype(BF16)

    def half_pair(source, row, tap):
        return jnp.concatenate([source[row + tap], source[row + tap + 1]], axis=1)

    def half_layer(product, target, low, high):
        chans = target.shape[1]
        for row in range(0, target.shape[0], 2):
            both = silu(across(product(row), chans, half_width))
            for now in range(2):
                line = both[:, now * half_width : (now + 1) * half_width]
                if row + now < low or row + now >= high:
                    line = line * inside(row + now, low, high)
                target[row + now] = line.astype(BF16)

    weight_down = beside(w_down)

    def down_product(row):
        lines = jnp.concatenate([half_pair(pooled, row, tap) for tap in range(3)], axis=0)
        return jnp.dot(weight_down, lines, preferred_element_type=F32)

    def deep_product(row):
        total = None
        for tap in range(3):
            part = jnp.dot(
                taps(w_deep, tap), half_pair(third, row, tap), preferred_element_type=F32
            )
            total = part if total is None else total + part
        return total

    half_layer(down_product, third, half_height - 2, 2 * half_height - 2)
    half_layer(deep_product, fourth, half_height - 3, 2 * half_height - 3)

    place = lax.broadcasted_iota(jnp.int32, (half_width, width), 0)
    target = lax.broadcasted_iota(jnp.int32, (half_width, width), 1) // 2
    spread = jnp.where(place == target, 1.0, 0.0).astype(BF16)
    deep = fourth.shape[1]
    wide = jnp.dot(
        fourth[...].reshape(-1, half_width), spread, preferred_element_type=F32
    ).astype(BF16).reshape(fourth.shape[0], deep, width)
    for row in range(2 * fourth.shape[0]):
        joined[row, chans:, :] = wide[row // 2]
        joined[row, :chans, :] = second[row + 4]

    def up_step(row, carry):
        total = None
        for tap in range(3):
            part = jnp.dot(taps(w_up, tap), joined[row + tap], preferred_element_type=F32)
            total = part if total is None else total + part
        line = silu(across(total, chans, width))
        fifth[row] = (line * inside(row, 1, height + 1)).astype(BF16)
        return carry

    lax.fori_loop(0, fifth.shape[0], up_step, 0, unroll=fifth.shape[0] // 2)

    colours = out_ref.shape[1]
    weight_out = beside(w_out)
    for row in range(height):
        lines = fifth[row : row + 3].reshape(3 * chans, width)
        total = jnp.dot(weight_out, lines, preferred_element_type=F32)
        line = across(total, w_out.shape[1], width)
        for colour in range(colours):
            final[colour, row : row + 1, :] = line[colour : colour + 1, :]
    out_ref[0] = final[...].astype(BF16)


def unet(where, band, height, w_in, w_mid, w_down, w_deep, w_up, w_out, colours):
    half = height // 2
    width = band.shape[2]
    one, two = w_mid.shape[1], w_deep.shape[1]
    return pl.pallas_call(
        unet_kernel,
        out_shape=(
            jax.ShapeDtypeStruct((1, colours, height, width), BF16),
            jax.ShapeDtypeStruct((8, LANES), F32),
        ),
        in_specs=[smem()] + [vmem()] * 7,
        out_specs=(vmem(), vmem()),
        scratch_shapes=[
            pltpu.VMEM((3 * height, w_in.shape[2], width), BF16),
            pltpu.VMEM((3 * height - 2, one, width), BF16),
            pltpu.VMEM((3 * height - 4, one, width), BF16),
            pltpu.VMEM((3 * half - 2, one, width // 2), BF16),
            pltpu.VMEM((3 * half - 4, two, width // 2), BF16),
            pltpu.VMEM((3 * half - 6, two, width // 2), BF16),
            pltpu.VMEM((height + 4, one + two, width), BF16),
            pltpu.VMEM((height + 2, one, width), BF16),
            pltpu.VMEM((colours, height, width), F32),
        ],
        compiler_params=params(20),
        cost_estimate=pl.CostEstimate(
            flops=3_000_000_000, bytes_accessed=2 * 1024 * 1024, transcendentals=500_000
        ),
        name="unet",
    )(where, band, w_in, w_mid, w_down, w_deep, w_up, w_out)


def on_device(
    bricks, sends, cells, fracs, sample_order, pending, w_in, w_mid, w_down, w_deep, w_up, w_out
):
    n_tile = lax.axis_size("tile")
    tile = lax.axis_index("tile")
    n_section = lax.axis_size("section")
    cap = sends.shape[3]
    height = pending.shape[2]
    width = pending.shape[3]
    samples = cells.shape[3]
    slots = n_tile * cap
    per_slot = samples // slots
    padded = -(-per_slot // BLOCK) * BLOCK

    def fill(part):
        if padded != per_slot:
            part = part.reshape(3, slots, per_slot)
            part = jnp.pad(part, ((0, 0), (0, 0), (0, padded - per_slot)))
        return part.reshape(3, slots * padded // LANES, LANES)

    def trim(found):
        if padded == per_slot:
            return found
        return found.reshape(slots, padded)[:, :per_slot].reshape(1, samples // LANES, LANES)

    places = positions(fill(cells), fill(fracs), n_tile)
    arrived = lax.all_to_all(places, "tile", split_axis=0, concat_axis=0, tiled=True)

    own_rows = pending[0].transpose(1, 0, 2)
    band = lax.all_gather(own_rows, "tile", axis=0, tiled=True)
    windows = windows_of(bricks)
    colours = w_out.shape[1]
    where = jnp.stack([tile, jnp.int32(n_tile)]).astype(jnp.int32)
    denoised, token = unet(
        where,
        band,
        height,
        jnp.pad(w_in, ((0, 0), (0, 0), (0, 16 - w_in.shape[2]))),
        w_mid,
        w_down,
        w_deep,
        w_up,
        jnp.pad(w_out, ((0, 0), (0, 16 - colours), (0, 0))),
        colours,
    )

    found = sample_values(sends[0, 0].T, windows, arrived, token)
    values = lax.all_to_all(found, "tile", split_axis=0, concat_axis=0, tiled=True)
    rendered = gbuffer(trim(values), sample_order, height, width)
    ring = [(i, (i + 1) % n_section) for i in range(n_section)]
    handoff = lax.ppermute(rendered, "section", ring)
    return (handoff, denoised)


def solution(mesh):
    in_specs = (
        P("tile", None),
        P("section", "tile", None, None),
        P("section", "tile", None, None),
        P("section", "tile", None, None),
        P("section", "tile", None, None),
        P("section", None, "tile", None),
        P(),
        P(),
        P(),
        P(),
        P(),
        P(),
    )
    out_specs = (P("section", None, "tile", None), P("section", None, "tile", None))
    return jax.shard_map(
        on_device, mesh=mesh, in_specs=in_specs, out_specs=out_specs, check_vma=False
    )
```

```python
import functools

import jax
import jax.numpy as jnp
from jax import lax
from jax.experimental import pallas as pl
from jax.experimental.pallas import tpu as pltpu
from jax.sharding import PartitionSpec as P

EDGE = 34
NSP = 4
NRAY = 8
NOS = 2
LANES = 128
BLOCK = 256
STRIDE = 6
WINDOWS = 6
MAIN = 32
TAIL = 16
BRICK_ROWS = WINDOWS * MAIN + TAIL
KDIM = 256

F32 = jnp.float32
BF16 = jnp.bfloat16
MIB = 1024 * 1024


def params(mib):
    return pltpu.CompilerParams(vmem_limit_bytes=mib * MIB)


def vmem():
    return pl.BlockSpec(memory_space=pltpu.VMEM)


def smem():
    return pl.BlockSpec(memory_space=pltpu.SMEM)


def positions_kernel(cells_ref, fracs_ref, out_ref, cells, fracs, arrivals):
    owners, rows, _ = out_ref.shape
    lines = rows // 3
    copies = []
    for axis in range(3):
        for number, (source, target) in enumerate(((cells_ref, cells), (fracs_ref, fracs))):
            copy = pltpu.make_async_copy(
                source.at[axis], target.at[axis], arrivals.at[2 * axis + number]
            )
            copy.start()
            copies.append(copy)
    for axis in range(3):
        copies[2 * axis].wait()
        copies[2 * axis + 1].wait()
        place = cells[axis].astype(F32) + fracs[axis]
        out_ref[:, axis * lines : (axis + 1) * lines, :] = place.reshape(owners, lines, LANES)


def positions(cells, fracs, owners):
    lines = cells.shape[1]
    return pl.pallas_call(
        positions_kernel,
        out_shape=jax.ShapeDtypeStruct((owners, 3 * lines // owners, LANES), F32),
        in_specs=[pl.BlockSpec(memory_space=pltpu.HBM)] * 2,
        out_specs=vmem(),
        scratch_shapes=[
            pltpu.VMEM(cells.shape, jnp.int32),
            pltpu.VMEM(fracs.shape, F32),
            pltpu.SemaphoreType.DMA((6,)),
        ],
        compiler_params=params(60),
        cost_estimate=pl.CostEstimate(
            flops=3 * lines * LANES, bytes_accessed=800 * lines * LANES, transcendentals=0
        ),
        name="positions",
    )(cells, fracs)


def windows_kernel(cube_ref, out_ref, wide, tail):
    count = cube_ref.shape[0]
    plane = EDGE * EDGE
    wide[...] = jnp.zeros_like(wide)
    wide[:, :EDGE, :plane] = cube_ref[...]
    column = lax.broadcasted_iota(jnp.int32, (1, KDIM), 1)
    main = (column // MAIN) * EDGE + column % MAIN
    rest = column - 7 * MAIN
    last = (rest % 8) * EDGE + MAIN + rest // 8
    source = jnp.where(column < 7 * MAIN, main, last)
    unused = (column >= 7 * MAIN) & ((rest % 8 == 7) | (rest >= TAIL))
    source = jnp.where(unused, -(1 << 20), source)
    for window in range(WINDOWS):
        first = window * STRIDE * EDGE
        low = first // LANES * LANES
        length = min(3 * LANES, wide.shape[2] - low)
        place = lax.broadcasted_iota(jnp.int32, (length, KDIM), 0)
        pick = jnp.where(place == source + (first - low), 1.0, 0.0).astype(BF16)
        found = jnp.dot(
            wide[:, :, low : low + length].reshape(-1, length),
            pick,
            preferred_element_type=F32,
        )
        found = found.reshape(count, 48, KDIM)
        out_ref[:, window * MAIN : (window + 1) * MAIN, :] = found[:, :MAIN, :].astype(BF16)
        tail[:, window : window + 1, :] = found[:, MAIN : MAIN + 1, :]
        tail[:, 8 + window : 9 + window, :] = found[:, MAIN + 1 : MAIN + 2, :]
    for row in (6, 7, 14, 15):
        tail[:, row : row + 1, :] = jnp.zeros((count, 1, KDIM), F32)
    out_ref[:, WINDOWS * MAIN :, :] = tail[...].astype(BF16)


def windows_of(bricks):
    count = bricks.shape[0]
    cube = bricks.reshape(count, EDGE, EDGE * EDGE)
    return pl.pallas_call(
        windows_kernel,
        out_shape=jax.ShapeDtypeStruct((count, BRICK_ROWS, KDIM), BF16),
        in_specs=[vmem()],
        out_specs=vmem(),
        scratch_shapes=[
            pltpu.VMEM((count, 48, 10 * LANES), BF16),
            pltpu.VMEM((count, TAIL, KDIM), F32),
        ],
        compiler_params=params(16),
        cost_estimate=pl.CostEstimate(
            flops=2 * count * 48 * 384 * KDIM * WINDOWS, bytes_accessed=4 * 1024 * 1024,
            transcendentals=0,
        ),
        name="brick_windows",
    )(cube)


def hat(distance):
    return jnp.maximum(1.0 - jnp.abs(distance), 0.0)


def blend(brick, px, py, pz):
    width = px.shape[1]
    places = lax.broadcasted_iota(jnp.int32, (MAIN, width), 0).astype(F32)
    eight = lax.broadcasted_iota(jnp.int32, (8, width), 0).astype(F32)
    places_low = places.astype(BF16)

    def tile(line):
        return jnp.broadcast_to(line, (TAIL, width)).astype(BF16)

    cell_y = jnp.floor(py)
    frac_y = py - cell_y
    both = MAIN // TAIL
    lower = jnp.concatenate([tile(cell_y)] * both, axis=0)
    low_share = jnp.concatenate([tile(1.0 - frac_y)] * both, axis=0)
    high_share = jnp.concatenate([tile(frac_y)] * both, axis=0)
    nothing = jnp.zeros((MAIN, width), BF16)
    offset = places_low - lower
    weight_y = jnp.where(
        offset == 0, low_share, jnp.where(offset == 1, high_share, nothing)
    )
    weight_z = hat(places - pz)
    window = jnp.clip(jnp.floor(px * (1.0 / STRIDE)), 0.0, WINDOWS - 1.0)
    weight_x = hat(eight - (px - STRIDE * window))
    parts = []
    for i in range(STRIDE + 1):
        share = tile(weight_x[i : i + 1])
        parts.append(weight_y * jnp.concatenate([share] * both, axis=0))
    parts.append(
        jnp.concatenate(
            [weight_x * hat(MAIN - py), weight_x * hat(MAIN + 1 - py)], axis=0
        ).astype(BF16)
    )
    parts.append(jnp.zeros((TAIL, width), BF16))
    plane = jnp.concatenate(parts, axis=0)
    found = jnp.dot(brick, plane, preferred_element_type=F32)
    chosen = found[:MAIN]
    for other in range(1, WINDOWS):
        chosen = jnp.where(
            window == float(other), found[other * MAIN : (other + 1) * MAIN], chosen
        )
    total = (chosen * weight_z).reshape(MAIN // 8, 8, width).sum(axis=0)
    base = WINDOWS * MAIN
    edges = found[base : base + 8] * hat(MAIN - pz) + found[base + 8 :] * hat(MAIN + 1 - pz)
    total = total + jnp.where(eight == window, edges, 0.0)
    return jnp.sum(total, axis=0, keepdims=True)


def samples_kernel(picks_ref, brick_ref, place_ref, after_ref, out_ref, values):
    owners, rows, _ = place_ref.shape
    cap = picks_ref.shape[0]
    lines = rows // 3
    per_slot = lines // 2 // cap

    def one_slot(slot, carry):
        renderer = slot // cap
        piece = slot % cap
        brick = brick_ref[picks_ref[piece, renderer]]
        for step in range(per_slot):
            row = 2 * (piece * per_slot + step)

            def line(axis):
                both = [
                    place_ref[renderer, pl.ds(axis * lines + row + half, 1), :]
                    for half in range(2)
                ]
                return jnp.concatenate(both, axis=1)

            value = blend(brick, line(0), line(1), line(2))
            for half in range(2):
                values[renderer, pl.ds(row + half, 1), :] = value[
                    :, half * LANES : (half + 1) * LANES
                ]
        return carry

    lax.fori_loop(0, owners * cap, one_slot, 0)
    out_ref[...] = values[...].astype(BF16)


def sample_values(picks, windows, places, after):
    owners, rows, _ = places.shape
    samples = owners * rows * LANES // 3
    shape = (owners, rows // 3, LANES)
    return pl.pallas_call(
        samples_kernel,
        out_shape=jax.ShapeDtypeStruct(shape, BF16),
        in_specs=[smem(), vmem(), vmem(), vmem()],
        out_specs=vmem(),
        scratch_shapes=[pltpu.VMEM(shape, F32)],
        compiler_params=params(16),
        cost_estimate=pl.CostEstimate(
            flops=2 * samples * KDIM * BRICK_ROWS, bytes_accessed=3 * 1024 * 1024,
            transcendentals=0,
        ),
        name="sample_values",
    )(picks, windows, places, after)


def gbuffer_kernel(value_ref, order_ref, out_ref, values):
    values[...] = value_ref[...].astype(F32).reshape(values.shape)
    height = out_ref.shape[2]

    def ray_of(number):
        rows_now = slice(number * height, (number + 1) * height)
        first, second = (
            values[pl.ds(2 * number * height + half, height, stride=2), :] for half in range(2)
        )
        parts = []
        for half in range(2):
            order = order_ref[0, 0, rows_now, half * LANES : (half + 1) * LANES]
            inner = order & (LANES - 1)
            parts.append(
                jnp.where(
                    order < LANES,
                    jnp.take_along_axis(first, inner, axis=1, mode="promise_in_bounds"),
                    jnp.take_along_axis(second, inner, axis=1, mode="promise_in_bounds"),
                )
            )
        return jnp.concatenate(parts, axis=1)

    remain = 1.0
    shade = 0.0
    depth = 0.0
    for step in range(NSP):
        ray = ray_of(step)
        half_tanh = 0.5 * jnp.tanh(ray)
        weight = remain * (0.5 + half_tanh)
        shade = shade + weight * ray
        depth = depth + weight * ((step + 1) / NSP)
        remain = remain * (0.5 - half_tanh)
    occlusion = 0.0
    for ray_number in range(NRAY):
        passing = 1.0
        for step in range(NOS):
            ray = ray_of(NSP + ray_number * NOS + step)
            passing = passing * (0.5 - 0.5 * jnp.tanh(ray))
        occlusion = occlusion + passing
    out_ref[0, 0] = shade.astype(BF16)
    out_ref[0, 1] = (1.0 - remain).astype(BF16)
    out_ref[0, 2] = depth.astype(BF16)
    out_ref[0, 3] = (occlusion * (1.0 / NRAY)).astype(BF16)


def gbuffer(values, order, height, width):
    total = order.shape[2]
    return pl.pallas_call(
        gbuffer_kernel,
        out_shape=jax.ShapeDtypeStruct((1, 4, height, width), BF16),
        in_specs=[vmem(), vmem()],
        out_specs=vmem(),
        scratch_shapes=[pltpu.VMEM((2 * total, LANES), F32)],
        compiler_params=params(16),
        cost_estimate=pl.CostEstimate(
            flops=20 * total * BLOCK, bytes_accessed=8 * total * BLOCK, transcendentals=0
        ),
        name="gbuffer",
    )(values, order)


def silu(field):
    half = 0.5 * field
    return half + half * jnp.tanh(half)


def shifted(rows, steps):
    lane = lax.broadcasted_iota(jnp.int32, (1, LANES), 1)
    edge = lane == (0 if steps == 1 else LANES - 1)
    moved = []
    for row in rows:
        tiles = [row[:, i : i + LANES] for i in range(0, row.shape[1], LANES)]
        tiles = [pltpu.roll(tile, steps % LANES, 1) for tile in tiles]
        for i, tile in enumerate(tiles):
            source = i - steps
            fill = tiles[source] if 0 <= source < len(tiles) else 0.0
            moved.append(jnp.where(edge, fill, tile))
    return jnp.concatenate(moved, axis=1)


def across(total, chans, row_width):
    left, middle, right = (total[i * chans : (i + 1) * chans] for i in range(3))

    def rows_of(part):
        return [part[:, i : i + row_width] for i in range(0, part.shape[1], row_width)]

    return middle + shifted(rows_of(left), 1) + shifted(rows_of(right), -1)


def taps(weight_ref, tap):
    _, out_chans, chans = weight_ref.shape
    return weight_ref[3 * tap : 3 * tap + 3].reshape(3 * out_chans, chans)


def beside(weight_ref):
    return jnp.concatenate([taps(weight_ref, tap) for tap in range(3)], axis=1)


def unet_kernel(
    where_ref, x_ref, w_in, w_mid, w_down, w_deep, w_up, w_out, out_ref, token_ref,
    first, second, pooled, third, fourth, joined, fifth, final,
):
    height = out_ref.shape[2]
    half_height = height // 2
    width = out_ref.shape[3]
    half_width = width // 2
    token_ref[...] = jnp.zeros_like(token_ref)
    above = jnp.where(where_ref[0] > 0, 1.0, 0.0)
    below = jnp.where(where_ref[0] < where_ref[1] - 1, 1.0, 0.0)

    def inside(row, low, high):
        return jnp.where(row < low, above, jnp.where(row >= high, below, 1.0))

    def full_layer(weight, source, target, low, high, unroll):
        chans = target.shape[1]
        depth = weight.shape[1]

        def step(row, carry):
            lines = source[pl.ds(row, 3)].reshape(depth, width)
            line = across(jnp.dot(weight, lines, preferred_element_type=F32), chans, width)
            target[row] = (silu(line) * inside(row, low, high)).astype(BF16)
            return carry

        lax.fori_loop(0, target.shape[0], step, 0, unroll=unroll)

    full_layer(beside(w_in), x_ref, first, height - 1, 2 * height - 1, first.shape[0] // 2)
    full_layer(beside(w_mid), first, second, height - 2, 2 * height - 2, second.shape[0] // 2)

    place = lax.broadcasted_iota(jnp.int32, (width, half_width), 0) // 2
    target = lax.broadcasted_iota(jnp.int32, (width, half_width), 1)
    shrink = jnp.where(place == target, 0.25, 0.0).astype(BF16)
    count, chans = second.shape[0], second.shape[1]
    pairs = jnp.dot(
        second[...].reshape(count * chans, width), shrink, preferred_element_type=F32
    ).reshape(count // 2, 2, chans, half_width)
    pooled[...] = (pairs[:, 0] + pairs[:, 1]).astype(BF16)

    def half_pair(source, row, tap):
        return jnp.concatenate([source[row + tap], source[row + tap + 1]], axis=1)

    def half_layer(product, target, low, high):
        chans = target.shape[1]
        for row in range(0, target.shape[0], 2):
            both = silu(across(product(row), chans, half_width))
            for now in range(2):
                line = both[:, now * half_width : (now + 1) * half_width]
                if row + now < low or row + now >= high:
                    line = line * inside(row + now, low, high)
                target[row + now] = line.astype(BF16)

    weight_down = beside(w_down)

    def down_product(row):
        lines = jnp.concatenate([half_pair(pooled, row, tap) for tap in range(3)], axis=0)
        return jnp.dot(weight_down, lines, preferred_element_type=F32)

    def deep_product(row):
        total = None
        for tap in range(3):
            part = jnp.dot(
                taps(w_deep, tap), half_pair(third, row, tap), preferred_element_type=F32
            )
            total = part if total is None else total + part
        return total

    half_layer(down_product, third, half_height - 2, 2 * half_height - 2)
    half_layer(deep_product, fourth, half_height - 3, 2 * half_height - 3)

    place = lax.broadcasted_iota(jnp.int32, (half_width, width), 0)
    target = lax.broadcasted_iota(jnp.int32, (half_width, width), 1) // 2
    spread = jnp.where(place == target, 1.0, 0.0).astype(BF16)
    deep = fourth.shape[1]
    wide = jnp.dot(
        fourth[...].reshape(-1, half_width), spread, preferred_element_type=F32
    ).astype(BF16).reshape(fourth.shape[0], deep, width)
    for row in range(2 * fourth.shape[0]):
        joined[row, chans:, :] = wide[row // 2]
        joined[row, :chans, :] = second[row + 4]

    def up_step(row, carry):
        total = None
        for tap in range(3):
            part = jnp.dot(taps(w_up, tap), joined[row + tap], preferred_element_type=F32)
            total = part if total is None else total + part
        line = silu(across(total, chans, width))
        fifth[row] = (line * inside(row, 1, height + 1)).astype(BF16)
        return carry

    lax.fori_loop(0, fifth.shape[0], up_step, 0, unroll=fifth.shape[0] // 2)

    colours = out_ref.shape[1]
    weight_out = beside(w_out)
    for row in range(height):
        lines = fifth[row : row + 3].reshape(3 * chans, width)
        total = jnp.dot(weight_out, lines, preferred_element_type=F32)
        line = across(total, w_out.shape[1], width)
        for colour in range(colours):
            final[colour, row : row + 1, :] = line[colour : colour + 1, :]
    out_ref[0] = final[...].astype(BF16)


def unet(where, field, w_in, w_mid, w_down, w_deep, w_up, w_out, colours):
    height = field.shape[0] // 3
    half = height // 2
    width = field.shape[2]
    one, two = w_mid.shape[1], w_deep.shape[1]
    return pl.pallas_call(
        unet_kernel,
        out_shape=(
            jax.ShapeDtypeStruct((1, colours, height, width), BF16),
            jax.ShapeDtypeStruct((8, LANES), F32),
        ),
        in_specs=[smem()] + [vmem()] * 7,
        out_specs=(vmem(), vmem()),
        scratch_shapes=[
            pltpu.VMEM((3 * height - 2, one, width), BF16),
            pltpu.VMEM((3 * height - 4, one, width), BF16),
            pltpu.VMEM((3 * half - 2, one, width // 2), BF16),
            pltpu.VMEM((3 * half - 4, two, width // 2), BF16),
            pltpu.VMEM((3 * half - 6, two, width // 2), BF16),
            pltpu.VMEM((height + 4, one + two, width), BF16),
            pltpu.VMEM((height + 2, one, width), BF16),
            pltpu.VMEM((colours, height, width), F32),
        ],
        compiler_params=params(20),
        cost_estimate=pl.CostEstimate(
            flops=3_000_000_000, bytes_accessed=2 * 1024 * 1024, transcendentals=500_000
        ),
        name="unet",
    )(where, field, w_in, w_mid, w_down, w_deep, w_up, w_out)


def on_device(
    bricks, sends, cells, fracs, sample_order, pending, w_in, w_mid, w_down, w_deep, w_up, w_out
):
    n_tile = lax.axis_size("tile")
    tile = lax.axis_index("tile")
    n_section = lax.axis_size("section")
    cap = sends.shape[3]
    height = pending.shape[2]
    width = pending.shape[3]
    samples = cells.shape[3]
    slots = n_tile * cap
    per_slot = samples // slots
    padded = -(-per_slot // BLOCK) * BLOCK

    def fill(part):
        if padded != per_slot:
            part = part.reshape(3, slots, per_slot)
            part = jnp.pad(part, ((0, 0), (0, 0), (0, padded - per_slot)))
        return part.reshape(3, slots * padded // LANES, LANES)

    def trim(found):
        if padded == per_slot:
            return found
        return found.reshape(slots, padded)[:, :per_slot].reshape(1, samples // LANES, LANES)

    down = [(i, i + 1) for i in range(n_tile - 1)]
    up = [(i + 1, i) for i in range(n_tile - 1)]
    over = lax.ppermute(pending, "tile", down)
    under = lax.ppermute(pending, "tile", up)
    places = positions(fill(cells), fill(fracs), n_tile)
    places, over, under, bricks = lax.optimization_barrier((places, over, under, bricks))
    arrived = lax.all_to_all(places, "tile", split_axis=0, concat_axis=0, tiled=True)

    windows = windows_of(bricks)
    field = jnp.concatenate([over[0], pending[0], under[0]], axis=1).transpose(1, 0, 2)
    field = jnp.pad(field, ((0, 0), (0, 16 - field.shape[1]), (0, 0)))
    colours = w_out.shape[1]
    where = jnp.stack([tile, jnp.int32(n_tile)]).astype(jnp.int32)
    denoised, token = unet(
        where,
        field,
        jnp.pad(w_in, ((0, 0), (0, 0), (0, 16 - w_in.shape[2]))),
        w_mid,
        w_down,
        w_deep,
        w_up,
        jnp.pad(w_out, ((0, 0), (0, 16 - colours), (0, 0))),
        colours,
    )

    found = sample_values(sends[0, 0].T, windows, arrived, token)
    values = lax.all_to_all(found, "tile", split_axis=0, concat_axis=0, tiled=True)
    rendered = gbuffer(trim(values), sample_order, height, width)
    ring = [(i, (i + 1) % n_section) for i in range(n_section)]
    handoff = lax.ppermute(rendered, "section", ring)
    return (handoff, denoised)


def solution(mesh):
    in_specs = (
        P("tile", None),
        P("section", "tile", None, None),
        P("section", "tile", None, None),
        P("section", "tile", None, None),
        P("section", "tile", None, None),
        P("section", None, "tile", None),
        P(),
        P(),
        P(),
        P(),
        P(),
        P(),
    )
    out_specs = (P("section", None, "tile", None), P("section", None, "tile", None))
    return jax.shard_map(
        on_device, mesh=mesh, in_specs=in_specs, out_specs=out_specs, check_vma=False
    )
```

```python
import functools

import jax
import jax.numpy as jnp
from jax import lax
from jax.experimental import pallas as pl
from jax.experimental.pallas import tpu as pltpu
from jax.sharding import PartitionSpec as P

EDGE = 34
NSP = 4
NRAY = 8
NOS = 2
LANES = 128
BLOCK = 256
STRIDE = 6
WINDOWS = 6
MAIN = 32
TAIL = 16
BRICK_ROWS = WINDOWS * MAIN + TAIL
KDIM = 256

F32 = jnp.float32
BF16 = jnp.bfloat16
MIB = 1024 * 1024


def params(mib):
    return pltpu.CompilerParams(vmem_limit_bytes=mib * MIB)


def vmem():
    return pl.BlockSpec(memory_space=pltpu.VMEM)


def smem():
    return pl.BlockSpec(memory_space=pltpu.SMEM)


def positions_kernel(cells_ref, fracs_ref, out_ref, cells, fracs, arrivals):
    owners, rows, _ = out_ref.shape
    lines = rows // 3
    copies = []
    for axis in range(3):
        for number, (source, target) in enumerate(((cells_ref, cells), (fracs_ref, fracs))):
            copy = pltpu.make_async_copy(
                source.at[axis], target.at[axis], arrivals.at[2 * axis + number]
            )
            copy.start()
            copies.append(copy)
    for axis in range(3):
        copies[2 * axis].wait()
        copies[2 * axis + 1].wait()
        place = cells[axis].astype(F32) + fracs[axis]
        out_ref[:, axis * lines : (axis + 1) * lines, :] = place.reshape(owners, lines, LANES)


def positions(cells, fracs, owners):
    lines = cells.shape[1]
    return pl.pallas_call(
        positions_kernel,
        out_shape=jax.ShapeDtypeStruct((owners, 3 * lines // owners, LANES), F32),
        in_specs=[pl.BlockSpec(memory_space=pltpu.HBM)] * 2,
        out_specs=vmem(),
        scratch_shapes=[
            pltpu.VMEM(cells.shape, jnp.int32),
            pltpu.VMEM(fracs.shape, F32),
            pltpu.SemaphoreType.DMA((6,)),
        ],
        compiler_params=params(60),
        cost_estimate=pl.CostEstimate(
            flops=3 * lines * LANES, bytes_accessed=800 * lines * LANES, transcendentals=0
        ),
        name="positions",
    )(cells, fracs)


def windows_kernel(cube_ref, out_ref, wide, tail):
    count = cube_ref.shape[0]
    plane = EDGE * EDGE
    wide[...] = jnp.zeros_like(wide)
    wide[:, :EDGE, :plane] = cube_ref[...]
    column = lax.broadcasted_iota(jnp.int32, (1, KDIM), 1)
    main = (column // MAIN) * EDGE + column % MAIN
    rest = column - 7 * MAIN
    last = (rest % 8) * EDGE + MAIN + rest // 8
    source = jnp.where(column < 7 * MAIN, main, last)
    unused = (column >= 7 * MAIN) & ((rest % 8 == 7) | (rest >= TAIL))
    source = jnp.where(unused, -(1 << 20), source)
    for window in range(WINDOWS):
        first = window * STRIDE * EDGE
        low = first // LANES * LANES
        length = min(3 * LANES, wide.shape[2] - low)
        place = lax.broadcasted_iota(jnp.int32, (length, KDIM), 0)
        pick = jnp.where(place == source + (first - low), 1.0, 0.0).astype(BF16)
        found = jnp.dot(
            wide[:, :, low : low + length].reshape(-1, length),
            pick,
            preferred_element_type=F32,
        )
        found = found.reshape(count, 48, KDIM)
        out_ref[:, window * MAIN : (window + 1) * MAIN, :] = found[:, :MAIN, :].astype(BF16)
        tail[:, window : window + 1, :] = found[:, MAIN : MAIN + 1, :]
        tail[:, 8 + window : 9 + window, :] = found[:, MAIN + 1 : MAIN + 2, :]
    for row in (6, 7, 14, 15):
        tail[:, row : row + 1, :] = jnp.zeros((count, 1, KDIM), F32)
    out_ref[:, WINDOWS * MAIN :, :] = tail[...].astype(BF16)


def windows_of(bricks):
    count = bricks.shape[0]
    cube = bricks.reshape(count, EDGE, EDGE * EDGE)
    return pl.pallas_call(
        windows_kernel,
        out_shape=jax.ShapeDtypeStruct((count, BRICK_ROWS, KDIM), BF16),
        in_specs=[vmem()],
        out_specs=vmem(),
        scratch_shapes=[
            pltpu.VMEM((count, 48, 10 * LANES), BF16),
            pltpu.VMEM((count, TAIL, KDIM), F32),
        ],
        compiler_params=params(16),
        cost_estimate=pl.CostEstimate(
            flops=2 * count * 48 * 384 * KDIM * WINDOWS, bytes_accessed=4 * 1024 * 1024,
            transcendentals=0,
        ),
        name="brick_windows",
    )(cube)


def hat(distance):
    return jnp.maximum(1.0 - jnp.abs(distance), 0.0)


def blend(brick, px, py, pz):
    width = px.shape[1]
    eight = lax.broadcasted_iota(jnp.int32, (8, width), 0).astype(F32)
    places = lax.broadcasted_iota(jnp.int32, (MAIN, width), 0).astype(F32).astype(BF16)

    def tile(rows):
        return jnp.concatenate([rows, rows], axis=0).astype(BF16)

    cell_y = jnp.floor(py)
    frac_y = py - cell_y
    lower, low_share, high_share = tile(cell_y), tile(1.0 - frac_y), tile(frac_y)
    nothing = jnp.zeros((TAIL, width), BF16)
    weight_y = []
    for start in range(0, MAIN, TAIL):
        offset = places[start : start + TAIL] - lower
        weight_y.append(
            jnp.where(offset == 0, low_share, jnp.where(offset == 1, high_share, nothing))
        )
    window = jnp.floor(px * (1.0 / STRIDE))
    weight_x = hat(eight - (px - STRIDE * window))
    parts = []
    for i in range(STRIDE + 1):
        share = tile(jnp.broadcast_to(weight_x[i : i + 1], (8, width)))
        parts += [share * part for part in weight_y]
    tail = [weight_x * hat(MAIN - py), weight_x * jnp.maximum(py - MAIN, 0.0)]
    parts.append(jnp.concatenate(tail, axis=0).astype(BF16))
    parts.append(nothing)
    plane = jnp.concatenate(parts, axis=0)
    found = jnp.dot(brick, plane, preferred_element_type=F32)
    groups = range(0, MAIN, 8)
    chosen = [found[row : row + 8] for row in groups]
    for other in range(1, WINDOWS):
        here = window == float(other)
        base = other * MAIN
        chosen = [
            jnp.where(here, found[base + row : base + row + 8], old)
            for row, old in zip(groups, chosen)
        ]
    base = WINDOWS * MAIN
    edges = found[base : base + 8] * hat(MAIN - pz)
    edges = edges + found[base + 8 :] * jnp.maximum(pz - MAIN, 0.0)
    total = jnp.where(eight == window, edges, 0.0)
    for row, part in zip(groups, chosen):
        total = total + part * hat((eight + float(row)) - pz)
    return total


def samples_kernel(
    picks_ref, brick_ref, place_ref, out_ref, token_ref, bricks, places, sums, arrivals
):
    owners, rows, _ = place_ref.shape
    cap = picks_ref.shape[0]
    lines = rows // 3
    per_slot = lines // 2 // cap
    token_ref[...] = jnp.zeros_like(token_ref)

    def fetches(renderer):
        held = renderer % 2
        copies = [
            pltpu.make_async_copy(
                place_ref.at[renderer], places.at[held], arrivals.at[held, cap]
            )
        ]
        for piece in range(cap):
            copies.append(
                pltpu.make_async_copy(
                    brick_ref.at[picks_ref[piece, renderer]],
                    bricks.at[held, piece],
                    arrivals.at[held, piece],
                )
            )
        return copies

    for renderer in range(2):
        for copy in fetches(renderer):
            copy.start()

    def one_renderer(renderer, carry):
        held = renderer % 2
        copies = fetches(renderer)
        copies[0].wait()
        for piece in range(cap):
            copies[1 + piece].wait()
            brick = bricks[held, piece]
            for step in range(per_slot):
                row = 2 * (piece * per_slot + step)

                def line(axis):
                    both = [
                        jnp.broadcast_to(
                            places[held, pl.ds(axis * lines + row + half, 1), :], (8, LANES)
                        )
                        for half in range(2)
                    ]
                    return jnp.concatenate(both, axis=1)

                total = blend(brick, line(0), line(1), line(2))
                for half in range(2):
                    sums[8 * (row + half) : 8 * (row + half + 1), :] = total[
                        :, half * LANES : (half + 1) * LANES
                    ]

        @pl.when(renderer + 2 < owners)
        def _():
            for copy in fetches(renderer + 2):
                copy.start()

        values = []
        for row in range(0, lines, 8):
            value = sums[pl.ds(8 * row, 8, stride=8), :]
            for other in range(1, 8):
                value = value + sums[pl.ds(8 * row + other, 8, stride=8), :]
            values.append(value)
        out_ref[renderer] = jnp.concatenate(values, axis=0).astype(BF16)
        return carry

    lax.fori_loop(0, owners, one_renderer, 0)


def sample_values(picks, windows, places):
    owners, rows, _ = places.shape
    cap = picks.shape[0]
    samples = owners * rows * LANES // 3
    hbm = pl.BlockSpec(memory_space=pltpu.HBM)
    return pl.pallas_call(
        samples_kernel,
        out_shape=(
            jax.ShapeDtypeStruct((owners, rows // 3, LANES), BF16),
            jax.ShapeDtypeStruct((8, LANES), F32),
        ),
        in_specs=[smem(), hbm, hbm],
        out_specs=(vmem(), vmem()),
        scratch_shapes=[
            pltpu.VMEM((2, cap, BRICK_ROWS, KDIM), BF16),
            pltpu.VMEM((2, rows, LANES), F32),
            pltpu.VMEM((8 * rows // 3, LANES), F32),
            pltpu.SemaphoreType.DMA((2, cap + 1)),
        ],
        compiler_params=params(60),
        cost_estimate=pl.CostEstimate(
            flops=2 * samples * KDIM * BRICK_ROWS, bytes_accessed=3 * MIB,
            transcendentals=0,
        ),
        name="sample_values",
    )(picks, windows, places)


def gbuffer_kernel(value_ref, order_ref, after_ref, out_ref, token_ref, values):
    token_ref[...] = jnp.zeros_like(token_ref)
    values[...] = value_ref[...].astype(F32).reshape(values.shape)
    height = out_ref.shape[2]

    def ray_of(number):
        rows_now = slice(number * height, (number + 1) * height)
        first, second = (
            values[pl.ds(2 * number * height + half, height, stride=2), :] for half in range(2)
        )
        parts = []
        for half in range(2):
            order = order_ref[0, 0, rows_now, half * LANES : (half + 1) * LANES]
            inner = order & (LANES - 1)
            parts.append(
                jnp.where(
                    order < LANES,
                    jnp.take_along_axis(first, inner, axis=1, mode="promise_in_bounds"),
                    jnp.take_along_axis(second, inner, axis=1, mode="promise_in_bounds"),
                )
            )
        return jnp.concatenate(parts, axis=1)

    remain = 1.0
    shade = 0.0
    depth = 0.0
    for step in range(NSP):
        ray = ray_of(step)
        half_tanh = 0.5 * jnp.tanh(ray)
        weight = remain * (0.5 + half_tanh)
        shade = shade + weight * ray
        depth = depth + weight * ((step + 1) / NSP)
        remain = remain * (0.5 - half_tanh)
    occlusion = 0.0
    for ray_number in range(NRAY):
        passing = 1.0
        for step in range(NOS):
            ray = ray_of(NSP + ray_number * NOS + step)
            passing = passing * (0.5 - 0.5 * jnp.tanh(ray))
        occlusion = occlusion + passing
    out_ref[0, 0] = shade.astype(BF16)
    out_ref[0, 1] = (1.0 - remain).astype(BF16)
    out_ref[0, 2] = depth.astype(BF16)
    out_ref[0, 3] = (occlusion * (1.0 / NRAY)).astype(BF16)


def gbuffer(values, order, after, height, width):
    total = order.shape[2]
    return pl.pallas_call(
        gbuffer_kernel,
        out_shape=(
            jax.ShapeDtypeStruct((1, 4, height, width), BF16),
            jax.ShapeDtypeStruct((8, LANES), F32),
        ),
        in_specs=[vmem()] * 3,
        out_specs=(vmem(), vmem()),
        scratch_shapes=[pltpu.VMEM((2 * total, LANES), F32)],
        compiler_params=params(16),
        cost_estimate=pl.CostEstimate(
            flops=20 * total * BLOCK, bytes_accessed=8 * total * BLOCK, transcendentals=0
        ),
        name="gbuffer",
    )(values, order, after)


def silu(field):
    half = 0.5 * field
    return half + half * jnp.tanh(half)


def shifted(rows, steps):
    lane = lax.broadcasted_iota(jnp.int32, (1, LANES), 1)
    edge = lane == (0 if steps == 1 else LANES - 1)
    moved = []
    for row in rows:
        tiles = [row[:, i : i + LANES] for i in range(0, row.shape[1], LANES)]
        tiles = [pltpu.roll(tile, steps % LANES, 1) for tile in tiles]
        for i, tile in enumerate(tiles):
            source = i - steps
            fill = tiles[source] if 0 <= source < len(tiles) else 0.0
            moved.append(jnp.where(edge, fill, tile))
    return jnp.concatenate(moved, axis=1)


def across(total, chans, row_width):
    left, middle, right = (total[i * chans : (i + 1) * chans] for i in range(3))

    def rows_of(part):
        return [part[:, i : i + row_width] for i in range(0, part.shape[1], row_width)]

    return middle + shifted(rows_of(left), 1) + shifted(rows_of(right), -1)


def taps(weight_ref, tap):
    _, out_chans, chans = weight_ref.shape
    return weight_ref[3 * tap : 3 * tap + 3].reshape(3 * out_chans, chans)


def beside(weight_ref):
    return jnp.concatenate([taps(weight_ref, tap) for tap in range(3)], axis=1)


def sides(where_ref):
    above = jnp.where(where_ref[0] > 0, 1.0, 0.0)
    below = jnp.where(where_ref[0] < where_ref[1] - 1, 1.0, 0.0)

    def inside(row, low, high):
        return jnp.where(row < low, above, jnp.where(row >= high, below, 1.0))

    return inside


def encoder_kernel(
    where_ref, x_ref, w_in, w_mid, w_down, w_deep, after_ref, skip_ref, fourth, token_ref,
    first, second, pooled, third,
):
    height = x_ref.shape[0] // 3
    half_height = height // 2
    width = x_ref.shape[2]
    half_width = width // 2
    inside = sides(where_ref)
    token_ref[...] = jnp.zeros_like(token_ref)

    def full_layer(weight, source, target, low, high, unroll):
        chans = target.shape[1]
        depth = weight.shape[1]

        def step(row, carry):
            lines = source[pl.ds(row, 3)].reshape(depth, width)
            line = across(jnp.dot(weight, lines, preferred_element_type=F32), chans, width)
            target[row] = (silu(line) * inside(row, low, high)).astype(BF16)
            return carry

        lax.fori_loop(0, target.shape[0], step, 0, unroll=unroll)

    full_layer(beside(w_in), x_ref, first, height - 1, 2 * height - 1, first.shape[0] // 2)
    full_layer(beside(w_mid), first, second, height - 2, 2 * height - 2, second.shape[0] // 2)

    place = lax.broadcasted_iota(jnp.int32, (width, half_width), 0) // 2
    target = lax.broadcasted_iota(jnp.int32, (width, half_width), 1)
    shrink = jnp.where(place == target, 0.25, 0.0).astype(BF16)
    count, chans = second.shape[0], second.shape[1]
    pairs = jnp.dot(
        second[...].reshape(count * chans, width), shrink, preferred_element_type=F32
    ).reshape(count // 2, 2, chans, half_width)
    pooled[...] = (pairs[:, 0] + pairs[:, 1]).astype(BF16)

    def half_pair(source, row, tap):
        return jnp.concatenate([source[row + tap], source[row + tap + 1]], axis=1)

    def half_layer(product, target, low, high):
        chans = target.shape[1]
        for row in range(0, target.shape[0], 2):
            both = silu(across(product(row), chans, half_width))
            for now in range(2):
                line = both[:, now * half_width : (now + 1) * half_width]
                if row + now < low or row + now >= high:
                    line = line * inside(row + now, low, high)
                target[row + now] = line.astype(BF16)

    weight_down = beside(w_down)

    def down_product(row):
        lines = jnp.concatenate([half_pair(pooled, row, tap) for tap in range(3)], axis=0)
        return jnp.dot(weight_down, lines, preferred_element_type=F32)

    def deep_product(row):
        total = None
        for tap in range(3):
            part = jnp.dot(
                taps(w_deep, tap), half_pair(third, row, tap), preferred_element_type=F32
            )
            total = part if total is None else total + part
        return total

    half_layer(down_product, third, half_height - 2, 2 * half_height - 2)
    half_layer(deep_product, fourth, half_height - 3, 2 * half_height - 3)

    skip_ref[...] = second[4 : 4 + skip_ref.shape[0]]


def decoder_kernel(
    where_ref, skip_ref, fourth, w_up, w_out, after_ref, out_ref, joined, fifth, final
):
    height = out_ref.shape[2]
    width = out_ref.shape[3]
    half_width = width // 2
    chans = skip_ref.shape[1]
    inside = sides(where_ref)
    place = lax.broadcasted_iota(jnp.int32, (half_width, width), 0)
    target = lax.broadcasted_iota(jnp.int32, (half_width, width), 1) // 2
    spread = jnp.where(place == target, 1.0, 0.0).astype(BF16)
    deep = fourth.shape[1]
    wide = jnp.dot(
        fourth[...].reshape(-1, half_width), spread, preferred_element_type=F32
    ).astype(BF16).reshape(fourth.shape[0], deep, width)
    for row in range(2 * fourth.shape[0]):
        joined[row, chans:, :] = wide[row // 2]
        joined[row, :chans, :] = skip_ref[row]

    def up_step(row, carry):
        total = None
        for tap in range(3):
            part = jnp.dot(taps(w_up, tap), joined[row + tap], preferred_element_type=F32)
            total = part if total is None else total + part
        line = silu(across(total, chans, width))
        fifth[row] = (line * inside(row, 1, height + 1)).astype(BF16)
        return carry

    lax.fori_loop(0, fifth.shape[0], up_step, 0, unroll=fifth.shape[0] // 2)

    colours = out_ref.shape[1]
    weight_out = beside(w_out)
    for row in range(height):
        lines = fifth[row : row + 3].reshape(3 * chans, width)
        total = jnp.dot(weight_out, lines, preferred_element_type=F32)
        line = across(total, w_out.shape[1], width)
        for colour in range(colours):
            final[colour, row : row + 1, :] = line[colour : colour + 1, :]
    out_ref[0] = final[...].astype(BF16)


def encoder(where, field, w_in, w_mid, w_down, w_deep, after):
    height = field.shape[0] // 3
    half = height // 2
    width = field.shape[2]
    one, two = w_mid.shape[1], w_deep.shape[1]
    return pl.pallas_call(
        encoder_kernel,
        out_shape=(
            jax.ShapeDtypeStruct((height + 4, one, width), BF16),
            jax.ShapeDtypeStruct((3 * half - 6, two, width // 2), BF16),
            jax.ShapeDtypeStruct((8, LANES), F32),
        ),
        in_specs=[smem()] + [vmem()] * 6,
        out_specs=(vmem(),) * 3,
        scratch_shapes=[
            pltpu.VMEM((3 * height - 2, one, width), BF16),
            pltpu.VMEM((3 * height - 4, one, width), BF16),
            pltpu.VMEM((3 * half - 2, one, width // 2), BF16),
            pltpu.VMEM((3 * half - 4, two, width // 2), BF16),
        ],
        compiler_params=params(16),
        cost_estimate=pl.CostEstimate(
            flops=2_000_000_000, bytes_accessed=2 * MIB, transcendentals=400_000
        ),
        name="encoder",
    )(where, field, w_in, w_mid, w_down, w_deep, after)


def decoder(where, skip, deep, w_up, w_out, after, height, colours):
    one = skip.shape[1]
    two = deep.shape[1]
    width = skip.shape[2]
    return pl.pallas_call(
        decoder_kernel,
        out_shape=jax.ShapeDtypeStruct((1, colours, height, width), BF16),
        in_specs=[smem()] + [vmem()] * 5,
        out_specs=vmem(),
        scratch_shapes=[
            pltpu.VMEM((height + 4, one + two, width), BF16),
            pltpu.VMEM((height + 2, one, width), BF16),
            pltpu.VMEM((colours, height, width), F32),
        ],
        compiler_params=params(16),
        cost_estimate=pl.CostEstimate(
            flops=1_000_000_000, bytes_accessed=MIB, transcendentals=100_000
        ),
        name="decoder",
    )(where, skip, deep, w_up, w_out, after)


def on_device(
    bricks, sends, cells, fracs, sample_order, pending, w_in, w_mid, w_down, w_deep, w_up, w_out
):
    n_tile = lax.axis_size("tile")
    tile = lax.axis_index("tile")
    n_section = lax.axis_size("section")
    cap = sends.shape[3]
    height = pending.shape[2]
    width = pending.shape[3]
    samples = cells.shape[3]
    slots = n_tile * cap
    per_slot = samples // slots
    padded = -(-per_slot // BLOCK) * BLOCK

    def fill(part):
        if padded != per_slot:
            part = part.reshape(3, slots, per_slot)
            part = jnp.pad(part, ((0, 0), (0, 0), (0, padded - per_slot)))
        return part.reshape(3, slots * padded // LANES, LANES)

    def trim(found):
        if padded == per_slot:
            return found
        return found.reshape(slots, padded)[:, :per_slot].reshape(1, samples // LANES, LANES)

    places = positions(fill(cells), fill(fracs), n_tile)
    places, bricks, pending = lax.optimization_barrier((places, bricks, pending))
    arrived = lax.all_to_all(places, "tile", split_axis=0, concat_axis=0, tiled=True)

    down = [(i, i + 1) for i in range(n_tile - 1)]
    up = [(i + 1, i) for i in range(n_tile - 1)]
    over = lax.ppermute(pending, "tile", down)
    under = lax.ppermute(pending, "tile", up)
    windows = windows_of(bricks)
    field = jnp.concatenate([over[0], pending[0], under[0]], axis=1).transpose(1, 0, 2)
    field = jnp.pad(field, ((0, 0), (0, 16 - field.shape[1]), (0, 0)))
    colours = w_out.shape[1]
    where = jnp.stack([tile, jnp.int32(n_tile)]).astype(jnp.int32)
    w_in = jnp.pad(w_in, ((0, 0), (0, 0), (0, 16 - w_in.shape[2])))
    w_out = jnp.pad(w_out, ((0, 0), (0, 16 - colours), (0, 0)))

    found, sampled = sample_values(sends[0, 0].T, windows, arrived)
    values = lax.all_to_all(found, "tile", split_axis=0, concat_axis=0, tiled=True)
    skip, deep, encoded = encoder(where, field, w_in, w_mid, w_down, w_deep, sampled)
    rendered, drawn = gbuffer(trim(values), sample_order, encoded, height, width)
    ring = [(i, (i + 1) % n_section) for i in range(n_section)]
    handoff = lax.ppermute(rendered, "section", ring)
    denoised = decoder(where, skip, deep, w_up, w_out, drawn, height, colours)
    return (handoff, denoised)


def solution(mesh):
    in_specs = (
        P("tile", None),
        P("section", "tile", None, None),
        P("section", "tile", None, None),
        P("section", "tile", None, None),
        P("section", "tile", None, None),
        P("section", None, "tile", None),
        P(),
        P(),
        P(),
        P(),
        P(),
        P(),
    )
    out_specs = (P("section", None, "tile", None), P("section", None, "tile", None))
    return jax.shard_map(
        on_device, mesh=mesh, in_specs=in_specs, out_specs=out_specs, check_vma=False
    )
```

```python
import functools

import jax
import jax.numpy as jnp
from jax import lax
from jax.experimental import pallas as pl
from jax.experimental.pallas import tpu as pltpu
from jax.sharding import PartitionSpec as P

EDGE = 34
NSP = 4
NRAY = 8
NOS = 2
LANES = 128
BLOCK = 256
STRIDE = 6
WINDOWS = 6
MAIN = 32
TAIL = 16
BRICK_ROWS = WINDOWS * MAIN + TAIL
KDIM = 256

F32 = jnp.float32
BF16 = jnp.bfloat16
MIB = 1024 * 1024


def params(mib):
    return pltpu.CompilerParams(vmem_limit_bytes=mib * MIB)


def vmem():
    return pl.BlockSpec(memory_space=pltpu.VMEM)


def smem():
    return pl.BlockSpec(memory_space=pltpu.SMEM)


def positions_kernel(cells_ref, fracs_ref, out_ref, cells, fracs, found, arrivals, departures):
    owners, rows, _ = out_ref.shape
    lines = rows // 3
    parts = arrivals.shape[1]
    share = owners // parts
    pieces = [(axis, part) for axis in range(3) for part in range(parts)]

    def reads(axis, part):
        span = pl.ds(part * share * lines, share * lines)
        return [
            pltpu.make_async_copy(
                source.at[axis, span], target.at[axis, span], arrivals.at[axis, part, number]
            )
            for number, (source, target) in enumerate(((cells_ref, cells), (fracs_ref, fracs)))
        ]

    def write(axis, part):
        place = (pl.ds(part * share, share), pl.ds(axis * lines, lines))
        return pltpu.make_async_copy(
            found.at[place], out_ref.at[place], departures.at[axis, part]
        )

    for piece in pieces:
        for copy in reads(*piece):
            copy.start()
    for axis, part in pieces:
        for copy in reads(axis, part):
            copy.wait()
        span = slice(part * share * lines, (part + 1) * share * lines)
        place = cells[axis, span].astype(F32) + fracs[axis, span]
        found[part * share : (part + 1) * share, axis * lines : (axis + 1) * lines, :] = (
            place.reshape(share, lines, LANES)
        )
        write(axis, part).start()
    for piece in pieces:
        write(*piece).wait()


def positions(cells, fracs, owners):
    lines = cells.shape[1]
    shape = (owners, 3 * lines // owners, LANES)
    hbm = pl.BlockSpec(memory_space=pltpu.HBM)
    return pl.pallas_call(
        positions_kernel,
        out_shape=jax.ShapeDtypeStruct(shape, F32),
        in_specs=[hbm, hbm],
        out_specs=hbm,
        scratch_shapes=[
            pltpu.VMEM(cells.shape, jnp.int32),
            pltpu.VMEM(fracs.shape, F32),
            pltpu.VMEM(shape, F32),
            pltpu.SemaphoreType.DMA((3, 2, 2)),
            pltpu.SemaphoreType.DMA((3, 2)),
        ],
        compiler_params=params(60),
        cost_estimate=pl.CostEstimate(
            flops=3 * lines * LANES, bytes_accessed=36 * lines * LANES, transcendentals=0
        ),
        name="positions",
    )(cells, fracs)


def windows_kernel(cube_ref, out_ref, wide, tail):
    count = cube_ref.shape[0]
    plane = EDGE * EDGE
    wide[...] = jnp.zeros_like(wide)
    wide[:, :EDGE, :plane] = cube_ref[...]
    column = lax.broadcasted_iota(jnp.int32, (1, KDIM), 1)
    main = (column // MAIN) * EDGE + column % MAIN
    rest = column - 7 * MAIN
    last = (rest % 8) * EDGE + MAIN + rest // 8
    source = jnp.where(column < 7 * MAIN, main, last)
    unused = (column >= 7 * MAIN) & ((rest % 8 == 7) | (rest >= TAIL))
    source = jnp.where(unused, -(1 << 20), source)
    for window in range(WINDOWS):
        first = window * STRIDE * EDGE
        low = first // LANES * LANES
        length = min(3 * LANES, wide.shape[2] - low)
        place = lax.broadcasted_iota(jnp.int32, (length, KDIM), 0)
        pick = jnp.where(place == source + (first - low), 1.0, 0.0).astype(BF16)
        found = jnp.dot(
            wide[:, :, low : low + length].reshape(-1, length),
            pick,
            preferred_element_type=F32,
        )
        found = found.reshape(count, 48, KDIM)
        out_ref[:, window * MAIN : (window + 1) * MAIN, :] = found[:, :MAIN, :].astype(BF16)
        tail[:, window : window + 1, :] = found[:, MAIN : MAIN + 1, :]
        tail[:, 8 + window : 9 + window, :] = found[:, MAIN + 1 : MAIN + 2, :]
    for row in (6, 7, 14, 15):
        tail[:, row : row + 1, :] = jnp.zeros((count, 1, KDIM), F32)
    out_ref[:, WINDOWS * MAIN :, :] = tail[...].astype(BF16)


def windows_of(bricks):
    count = bricks.shape[0]
    cube = bricks.reshape(count, EDGE, EDGE * EDGE)
    return pl.pallas_call(
        windows_kernel,
        out_shape=jax.ShapeDtypeStruct((count, BRICK_ROWS, KDIM), BF16),
        in_specs=[vmem()],
        out_specs=vmem(),
        scratch_shapes=[
            pltpu.VMEM((count, 48, 10 * LANES), BF16),
            pltpu.VMEM((count, TAIL, KDIM), F32),
        ],
        compiler_params=params(16),
        cost_estimate=pl.CostEstimate(
            flops=2 * count * 48 * 384 * KDIM * WINDOWS, bytes_accessed=4 * 1024 * 1024,
            transcendentals=0,
        ),
        name="brick_windows",
    )(cube)


def hat(distance):
    return jnp.maximum(1.0 - jnp.abs(distance), 0.0)


def blend(brick, px, py, pz):
    width = px.shape[1]
    eight = lax.broadcasted_iota(jnp.int32, (8, width), 0).astype(F32)
    places = lax.broadcasted_iota(jnp.int32, (MAIN, width), 0).astype(F32).astype(BF16)

    def tile(rows):
        return jnp.concatenate([rows, rows], axis=0).astype(BF16)

    cell_y = jnp.floor(py)
    frac_y = py - cell_y
    lower, low_share, high_share = tile(cell_y), tile(1.0 - frac_y), tile(frac_y)
    nothing = jnp.zeros((TAIL, width), BF16)
    weight_y = []
    for start in range(0, MAIN, TAIL):
        offset = places[start : start + TAIL] - lower
        weight_y.append(
            jnp.where(offset == 0, low_share, jnp.where(offset == 1, high_share, nothing))
        )
    window = jnp.floor(px * (1.0 / STRIDE))
    weight_x = hat(eight - (px - STRIDE * window))
    parts = []
    for i in range(STRIDE + 1):
        share = tile(jnp.broadcast_to(weight_x[i : i + 1], (8, width)))
        parts += [share * part for part in weight_y]
    tail = [weight_x * hat(MAIN - py), weight_x * jnp.maximum(py - MAIN, 0.0)]
    parts.append(jnp.concatenate(tail, axis=0).astype(BF16))
    parts.append(nothing)
    plane = jnp.concatenate(parts, axis=0)
    found = jnp.dot(brick, plane, preferred_element_type=F32)
    groups = range(0, MAIN, 8)
    chosen = [found[row : row + 8] for row in groups]
    for other in range(1, WINDOWS):
        here = window == float(other)
        base = other * MAIN
        chosen = [
            jnp.where(here, found[base + row : base + row + 8], old)
            for row, old in zip(groups, chosen)
        ]
    base = WINDOWS * MAIN
    edges = found[base : base + 8] * hat(MAIN - pz)
    edges = edges + found[base + 8 :] * jnp.maximum(pz - MAIN, 0.0)
    total = jnp.where(eight == window, edges, 0.0)
    for row, part in zip(groups, chosen):
        total = total + part * hat((eight + float(row)) - pz)
    return total


def samples_kernel(
    own, where_ref, picks_ref, brick_ref, place_ref, *rest
):
    if own:
        out_ref, bricks, places, sums, arrivals = rest
    else:
        own_ref, out_ref, bricks, places, sums, arrivals = rest
    owners, rows, _ = place_ref.shape
    cap = picks_ref.shape[0]
    lines = rows // 3
    per_slot = lines // 2 // cap
    count = 1 if own else owners - 1
    tile = where_ref[0]
    if not own:
        out_ref[tile] = own_ref[0]

    def renderer_of(turn):
        return tile if own else lax.rem(tile + 1 + turn, owners)

    def fetches(turn):
        held = turn % 2
        renderer = renderer_of(turn)
        copies = [
            pltpu.make_async_copy(
                place_ref.at[renderer], places.at[held], arrivals.at[held, cap]
            )
        ]
        for piece in range(cap):
            copies.append(
                pltpu.make_async_copy(
                    brick_ref.at[picks_ref[piece, renderer]],
                    bricks.at[held, piece],
                    arrivals.at[held, piece],
                )
            )
        return copies

    for turn in range(min(2, count)):
        for copy in fetches(turn):
            copy.start()

    def one_turn(turn, carry):
        held = turn % 2
        copies = fetches(turn)
        copies[0].wait()
        for piece in range(cap):
            copies[1 + piece].wait()
            brick = bricks[held, piece]
            for step in range(per_slot):
                row = 2 * (piece * per_slot + step)

                def line(axis):
                    both = [
                        jnp.broadcast_to(
                            places[held, pl.ds(axis * lines + row + half, 1), :], (8, LANES)
                        )
                        for half in range(2)
                    ]
                    return jnp.concatenate(both, axis=1)

                total = blend(brick, line(0), line(1), line(2))
                for half in range(2):
                    sums[8 * (row + half) : 8 * (row + half + 1), :] = total[
                        :, half * LANES : (half + 1) * LANES
                    ]

        @pl.when(turn + 2 < count)
        def _():
            for copy in fetches(turn + 2):
                copy.start()

        values = []
        for row in range(0, lines, 8):
            value = sums[pl.ds(8 * row, 8, stride=8), :]
            for other in range(1, 8):
                value = value + sums[pl.ds(8 * row + other, 8, stride=8), :]
            values.append(value)
        out_ref[0 if own else renderer_of(turn)] = jnp.concatenate(values, axis=0).astype(BF16)
        return carry

    lax.fori_loop(0, count, one_turn, 0)


def sample_values(where, picks, windows, places, own_values=None):
    owners, rows, _ = places.shape
    cap = picks.shape[0]
    own = own_values is None
    count = 1 if own else owners - 1
    samples = count * rows * LANES // 3
    some = pl.BlockSpec(memory_space=pl.ANY)
    extra = () if own else (own_values,)
    return pl.pallas_call(
        functools.partial(samples_kernel, own),
        out_shape=jax.ShapeDtypeStruct((1 if own else owners, rows // 3, LANES), BF16),
        in_specs=[smem(), smem(), some, some] + [vmem()] * len(extra),
        out_specs=vmem(),
        scratch_shapes=[
            pltpu.VMEM((2, cap, BRICK_ROWS, KDIM), BF16),
            pltpu.VMEM((2, rows, LANES), F32),
            pltpu.VMEM((8 * rows // 3, LANES), F32),
            pltpu.SemaphoreType.DMA((2, cap + 1)),
        ],
        compiler_params=params(59),
        cost_estimate=pl.CostEstimate(
            flops=2 * samples * KDIM * BRICK_ROWS, bytes_accessed=count * MIB // 4,
            transcendentals=0,
        ),
        name="own_values" if own else "sample_values",
    )(where, picks, windows, places, *extra)


def gbuffer_kernel(value_ref, order_ref, out_ref, values):
    values[...] = value_ref[...].astype(F32).reshape(values.shape)
    height = out_ref.shape[2]

    def ray_of(number):
        rows_now = slice(number * height, (number + 1) * height)
        first, second = (
            values[pl.ds(2 * number * height + half, height, stride=2), :] for half in range(2)
        )
        parts = []
        for half in range(2):
            order = order_ref[0, 0, rows_now, half * LANES : (half + 1) * LANES]
            inner = order & (LANES - 1)
            parts.append(
                jnp.where(
                    order < LANES,
                    jnp.take_along_axis(first, inner, axis=1, mode="promise_in_bounds"),
                    jnp.take_along_axis(second, inner, axis=1, mode="promise_in_bounds"),
                )
            )
        return jnp.concatenate(parts, axis=1)

    remain = 1.0
    shade = 0.0
    depth = 0.0
    for step in range(NSP):
        ray = ray_of(step)
        half_tanh = 0.5 * jnp.tanh(ray)
        weight = remain * (0.5 + half_tanh)
        shade = shade + weight * ray
        depth = depth + weight * ((step + 1) / NSP)
        remain = remain * (0.5 - half_tanh)
    occlusion = 0.0
    for ray_number in range(NRAY):
        passing = 1.0
        for step in range(NOS):
            ray = ray_of(NSP + ray_number * NOS + step)
            passing = passing * (0.5 - 0.5 * jnp.tanh(ray))
        occlusion = occlusion + passing
    out_ref[0, 0] = shade.astype(BF16)
    out_ref[0, 1] = (1.0 - remain).astype(BF16)
    out_ref[0, 2] = depth.astype(BF16)
    out_ref[0, 3] = (occlusion * (1.0 / NRAY)).astype(BF16)


def gbuffer(values, order, height, width):
    total = order.shape[2]
    return pl.pallas_call(
        gbuffer_kernel,
        out_shape=jax.ShapeDtypeStruct((1, 4, height, width), BF16),
        in_specs=[vmem(), vmem()],
        out_specs=vmem(),
        scratch_shapes=[pltpu.VMEM((2 * total, LANES), F32)],
        compiler_params=params(16),
        cost_estimate=pl.CostEstimate(
            flops=20 * total * BLOCK, bytes_accessed=8 * total * BLOCK, transcendentals=0
        ),
        name="gbuffer",
    )(values, order)


def silu(field):
    half = 0.5 * field
    return half + half * jnp.tanh(half)


def shifted(rows, steps):
    lane = lax.broadcasted_iota(jnp.int32, (1, LANES), 1)
    edge = lane == (0 if steps == 1 else LANES - 1)
    moved = []
    for row in rows:
        tiles = [row[:, i : i + LANES] for i in range(0, row.shape[1], LANES)]
        tiles = [pltpu.roll(tile, steps % LANES, 1) for tile in tiles]
        for i, tile in enumerate(tiles):
            source = i - steps
            fill = tiles[source] if 0 <= source < len(tiles) else 0.0
            moved.append(jnp.where(edge, fill, tile))
    return jnp.concatenate(moved, axis=1)


def across(total, chans, row_width):
    left, middle, right = (total[i * chans : (i + 1) * chans] for i in range(3))

    def rows_of(part):
        return [part[:, i : i + row_width] for i in range(0, part.shape[1], row_width)]

    return middle + shifted(rows_of(left), 1) + shifted(rows_of(right), -1)


def taps(weight_ref, tap):
    _, out_chans, chans = weight_ref.shape
    return weight_ref[3 * tap : 3 * tap + 3].reshape(3 * out_chans, chans)


def beside(weight_ref):
    return jnp.concatenate([taps(weight_ref, tap) for tap in range(3)], axis=1)


def sides(where_ref):
    above = jnp.where(where_ref[0] > 0, 1.0, 0.0)
    below = jnp.where(where_ref[0] < where_ref[1] - 1, 1.0, 0.0)

    def inside(row, low, high):
        return jnp.where(row < low, above, jnp.where(row >= high, below, 1.0))

    return inside


def encoder_kernel(
    where_ref, x_ref, w_in, w_mid, w_down, w_deep, skip_ref, fourth,
    first, second, pooled, third,
):
    height = x_ref.shape[0] // 3
    half_height = height // 2
    width = x_ref.shape[2]
    half_width = width // 2
    inside = sides(where_ref)

    def full_layer(weight, source, target, low, high, unroll):
        chans = target.shape[1]
        depth = weight.shape[1]

        def step(row, carry):
            lines = source[pl.ds(row, 3)].reshape(depth, width)
            line = across(jnp.dot(weight, lines, preferred_element_type=F32), chans, width)
            target[row] = (silu(line) * inside(row, low, high)).astype(BF16)
            return carry

        lax.fori_loop(0, target.shape[0], step, 0, unroll=unroll)

    full_layer(beside(w_in), x_ref, first, height - 1, 2 * height - 1, first.shape[0] // 2)
    full_layer(beside(w_mid), first, second, height - 2, 2 * height - 2, second.shape[0] // 2)

    place = lax.broadcasted_iota(jnp.int32, (width, half_width), 0) // 2
    target = lax.broadcasted_iota(jnp.int32, (width, half_width), 1)
    shrink = jnp.where(place == target, 0.25, 0.0).astype(BF16)
    count, chans = second.shape[0], second.shape[1]
    pairs = jnp.dot(
        second[...].reshape(count * chans, width), shrink, preferred_element_type=F32
    ).reshape(count // 2, 2, chans, half_width)
    pooled[...] = (pairs[:, 0] + pairs[:, 1]).astype(BF16)

    def half_pair(source, row, tap):
        return jnp.concatenate([source[row + tap], source[row + tap + 1]], axis=1)

    def half_layer(product, target, low, high):
        chans = target.shape[1]
        for row in range(0, target.shape[0], 2):
            both = silu(across(product(row), chans, half_width))
            for now in range(2):
                line = both[:, now * half_width : (now + 1) * half_width]
                if row + now < low or row + now >= high:
                    line = line * inside(row + now, low, high)
                target[row + now] = line.astype(BF16)

    weight_down = beside(w_down)

    def down_product(row):
        lines = jnp.concatenate([half_pair(pooled, row, tap) for tap in range(3)], axis=0)
        return jnp.dot(weight_down, lines, preferred_element_type=F32)

    def deep_product(row):
        total = None
        for tap in range(3):
            part = jnp.dot(
                taps(w_deep, tap), half_pair(third, row, tap), preferred_element_type=F32
            )
            total = part if total is None else total + part
        return total

    half_layer(down_product, third, half_height - 2, 2 * half_height - 2)
    half_layer(deep_product, fourth, half_height - 3, 2 * half_height - 3)

    skip_ref[...] = second[4 : 4 + skip_ref.shape[0]]


def decoder_kernel(
    where_ref, skip_ref, fourth, w_up, w_out, out_ref, joined, fifth, final
):
    height = out_ref.shape[2]
    width = out_ref.shape[3]
    half_width = width // 2
    chans = skip_ref.shape[1]
    inside = sides(where_ref)
    place = lax.broadcasted_iota(jnp.int32, (half_width, width), 0)
    target = lax.broadcasted_iota(jnp.int32, (half_width, width), 1) // 2
    spread = jnp.where(place == target, 1.0, 0.0).astype(BF16)
    deep = fourth.shape[1]
    wide = jnp.dot(
        fourth[...].reshape(-1, half_width), spread, preferred_element_type=F32
    ).astype(BF16).reshape(fourth.shape[0], deep, width)
    for row in range(2 * fourth.shape[0]):
        joined[row, chans:, :] = wide[row // 2]
        joined[row, :chans, :] = skip_ref[row]

    def up_step(row, carry):
        total = None
        for tap in range(3):
            part = jnp.dot(taps(w_up, tap), joined[row + tap], preferred_element_type=F32)
            total = part if total is None else total + part
        line = silu(across(total, chans, width))
        fifth[row] = (line * inside(row, 1, height + 1)).astype(BF16)
        return carry

    lax.fori_loop(0, fifth.shape[0], up_step, 0, unroll=fifth.shape[0] // 2)

    colours = out_ref.shape[1]
    weight_out = beside(w_out)
    for row in range(height):
        lines = fifth[row : row + 3].reshape(3 * chans, width)
        total = jnp.dot(weight_out, lines, preferred_element_type=F32)
        line = across(total, w_out.shape[1], width)
        for colour in range(colours):
            final[colour, row : row + 1, :] = line[colour : colour + 1, :]
    out_ref[0] = final[...].astype(BF16)


def encoder(where, field, w_in, w_mid, w_down, w_deep):
    height = field.shape[0] // 3
    half = height // 2
    width = field.shape[2]
    one, two = w_mid.shape[1], w_deep.shape[1]
    return pl.pallas_call(
        encoder_kernel,
        out_shape=(
            jax.ShapeDtypeStruct((height + 4, one, width), BF16),
            jax.ShapeDtypeStruct((3 * half - 6, two, width // 2), BF16),
        ),
        in_specs=[smem()] + [vmem()] * 5,
        out_specs=(vmem(), vmem()),
        scratch_shapes=[
            pltpu.VMEM((3 * height - 2, one, width), BF16),
            pltpu.VMEM((3 * height - 4, one, width), BF16),
            pltpu.VMEM((3 * half - 2, one, width // 2), BF16),
            pltpu.VMEM((3 * half - 4, two, width // 2), BF16),
        ],
        compiler_params=params(16),
        cost_estimate=pl.CostEstimate(
            flops=2_000_000_000, bytes_accessed=2 * MIB, transcendentals=400_000
        ),
        name="encoder",
    )(where, field, w_in, w_mid, w_down, w_deep)


def decoder(where, skip, deep, w_up, w_out, height, colours):
    one = skip.shape[1]
    two = deep.shape[1]
    width = skip.shape[2]
    return pl.pallas_call(
        decoder_kernel,
        out_shape=jax.ShapeDtypeStruct((1, colours, height, width), BF16),
        in_specs=[smem()] + [vmem()] * 4,
        out_specs=vmem(),
        scratch_shapes=[
            pltpu.VMEM((height + 4, one + two, width), BF16),
            pltpu.VMEM((height + 2, one, width), BF16),
            pltpu.VMEM((colours, height, width), F32),
        ],
        compiler_params=params(16),
        cost_estimate=pl.CostEstimate(
            flops=1_000_000_000, bytes_accessed=MIB, transcendentals=100_000
        ),
        name="decoder",
    )(where, skip, deep, w_up, w_out)


def on_device(
    bricks, sends, cells, fracs, sample_order, pending, w_in, w_mid, w_down, w_deep, w_up, w_out
):
    n_tile = lax.axis_size("tile")
    tile = lax.axis_index("tile")
    n_section = lax.axis_size("section")
    cap = sends.shape[3]
    height = pending.shape[2]
    width = pending.shape[3]
    samples = cells.shape[3]
    slots = n_tile * cap
    per_slot = samples // slots
    padded = -(-per_slot // BLOCK) * BLOCK

    def fill(part):
        if padded != per_slot:
            part = part.reshape(3, slots, per_slot)
            part = jnp.pad(part, ((0, 0), (0, 0), (0, padded - per_slot)))
        return part.reshape(3, slots * padded // LANES, LANES)

    def trim(found):
        if padded == per_slot:
            return found
        return found.reshape(slots, padded)[:, :per_slot].reshape(1, samples // LANES, LANES)

    places = positions(fill(cells), fill(fracs), n_tile)
    places, bricks, pending = lax.optimization_barrier((places, bricks, pending))
    arrived = lax.all_to_all(places, "tile", split_axis=0, concat_axis=0, tiled=True)

    down = [(i, i + 1) for i in range(n_tile - 1)]
    up = [(i + 1, i) for i in range(n_tile - 1)]
    over = lax.ppermute(pending, "tile", down)
    under = lax.ppermute(pending, "tile", up)
    windows = windows_of(bricks)
    where = jnp.stack([tile, jnp.int32(n_tile)]).astype(jnp.int32)
    picks = sends[0, 0].T
    own_values = sample_values(where, picks, windows, places)
    found = sample_values(where, picks, windows, arrived, own_values)

    over, under, pending, found = lax.optimization_barrier((over, under, pending, found))
    values = lax.all_to_all(found, "tile", split_axis=0, concat_axis=0, tiled=True)
    field = jnp.concatenate([over[0], pending[0], under[0]], axis=1).transpose(1, 0, 2)
    field = jnp.pad(field, ((0, 0), (0, 16 - field.shape[1]), (0, 0)))
    colours = w_out.shape[1]
    w_in = jnp.pad(w_in, ((0, 0), (0, 0), (0, 16 - w_in.shape[2])))
    w_out = jnp.pad(w_out, ((0, 0), (0, 16 - colours), (0, 0)))
    skip, deep = encoder(where, field, w_in, w_mid, w_down, w_deep)
    values, skip, deep = lax.optimization_barrier((values, skip, deep))
    rendered = gbuffer(trim(values), sample_order, height, width)
    rendered, skip, deep = lax.optimization_barrier((rendered, skip, deep))
    ring = [(i, (i + 1) % n_section) for i in range(n_section)]
    handoff = lax.ppermute(rendered, "section", ring)
    denoised = decoder(where, skip, deep, w_up, w_out, height, colours)
    return (handoff, denoised)


def solution(mesh):
    in_specs = (
        P("tile", None),
        P("section", "tile", None, None),
        P("section", "tile", None, None),
        P("section", "tile", None, None),
        P("section", "tile", None, None),
        P("section", None, "tile", None),
        P(),
        P(),
        P(),
        P(),
        P(),
        P(),
    )
    out_specs = (P("section", None, "tile", None), P("section", None, "tile", None))
    return jax.shard_map(
        on_device, mesh=mesh, in_specs=in_specs, out_specs=out_specs, check_vma=False
    )
```

```python
import functools

import jax
import jax.numpy as jnp
from jax import lax
from jax.experimental import pallas as pl
from jax.experimental.pallas import tpu as pltpu
from jax.sharding import PartitionSpec as P

EDGE = 34
NSP = 4
NRAY = 8
NOS = 2
LANES = 128
BLOCK = 256
STRIDE = 6
WINDOWS = 6
MAIN = 32
TAIL = 16
BRICK_ROWS = WINDOWS * MAIN + TAIL
KDIM = 256

F32 = jnp.float32
BF16 = jnp.bfloat16
MIB = 1024 * 1024


def params(mib):
    return pltpu.CompilerParams(vmem_limit_bytes=mib * MIB)


def vmem():
    return pl.BlockSpec(memory_space=pltpu.VMEM)


def smem():
    return pl.BlockSpec(memory_space=pltpu.SMEM)


def positions_kernel(cells_ref, fracs_ref, out_ref, cells, fracs, found, arrivals, departures):
    owners, rows, _ = out_ref.shape
    lines = rows // 3
    parts = arrivals.shape[1]
    share = owners // parts
    pieces = [(axis, part) for axis in range(3) for part in range(parts)]

    def reads(axis, part):
        span = pl.ds(part * share * lines, share * lines)
        return [
            pltpu.make_async_copy(
                source.at[axis, span], target.at[axis, span], arrivals.at[axis, part, number]
            )
            for number, (source, target) in enumerate(((cells_ref, cells), (fracs_ref, fracs)))
        ]

    def write(axis, part):
        place = (pl.ds(part * share, share), pl.ds(axis * lines, lines))
        return pltpu.make_async_copy(
            found.at[place], out_ref.at[place], departures.at[axis, part]
        )

    for piece in pieces:
        for copy in reads(*piece):
            copy.start()
    for axis, part in pieces:
        for copy in reads(axis, part):
            copy.wait()
        span = slice(part * share * lines, (part + 1) * share * lines)
        place = cells[axis, span].astype(F32) + fracs[axis, span]
        found[part * share : (part + 1) * share, axis * lines : (axis + 1) * lines, :] = (
            place.reshape(share, lines, LANES)
        )
        write(axis, part).start()
    for piece in pieces:
        write(*piece).wait()


def positions(cells, fracs, owners):
    lines = cells.shape[1]
    shape = (owners, 3 * lines // owners, LANES)
    hbm = pl.BlockSpec(memory_space=pltpu.HBM)
    return pl.pallas_call(
        positions_kernel,
        out_shape=jax.ShapeDtypeStruct(shape, F32),
        in_specs=[hbm, hbm],
        out_specs=hbm,
        scratch_shapes=[
            pltpu.VMEM(cells.shape, jnp.int32),
            pltpu.VMEM(fracs.shape, F32),
            pltpu.VMEM(shape, F32),
            pltpu.SemaphoreType.DMA((3, 2, 2)),
            pltpu.SemaphoreType.DMA((3, 2)),
        ],
        compiler_params=params(60),
        cost_estimate=pl.CostEstimate(
            flops=3 * lines * LANES, bytes_accessed=36 * lines * LANES, transcendentals=0
        ),
        name="positions",
    )(cells, fracs)


def windows_kernel(cube_ref, out_ref, wide, tail):
    count = cube_ref.shape[0]
    plane = EDGE * EDGE
    wide[...] = jnp.zeros_like(wide)
    wide[:, :EDGE, :plane] = cube_ref[...]
    column = lax.broadcasted_iota(jnp.int32, (1, KDIM), 1)
    main = (column // MAIN) * EDGE + column % MAIN
    rest = column - 7 * MAIN
    last = (rest % 8) * EDGE + MAIN + rest // 8
    source = jnp.where(column < 7 * MAIN, main, last)
    unused = (column >= 7 * MAIN) & ((rest % 8 == 7) | (rest >= TAIL))
    source = jnp.where(unused, -(1 << 20), source)
    for window in range(WINDOWS):
        first = window * STRIDE * EDGE
        low = first // LANES * LANES
        length = min(3 * LANES, wide.shape[2] - low)
        place = lax.broadcasted_iota(jnp.int32, (length, KDIM), 0)
        pick = jnp.where(place == source + (first - low), 1.0, 0.0).astype(BF16)
        found = jnp.dot(
            wide[:, :, low : low + length].reshape(-1, length),
            pick,
            preferred_element_type=F32,
        )
        found = found.reshape(count, 48, KDIM)
        out_ref[:, window * MAIN : (window + 1) * MAIN, :] = found[:, :MAIN, :].astype(BF16)
        tail[:, window : window + 1, :] = found[:, MAIN : MAIN + 1, :]
        tail[:, 8 + window : 9 + window, :] = found[:, MAIN + 1 : MAIN + 2, :]
    for row in (6, 7, 14, 15):
        tail[:, row : row + 1, :] = jnp.zeros((count, 1, KDIM), F32)
    out_ref[:, WINDOWS * MAIN :, :] = tail[...].astype(BF16)


def windows_of(bricks):
    count = bricks.shape[0]
    cube = bricks.reshape(count, EDGE, EDGE * EDGE)
    return pl.pallas_call(
        windows_kernel,
        out_shape=jax.ShapeDtypeStruct((count, BRICK_ROWS, KDIM), BF16),
        in_specs=[vmem()],
        out_specs=vmem(),
        scratch_shapes=[
            pltpu.VMEM((count, 48, 10 * LANES), BF16),
            pltpu.VMEM((count, TAIL, KDIM), F32),
        ],
        compiler_params=params(16),
        cost_estimate=pl.CostEstimate(
            flops=2 * count * 48 * 384 * KDIM * WINDOWS, bytes_accessed=4 * 1024 * 1024,
            transcendentals=0,
        ),
        name="brick_windows",
    )(cube)


def hat(distance):
    return jnp.maximum(1.0 - jnp.abs(distance), 0.0)


def blend(brick, px, py, pz):
    width = px.shape[1]
    eight = lax.broadcasted_iota(jnp.int32, (8, width), 0).astype(F32)
    places = lax.broadcasted_iota(jnp.int32, (MAIN, width), 0).astype(F32).astype(BF16)

    def tile(rows):
        return jnp.concatenate([rows, rows], axis=0).astype(BF16)

    cell_y = jnp.floor(py)
    frac_y = py - cell_y
    lower, low_share, high_share = tile(cell_y), tile(1.0 - frac_y), tile(frac_y)
    nothing = jnp.zeros((TAIL, width), BF16)
    weight_y = []
    for start in range(0, MAIN, TAIL):
        offset = places[start : start + TAIL] - lower
        weight_y.append(
            jnp.where(offset == 0, low_share, jnp.where(offset == 1, high_share, nothing))
        )
    window = jnp.floor(px * (1.0 / STRIDE))
    weight_x = hat(eight - (px - STRIDE * window))
    parts = []
    for i in range(STRIDE + 1):
        share = tile(jnp.broadcast_to(weight_x[i : i + 1], (8, width)))
        parts += [share * part for part in weight_y]
    tail = [weight_x * hat(MAIN - py), weight_x * jnp.maximum(py - MAIN, 0.0)]
    parts.append(jnp.concatenate(tail, axis=0).astype(BF16))
    parts.append(nothing)
    plane = jnp.concatenate(parts, axis=0)
    found = jnp.dot(brick, plane, preferred_element_type=F32)
    groups = range(0, MAIN, 8)
    chosen = [found[row : row + 8] for row in groups]
    for other in range(1, WINDOWS):
        here = window == float(other)
        base = other * MAIN
        chosen = [
            jnp.where(here, found[base + row : base + row + 8], old)
            for row, old in zip(groups, chosen)
        ]
    base = WINDOWS * MAIN
    edges = found[base : base + 8] * hat(MAIN - pz)
    edges = edges + found[base + 8 :] * jnp.maximum(pz - MAIN, 0.0)
    total = jnp.where(eight == window, edges, 0.0)
    for row, part in zip(groups, chosen):
        total = total + part * hat((eight + float(row)) - pz)
    return total


def samples_kernel(picks_ref, brick_ref, place_ref, out_ref, bricks, places, sums, arrivals):
    owners, rows, _ = place_ref.shape
    cap = picks_ref.shape[0]
    lines = rows // 3
    per_slot = lines // 2 // cap
    group = places.shape[1]
    turns = owners // group

    def fetches(turn):
        held = turn % 2
        copies = []
        for member in range(group):
            renderer = turn * group + member
            copies.append(
                pltpu.make_async_copy(
                    place_ref.at[renderer],
                    places.at[held, member],
                    arrivals.at[held, member, cap],
                )
            )
            for piece in range(cap):
                copies.append(
                    pltpu.make_async_copy(
                        brick_ref.at[picks_ref[piece, renderer]],
                        bricks.at[held, member, piece],
                        arrivals.at[held, member, piece],
                    )
                )
        return copies

    for turn in range(min(2, turns)):
        for copy in fetches(turn):
            copy.start()

    def one_turn(turn, carry):
        held = turn % 2
        for copy in fetches(turn):
            copy.wait()
        for member in range(group):
            for piece in range(cap):
                brick = bricks[held, member, piece]
                for step in range(per_slot):
                    row = 2 * (piece * per_slot + step)

                    def line(axis):
                        both = [
                            jnp.broadcast_to(
                                places[held, member, pl.ds(axis * lines + row + half, 1), :],
                                (8, LANES),
                            )
                            for half in range(2)
                        ]
                        return jnp.concatenate(both, axis=1)

                    total = blend(brick, line(0), line(1), line(2))
                    for half in range(2):
                        sums[member, 8 * (row + half) : 8 * (row + half + 1), :] = total[
                            :, half * LANES : (half + 1) * LANES
                        ]
            values = []
            for row in range(0, lines, 8):
                value = sums[member, pl.ds(8 * row, 8, stride=8), :]
                for other in range(1, 8):
                    value = value + sums[member, pl.ds(8 * row + other, 8, stride=8), :]
                values.append(value)
            out_ref[turn * group + member] = jnp.concatenate(values, axis=0).astype(BF16)

        @pl.when(turn + 2 < turns)
        def _():
            for copy in fetches(turn + 2):
                copy.start()

        return carry

    lax.fori_loop(0, turns, one_turn, 0)


def sample_values(picks, windows, places):
    owners, rows, _ = places.shape
    cap = picks.shape[0]
    group = 2 if owners % 2 == 0 else 1
    samples = owners * rows * LANES // 3
    some = pl.BlockSpec(memory_space=pl.ANY)
    return pl.pallas_call(
        samples_kernel,
        out_shape=jax.ShapeDtypeStruct((owners, rows // 3, LANES), BF16),
        in_specs=[smem(), some, some],
        out_specs=vmem(),
        scratch_shapes=[
            pltpu.VMEM((2, group, cap, BRICK_ROWS, KDIM), BF16),
            pltpu.VMEM((2, group, rows, LANES), F32),
            pltpu.VMEM((group, 8 * rows // 3, LANES), F32),
            pltpu.SemaphoreType.DMA((2, group, cap + 1)),
        ],
        compiler_params=params(59),
        cost_estimate=pl.CostEstimate(
            flops=2 * samples * KDIM * BRICK_ROWS, bytes_accessed=3 * MIB,
            transcendentals=0,
        ),
        name="sample_values",
    )(picks, windows, places)


def gbuffer_kernel(value_ref, order_ref, out_ref, values):
    values[...] = value_ref[...].astype(F32).reshape(values.shape)
    height = out_ref.shape[2]

    def ray_of(number):
        rows_now = slice(number * height, (number + 1) * height)
        first, second = (
            values[pl.ds(2 * number * height + half, height, stride=2), :] for half in range(2)
        )
        parts = []
        for half in range(2):
            order = order_ref[0, 0, rows_now, half * LANES : (half + 1) * LANES]
            inner = order & (LANES - 1)
            parts.append(
                jnp.where(
                    order < LANES,
                    jnp.take_along_axis(first, inner, axis=1, mode="promise_in_bounds"),
                    jnp.take_along_axis(second, inner, axis=1, mode="promise_in_bounds"),
                )
            )
        return jnp.concatenate(parts, axis=1)

    remain = 1.0
    shade = 0.0
    depth = 0.0
    for step in range(NSP):
        ray = ray_of(step)
        half_tanh = 0.5 * jnp.tanh(ray)
        weight = remain * (0.5 + half_tanh)
        shade = shade + weight * ray
        depth = depth + weight * ((step + 1) / NSP)
        remain = remain * (0.5 - half_tanh)
    occlusion = 0.0
    for ray_number in range(NRAY):
        passing = 1.0
        for step in range(NOS):
            ray = ray_of(NSP + ray_number * NOS + step)
            passing = passing * (0.5 - 0.5 * jnp.tanh(ray))
        occlusion = occlusion + passing
    out_ref[0, 0] = shade.astype(BF16)
    out_ref[0, 1] = (1.0 - remain).astype(BF16)
    out_ref[0, 2] = depth.astype(BF16)
    out_ref[0, 3] = (occlusion * (1.0 / NRAY)).astype(BF16)


def gbuffer(values, order, height, width):
    total = order.shape[2]
    return pl.pallas_call(
        gbuffer_kernel,
        out_shape=jax.ShapeDtypeStruct((1, 4, height, width), BF16),
        in_specs=[vmem(), vmem()],
        out_specs=vmem(),
        scratch_shapes=[pltpu.VMEM((2 * total, LANES), F32)],
        compiler_params=params(16),
        cost_estimate=pl.CostEstimate(
            flops=20 * total * BLOCK, bytes_accessed=8 * total * BLOCK, transcendentals=0
        ),
        name="gbuffer",
    )(values, order)


def silu(field):
    half = 0.5 * field
    return half + half * jnp.tanh(half)


def shifted(rows, steps):
    lane = lax.broadcasted_iota(jnp.int32, (1, LANES), 1)
    edge = lane == (0 if steps == 1 else LANES - 1)
    moved = []
    for row in rows:
        tiles = [row[:, i : i + LANES] for i in range(0, row.shape[1], LANES)]
        tiles = [pltpu.roll(tile, steps % LANES, 1) for tile in tiles]
        for i, tile in enumerate(tiles):
            source = i - steps
            fill = tiles[source] if 0 <= source < len(tiles) else 0.0
            moved.append(jnp.where(edge, fill, tile))
    return jnp.concatenate(moved, axis=1)


def across(total, chans, row_width):
    left, middle, right = (total[i * chans : (i + 1) * chans] for i in range(3))

    def rows_of(part):
        return [part[:, i : i + row_width] for i in range(0, part.shape[1], row_width)]

    return middle + shifted(rows_of(left), 1) + shifted(rows_of(right), -1)


def taps(weight_ref, tap):
    _, out_chans, chans = weight_ref.shape
    return weight_ref[3 * tap : 3 * tap + 3].reshape(3 * out_chans, chans)


def beside(weight_ref):
    return jnp.concatenate([taps(weight_ref, tap) for tap in range(3)], axis=1)


def sides(where_ref):
    above = jnp.where(where_ref[0] > 0, 1.0, 0.0)
    below = jnp.where(where_ref[0] < where_ref[1] - 1, 1.0, 0.0)

    def inside(row, low, high):
        return jnp.where(row < low, above, jnp.where(row >= high, below, 1.0))

    return inside


def stem_kernel(where_ref, x_ref, w_in, w_mid, second, first):
    height = x_ref.shape[0] // 3
    width = x_ref.shape[2]
    inside = sides(where_ref)

    def full_layer(weight, source, target, low, high, unroll):
        chans = target.shape[1]
        depth = weight.shape[1]

        def step(row, carry):
            lines = source[pl.ds(row, 3)].reshape(depth, width)
            line = across(jnp.dot(weight, lines, preferred_element_type=F32), chans, width)
            target[row] = (silu(line) * inside(row, low, high)).astype(BF16)
            return carry

        lax.fori_loop(0, target.shape[0], step, 0, unroll=unroll)

    full_layer(beside(w_in), x_ref, first, height - 1, 2 * height - 1, first.shape[0] // 2)
    full_layer(beside(w_mid), first, second, height - 2, 2 * height - 2, second.shape[0] // 2)


def middle_kernel(where_ref, second, w_down, w_deep, fourth, pooled, third):
    count, chans, width = second.shape
    half_height = (count + 4) // 6
    half_width = width // 2
    inside = sides(where_ref)
    place = lax.broadcasted_iota(jnp.int32, (width, half_width), 0) // 2
    target = lax.broadcasted_iota(jnp.int32, (width, half_width), 1)
    shrink = jnp.where(place == target, 0.25, 0.0).astype(BF16)
    pairs = jnp.dot(
        second[...].reshape(count * chans, width), shrink, preferred_element_type=F32
    ).reshape(count // 2, 2, chans, half_width)
    pooled[...] = (pairs[:, 0] + pairs[:, 1]).astype(BF16)

    def half_pair(source, row, tap):
        return jnp.concatenate([source[row + tap], source[row + tap + 1]], axis=1)

    def half_layer(product, target, low, high):
        chans = target.shape[1]
        for row in range(0, target.shape[0], 2):
            both = silu(across(product(row), chans, half_width))
            for now in range(2):
                line = both[:, now * half_width : (now + 1) * half_width]
                if row + now < low or row + now >= high:
                    line = line * inside(row + now, low, high)
                target[row + now] = line.astype(BF16)

    weight_down = beside(w_down)

    def down_product(row):
        lines = jnp.concatenate([half_pair(pooled, row, tap) for tap in range(3)], axis=0)
        return jnp.dot(weight_down, lines, preferred_element_type=F32)

    def deep_product(row):
        total = None
        for tap in range(3):
            part = jnp.dot(
                taps(w_deep, tap), half_pair(third, row, tap), preferred_element_type=F32
            )
            total = part if total is None else total + part
        return total

    half_layer(down_product, third, half_height - 2, 2 * half_height - 2)
    half_layer(deep_product, fourth, half_height - 3, 2 * half_height - 3)


def decoder_kernel(
    where_ref, second, fourth, w_up, w_out, out_ref, joined, fifth, final
):
    height = out_ref.shape[2]
    width = out_ref.shape[3]
    half_width = width // 2
    chans = second.shape[1]
    inside = sides(where_ref)
    place = lax.broadcasted_iota(jnp.int32, (half_width, width), 0)
    target = lax.broadcasted_iota(jnp.int32, (half_width, width), 1) // 2
    spread = jnp.where(place == target, 1.0, 0.0).astype(BF16)
    deep = fourth.shape[1]
    wide = jnp.dot(
        fourth[...].reshape(-1, half_width), spread, preferred_element_type=F32
    ).astype(BF16).reshape(fourth.shape[0], deep, width)
    for row in range(2 * fourth.shape[0]):
        joined[row, chans:, :] = wide[row // 2]
        joined[row, :chans, :] = second[row + 4]

    def up_step(row, carry):
        total = None
        for tap in range(3):
            part = jnp.dot(taps(w_up, tap), joined[row + tap], preferred_element_type=F32)
            total = part if total is None else total + part
        line = silu(across(total, chans, width))
        fifth[row] = (line * inside(row, 1, height + 1)).astype(BF16)
        return carry

    lax.fori_loop(0, fifth.shape[0], up_step, 0, unroll=fifth.shape[0] // 2)

    colours = out_ref.shape[1]
    weight_out = beside(w_out)
    for row in range(height):
        lines = fifth[row : row + 3].reshape(3 * chans, width)
        total = jnp.dot(weight_out, lines, preferred_element_type=F32)
        line = across(total, w_out.shape[1], width)
        for colour in range(colours):
            final[colour, row : row + 1, :] = line[colour : colour + 1, :]
    out_ref[0] = final[...].astype(BF16)


def stem(where, field, w_in, w_mid):
    height = field.shape[0] // 3
    width = field.shape[2]
    one = w_mid.shape[1]
    return pl.pallas_call(
        stem_kernel,
        out_shape=jax.ShapeDtypeStruct((3 * height - 4, one, width), BF16),
        in_specs=[smem()] + [vmem()] * 3,
        out_specs=vmem(),
        scratch_shapes=[pltpu.VMEM((3 * height - 2, one, width), BF16)],
        compiler_params=params(16),
        cost_estimate=pl.CostEstimate(
            flops=1_000_000_000, bytes_accessed=MIB, transcendentals=300_000
        ),
        name="stem",
    )(where, field, w_in, w_mid)


def middle(where, second, w_down, w_deep):
    rows, one, width = second.shape
    half = (rows + 4) // 6
    two = w_deep.shape[1]
    return pl.pallas_call(
        middle_kernel,
        out_shape=jax.ShapeDtypeStruct((3 * half - 6, two, width // 2), BF16),
        in_specs=[smem()] + [vmem()] * 3,
        out_specs=vmem(),
        scratch_shapes=[
            pltpu.VMEM((3 * half - 2, one, width // 2), BF16),
            pltpu.VMEM((3 * half - 4, two, width // 2), BF16),
        ],
        compiler_params=params(16),
        cost_estimate=pl.CostEstimate(
            flops=1_000_000_000, bytes_accessed=MIB, transcendentals=200_000
        ),
        name="middle",
    )(where, second, w_down, w_deep)


def decoder(where, second, deep, w_up, w_out, height, colours):
    one = second.shape[1]
    two = deep.shape[1]
    width = second.shape[2]
    return pl.pallas_call(
        decoder_kernel,
        out_shape=jax.ShapeDtypeStruct((1, colours, height, width), BF16),
        in_specs=[smem()] + [vmem()] * 4,
        out_specs=vmem(),
        scratch_shapes=[
            pltpu.VMEM((height + 4, one + two, width), BF16),
            pltpu.VMEM((height + 2, one, width), BF16),
            pltpu.VMEM((colours, height, width), F32),
        ],
        compiler_params=params(16),
        cost_estimate=pl.CostEstimate(
            flops=1_000_000_000, bytes_accessed=MIB, transcendentals=100_000
        ),
        name="decoder",
    )(where, second, deep, w_up, w_out)


def on_device(
    bricks, sends, cells, fracs, sample_order, pending, w_in, w_mid, w_down, w_deep, w_up, w_out
):
    n_tile = lax.axis_size("tile")
    tile = lax.axis_index("tile")
    n_section = lax.axis_size("section")
    cap = sends.shape[3]
    height = pending.shape[2]
    width = pending.shape[3]
    samples = cells.shape[3]
    slots = n_tile * cap
    per_slot = samples // slots
    padded = -(-per_slot // BLOCK) * BLOCK

    def fill(part):
        if padded != per_slot:
            part = part.reshape(3, slots, per_slot)
            part = jnp.pad(part, ((0, 0), (0, 0), (0, padded - per_slot)))
        return part.reshape(3, slots * padded // LANES, LANES)

    def trim(found):
        if padded == per_slot:
            return found
        return found.reshape(slots, padded)[:, :per_slot].reshape(1, samples // LANES, LANES)

    places = positions(fill(cells), fill(fracs), n_tile)
    places, bricks, pending = lax.optimization_barrier((places, bricks, pending))
    arrived = lax.all_to_all(places, "tile", split_axis=0, concat_axis=0, tiled=True)

    down = [(i, i + 1) for i in range(n_tile - 1)]
    up = [(i + 1, i) for i in range(n_tile - 1)]
    over = lax.ppermute(pending, "tile", down)
    under = lax.ppermute(pending, "tile", up)
    windows = windows_of(bricks)
    where = jnp.stack([tile, jnp.int32(n_tile)]).astype(jnp.int32)
    picks = sends[0, 0].T
    field = jnp.concatenate([over[0], pending[0], under[0]], axis=1).transpose(1, 0, 2)
    field = jnp.pad(field, ((0, 0), (0, 16 - field.shape[1]), (0, 0)))
    colours = w_out.shape[1]
    w_in = jnp.pad(w_in, ((0, 0), (0, 0), (0, 16 - w_in.shape[2])))
    w_out = jnp.pad(w_out, ((0, 0), (0, 16 - colours), (0, 0)))

    second = stem(where, field, w_in, w_mid)
    arrived, second, w_down, w_out = lax.optimization_barrier((arrived, second, w_down, w_out))
    found = sample_values(picks, windows, arrived)
    found, second = lax.optimization_barrier((found, second))
    values = lax.all_to_all(found, "tile", split_axis=0, concat_axis=0, tiled=True)
    deep = middle(where, second, w_down, w_deep)
    values, deep = lax.optimization_barrier((values, deep))
    rendered = gbuffer(trim(values), sample_order, height, width)
    rendered, deep = lax.optimization_barrier((rendered, deep))
    ring = [(i, (i + 1) % n_section) for i in range(n_section)]
    handoff = lax.ppermute(rendered, "section", ring)
    denoised = decoder(where, second, deep, w_up, w_out, height, colours)
    return (handoff, denoised)


def solution(mesh):
    in_specs = (
        P("tile", None),
        P("section", "tile", None, None),
        P("section", "tile", None, None),
        P("section", "tile", None, None),
        P("section", "tile", None, None),
        P("section", None, "tile", None),
        P(),
        P(),
        P(),
        P(),
        P(),
        P(),
    )
    out_specs = (P("section", None, "tile", None), P("section", None, "tile", None))
    return jax.shard_map(
        on_device, mesh=mesh, in_specs=in_specs, out_specs=out_specs, check_vma=False
    )
```

```python
import functools

import jax
import jax.numpy as jnp
from jax import lax
from jax.experimental import pallas as pl
from jax.experimental.pallas import tpu as pltpu
from jax.sharding import PartitionSpec as P

EDGE = 34
NSP = 4
NRAY = 8
NOS = 2
LANES = 128
BLOCK = 256
STRIDE = 6
WINDOWS = 6
MAIN = 32
TAIL = 16
BRICK_ROWS = WINDOWS * MAIN + TAIL
KDIM = 256

F32 = jnp.float32
BF16 = jnp.bfloat16
MIB = 1024 * 1024


def params(mib):
    return pltpu.CompilerParams(vmem_limit_bytes=mib * MIB)


def vmem():
    return pl.BlockSpec(memory_space=pltpu.VMEM)


def smem():
    return pl.BlockSpec(memory_space=pltpu.SMEM)


def positions_kernel(cells_ref, fracs_ref, out_ref, cells, fracs, found, arrivals, departures):
    owners, rows, _ = out_ref.shape
    lines = rows // 3
    parts = arrivals.shape[1]
    share = owners // parts
    pieces = [(axis, part) for axis in range(3) for part in range(parts)]

    def reads(axis, part):
        span = pl.ds(part * share * lines, share * lines)
        return [
            pltpu.make_async_copy(
                source.at[axis, span], target.at[axis, span], arrivals.at[axis, part, number]
            )
            for number, (source, target) in enumerate(((cells_ref, cells), (fracs_ref, fracs)))
        ]

    def write(axis, part):
        place = (pl.ds(part * share, share), pl.ds(axis * lines, lines))
        return pltpu.make_async_copy(
            found.at[place], out_ref.at[place], departures.at[axis, part]
        )

    for piece in pieces:
        for copy in reads(*piece):
            copy.start()
    for axis, part in pieces:
        for copy in reads(axis, part):
            copy.wait()
        span = slice(part * share * lines, (part + 1) * share * lines)
        place = cells[axis, span].astype(F32) + fracs[axis, span]
        found[part * share : (part + 1) * share, axis * lines : (axis + 1) * lines, :] = (
            place.reshape(share, lines, LANES)
        )
        write(axis, part).start()
    for piece in pieces:
        write(*piece).wait()


def positions(cells, fracs, owners):
    lines = cells.shape[1]
    shape = (owners, 3 * lines // owners, LANES)
    hbm = pl.BlockSpec(memory_space=pltpu.HBM)
    return pl.pallas_call(
        positions_kernel,
        out_shape=jax.ShapeDtypeStruct(shape, F32),
        in_specs=[hbm, hbm],
        out_specs=hbm,
        scratch_shapes=[
            pltpu.VMEM(cells.shape, jnp.int32),
            pltpu.VMEM(fracs.shape, F32),
            pltpu.VMEM(shape, F32),
            pltpu.SemaphoreType.DMA((3, 2, 2)),
            pltpu.SemaphoreType.DMA((3, 2)),
        ],
        compiler_params=params(60),
        cost_estimate=pl.CostEstimate(
            flops=3 * lines * LANES, bytes_accessed=36 * lines * LANES, transcendentals=0
        ),
        name="positions",
    )(cells, fracs)


def windows_kernel(cube_ref, out_ref, wide, tail):
    count = cube_ref.shape[0]
    plane = EDGE * EDGE
    wide[...] = jnp.zeros_like(wide)
    wide[:, :EDGE, :plane] = cube_ref[...]
    column = lax.broadcasted_iota(jnp.int32, (1, KDIM), 1)
    main = (column // MAIN) * EDGE + column % MAIN
    rest = column - 7 * MAIN
    last = (rest % 8) * EDGE + MAIN + rest // 8
    source = jnp.where(column < 7 * MAIN, main, last)
    unused = (column >= 7 * MAIN) & ((rest % 8 == 7) | (rest >= TAIL))
    source = jnp.where(unused, -(1 << 20), source)
    for window in range(WINDOWS):
        first = window * STRIDE * EDGE
        low = first // LANES * LANES
        length = min(3 * LANES, wide.shape[2] - low)
        place = lax.broadcasted_iota(jnp.int32, (length, KDIM), 0)
        pick = jnp.where(place == source + (first - low), 1.0, 0.0).astype(BF16)
        found = jnp.dot(
            wide[:, :, low : low + length].reshape(-1, length),
            pick,
            preferred_element_type=F32,
        )
        found = found.reshape(count, 48, KDIM)
        out_ref[:, window * MAIN : (window + 1) * MAIN, :] = found[:, :MAIN, :].astype(BF16)
        tail[:, window : window + 1, :] = found[:, MAIN : MAIN + 1, :]
        tail[:, 8 + window : 9 + window, :] = found[:, MAIN + 1 : MAIN + 2, :]
    for row in (6, 7, 14, 15):
        tail[:, row : row + 1, :] = jnp.zeros((count, 1, KDIM), F32)
    out_ref[:, WINDOWS * MAIN :, :] = tail[...].astype(BF16)


def windows_of(bricks):
    count = bricks.shape[0]
    cube = bricks.reshape(count, EDGE, EDGE * EDGE)
    return pl.pallas_call(
        windows_kernel,
        out_shape=jax.ShapeDtypeStruct((count, BRICK_ROWS, KDIM), BF16),
        in_specs=[vmem()],
        out_specs=vmem(),
        scratch_shapes=[
            pltpu.VMEM((count, 48, 10 * LANES), BF16),
            pltpu.VMEM((count, TAIL, KDIM), F32),
        ],
        compiler_params=params(16),
        cost_estimate=pl.CostEstimate(
            flops=2 * count * 48 * 384 * KDIM * WINDOWS, bytes_accessed=4 * 1024 * 1024,
            transcendentals=0,
        ),
        name="brick_windows",
    )(cube)


def hat(distance):
    return jnp.maximum(1.0 - jnp.abs(distance), 0.0)


def blend(brick, px, py, pz):
    width = px.shape[1]
    eight = lax.broadcasted_iota(jnp.int32, (8, width), 0).astype(F32)
    places = lax.broadcasted_iota(jnp.int32, (MAIN, width), 0).astype(F32).astype(BF16)

    def tile(rows):
        return jnp.concatenate([rows, rows], axis=0).astype(BF16)

    cell_y = jnp.floor(py)
    frac_y = py - cell_y
    lower, low_share, high_share = tile(cell_y), tile(1.0 - frac_y), tile(frac_y)
    nothing = jnp.zeros((TAIL, width), BF16)
    weight_y = []
    for start in range(0, MAIN, TAIL):
        offset = places[start : start + TAIL] - lower
        weight_y.append(
            jnp.where(offset == 0, low_share, jnp.where(offset == 1, high_share, nothing))
        )
    window = jnp.floor(px * (1.0 / STRIDE))
    weight_x = hat(eight - (px - STRIDE * window))
    parts = []
    for i in range(STRIDE + 1):
        share = tile(jnp.broadcast_to(weight_x[i : i + 1], (8, width)))
        parts += [share * part for part in weight_y]
    tail = [weight_x * hat(MAIN - py), weight_x * jnp.maximum(py - MAIN, 0.0)]
    parts.append(jnp.concatenate(tail, axis=0).astype(BF16))
    parts.append(nothing)
    plane = jnp.concatenate(parts, axis=0)
    found = jnp.dot(brick, plane, preferred_element_type=F32)
    groups = range(0, MAIN, 8)
    chosen = [found[row : row + 8] for row in groups]
    for other in range(1, WINDOWS):
        here = window == float(other)
        base = other * MAIN
        chosen = [
            jnp.where(here, found[base + row : base + row + 8], old)
            for row, old in zip(groups, chosen)
        ]
    base = WINDOWS * MAIN
    edges = found[base : base + 8] * hat(MAIN - pz)
    edges = edges + found[base + 8 :] * jnp.maximum(pz - MAIN, 0.0)
    total = jnp.where(eight == window, edges, 0.0)
    for row, part in zip(groups, chosen):
        total = total + part * hat((eight + float(row)) - pz)
    return total


def samples_kernel(picks_ref, brick_ref, place_ref, out_ref, bricks, places, sums, arrivals):
    owners, rows, _ = place_ref.shape
    cap = picks_ref.shape[0]
    lines = rows // 3
    per_slot = lines // 2 // cap
    group = places.shape[1]
    turns = owners // group

    def fetches(turn):
        held = turn % 2
        copies = []
        for member in range(group):
            renderer = turn * group + member
            copies.append(
                pltpu.make_async_copy(
                    place_ref.at[renderer],
                    places.at[held, member],
                    arrivals.at[held, member, cap],
                )
            )
            for piece in range(cap):
                copies.append(
                    pltpu.make_async_copy(
                        brick_ref.at[picks_ref[piece, renderer]],
                        bricks.at[held, member, piece],
                        arrivals.at[held, member, piece],
                    )
                )
        return copies

    for turn in range(min(2, turns)):
        for copy in fetches(turn):
            copy.start()

    def one_turn(turn, carry):
        held = turn % 2
        for copy in fetches(turn):
            copy.wait()
        for member in range(group):
            for piece in range(cap):
                brick = bricks[held, member, piece]
                for step in range(per_slot):
                    row = 2 * (piece * per_slot + step)

                    def line(axis):
                        both = [
                            jnp.broadcast_to(
                                places[held, member, pl.ds(axis * lines + row + half, 1), :],
                                (8, LANES),
                            )
                            for half in range(2)
                        ]
                        return jnp.concatenate(both, axis=1)

                    total = blend(brick, line(0), line(1), line(2))
                    for half in range(2):
                        sums[member, 8 * (row + half) : 8 * (row + half + 1), :] = total[
                            :, half * LANES : (half + 1) * LANES
                        ]
            values = []
            for row in range(0, lines, 8):
                value = sums[member, pl.ds(8 * row, 8, stride=8), :]
                for other in range(1, 8):
                    value = value + sums[member, pl.ds(8 * row + other, 8, stride=8), :]
                values.append(value)
            out_ref[turn * group + member] = jnp.concatenate(values, axis=0).astype(BF16)

        @pl.when(turn + 2 < turns)
        def _():
            for copy in fetches(turn + 2):
                copy.start()

        return carry

    lax.fori_loop(0, turns, one_turn, 0)


def sample_values(picks, windows, places):
    owners, rows, _ = places.shape
    cap = picks.shape[0]
    group = 2 if owners % 2 == 0 else 1
    samples = owners * rows * LANES // 3
    some = pl.BlockSpec(memory_space=pl.ANY)
    return pl.pallas_call(
        samples_kernel,
        out_shape=jax.ShapeDtypeStruct((owners, rows // 3, LANES), BF16),
        in_specs=[smem(), some, some],
        out_specs=vmem(),
        scratch_shapes=[
            pltpu.VMEM((2, group, cap, BRICK_ROWS, KDIM), BF16),
            pltpu.VMEM((2, group, rows, LANES), F32),
            pltpu.VMEM((group, 8 * rows // 3, LANES), F32),
            pltpu.SemaphoreType.DMA((2, group, cap + 1)),
        ],
        compiler_params=params(59),
        cost_estimate=pl.CostEstimate(
            flops=2 * samples * KDIM * BRICK_ROWS, bytes_accessed=3 * MIB,
            transcendentals=0,
        ),
        name="sample_values",
    )(picks, windows, places)


def gbuffer_kernel(value_ref, order_ref, out_ref, values):
    values[...] = value_ref[...].astype(F32).reshape(values.shape)
    height = out_ref.shape[2]

    def ray_of(number):
        rows_now = slice(number * height, (number + 1) * height)
        first, second = (
            values[pl.ds(2 * number * height + half, height, stride=2), :] for half in range(2)
        )
        parts = []
        for half in range(2):
            order = order_ref[0, 0, rows_now, half * LANES : (half + 1) * LANES]
            inner = order & (LANES - 1)
            parts.append(
                jnp.where(
                    order < LANES,
                    jnp.take_along_axis(first, inner, axis=1, mode="promise_in_bounds"),
                    jnp.take_along_axis(second, inner, axis=1, mode="promise_in_bounds"),
                )
            )
        return jnp.concatenate(parts, axis=1)

    remain = 1.0
    shade = 0.0
    depth = 0.0
    for step in range(NSP):
        ray = ray_of(step)
        half_tanh = 0.5 * jnp.tanh(ray)
        weight = remain * (0.5 + half_tanh)
        shade = shade + weight * ray
        depth = depth + weight * ((step + 1) / NSP)
        remain = remain * (0.5 - half_tanh)
    occlusion = 0.0
    for ray_number in range(NRAY):
        passing = 1.0
        for step in range(NOS):
            ray = ray_of(NSP + ray_number * NOS + step)
            passing = passing * (0.5 - 0.5 * jnp.tanh(ray))
        occlusion = occlusion + passing
    out_ref[0, 0] = shade.astype(BF16)
    out_ref[0, 1] = (1.0 - remain).astype(BF16)
    out_ref[0, 2] = depth.astype(BF16)
    out_ref[0, 3] = (occlusion * (1.0 / NRAY)).astype(BF16)


def gbuffer(values, order, height, width):
    total = order.shape[2]
    return pl.pallas_call(
        gbuffer_kernel,
        out_shape=jax.ShapeDtypeStruct((1, 4, height, width), BF16),
        in_specs=[vmem(), vmem()],
        out_specs=vmem(),
        scratch_shapes=[pltpu.VMEM((2 * total, LANES), F32)],
        compiler_params=params(16),
        cost_estimate=pl.CostEstimate(
            flops=20 * total * BLOCK, bytes_accessed=8 * total * BLOCK, transcendentals=0
        ),
        name="gbuffer",
    )(values, order)


def silu(field):
    half = 0.5 * field
    return half + half * jnp.tanh(half)


def shifted(rows, steps):
    lane = lax.broadcasted_iota(jnp.int32, (1, LANES), 1)
    edge = lane == (0 if steps == 1 else LANES - 1)
    moved = []
    for row in rows:
        tiles = [row[:, i : i + LANES] for i in range(0, row.shape[1], LANES)]
        tiles = [pltpu.roll(tile, steps % LANES, 1) for tile in tiles]
        for i, tile in enumerate(tiles):
            source = i - steps
            fill = tiles[source] if 0 <= source < len(tiles) else 0.0
            moved.append(jnp.where(edge, fill, tile))
    return jnp.concatenate(moved, axis=1)


def across(total, chans, row_width):
    left, middle, right = (total[i * chans : (i + 1) * chans] for i in range(3))

    def rows_of(part):
        return [part[:, i : i + row_width] for i in range(0, part.shape[1], row_width)]

    return middle + shifted(rows_of(left), 1) + shifted(rows_of(right), -1)


def taps(weight_ref, tap):
    _, out_chans, chans = weight_ref.shape
    return weight_ref[3 * tap : 3 * tap + 3].reshape(3 * out_chans, chans)


def beside(weight_ref):
    return jnp.concatenate([taps(weight_ref, tap) for tap in range(3)], axis=1)


def sides(where_ref):
    above = jnp.where(where_ref[0] > 0, 1.0, 0.0)
    below = jnp.where(where_ref[0] < where_ref[1] - 1, 1.0, 0.0)

    def inside(row, low, high):
        return jnp.where(row < low, above, jnp.where(row >= high, below, 1.0))

    return inside


def stem_kernel(where_ref, x_ref, w_in, w_mid, second, first):
    height = x_ref.shape[0] // 3
    width = x_ref.shape[2]
    inside = sides(where_ref)

    def full_layer(weight, source, target, low, high, unroll):
        chans = target.shape[1]
        depth = weight.shape[1]

        def step(row, carry):
            lines = source[pl.ds(row, 3)].reshape(depth, width)
            line = across(jnp.dot(weight, lines, preferred_element_type=F32), chans, width)
            target[row] = (silu(line) * inside(row, low, high)).astype(BF16)
            return carry

        lax.fori_loop(0, target.shape[0], step, 0, unroll=unroll)

    full_layer(beside(w_in), x_ref, first, height - 1, 2 * height - 1, first.shape[0] // 2)
    full_layer(beside(w_mid), first, second, height - 2, 2 * height - 2, second.shape[0] // 2)


def middle_kernel(where_ref, second, w_down, w_deep, fourth, pooled, third):
    count, chans, width = second.shape
    half_height = (count + 4) // 6
    half_width = width // 2
    inside = sides(where_ref)
    place = lax.broadcasted_iota(jnp.int32, (width, half_width), 0) // 2
    target = lax.broadcasted_iota(jnp.int32, (width, half_width), 1)
    shrink = jnp.where(place == target, 0.25, 0.0).astype(BF16)
    pairs = jnp.dot(
        second[...].reshape(count * chans, width), shrink, preferred_element_type=F32
    ).reshape(count // 2, 2, chans, half_width)
    pooled[...] = (pairs[:, 0] + pairs[:, 1]).astype(BF16)

    def half_pair(source, row, tap):
        return jnp.concatenate([source[row + tap], source[row + tap + 1]], axis=1)

    def half_layer(product, target, low, high):
        chans = target.shape[1]
        for row in range(0, target.shape[0], 2):
            both = silu(across(product(row), chans, half_width))
            for now in range(2):
                line = both[:, now * half_width : (now + 1) * half_width]
                if row + now < low or row + now >= high:
                    line = line * inside(row + now, low, high)
                target[row + now] = line.astype(BF16)

    weight_down = beside(w_down)

    def down_product(row):
        lines = jnp.concatenate([half_pair(pooled, row, tap) for tap in range(3)], axis=0)
        return jnp.dot(weight_down, lines, preferred_element_type=F32)

    def deep_product(row):
        total = None
        for tap in range(3):
            part = jnp.dot(
                taps(w_deep, tap), half_pair(third, row, tap), preferred_element_type=F32
            )
            total = part if total is None else total + part
        return total

    half_layer(down_product, third, half_height - 2, 2 * half_height - 2)
    half_layer(deep_product, fourth, half_height - 3, 2 * half_height - 3)


def decoder_kernel(
    where_ref, second, fourth, w_up, w_out, out_ref, joined, fifth, final
):
    height = out_ref.shape[2]
    width = out_ref.shape[3]
    half_width = width // 2
    chans = second.shape[1]
    inside = sides(where_ref)
    place = lax.broadcasted_iota(jnp.int32, (half_width, width), 0)
    target = lax.broadcasted_iota(jnp.int32, (half_width, width), 1) // 2
    spread = jnp.where(place == target, 1.0, 0.0).astype(BF16)
    deep = fourth.shape[1]
    wide = jnp.dot(
        fourth[...].reshape(-1, half_width), spread, preferred_element_type=F32
    ).astype(BF16).reshape(fourth.shape[0], deep, width)
    for row in range(2 * fourth.shape[0]):
        joined[row, chans:, :] = wide[row // 2]
        joined[row, :chans, :] = second[row + 4]

    def up_step(row, carry):
        total = None
        for tap in range(3):
            part = jnp.dot(taps(w_up, tap), joined[row + tap], preferred_element_type=F32)
            total = part if total is None else total + part
        line = silu(across(total, chans, width))
        fifth[row] = (line * inside(row, 1, height + 1)).astype(BF16)
        return carry

    lax.fori_loop(0, fifth.shape[0], up_step, 0, unroll=fifth.shape[0] // 2)

    colours = out_ref.shape[1]
    weight_out = beside(w_out)
    for row in range(height):
        lines = fifth[row : row + 3].reshape(3 * chans, width)
        total = jnp.dot(weight_out, lines, preferred_element_type=F32)
        line = across(total, w_out.shape[1], width)
        for colour in range(colours):
            final[colour, row : row + 1, :] = line[colour : colour + 1, :]
    out_ref[0] = final[...].astype(BF16)


def stem(where, field, w_in, w_mid):
    height = field.shape[0] // 3
    width = field.shape[2]
    one = w_mid.shape[1]
    return pl.pallas_call(
        stem_kernel,
        out_shape=jax.ShapeDtypeStruct((3 * height - 4, one, width), BF16),
        in_specs=[smem()] + [vmem()] * 3,
        out_specs=vmem(),
        scratch_shapes=[pltpu.VMEM((3 * height - 2, one, width), BF16)],
        compiler_params=params(16),
        cost_estimate=pl.CostEstimate(
            flops=1_000_000_000, bytes_accessed=MIB, transcendentals=300_000
        ),
        name="stem",
    )(where, field, w_in, w_mid)


def middle(where, second, w_down, w_deep):
    rows, one, width = second.shape
    half = (rows + 4) // 6
    two = w_deep.shape[1]
    return pl.pallas_call(
        middle_kernel,
        out_shape=jax.ShapeDtypeStruct((3 * half - 6, two, width // 2), BF16),
        in_specs=[smem()] + [vmem()] * 3,
        out_specs=vmem(),
        scratch_shapes=[
            pltpu.VMEM((3 * half - 2, one, width // 2), BF16),
            pltpu.VMEM((3 * half - 4, two, width // 2), BF16),
        ],
        compiler_params=params(16),
        cost_estimate=pl.CostEstimate(
            flops=1_000_000_000, bytes_accessed=MIB, transcendentals=200_000
        ),
        name="middle",
    )(where, second, w_down, w_deep)


def decoder(where, second, deep, w_up, w_out, height, colours):
    one = second.shape[1]
    two = deep.shape[1]
    width = second.shape[2]
    return pl.pallas_call(
        decoder_kernel,
        out_shape=jax.ShapeDtypeStruct((1, colours, height, width), BF16),
        in_specs=[smem()] + [vmem()] * 4,
        out_specs=vmem(),
        scratch_shapes=[
            pltpu.VMEM((height + 4, one + two, width), BF16),
            pltpu.VMEM((height + 2, one, width), BF16),
            pltpu.VMEM((colours, height, width), F32),
        ],
        compiler_params=params(16),
        cost_estimate=pl.CostEstimate(
            flops=1_000_000_000, bytes_accessed=MIB, transcendentals=100_000
        ),
        name="decoder",
    )(where, second, deep, w_up, w_out)


def on_device(
    bricks, sends, cells, fracs, sample_order, pending, w_in, w_mid, w_down, w_deep, w_up, w_out
):
    n_tile = lax.axis_size("tile")
    tile = lax.axis_index("tile")
    n_section = lax.axis_size("section")
    cap = sends.shape[3]
    height = pending.shape[2]
    width = pending.shape[3]
    samples = cells.shape[3]
    slots = n_tile * cap
    per_slot = samples // slots
    padded = -(-per_slot // BLOCK) * BLOCK

    def fill(part):
        if padded != per_slot:
            part = part.reshape(3, slots, per_slot)
            part = jnp.pad(part, ((0, 0), (0, 0), (0, padded - per_slot)))
        return part.reshape(3, slots * padded // LANES, LANES)

    def trim(found):
        if padded == per_slot:
            return found
        return found.reshape(slots, padded)[:, :per_slot].reshape(1, samples // LANES, LANES)

    places = positions(fill(cells), fill(fracs), n_tile)
    places, bricks, pending = lax.optimization_barrier((places, bricks, pending))
    arrived = lax.all_to_all(places, "tile", split_axis=0, concat_axis=0, tiled=True)

    down = [(i, i + 1) for i in range(n_tile - 1)]
    up = [(i + 1, i) for i in range(n_tile - 1)]
    over = lax.ppermute(pending, "tile", down)
    under = lax.ppermute(pending, "tile", up)
    windows = windows_of(bricks)
    where = jnp.stack([tile, jnp.int32(n_tile)]).astype(jnp.int32)
    picks = sends[0, 0].T
    found = sample_values(picks, windows, arrived)

    found, over, under, pending, w_in, w_down, w_out = lax.optimization_barrier(
        (found, over, under, pending, w_in, w_down, w_out)
    )
    values = lax.all_to_all(found, "tile", split_axis=0, concat_axis=0, tiled=True)
    field = jnp.concatenate([over[0], pending[0], under[0]], axis=1).transpose(1, 0, 2)
    field = jnp.pad(field, ((0, 0), (0, 16 - field.shape[1]), (0, 0)))
    colours = w_out.shape[1]
    w_in = jnp.pad(w_in, ((0, 0), (0, 0), (0, 16 - w_in.shape[2])))
    w_out = jnp.pad(w_out, ((0, 0), (0, 16 - colours), (0, 0)))
    second = stem(where, field, w_in, w_mid)
    deep = middle(where, second, w_down, w_deep)
    values, deep = lax.optimization_barrier((values, deep))
    rendered = gbuffer(trim(values), sample_order, height, width)
    rendered, deep = lax.optimization_barrier((rendered, deep))
    ring = [(i, (i + 1) % n_section) for i in range(n_section)]
    handoff = lax.ppermute(rendered, "section", ring)
    denoised = decoder(where, second, deep, w_up, w_out, height, colours)
    return (handoff, denoised)


def solution(mesh):
    in_specs = (
        P("tile", None),
        P("section", "tile", None, None),
        P("section", "tile", None, None),
        P("section", "tile", None, None),
        P("section", "tile", None, None),
        P("section", None, "tile", None),
        P(),
        P(),
        P(),
        P(),
        P(),
        P(),
    )
    out_specs = (P("section", None, "tile", None), P("section", None, "tile", None))
    return jax.shard_map(
        on_device, mesh=mesh, in_specs=in_specs, out_specs=out_specs, check_vma=False
    )
```

```python
import functools

import jax
import jax.numpy as jnp
from jax import lax
from jax.experimental import pallas as pl
from jax.experimental.pallas import tpu as pltpu
from jax.sharding import PartitionSpec as P

EDGE = 34
NSP = 4
NRAY = 8
NOS = 2
LANES = 128
BLOCK = 256
STRIDE = 6
WINDOWS = 6
MAIN = 32
TAIL = 16
BRICK_ROWS = WINDOWS * MAIN + TAIL
KDIM = 256

F32 = jnp.float32
BF16 = jnp.bfloat16
MIB = 1024 * 1024


def params(mib):
    return pltpu.CompilerParams(vmem_limit_bytes=mib * MIB)


def vmem():
    return pl.BlockSpec(memory_space=pltpu.VMEM)


def smem():
    return pl.BlockSpec(memory_space=pltpu.SMEM)


def positions_kernel(cells_ref, fracs_ref, out_ref, cells, fracs, found, arrivals, departures):
    owners, rows, _ = out_ref.shape
    lines = rows // 3
    parts = arrivals.shape[1]
    share = owners // parts
    pieces = [(axis, part) for axis in range(3) for part in range(parts)]

    def reads(axis, part):
        span = pl.ds(part * share * lines, share * lines)
        return [
            pltpu.make_async_copy(
                source.at[axis, span], target.at[axis, span], arrivals.at[axis, part, number]
            )
            for number, (source, target) in enumerate(((cells_ref, cells), (fracs_ref, fracs)))
        ]

    def write(axis, part):
        place = (pl.ds(part * share, share), pl.ds(axis * lines, lines))
        return pltpu.make_async_copy(
            found.at[place], out_ref.at[place], departures.at[axis, part]
        )

    for piece in pieces:
        for copy in reads(*piece):
            copy.start()
    for axis, part in pieces:
        for copy in reads(axis, part):
            copy.wait()
        span = slice(part * share * lines, (part + 1) * share * lines)
        place = cells[axis, span].astype(F32) + fracs[axis, span]
        found[part * share : (part + 1) * share, axis * lines : (axis + 1) * lines, :] = (
            place.reshape(share, lines, LANES)
        )
        write(axis, part).start()
    for piece in pieces:
        write(*piece).wait()


def positions(cells, fracs, owners):
    lines = cells.shape[1]
    shape = (owners, 3 * lines // owners, LANES)
    hbm = pl.BlockSpec(memory_space=pltpu.HBM)
    return pl.pallas_call(
        positions_kernel,
        out_shape=jax.ShapeDtypeStruct(shape, F32),
        in_specs=[hbm, hbm],
        out_specs=hbm,
        scratch_shapes=[
            pltpu.VMEM(cells.shape, jnp.int32),
            pltpu.VMEM(fracs.shape, F32),
            pltpu.VMEM(shape, F32),
            pltpu.SemaphoreType.DMA((3, 2, 2)),
            pltpu.SemaphoreType.DMA((3, 2)),
        ],
        compiler_params=params(60),
        cost_estimate=pl.CostEstimate(
            flops=3 * lines * LANES, bytes_accessed=36 * lines * LANES, transcendentals=0
        ),
        name="positions",
    )(cells, fracs)


def windows_kernel(
    where_ref, picks_ref, cube_ref, place_ref, out_ref, own_ref,
    wide, tail, places, sums, arrival,
):
    tile = where_ref[0]
    own_places = pltpu.make_async_copy(place_ref.at[tile], places, arrival)
    own_places.start()
    count = cube_ref.shape[0]
    plane = EDGE * EDGE
    wide[...] = jnp.zeros_like(wide)
    wide[:, :EDGE, :plane] = cube_ref[...]
    column = lax.broadcasted_iota(jnp.int32, (1, KDIM), 1)
    main = (column // MAIN) * EDGE + column % MAIN
    rest = column - 7 * MAIN
    last = (rest % 8) * EDGE + MAIN + rest // 8
    source = jnp.where(column < 7 * MAIN, main, last)
    unused = (column >= 7 * MAIN) & ((rest % 8 == 7) | (rest >= TAIL))
    source = jnp.where(unused, -(1 << 20), source)
    for window in range(WINDOWS):
        first = window * STRIDE * EDGE
        low = first // LANES * LANES
        length = min(3 * LANES, wide.shape[2] - low)
        place = lax.broadcasted_iota(jnp.int32, (length, KDIM), 0)
        pick = jnp.where(place == source + (first - low), 1.0, 0.0).astype(BF16)
        found = jnp.dot(
            wide[:, :, low : low + length].reshape(-1, length),
            pick,
            preferred_element_type=F32,
        )
        found = found.reshape(count, 48, KDIM)
        out_ref[:, window * MAIN : (window + 1) * MAIN, :] = found[:, :MAIN, :].astype(BF16)
        tail[:, window : window + 1, :] = found[:, MAIN : MAIN + 1, :]
        tail[:, 8 + window : 9 + window, :] = found[:, MAIN + 1 : MAIN + 2, :]
    for row in (6, 7, 14, 15):
        tail[:, row : row + 1, :] = jnp.zeros((count, 1, KDIM), F32)
    out_ref[:, WINDOWS * MAIN :, :] = tail[...].astype(BF16)

    own_places.wait()
    cap = picks_ref.shape[0]
    lines = places.shape[0] // 3
    part = lines // cap

    def one_slot(piece, carry):
        brick = out_ref[picks_ref[piece, tile]]
        slot_sums(brick, places, sums, piece * part, part // 2)
        return carry

    lax.fori_loop(0, cap, one_slot, 0)
    own_ref[0] = line_values(sums, lines)


def windows_of(where, picks, bricks, places):
    count = bricks.shape[0]
    cube = bricks.reshape(count, EDGE, EDGE * EDGE)
    rows = places.shape[1]
    return pl.pallas_call(
        windows_kernel,
        out_shape=(
            jax.ShapeDtypeStruct((count, BRICK_ROWS, KDIM), BF16),
            jax.ShapeDtypeStruct((1, rows // 3, LANES), BF16),
        ),
        in_specs=[smem(), smem(), vmem(), pl.BlockSpec(memory_space=pl.ANY)],
        out_specs=(vmem(), vmem()),
        scratch_shapes=[
            pltpu.VMEM((count, 48, 10 * LANES), BF16),
            pltpu.VMEM((count, TAIL, KDIM), F32),
            pltpu.VMEM((rows, LANES), F32),
            pltpu.VMEM((8 * rows // 3, LANES), F32),
            pltpu.SemaphoreType.DMA,
        ],
        compiler_params=params(16),
        cost_estimate=pl.CostEstimate(
            flops=2 * count * 48 * 384 * KDIM * WINDOWS, bytes_accessed=4 * MIB,
            transcendentals=0,
        ),
        name="brick_windows",
    )(where, picks, cube, places)


def hat(distance):
    return jnp.maximum(1.0 - jnp.abs(distance), 0.0)


def blend(brick, px, py, pz):
    width = px.shape[1]
    eight = lax.broadcasted_iota(jnp.int32, (8, width), 0).astype(F32)
    places = lax.broadcasted_iota(jnp.int32, (MAIN, width), 0).astype(F32).astype(BF16)

    def tile(rows):
        return jnp.concatenate([rows, rows], axis=0).astype(BF16)

    cell_y = jnp.floor(py)
    frac_y = py - cell_y
    lower, low_share, high_share = tile(cell_y), tile(1.0 - frac_y), tile(frac_y)
    nothing = jnp.zeros((TAIL, width), BF16)
    weight_y = []
    for start in range(0, MAIN, TAIL):
        offset = places[start : start + TAIL] - lower
        weight_y.append(
            jnp.where(offset == 0, low_share, jnp.where(offset == 1, high_share, nothing))
        )
    window = jnp.floor(px * (1.0 / STRIDE))
    weight_x = hat(eight - (px - STRIDE * window))
    parts = []
    for i in range(STRIDE + 1):
        share = tile(jnp.broadcast_to(weight_x[i : i + 1], (8, width)))
        parts += [share * part for part in weight_y]
    tail = [weight_x * hat(MAIN - py), weight_x * jnp.maximum(py - MAIN, 0.0)]
    parts.append(jnp.concatenate(tail, axis=0).astype(BF16))
    parts.append(nothing)
    plane = jnp.concatenate(parts, axis=0)
    found = jnp.dot(brick, plane, preferred_element_type=F32)
    groups = range(0, MAIN, 8)
    chosen = [found[row : row + 8] for row in groups]
    for other in range(1, WINDOWS):
        here = window == float(other)
        base = other * MAIN
        chosen = [
            jnp.where(here, found[base + row : base + row + 8], old)
            for row, old in zip(groups, chosen)
        ]
    base = WINDOWS * MAIN
    edges = found[base : base + 8] * hat(MAIN - pz)
    edges = edges + found[base + 8 :] * jnp.maximum(pz - MAIN, 0.0)
    total = jnp.where(eight == window, edges, 0.0)
    for row, part in zip(groups, chosen):
        total = total + part * hat((eight + float(row)) - pz)
    return total


def slot_sums(brick, places, sums, first, blocks):
    lines = places.shape[0] // 3
    for step in range(blocks):
        row = first + 2 * step

        def line(axis):
            both = [
                jnp.broadcast_to(places[pl.ds(axis * lines + row + half, 1), :], (8, LANES))
                for half in range(2)
            ]
            return jnp.concatenate(both, axis=1)

        total = blend(brick, line(0), line(1), line(2))
        for half in range(2):
            sums[pl.ds(pl.multiple_of(8 * (row + half), 8), 8), :] = total[
                :, half * LANES : (half + 1) * LANES
            ]


def line_values(sums, lines):
    values = []
    for row in range(0, lines, 8):
        value = sums[pl.ds(8 * row, 8, stride=8), :]
        for other in range(1, 8):
            value = value + sums[pl.ds(8 * row + other, 8, stride=8), :]
        values.append(value)
    return jnp.concatenate(values, axis=0).astype(BF16)


def samples_kernel(
    where_ref, picks_ref, brick_ref, place_ref, own_ref, out_ref, bricks, places, sums, arrivals
):
    owners, rows, _ = place_ref.shape
    cap = picks_ref.shape[0]
    lines = rows // 3
    part = lines // cap
    turns = owners - 1
    tile = where_ref[0]
    out_ref[tile] = own_ref[0]

    def renderer_of(turn):
        return lax.rem(tile + 1 + turn, owners)

    def fetches(turn):
        held = turn % 2
        renderer = renderer_of(turn)
        copies = [
            pltpu.make_async_copy(
                place_ref.at[renderer], places.at[held], arrivals.at[held, cap]
            )
        ]
        for piece in range(cap):
            copies.append(
                pltpu.make_async_copy(
                    brick_ref.at[picks_ref[piece, renderer]],
                    bricks.at[held, piece],
                    arrivals.at[held, piece],
                )
            )
        return copies

    for turn in range(min(2, turns)):
        for copy in fetches(turn):
            copy.start()

    def one_turn(turn, carry):
        held = turn % 2
        for copy in fetches(turn):
            copy.wait()
        for piece in range(cap):
            slot_sums(bricks[held, piece], places.at[held], sums, piece * part, part // 2)
        out_ref[renderer_of(turn)] = line_values(sums, lines)

        @pl.when(turn + 2 < turns)
        def _():
            for copy in fetches(turn + 2):
                copy.start()

        return carry

    lax.fori_loop(0, turns, one_turn, 0)


def sample_values(where, picks, windows, places, own):
    owners, rows, _ = places.shape
    cap = picks.shape[0]
    samples = owners * rows * LANES // 3
    some = pl.BlockSpec(memory_space=pl.ANY)
    return pl.pallas_call(
        samples_kernel,
        out_shape=jax.ShapeDtypeStruct((owners, rows // 3, LANES), BF16),
        in_specs=[smem(), smem(), some, some, vmem()],
        out_specs=vmem(),
        scratch_shapes=[
            pltpu.VMEM((2, cap, BRICK_ROWS, KDIM), BF16),
            pltpu.VMEM((2, rows, LANES), F32),
            pltpu.VMEM((8 * rows // 3, LANES), F32),
            pltpu.SemaphoreType.DMA((2, cap + 1)),
        ],
        compiler_params=pltpu.CompilerParams(vmem_limit_bytes=61_600_000),
        cost_estimate=pl.CostEstimate(
            flops=2 * samples * KDIM * BRICK_ROWS, bytes_accessed=3 * MIB,
            transcendentals=0,
        ),
        name="sample_values",
    )(where, picks, windows, places, own)


def gbuffer_kernel(value_ref, order_ref, out_ref, values):
    values[...] = value_ref[...].astype(F32).reshape(values.shape)
    height = out_ref.shape[2]

    def ray_of(number):
        rows_now = slice(number * height, (number + 1) * height)
        first, second = (
            values[pl.ds(2 * number * height + half, height, stride=2), :] for half in range(2)
        )
        parts = []
        for half in range(2):
            order = order_ref[0, 0, rows_now, half * LANES : (half + 1) * LANES]
            inner = order & (LANES - 1)
            parts.append(
                jnp.where(
                    order < LANES,
                    jnp.take_along_axis(first, inner, axis=1, mode="promise_in_bounds"),
                    jnp.take_along_axis(second, inner, axis=1, mode="promise_in_bounds"),
                )
            )
        return jnp.concatenate(parts, axis=1)

    remain = 1.0
    shade = 0.0
    depth = 0.0
    for step in range(NSP):
        ray = ray_of(step)
        half_tanh = 0.5 * jnp.tanh(ray)
        weight = remain * (0.5 + half_tanh)
        shade = shade + weight * ray
        depth = depth + weight * ((step + 1) / NSP)
        remain = remain * (0.5 - half_tanh)
    occlusion = 0.0
    for ray_number in range(NRAY):
        passing = 1.0
        for step in range(NOS):
            ray = ray_of(NSP + ray_number * NOS + step)
            passing = passing * (0.5 - 0.5 * jnp.tanh(ray))
        occlusion = occlusion + passing
    out_ref[0, 0] = shade.astype(BF16)
    out_ref[0, 1] = (1.0 - remain).astype(BF16)
    out_ref[0, 2] = depth.astype(BF16)
    out_ref[0, 3] = (occlusion * (1.0 / NRAY)).astype(BF16)


def gbuffer(values, order, height, width):
    total = order.shape[2]
    return pl.pallas_call(
        gbuffer_kernel,
        out_shape=jax.ShapeDtypeStruct((1, 4, height, width), BF16),
        in_specs=[vmem(), vmem()],
        out_specs=vmem(),
        scratch_shapes=[pltpu.VMEM((2 * total, LANES), F32)],
        compiler_params=params(16),
        cost_estimate=pl.CostEstimate(
            flops=20 * total * BLOCK, bytes_accessed=8 * total * BLOCK, transcendentals=0
        ),
        name="gbuffer",
    )(values, order)


def silu(field):
    half = 0.5 * field
    return half + half * jnp.tanh(half)


def shifted(rows, steps):
    lane = lax.broadcasted_iota(jnp.int32, (1, LANES), 1)
    edge = lane == (0 if steps == 1 else LANES - 1)
    moved = []
    for row in rows:
        tiles = [row[:, i : i + LANES] for i in range(0, row.shape[1], LANES)]
        tiles = [pltpu.roll(tile, steps % LANES, 1) for tile in tiles]
        for i, tile in enumerate(tiles):
            source = i - steps
            fill = tiles[source] if 0 <= source < len(tiles) else 0.0
            moved.append(jnp.where(edge, fill, tile))
    return jnp.concatenate(moved, axis=1)


def across(total, chans, row_width):
    left, middle, right = (total[i * chans : (i + 1) * chans] for i in range(3))

    def rows_of(part):
        return [part[:, i : i + row_width] for i in range(0, part.shape[1], row_width)]

    return middle + shifted(rows_of(left), 1) + shifted(rows_of(right), -1)


def taps(weight_ref, tap):
    _, out_chans, chans = weight_ref.shape
    return weight_ref[3 * tap : 3 * tap + 3].reshape(3 * out_chans, chans)


def beside(weight_ref):
    return jnp.concatenate([taps(weight_ref, tap) for tap in range(3)], axis=1)


def sides(where_ref):
    above = jnp.where(where_ref[0] > 0, 1.0, 0.0)
    below = jnp.where(where_ref[0] < where_ref[1] - 1, 1.0, 0.0)

    def inside(row, low, high):
        return jnp.where(row < low, above, jnp.where(row >= high, below, 1.0))

    return inside


def turned(weight_ref):
    _, chans, out_chans = weight_ref.shape
    here = lax.broadcasted_iota(jnp.int32, (out_chans, out_chans), 0)
    there = lax.broadcasted_iota(jnp.int32, (out_chans, out_chans), 1)
    unit = jnp.where(here == there, 1.0, 0.0).astype(BF16)
    rows = []
    for column in range(3):
        stack = jnp.concatenate([weight_ref[3 * tap + column] for tap in range(3)], axis=0)
        rows.append(
            lax.dot_general(
                unit, stack, (((1,), (1,)), ((), ())), preferred_element_type=F32
            )
        )
    return jnp.concatenate(rows, axis=0).astype(BF16)


def stem_kernel(where_ref, x_ref, w_in, w_mid, second, first):
    height = x_ref.shape[0] // 3
    width = x_ref.shape[2]
    inside = sides(where_ref)

    def full_layer(weight, source, target, low, high, unroll):
        chans = target.shape[1]
        depth = weight.shape[1]

        def step(row, carry):
            lines = source[pl.ds(row, 3)].reshape(depth, width)
            line = across(jnp.dot(weight, lines, preferred_element_type=F32), chans, width)
            target[row] = (silu(line) * inside(row, low, high)).astype(BF16)
            return carry

        lax.fori_loop(0, target.shape[0], step, 0, unroll=unroll)

    full_layer(turned(w_in), x_ref, first, height - 1, 2 * height - 1, first.shape[0] // 2)
    full_layer(beside(w_mid), first, second, height - 2, 2 * height - 2, second.shape[0] // 4)


def middle_kernel(where_ref, second, w_down, w_deep, fourth, pooled, third):
    count, chans, width = second.shape
    half_height = (count + 4) // 6
    half_width = width // 2
    inside = sides(where_ref)
    place = lax.broadcasted_iota(jnp.int32, (width, half_width), 0) // 2
    target = lax.broadcasted_iota(jnp.int32, (width, half_width), 1)
    shrink = jnp.where(place == target, 0.25, 0.0).astype(BF16)
    pairs = jnp.dot(
        second[...].reshape(count * chans, width), shrink, preferred_element_type=F32
    ).reshape(count // 2, 2, chans, half_width)
    pooled[...] = (pairs[:, 0] + pairs[:, 1]).astype(BF16)

    def half_pair(source, row, tap):
        return jnp.concatenate([source[row + tap], source[row + tap + 1]], axis=1)

    def half_layer(product, target, low, high):
        chans = target.shape[1]
        for row in range(0, target.shape[0], 2):
            both = silu(across(product(row), chans, half_width))
            for now in range(2):
                line = both[:, now * half_width : (now + 1) * half_width]
                if row + now < low or row + now >= high:
                    line = line * inside(row + now, low, high)
                target[row + now] = line.astype(BF16)

    weight_down = turned(w_down)

    def down_product(row):
        lines = jnp.concatenate([half_pair(pooled, row, tap) for tap in range(3)], axis=0)
        return jnp.dot(weight_down, lines, preferred_element_type=F32)

    def deep_product(row):
        total = None
        for tap in range(3):
            part = jnp.dot(
                taps(w_deep, tap), half_pair(third, row, tap), preferred_element_type=F32
            )
            total = part if total is None else total + part
        return total

    half_layer(down_product, third, half_height - 2, 2 * half_height - 2)
    half_layer(deep_product, fourth, half_height - 3, 2 * half_height - 3)


def decoder_kernel(
    where_ref, second, fourth, w_up, w_out, out_ref, joined, fifth, final
):
    height = out_ref.shape[2]
    width = out_ref.shape[3]
    half_width = width // 2
    chans = second.shape[1]
    inside = sides(where_ref)
    place = lax.broadcasted_iota(jnp.int32, (half_width, width), 0)
    target = lax.broadcasted_iota(jnp.int32, (half_width, width), 1) // 2
    spread = jnp.where(place == target, 1.0, 0.0).astype(BF16)
    deep = fourth.shape[1]
    wide = jnp.dot(
        fourth[...].reshape(-1, half_width), spread, preferred_element_type=F32
    ).astype(BF16).reshape(fourth.shape[0], deep, width)
    for row in range(2 * fourth.shape[0]):
        joined[row, chans:, :] = wide[row // 2]
        joined[row, :chans, :] = second[row + 4]

    def up_step(row, carry):
        total = None
        for tap in range(3):
            part = jnp.dot(taps(w_up, tap), joined[row + tap], preferred_element_type=F32)
            total = part if total is None else total + part
        line = silu(across(total, chans, width))
        fifth[row] = (line * inside(row, 1, height + 1)).astype(BF16)
        return carry

    lax.fori_loop(0, fifth.shape[0], up_step, 0, unroll=fifth.shape[0] // 2)

    colours = out_ref.shape[1]
    weight_out = beside(w_out)
    for row in range(height):
        lines = fifth[row : row + 3].reshape(3 * chans, width)
        total = jnp.dot(weight_out, lines, preferred_element_type=F32)
        line = across(total, w_out.shape[1], width)
        for colour in range(colours):
            final[colour, row : row + 1, :] = line[colour : colour + 1, :]
    out_ref[0] = final[...].astype(BF16)


def stem(where, field, w_in, w_mid):
    height = field.shape[0] // 3
    width = field.shape[2]
    one = w_mid.shape[1]
    return pl.pallas_call(
        stem_kernel,
        out_shape=jax.ShapeDtypeStruct((3 * height - 4, one, width), BF16),
        in_specs=[smem()] + [vmem()] * 3,
        out_specs=vmem(),
        scratch_shapes=[pltpu.VMEM((3 * height - 2, one, width), BF16)],
        compiler_params=params(16),
        cost_estimate=pl.CostEstimate(
            flops=1_000_000_000, bytes_accessed=MIB, transcendentals=300_000
        ),
        name="stem",
    )(where, field, w_in, w_mid)


def middle(where, second, w_down, w_deep):
    rows, one, width = second.shape
    half = (rows + 4) // 6
    two = w_deep.shape[1]
    return pl.pallas_call(
        middle_kernel,
        out_shape=jax.ShapeDtypeStruct((3 * half - 6, two, width // 2), BF16),
        in_specs=[smem()] + [vmem()] * 3,
        out_specs=vmem(),
        scratch_shapes=[
            pltpu.VMEM((3 * half - 2, one, width // 2), BF16),
            pltpu.VMEM((3 * half - 4, two, width // 2), BF16),
        ],
        compiler_params=params(16),
        cost_estimate=pl.CostEstimate(
            flops=1_000_000_000, bytes_accessed=MIB, transcendentals=200_000
        ),
        name="middle",
    )(where, second, w_down, w_deep)


def decoder(where, second, deep, w_up, w_out, height, colours):
    one = second.shape[1]
    two = deep.shape[1]
    width = second.shape[2]
    return pl.pallas_call(
        decoder_kernel,
        out_shape=jax.ShapeDtypeStruct((1, colours, height, width), BF16),
        in_specs=[smem()] + [vmem()] * 4,
        out_specs=vmem(),
        scratch_shapes=[
            pltpu.VMEM((height + 4, one + two, width), BF16),
            pltpu.VMEM((height + 2, one, width), BF16),
            pltpu.VMEM((colours, height, width), F32),
        ],
        compiler_params=params(16),
        cost_estimate=pl.CostEstimate(
            flops=1_000_000_000, bytes_accessed=MIB, transcendentals=100_000
        ),
        name="decoder",
    )(where, second, deep, w_up, w_out)


def on_device(
    bricks, sends, cells, fracs, sample_order, pending, w_in, w_mid, w_down, w_deep, w_up, w_out
):
    n_tile = lax.axis_size("tile")
    tile = lax.axis_index("tile")
    n_section = lax.axis_size("section")
    cap = sends.shape[3]
    height = pending.shape[2]
    width = pending.shape[3]
    samples = cells.shape[3]
    slots = n_tile * cap
    per_slot = samples // slots
    padded = -(-per_slot // BLOCK) * BLOCK

    def fill(part):
        if padded != per_slot:
            part = part.reshape(3, slots, per_slot)
            part = jnp.pad(part, ((0, 0), (0, 0), (0, padded - per_slot)))
        return part.reshape(3, slots * padded // LANES, LANES)

    def trim(found):
        if padded == per_slot:
            return found
        return found.reshape(slots, padded)[:, :per_slot].reshape(1, samples // LANES, LANES)

    places = positions(fill(cells), fill(fracs), n_tile)
    places, bricks, pending = lax.optimization_barrier((places, bricks, pending))
    arrived = lax.all_to_all(places, "tile", split_axis=0, concat_axis=0, tiled=True)

    down = [(i, i + 1) for i in range(n_tile - 1)]
    up = [(i + 1, i) for i in range(n_tile - 1)]
    over = lax.ppermute(pending, "tile", down)
    under = lax.ppermute(pending, "tile", up)
    where = jnp.stack([tile, jnp.int32(n_tile)]).astype(jnp.int32)
    picks = sends[0, 0].T
    colours = w_out.shape[1]
    w_in = w_in.transpose(0, 2, 1)
    w_in = jnp.pad(w_in, ((0, 0), (0, 16 - w_in.shape[1]), (0, 0)))
    w_out = jnp.pad(w_out, ((0, 0), (0, 16 - colours), (0, 0)))
    windows, own = windows_of(where, picks, bricks, places)
    arrived, w_in, w_out = lax.optimization_barrier((arrived, w_in, w_out))
    found = sample_values(where, picks, windows, arrived, own)

    found, over, under, pending = lax.optimization_barrier((found, over, under, pending))
    values = lax.all_to_all(found, "tile", split_axis=0, concat_axis=0, tiled=True)
    field = jnp.concatenate([over[0], pending[0], under[0]], axis=1).transpose(1, 0, 2)
    field = jnp.pad(field, ((0, 0), (0, 16 - field.shape[1]), (0, 0)))
    second = stem(where, field, w_in, w_mid)
    deep = middle(where, second, w_down.transpose(0, 2, 1), w_deep)
    values, deep = lax.optimization_barrier((values, deep))
    rendered = gbuffer(trim(values), sample_order, height, width)
    rendered, deep = lax.optimization_barrier((rendered, deep))
    ring = [(i, (i + 1) % n_section) for i in range(n_section)]
    handoff = lax.ppermute(rendered, "section", ring)
    denoised = decoder(where, second, deep, w_up, w_out, height, colours)
    return (handoff, denoised)


def solution(mesh):
    in_specs = (
        P("tile", None),
        P("section", "tile", None, None),
        P("section", "tile", None, None),
        P("section", "tile", None, None),
        P("section", "tile", None, None),
        P("section", None, "tile", None),
        P(),
        P(),
        P(),
        P(),
        P(),
        P(),
    )
    out_specs = (P("section", None, "tile", None), P("section", None, "tile", None))
    return jax.shard_map(
        on_device, mesh=mesh, in_specs=in_specs, out_specs=out_specs, check_vma=False
    )
```

```python
import functools

import jax
import jax.numpy as jnp
from jax import lax
from jax.experimental import pallas as pl
from jax.experimental.pallas import tpu as pltpu
from jax.sharding import PartitionSpec as P

EDGE = 34
NSP = 4
NRAY = 8
NOS = 2
LANES = 128
BLOCK = 256
STRIDE = 6
WINDOWS = 6
MAIN = 32
TAIL = 16
BRICK_ROWS = WINDOWS * MAIN + TAIL
KDIM = 256

F32 = jnp.float32
BF16 = jnp.bfloat16
MIB = 1024 * 1024


def params(mib):
    return pltpu.CompilerParams(vmem_limit_bytes=mib * MIB)


def vmem():
    return pl.BlockSpec(memory_space=pltpu.VMEM)


def smem():
    return pl.BlockSpec(memory_space=pltpu.SMEM)


def windows_kernel(
    where_ref, picks_ref, cube_ref, place_ref, out_ref, wide, tail, places, sums, arrival
):
    tile = where_ref[0]
    own_places = pltpu.make_async_copy(place_ref.at[tile], places, arrival)
    own_places.start()
    count = cube_ref.shape[0]
    plane = EDGE * EDGE
    wide[...] = jnp.zeros_like(wide)
    wide[:, :EDGE, :plane] = cube_ref[...]
    column = lax.broadcasted_iota(jnp.int32, (1, KDIM), 1)
    main = (column // MAIN) * EDGE + column % MAIN
    rest = column - 7 * MAIN
    last = (rest % 8) * EDGE + MAIN + rest // 8
    source = jnp.where(column < 7 * MAIN, main, last)
    unused = (column >= 7 * MAIN) & ((rest % 8 == 7) | (rest >= TAIL))
    source = jnp.where(unused, -(1 << 20), source)
    for window in range(WINDOWS):
        first = window * STRIDE * EDGE
        low = first // LANES * LANES
        length = min(3 * LANES, wide.shape[2] - low)
        place = lax.broadcasted_iota(jnp.int32, (length, KDIM), 0)
        pick = jnp.where(place == source + (first - low), 1.0, 0.0).astype(BF16)
        found = jnp.dot(
            wide[:, :, low : low + length].reshape(-1, length),
            pick,
            preferred_element_type=F32,
        )
        found = found.reshape(count, 48, KDIM)
        out_ref[:count, window * MAIN : (window + 1) * MAIN, :] = found[:, :MAIN, :].astype(BF16)
        tail[:, window : window + 1, :] = found[:, MAIN : MAIN + 1, :]
        tail[:, 8 + window : 9 + window, :] = found[:, MAIN + 1 : MAIN + 2, :]
    for row in (6, 7, 14, 15):
        tail[:, row : row + 1, :] = jnp.zeros((count, 1, KDIM), F32)
    out_ref[:count, WINDOWS * MAIN :, :] = tail[...].astype(BF16)

    own_places.wait()
    cap = picks_ref.shape[0]
    lines = places.shape[0] // 3
    part = lines // cap

    def one_slot(piece, carry):
        brick = out_ref[picks_ref[piece, tile]]
        slot_sums(brick, places, sums, piece * part, part // 2)
        return carry

    lax.fori_loop(0, cap, one_slot, 0)
    out_ref[count, : whole_tiles(lines), :LANES] = line_values(sums, lines, whole_tiles(lines))


def windows_of(where, picks, bricks, places):
    count = bricks.shape[0]
    cube = bricks.reshape(count, EDGE, EDGE * EDGE)
    rows = places.shape[1]
    return pl.pallas_call(
        windows_kernel,
        out_shape=jax.ShapeDtypeStruct((count + 1, BRICK_ROWS, KDIM), BF16),
        in_specs=[smem(), smem(), vmem(), pl.BlockSpec(memory_space=pl.ANY)],
        out_specs=vmem(),
        scratch_shapes=[
            pltpu.VMEM((count, 48, 10 * LANES), BF16),
            pltpu.VMEM((count, TAIL, KDIM), F32),
            pltpu.VMEM((rows, LANES), F32),
            pltpu.VMEM((8 * rows // 3, LANES), F32),
            pltpu.SemaphoreType.DMA,
        ],
        compiler_params=params(16),
        cost_estimate=pl.CostEstimate(
            flops=2 * count * 48 * 384 * KDIM * WINDOWS, bytes_accessed=4 * MIB,
            transcendentals=0,
        ),
        name="brick_windows",
    )(where, picks, cube, places)


def hat(distance):
    return jnp.maximum(1.0 - jnp.abs(distance), 0.0)


def blend(brick, px, py, pz):
    width = px.shape[1]
    eight = lax.broadcasted_iota(jnp.int32, (8, width), 0).astype(F32)
    places = lax.broadcasted_iota(jnp.int32, (MAIN, width), 0).astype(F32).astype(BF16)

    def tile(rows):
        return jnp.concatenate([rows, rows], axis=0).astype(BF16)

    cell_y = jnp.floor(py)
    frac_y = py - cell_y
    lower, low_share, high_share = tile(cell_y), tile(1.0 - frac_y), tile(frac_y)
    nothing = jnp.zeros((TAIL, width), BF16)
    weight_y = []
    for start in range(0, MAIN, TAIL):
        offset = places[start : start + TAIL] - lower
        weight_y.append(
            jnp.where(offset == 0, low_share, jnp.where(offset == 1, high_share, nothing))
        )
    window = jnp.floor(px * (1.0 / STRIDE))
    weight_x = hat(eight - (px - STRIDE * window))
    parts = []
    for i in range(STRIDE + 1):
        share = tile(jnp.broadcast_to(weight_x[i : i + 1], (8, width)))
        parts += [share * part for part in weight_y]
    tail = [weight_x * hat(MAIN - py), weight_x * jnp.maximum(py - MAIN, 0.0)]
    parts.append(jnp.concatenate(tail, axis=0).astype(BF16))
    parts.append(nothing)
    plane = jnp.concatenate(parts, axis=0)
    found = jnp.dot(brick, plane, preferred_element_type=F32)
    groups = range(0, MAIN, 8)
    chosen = [found[row : row + 8] for row in groups]
    for other in range(1, WINDOWS):
        here = window == float(other)
        base = other * MAIN
        chosen = [
            jnp.where(here, found[base + row : base + row + 8], old)
            for row, old in zip(groups, chosen)
        ]
    base = WINDOWS * MAIN
    edges = found[base : base + 8] * hat(MAIN - pz)
    edges = edges + found[base + 8 :] * jnp.maximum(pz - MAIN, 0.0)
    total = jnp.where(eight == window, edges, 0.0)
    for row, part in zip(groups, chosen):
        total = total + part * hat((eight + float(row)) - pz)
    return total


def slot_sums(brick, places, sums, first, blocks):
    lines = places.shape[0] // 3
    for step in range(blocks):
        row = first + 2 * step

        def line(axis):
            both = [
                jnp.broadcast_to(places[pl.ds(axis * lines + row + half, 1), :], (8, LANES))
                for half in range(2)
            ]
            return jnp.concatenate(both, axis=1)

        total = blend(brick, line(0), line(1), line(2))
        for half in range(2):
            sums[pl.ds(pl.multiple_of(8 * (row + half), 8), 8), :] = total[
                :, half * LANES : (half + 1) * LANES
            ]


def whole_tiles(lines):
    return -(-lines // TAIL) * TAIL


def line_values(sums, lines, height):
    values = []
    for row in range(0, lines, 8):
        value = sums[pl.ds(8 * row, 8, stride=8), :]
        for other in range(1, 8):
            value = value + sums[pl.ds(8 * row + other, 8, stride=8), :]
        values.append(value)
    if height > lines:
        values.append(jnp.zeros((height - lines, LANES), F32))
    return jnp.concatenate(values, axis=0).astype(BF16)


def samples_kernel(
    where_ref, picks_ref, brick_ref, place_ref, out_ref, bricks, places, sums, own, arrivals,
    own_arrival,
):
    owners, rows, _ = place_ref.shape
    cap = picks_ref.shape[0]
    lines = rows // 3
    part = lines // cap
    turns = owners - 1
    tile = where_ref[0]
    own_values = pltpu.make_async_copy(
        brick_ref.at[brick_ref.shape[0] - 1, pl.ds(0, own.shape[0]), pl.ds(0, LANES)],
        own,
        own_arrival,
    )

    def renderer_of(turn):
        return lax.rem(tile + 1 + turn, owners)

    def fetches(turn):
        held = turn % 2
        renderer = renderer_of(turn)
        copies = [
            pltpu.make_async_copy(
                place_ref.at[renderer], places.at[held], arrivals.at[held, cap]
            )
        ]
        for piece in range(cap):
            copies.append(
                pltpu.make_async_copy(
                    brick_ref.at[picks_ref[piece, renderer]],
                    bricks.at[held, piece],
                    arrivals.at[held, piece],
                )
            )
        return copies

    for turn in range(min(2, turns)):
        for copy in fetches(turn):
            copy.start()

    def one_turn(turn, carry):
        held = turn % 2
        for copy in fetches(turn):
            copy.wait()
        for piece in range(cap):
            slot_sums(bricks[held, piece], places.at[held], sums, piece * part, part // 2)
        out_ref[renderer_of(turn)] = line_values(sums, lines, lines)

        @pl.when(turn + 2 < turns)
        def _():
            for copy in fetches(turn + 2):
                copy.start()

        return carry

    own_values.start()
    lax.fori_loop(0, turns, one_turn, 0)
    own_values.wait()
    out_ref[tile] = own[...].astype(F32)[:lines].astype(BF16)


def sample_values(where, picks, windows, places):
    owners, rows, _ = places.shape
    cap = picks.shape[0]
    samples = owners * rows * LANES // 3
    some = pl.BlockSpec(memory_space=pl.ANY)
    return pl.pallas_call(
        samples_kernel,
        out_shape=jax.ShapeDtypeStruct((owners, rows // 3, LANES), BF16),
        in_specs=[smem(), smem(), some, some],
        out_specs=vmem(),
        scratch_shapes=[
            pltpu.VMEM((2, cap, BRICK_ROWS, KDIM), BF16),
            pltpu.VMEM((2, rows, LANES), F32),
            pltpu.VMEM((8 * rows // 3, LANES), F32),
            pltpu.VMEM((whole_tiles(rows // 3), LANES), BF16),
            pltpu.SemaphoreType.DMA((2, cap + 1)),
            pltpu.SemaphoreType.DMA,
        ],
        compiler_params=pltpu.CompilerParams(vmem_limit_bytes=61_600_000),
        cost_estimate=pl.CostEstimate(
            flops=2 * samples * KDIM * BRICK_ROWS, bytes_accessed=3 * MIB,
            transcendentals=0,
        ),
        name="sample_values",
    )(where, picks, windows, places)


def gbuffer_kernel(value_ref, order_ref, out_ref, values):
    values[...] = value_ref[...].astype(F32).reshape(values.shape)
    height = out_ref.shape[2]

    def ray_of(number):
        rows_now = slice(number * height, (number + 1) * height)
        first, second = (
            values[pl.ds(2 * number * height + half, height, stride=2), :] for half in range(2)
        )
        parts = []
        for half in range(2):
            order = order_ref[0, 0, rows_now, half * LANES : (half + 1) * LANES]
            inner = order & (LANES - 1)
            parts.append(
                jnp.where(
                    order < LANES,
                    jnp.take_along_axis(first, inner, axis=1, mode="promise_in_bounds"),
                    jnp.take_along_axis(second, inner, axis=1, mode="promise_in_bounds"),
                )
            )
        return jnp.concatenate(parts, axis=1)

    remain = 1.0
    shade = 0.0
    depth = 0.0
    for step in range(NSP):
        ray = ray_of(step)
        half_tanh = 0.5 * jnp.tanh(ray)
        weight = remain * (0.5 + half_tanh)
        shade = shade + weight * ray
        depth = depth + weight * ((step + 1) / NSP)
        remain = remain * (0.5 - half_tanh)
    occlusion = 0.0
    for ray_number in range(NRAY):
        passing = 1.0
        for step in range(NOS):
            ray = ray_of(NSP + ray_number * NOS + step)
            passing = passing * (0.5 - 0.5 * jnp.tanh(ray))
        occlusion = occlusion + passing
    out_ref[0, 0] = shade.astype(BF16)
    out_ref[0, 1] = (1.0 - remain).astype(BF16)
    out_ref[0, 2] = depth.astype(BF16)
    out_ref[0, 3] = (occlusion * (1.0 / NRAY)).astype(BF16)


def gbuffer(values, order, height, width):
    total = order.shape[2]
    return pl.pallas_call(
        gbuffer_kernel,
        out_shape=jax.ShapeDtypeStruct((1, 4, height, width), BF16),
        in_specs=[vmem(), vmem()],
        out_specs=vmem(),
        scratch_shapes=[pltpu.VMEM((2 * total, LANES), F32)],
        compiler_params=params(16),
        cost_estimate=pl.CostEstimate(
            flops=20 * total * BLOCK, bytes_accessed=8 * total * BLOCK, transcendentals=0
        ),
        name="gbuffer",
    )(values, order)


def silu(field):
    half = 0.5 * field
    return half + half * jnp.tanh(half)


def shifted(rows, steps):
    lane = lax.broadcasted_iota(jnp.int32, (1, LANES), 1)
    edge = lane == (0 if steps == 1 else LANES - 1)
    moved = []
    for row in rows:
        tiles = [row[:, i : i + LANES] for i in range(0, row.shape[1], LANES)]
        tiles = [pltpu.roll(tile, steps % LANES, 1) for tile in tiles]
        for i, tile in enumerate(tiles):
            source = i - steps
            fill = tiles[source] if 0 <= source < len(tiles) else 0.0
            moved.append(jnp.where(edge, fill, tile))
    return jnp.concatenate(moved, axis=1)


def across(total, chans, row_width):
    left, middle, right = (total[i * chans : (i + 1) * chans] for i in range(3))

    def rows_of(part):
        return [part[:, i : i + row_width] for i in range(0, part.shape[1], row_width)]

    return middle + shifted(rows_of(left), 1) + shifted(rows_of(right), -1)


def taps(weight_ref, tap):
    _, out_chans, chans = weight_ref.shape
    return weight_ref[3 * tap : 3 * tap + 3].reshape(3 * out_chans, chans)


def beside(weight_ref):
    return jnp.concatenate([taps(weight_ref, tap) for tap in range(3)], axis=1)


def sides(where_ref):
    above = jnp.where(where_ref[0] > 0, 1.0, 0.0)
    below = jnp.where(where_ref[0] < where_ref[1] - 1, 1.0, 0.0)

    def inside(row, low, high):
        return jnp.where(row < low, above, jnp.where(row >= high, below, 1.0))

    return inside


def turned(weight_ref):
    _, chans, out_chans = weight_ref.shape
    here = lax.broadcasted_iota(jnp.int32, (out_chans, out_chans), 0)
    there = lax.broadcasted_iota(jnp.int32, (out_chans, out_chans), 1)
    unit = jnp.where(here == there, 1.0, 0.0).astype(BF16)
    rows = []
    for column in range(3):
        stack = jnp.concatenate([weight_ref[3 * tap + column] for tap in range(3)], axis=0)
        rows.append(
            lax.dot_general(
                unit, stack, (((1,), (1,)), ((), ())), preferred_element_type=F32
            )
        )
    return jnp.concatenate(rows, axis=0).astype(BF16)


def stem_kernel(where_ref, x_ref, w_in, w_mid, second, first):
    height = x_ref.shape[0] // 3
    width = x_ref.shape[2]
    inside = sides(where_ref)

    def full_layer(weight, source, target, low, high, unroll):
        chans = target.shape[1]
        depth = weight.shape[1]

        def step(row, carry):
            lines = source[pl.ds(row, 3)].reshape(depth, width)
            line = across(jnp.dot(weight, lines, preferred_element_type=F32), chans, width)
            target[row] = (silu(line) * inside(row, low, high)).astype(BF16)
            return carry

        lax.fori_loop(0, target.shape[0], step, 0, unroll=unroll)

    full_layer(turned(w_in), x_ref, first, height - 1, 2 * height - 1, first.shape[0])
    full_layer(beside(w_mid), first, second, height - 2, 2 * height - 2, second.shape[0])


def middle_kernel(where_ref, second, w_down, w_deep, fourth, pooled, third):
    count, chans, width = second.shape
    half_height = (count + 4) // 6
    half_width = width // 2
    inside = sides(where_ref)
    place = lax.broadcasted_iota(jnp.int32, (width, half_width), 0) // 2
    target = lax.broadcasted_iota(jnp.int32, (width, half_width), 1)
    shrink = jnp.where(place == target, 0.25, 0.0).astype(BF16)
    pairs = jnp.dot(
        second[...].reshape(count * chans, width), shrink, preferred_element_type=F32
    ).reshape(count // 2, 2, chans, half_width)
    pooled[...] = (pairs[:, 0] + pairs[:, 1]).astype(BF16)

    def half_pair(source, row, tap):
        return jnp.concatenate([source[row + tap], source[row + tap + 1]], axis=1)

    def half_layer(product, target, low, high):
        chans = target.shape[1]
        for row in range(0, target.shape[0], 2):
            both = silu(across(product(row), chans, half_width))
            for now in range(2):
                line = both[:, now * half_width : (now + 1) * half_width]
                if row + now < low or row + now >= high:
                    line = line * inside(row + now, low, high)
                target[row + now] = line.astype(BF16)

    weight_down = turned(w_down)

    def down_product(row):
        lines = jnp.concatenate([half_pair(pooled, row, tap) for tap in range(3)], axis=0)
        return jnp.dot(weight_down, lines, preferred_element_type=F32)

    def deep_product(row):
        total = None
        for tap in range(3):
            part = jnp.dot(
                taps(w_deep, tap), half_pair(third, row, tap), preferred_element_type=F32
            )
            total = part if total is None else total + part
        return total

    half_layer(down_product, third, half_height - 2, 2 * half_height - 2)
    half_layer(deep_product, fourth, half_height - 3, 2 * half_height - 3)


def decoder_kernel(
    where_ref, second, fourth, w_up, w_out, out_ref, joined, fifth, final
):
    height = out_ref.shape[2]
    width = out_ref.shape[3]
    half_width = width // 2
    chans = second.shape[1]
    inside = sides(where_ref)
    place = lax.broadcasted_iota(jnp.int32, (half_width, width), 0)
    target = lax.broadcasted_iota(jnp.int32, (half_width, width), 1) // 2
    spread = jnp.where(place == target, 1.0, 0.0).astype(BF16)
    deep = fourth.shape[1]
    wide = jnp.dot(
        fourth[...].reshape(-1, half_width), spread, preferred_element_type=F32
    ).astype(BF16).reshape(fourth.shape[0], deep, width)
    for row in range(2 * fourth.shape[0]):
        joined[row, chans:, :] = wide[row // 2]
        joined[row, :chans, :] = second[row + 4]

    def up_step(row, carry):
        total = None
        for tap in range(3):
            part = jnp.dot(taps(w_up, tap), joined[row + tap], preferred_element_type=F32)
            total = part if total is None else total + part
        line = silu(across(total, chans, width))
        fifth[row] = (line * inside(row, 1, height + 1)).astype(BF16)
        return carry

    lax.fori_loop(0, fifth.shape[0], up_step, 0, unroll=fifth.shape[0])

    colours = out_ref.shape[1]
    weight_out = beside(w_out)
    for row in range(height):
        lines = fifth[row : row + 3].reshape(3 * chans, width)
        total = jnp.dot(weight_out, lines, preferred_element_type=F32)
        line = across(total, w_out.shape[1], width)
        for colour in range(colours):
            final[colour, row : row + 1, :] = line[colour : colour + 1, :]
    out_ref[0] = final[...].astype(BF16)


def stem(where, field, w_in, w_mid):
    height = field.shape[0] // 3
    width = field.shape[2]
    one = w_mid.shape[1]
    return pl.pallas_call(
        stem_kernel,
        out_shape=jax.ShapeDtypeStruct((3 * height - 4, one, width), BF16),
        in_specs=[smem()] + [vmem()] * 3,
        out_specs=vmem(),
        scratch_shapes=[pltpu.VMEM((3 * height - 2, one, width), BF16)],
        compiler_params=params(16),
        cost_estimate=pl.CostEstimate(
            flops=1_000_000_000, bytes_accessed=MIB, transcendentals=300_000
        ),
        name="stem",
    )(where, field, w_in, w_mid)


def middle(where, second, w_down, w_deep):
    rows, one, width = second.shape
    half = (rows + 4) // 6
    two = w_deep.shape[1]
    return pl.pallas_call(
        middle_kernel,
        out_shape=jax.ShapeDtypeStruct((3 * half - 6, two, width // 2), BF16),
        in_specs=[smem()] + [vmem()] * 3,
        out_specs=vmem(),
        scratch_shapes=[
            pltpu.VMEM((3 * half - 2, one, width // 2), BF16),
            pltpu.VMEM((3 * half - 4, two, width // 2), BF16),
        ],
        compiler_params=params(16),
        cost_estimate=pl.CostEstimate(
            flops=1_000_000_000, bytes_accessed=MIB, transcendentals=200_000
        ),
        name="middle",
    )(where, second, w_down, w_deep)


def decoder(where, second, deep, w_up, w_out, height, colours):
    one = second.shape[1]
    two = deep.shape[1]
    width = second.shape[2]
    return pl.pallas_call(
        decoder_kernel,
        out_shape=jax.ShapeDtypeStruct((1, colours, height, width), BF16),
        in_specs=[smem()] + [vmem()] * 4,
        out_specs=vmem(),
        scratch_shapes=[
            pltpu.VMEM((height + 4, one + two, width), BF16),
            pltpu.VMEM((height + 2, one, width), BF16),
            pltpu.VMEM((colours, height, width), F32),
        ],
        compiler_params=params(16),
        cost_estimate=pl.CostEstimate(
            flops=1_000_000_000, bytes_accessed=MIB, transcendentals=100_000
        ),
        name="decoder",
    )(where, second, deep, w_up, w_out)


def on_device(
    bricks, sends, cells, fracs, sample_order, pending, w_in, w_mid, w_down, w_deep, w_up, w_out
):
    n_tile = lax.axis_size("tile")
    tile = lax.axis_index("tile")
    n_section = lax.axis_size("section")
    cap = sends.shape[3]
    height = pending.shape[2]
    width = pending.shape[3]
    samples = cells.shape[3]
    slots = n_tile * cap
    per_slot = samples // slots
    padded = -(-per_slot // BLOCK) * BLOCK

    def fill(part):
        if padded != per_slot:
            part = part.reshape(3, slots, per_slot)
            part = jnp.pad(part, ((0, 0), (0, 0), (0, padded - per_slot)))
        return part.reshape(3, slots * padded // LANES, LANES)

    def trim(found):
        if padded == per_slot:
            return found
        return found.reshape(slots, padded)[:, :per_slot].reshape(1, samples // LANES, LANES)

    places = fill(cells).astype(F32) + fill(fracs)
    places = places.reshape(3, n_tile, -1, LANES).transpose(1, 0, 2, 3).reshape(n_tile, -1, LANES)
    places, bricks, pending = lax.optimization_barrier((places, bricks, pending))
    arrived = lax.all_to_all(places, "tile", split_axis=0, concat_axis=0, tiled=True)

    down = [(i, i + 1) for i in range(n_tile - 1)]
    up = [(i + 1, i) for i in range(n_tile - 1)]
    over = lax.ppermute(pending, "tile", down)
    under = lax.ppermute(pending, "tile", up)
    where = jnp.stack([tile, jnp.int32(n_tile)]).astype(jnp.int32)
    picks = sends[0, 0].T
    colours = w_out.shape[1]
    w_in = w_in.transpose(0, 2, 1)
    w_in = jnp.pad(w_in, ((0, 0), (0, 16 - w_in.shape[1]), (0, 0)))
    w_out = jnp.pad(w_out, ((0, 0), (0, 16 - colours), (0, 0)))
    windows = windows_of(where, picks, bricks, places)
    arrived, w_in, w_out = lax.optimization_barrier((arrived, w_in, w_out))
    found = sample_values(where, picks, windows, arrived)

    found, over, under, pending = lax.optimization_barrier((found, over, under, pending))
    values = lax.all_to_all(found, "tile", split_axis=0, concat_axis=0, tiled=True)
    field = jnp.concatenate([over[0], pending[0], under[0]], axis=1).transpose(1, 0, 2)
    field = jnp.pad(field, ((0, 0), (0, 16 - field.shape[1]), (0, 0)))
    second = stem(where, field, w_in, w_mid)
    deep = middle(where, second, w_down.transpose(0, 2, 1), w_deep)
    values, deep = lax.optimization_barrier((values, deep))
    rendered = gbuffer(trim(values), sample_order, height, width)
    rendered, deep = lax.optimization_barrier((rendered, deep))
    ring = [(i, (i + 1) % n_section) for i in range(n_section)]
    handoff = lax.ppermute(rendered, "section", ring)
    denoised = decoder(where, second, deep, w_up, w_out, height, colours)
    return (handoff, denoised)


def solution(mesh):
    in_specs = (
        P("tile", None),
        P("section", "tile", None, None),
        P("section", "tile", None, None),
        P("section", "tile", None, None),
        P("section", "tile", None, None),
        P("section", None, "tile", None),
        P(),
        P(),
        P(),
        P(),
        P(),
        P(),
    )
    out_specs = (P("section", None, "tile", None), P("section", None, "tile", None))
    return jax.shard_map(
        on_device, mesh=mesh, in_specs=in_specs, out_specs=out_specs, check_vma=False
    )
```

```python
import functools

import jax
import jax.numpy as jnp
from jax import lax
from jax.experimental import pallas as pl
from jax.experimental.pallas import tpu as pltpu
from jax.sharding import PartitionSpec as P

EDGE = 34
NSP = 4
NRAY = 8
NOS = 2
LANES = 128
BLOCK = 256
STRIDE = 6
WINDOWS = 6
MAIN = 32
TAIL = 16
BRICK_ROWS = WINDOWS * MAIN + TAIL
KDIM = 256

F32 = jnp.float32
BF16 = jnp.bfloat16
MIB = 1024 * 1024


def params(mib):
    return pltpu.CompilerParams(vmem_limit_bytes=mib * MIB)


def vmem():
    return pl.BlockSpec(memory_space=pltpu.VMEM)


def smem():
    return pl.BlockSpec(memory_space=pltpu.SMEM)


def positions_kernel(cells_ref, fracs_ref, out_ref, cells, fracs, found, arrivals, departures):
    owners, rows, _ = out_ref.shape
    lines = rows // 3
    parts = arrivals.shape[1]
    share = owners // parts
    pieces = [(axis, part) for axis in range(3) for part in range(parts)]

    def reads(axis, part):
        span = pl.ds(part * share * lines, share * lines)
        return [
            pltpu.make_async_copy(
                source.at[axis, span], target.at[axis, span], arrivals.at[axis, part, number]
            )
            for number, (source, target) in enumerate(((cells_ref, cells), (fracs_ref, fracs)))
        ]

    def write(axis, part):
        place = (pl.ds(part * share, share), pl.ds(axis * lines, lines))
        return pltpu.make_async_copy(
            found.at[place], out_ref.at[place], departures.at[axis, part]
        )

    for piece in pieces:
        for copy in reads(*piece):
            copy.start()
    for axis, part in pieces:
        for copy in reads(axis, part):
            copy.wait()
        span = slice(part * share * lines, (part + 1) * share * lines)
        place = cells[axis, span].astype(F32) + fracs[axis, span]
        found[part * share : (part + 1) * share, axis * lines : (axis + 1) * lines, :] = (
            place.reshape(share, lines, LANES)
        )
        write(axis, part).start()
    for piece in pieces:
        write(*piece).wait()


def positions(cells, fracs, owners):
    lines = cells.shape[1]
    shape = (owners, 3 * lines // owners, LANES)
    hbm = pl.BlockSpec(memory_space=pltpu.HBM)
    return pl.pallas_call(
        positions_kernel,
        out_shape=jax.ShapeDtypeStruct(shape, F32),
        in_specs=[hbm, hbm],
        out_specs=hbm,
        scratch_shapes=[
            pltpu.VMEM(cells.shape, jnp.int32),
            pltpu.VMEM(fracs.shape, F32),
            pltpu.VMEM(shape, F32),
            pltpu.SemaphoreType.DMA((3, 2, 2)),
            pltpu.SemaphoreType.DMA((3, 2)),
        ],
        compiler_params=params(60),
        cost_estimate=pl.CostEstimate(
            flops=3 * lines * LANES, bytes_accessed=36 * lines * LANES, transcendentals=0
        ),
        name="positions",
    )(cells, fracs)


def windows_kernel(
    where_ref, picks_ref, cube_ref, place_ref, out_ref, wide, tail, places, sums, arrival
):
    tile = where_ref[0]
    own_places = pltpu.make_async_copy(place_ref.at[tile], places, arrival)
    own_places.start()
    count = cube_ref.shape[0]
    plane = EDGE * EDGE
    wide[...] = jnp.zeros_like(wide)
    wide[:, :EDGE, :plane] = cube_ref[...]
    column = lax.broadcasted_iota(jnp.int32, (1, KDIM), 1)
    main = (column // MAIN) * EDGE + column % MAIN
    rest = column - 7 * MAIN
    last = (rest % 8) * EDGE + MAIN + rest // 8
    source = jnp.where(column < 7 * MAIN, main, last)
    unused = (column >= 7 * MAIN) & ((rest % 8 == 7) | (rest >= TAIL))
    source = jnp.where(unused, -(1 << 20), source)
    for window in range(WINDOWS):
        first = window * STRIDE * EDGE
        low = first // LANES * LANES
        length = min(3 * LANES, wide.shape[2] - low)
        place = lax.broadcasted_iota(jnp.int32, (length, KDIM), 0)
        pick = jnp.where(place == source + (first - low), 1.0, 0.0).astype(BF16)
        found = jnp.dot(
            wide[:, :, low : low + length].reshape(-1, length),
            pick,
            preferred_element_type=F32,
        )
        found = found.reshape(count, 48, KDIM)
        out_ref[:count, window * MAIN : (window + 1) * MAIN, :] = found[:, :MAIN, :].astype(BF16)
        tail[:, window : window + 1, :] = found[:, MAIN : MAIN + 1, :]
        tail[:, 8 + window : 9 + window, :] = found[:, MAIN + 1 : MAIN + 2, :]
    for row in (6, 7, 14, 15):
        tail[:, row : row + 1, :] = jnp.zeros((count, 1, KDIM), F32)
    out_ref[:count, WINDOWS * MAIN :, :] = tail[...].astype(BF16)

    own_places.wait()
    cap = picks_ref.shape[0]
    lines = places.shape[0] // 3
    part = lines // cap

    def one_slot(piece, carry):
        brick = out_ref[picks_ref[piece, tile]]
        slot_sums(brick, places, sums, piece * part, part // 2)
        return carry

    lax.fori_loop(0, cap, one_slot, 0)
    out_ref[count, : whole_tiles(lines), :LANES] = line_values(sums, lines, whole_tiles(lines))


def windows_of(where, picks, bricks, places):
    count = bricks.shape[0]
    cube = bricks.reshape(count, EDGE, EDGE * EDGE)
    rows = places.shape[1]
    return pl.pallas_call(
        windows_kernel,
        out_shape=jax.ShapeDtypeStruct((count + 1, BRICK_ROWS, KDIM), BF16),
        in_specs=[smem(), smem(), vmem(), pl.BlockSpec(memory_space=pl.ANY)],
        out_specs=vmem(),
        scratch_shapes=[
            pltpu.VMEM((count, 48, 10 * LANES), BF16),
            pltpu.VMEM((count, TAIL, KDIM), F32),
            pltpu.VMEM((rows, LANES), F32),
            pltpu.VMEM((8 * rows // 3, LANES), F32),
            pltpu.SemaphoreType.DMA,
        ],
        compiler_params=params(16),
        cost_estimate=pl.CostEstimate(
            flops=2 * count * 48 * 384 * KDIM * WINDOWS, bytes_accessed=4 * MIB,
            transcendentals=0,
        ),
        name="brick_windows",
    )(where, picks, cube, places)


def hat(distance):
    return jnp.maximum(1.0 - jnp.abs(distance), 0.0)


def blend(brick, px, py, pz):
    width = px.shape[1]
    eight = lax.broadcasted_iota(jnp.int32, (8, width), 0).astype(F32)
    places = lax.broadcasted_iota(jnp.int32, (MAIN, width), 0).astype(F32).astype(BF16)

    def tile(rows):
        return jnp.concatenate([rows, rows], axis=0).astype(BF16)

    cell_y = jnp.floor(py)
    frac_y = py - cell_y
    lower, low_share, high_share = tile(cell_y), tile(1.0 - frac_y), tile(frac_y)
    nothing = jnp.zeros((TAIL, width), BF16)
    weight_y = []
    for start in range(0, MAIN, TAIL):
        offset = places[start : start + TAIL] - lower
        weight_y.append(
            jnp.where(offset == 0, low_share, jnp.where(offset == 1, high_share, nothing))
        )
    window = jnp.floor(px * (1.0 / STRIDE))
    weight_x = hat(eight - (px - STRIDE * window))
    parts = []
    for i in range(STRIDE + 1):
        share = tile(jnp.broadcast_to(weight_x[i : i + 1], (8, width)))
        parts += [share * part for part in weight_y]
    tail = [weight_x * hat(MAIN - py), weight_x * jnp.maximum(py - MAIN, 0.0)]
    parts.append(jnp.concatenate(tail, axis=0).astype(BF16))
    parts.append(nothing)
    plane = jnp.concatenate(parts, axis=0)
    found = jnp.dot(brick, plane, preferred_element_type=F32)
    groups = range(0, MAIN, 8)
    chosen = [found[row : row + 8] for row in groups]
    for other in range(1, WINDOWS):
        here = window == float(other)
        base = other * MAIN
        chosen = [
            jnp.where(here, found[base + row : base + row + 8], old)
            for row, old in zip(groups, chosen)
        ]
    base = WINDOWS * MAIN
    edges = found[base : base + 8] * hat(MAIN - pz)
    edges = edges + found[base + 8 :] * jnp.maximum(pz - MAIN, 0.0)
    total = jnp.where(eight == window, edges, 0.0)
    for row, part in zip(groups, chosen):
        total = total + part * hat((eight + float(row)) - pz)
    return total


def slot_sums(brick, places, sums, first, blocks):
    lines = places.shape[0] // 3
    for step in range(blocks):
        row = first + 2 * step

        def line(axis):
            both = [
                jnp.broadcast_to(places[pl.ds(axis * lines + row + half, 1), :], (8, LANES))
                for half in range(2)
            ]
            return jnp.concatenate(both, axis=1)

        total = blend(brick, line(0), line(1), line(2))
        for half in range(2):
            sums[pl.ds(pl.multiple_of(8 * (row + half), 8), 8), :] = total[
                :, half * LANES : (half + 1) * LANES
            ]


def whole_tiles(lines):
    return -(-lines // TAIL) * TAIL


def line_values(sums, lines, height):
    values = []
    for row in range(0, lines, 8):
        value = sums[pl.ds(8 * row, 8, stride=8), :]
        for other in range(1, 8):
            value = value + sums[pl.ds(8 * row + other, 8, stride=8), :]
        values.append(value)
    if height > lines:
        values.append(jnp.zeros((height - lines, LANES), F32))
    return jnp.concatenate(values, axis=0).astype(BF16)


def samples_kernel(
    where_ref, picks_ref, brick_ref, place_ref, out_ref, bricks, places, sums, own, arrivals,
    own_arrival,
):
    owners, rows, _ = place_ref.shape
    cap = picks_ref.shape[0]
    lines = rows // 3
    part = lines // cap
    turns = owners - 1
    tile = where_ref[0]
    pairs, rest = turns // 2, turns % 2
    own_values = pltpu.make_async_copy(
        brick_ref.at[brick_ref.shape[0] - 1, pl.ds(0, own.shape[0]), pl.ds(0, LANES)],
        own,
        own_arrival,
    )

    def renderer_of(number):
        return lax.rem(tile + 1 + number, owners)

    def fetches(turn, members):
        held = turn % 2
        copies = []
        for member in range(members):
            renderer = renderer_of(2 * turn + member)
            copies.append(
                pltpu.make_async_copy(
                    place_ref.at[renderer],
                    places.at[held, member],
                    arrivals.at[held, member, cap],
                )
            )
            for piece in range(cap):
                copies.append(
                    pltpu.make_async_copy(
                        brick_ref.at[picks_ref[piece, renderer]],
                        bricks.at[held, member, piece],
                        arrivals.at[held, member, piece],
                    )
                )
        return copies

    def start(turn, members):
        for copy in fetches(turn, members):
            copy.start()

    def work(turn, members):
        held = turn % 2
        for copy in fetches(turn, members):
            copy.wait()
        for member in range(members):
            for piece in range(cap):
                slot_sums(
                    bricks[held, member, piece],
                    places.at[held, member],
                    sums.at[member],
                    piece * part,
                    part // 2,
                )
        for member in range(members):
            out_ref[renderer_of(2 * turn + member)] = line_values(
                sums.at[member], lines, lines
            )

    def one_pair(turn, carry):
        work(turn, 2)

        @pl.when(turn + 2 < pairs)
        def _():
            start(turn + 2, 2)

        if rest:

            @pl.when(turn + 2 == pairs)
            def _():
                start(pairs, 1)

        return carry

    for turn in range(min(2, pairs)):
        start(turn, 2)
    if rest and pairs < 2:
        start(pairs, 1)
    own_values.start()
    lax.fori_loop(0, pairs, one_pair, 0)
    if rest:
        work(pairs, 1)
    own_values.wait()
    out_ref[tile] = own[...].astype(F32)[:lines].astype(BF16)


def sample_values(where, picks, windows, places):
    owners, rows, _ = places.shape
    cap = picks.shape[0]
    samples = owners * rows * LANES // 3
    some = pl.BlockSpec(memory_space=pl.ANY)
    return pl.pallas_call(
        samples_kernel,
        out_shape=jax.ShapeDtypeStruct((owners, rows // 3, LANES), BF16),
        in_specs=[smem(), smem(), some, some],
        out_specs=vmem(),
        scratch_shapes=[
            pltpu.VMEM((2, 2, cap, BRICK_ROWS, KDIM), BF16),
            pltpu.VMEM((2, 2, rows, LANES), F32),
            pltpu.VMEM((2, 8 * rows // 3, LANES), F32),
            pltpu.VMEM((whole_tiles(rows // 3), LANES), BF16),
            pltpu.SemaphoreType.DMA((2, 2, cap + 1)),
            pltpu.SemaphoreType.DMA,
        ],
        compiler_params=pltpu.CompilerParams(vmem_limit_bytes=61_600_000),
        cost_estimate=pl.CostEstimate(
            flops=2 * samples * KDIM * BRICK_ROWS, bytes_accessed=3 * MIB,
            transcendentals=0,
        ),
        name="sample_values",
    )(where, picks, windows, places)


def gbuffer_kernel(value_ref, order_ref, out_ref, values):
    values[...] = value_ref[...].astype(F32).reshape(values.shape)
    height = out_ref.shape[2]

    def ray_of(number):
        rows_now = slice(number * height, (number + 1) * height)
        first, second = (
            values[pl.ds(2 * number * height + half, height, stride=2), :] for half in range(2)
        )
        parts = []
        for half in range(2):
            order = order_ref[0, 0, rows_now, half * LANES : (half + 1) * LANES]
            inner = order & (LANES - 1)
            parts.append(
                jnp.where(
                    order < LANES,
                    jnp.take_along_axis(first, inner, axis=1, mode="promise_in_bounds"),
                    jnp.take_along_axis(second, inner, axis=1, mode="promise_in_bounds"),
                )
            )
        return jnp.concatenate(parts, axis=1)

    remain = 1.0
    shade = 0.0
    depth = 0.0
    for step in range(NSP):
        ray = ray_of(step)
        half_tanh = 0.5 * jnp.tanh(ray)
        weight = remain * (0.5 + half_tanh)
        shade = shade + weight * ray
        depth = depth + weight * ((step + 1) / NSP)
        remain = remain * (0.5 - half_tanh)
    occlusion = 0.0
    for ray_number in range(NRAY):
        passing = 1.0
        for step in range(NOS):
            ray = ray_of(NSP + ray_number * NOS + step)
            passing = passing * (0.5 - 0.5 * jnp.tanh(ray))
        occlusion = occlusion + passing
    out_ref[0, 0] = shade.astype(BF16)
    out_ref[0, 1] = (1.0 - remain).astype(BF16)
    out_ref[0, 2] = depth.astype(BF16)
    out_ref[0, 3] = (occlusion * (1.0 / NRAY)).astype(BF16)


def gbuffer(values, order, height, width):
    total = order.shape[2]
    return pl.pallas_call(
        gbuffer_kernel,
        out_shape=jax.ShapeDtypeStruct((1, 4, height, width), BF16),
        in_specs=[vmem(), vmem()],
        out_specs=vmem(),
        scratch_shapes=[pltpu.VMEM((2 * total, LANES), F32)],
        compiler_params=params(16),
        cost_estimate=pl.CostEstimate(
            flops=20 * total * BLOCK, bytes_accessed=8 * total * BLOCK, transcendentals=0
        ),
        name="gbuffer",
    )(values, order)


def silu(field):
    half = 0.5 * field
    return half + half * jnp.tanh(half)


def shifted(rows, steps):
    lane = lax.broadcasted_iota(jnp.int32, (1, LANES), 1)
    edge = lane == (0 if steps == 1 else LANES - 1)
    moved = []
    for row in rows:
        tiles = [row[:, i : i + LANES] for i in range(0, row.shape[1], LANES)]
        tiles = [pltpu.roll(tile, steps % LANES, 1) for tile in tiles]
        for i, tile in enumerate(tiles):
            source = i - steps
            fill = tiles[source] if 0 <= source < len(tiles) else 0.0
            moved.append(jnp.where(edge, fill, tile))
    return jnp.concatenate(moved, axis=1)


def across(total, chans, row_width):
    left, middle, right = (total[i * chans : (i + 1) * chans] for i in range(3))

    def rows_of(part):
        return [part[:, i : i + row_width] for i in range(0, part.shape[1], row_width)]

    return middle + shifted(rows_of(left), 1) + shifted(rows_of(right), -1)


def taps(weight_ref, tap):
    _, out_chans, chans = weight_ref.shape
    return weight_ref[3 * tap : 3 * tap + 3].reshape(3 * out_chans, chans)


def beside(weight_ref):
    return jnp.concatenate([taps(weight_ref, tap) for tap in range(3)], axis=1)


def sides(where_ref):
    above = jnp.where(where_ref[0] > 0, 1.0, 0.0)
    below = jnp.where(where_ref[0] < where_ref[1] - 1, 1.0, 0.0)

    def inside(row, low, high):
        return jnp.where(row < low, above, jnp.where(row >= high, below, 1.0))

    return inside


def turned(weight_ref):
    _, chans, out_chans = weight_ref.shape
    here = lax.broadcasted_iota(jnp.int32, (out_chans, out_chans), 0)
    there = lax.broadcasted_iota(jnp.int32, (out_chans, out_chans), 1)
    unit = jnp.where(here == there, 1.0, 0.0).astype(BF16)
    rows = []
    for column in range(3):
        stack = jnp.concatenate([weight_ref[3 * tap + column] for tap in range(3)], axis=0)
        rows.append(
            lax.dot_general(
                unit, stack, (((1,), (1,)), ((), ())), preferred_element_type=F32
            )
        )
    return jnp.concatenate(rows, axis=0).astype(BF16)


def stem_kernel(where_ref, x_ref, w_in, w_mid, second, first):
    height = x_ref.shape[0] // 3
    width = x_ref.shape[2]
    inside = sides(where_ref)

    def full_layer(weight, source, target, low, high, unroll):
        chans = target.shape[1]
        depth = weight.shape[1]

        def step(row, carry):
            lines = source[pl.ds(row, 3)].reshape(depth, width)
            line = across(jnp.dot(weight, lines, preferred_element_type=F32), chans, width)
            target[row] = (silu(line) * inside(row, low, high)).astype(BF16)
            return carry

        lax.fori_loop(0, target.shape[0], step, 0, unroll=unroll)

    full_layer(turned(w_in), x_ref, first, height - 1, 2 * height - 1, first.shape[0])
    full_layer(beside(w_mid), first, second, height - 2, 2 * height - 2, second.shape[0])


def half_pair(source, row, tap):
    return jnp.concatenate([source[row + tap], source[row + tap + 1]], axis=1)


def half_layer(product, target, inside, low, high):
    chans, half_width = target.shape[1], target.shape[2]
    for row in range(0, target.shape[0], 2):
        both = silu(across(product(row), chans, half_width))
        for now in range(2):
            line = both[:, now * half_width : (now + 1) * half_width]
            if row + now < low or row + now >= high:
                line = line * inside(row + now, low, high)
            target[row + now] = line.astype(BF16)


def middle_kernel(where_ref, second, w_down, third, pooled):
    count, chans, width = second.shape
    half_height = (count + 4) // 6
    half_width = width // 2
    inside = sides(where_ref)
    place = lax.broadcasted_iota(jnp.int32, (width, half_width), 0) // 2
    target = lax.broadcasted_iota(jnp.int32, (width, half_width), 1)
    shrink = jnp.where(place == target, 0.25, 0.0).astype(BF16)
    pairs = jnp.dot(
        second[...].reshape(count * chans, width), shrink, preferred_element_type=F32
    ).reshape(count // 2, 2, chans, half_width)
    pooled[...] = (pairs[:, 0] + pairs[:, 1]).astype(BF16)
    weight_down = turned(w_down)

    def down_product(row):
        lines = jnp.concatenate([half_pair(pooled, row, tap) for tap in range(3)], axis=0)
        return jnp.dot(weight_down, lines, preferred_element_type=F32)

    half_layer(down_product, third, inside, half_height - 2, 2 * half_height - 2)


def decoder_kernel(
    where_ref, second, third, w_deep, w_up, w_out, out_ref, fourth, joined, fifth, final
):
    height = out_ref.shape[2]
    half_height = height // 2
    width = out_ref.shape[3]
    half_width = width // 2
    chans = second.shape[1]
    inside = sides(where_ref)

    def deep_product(row):
        total = None
        for tap in range(3):
            part = jnp.dot(
                taps(w_deep, tap), half_pair(third, row, tap), preferred_element_type=F32
            )
            total = part if total is None else total + part
        return total

    half_layer(deep_product, fourth, inside, half_height - 3, 2 * half_height - 3)
    place = lax.broadcasted_iota(jnp.int32, (half_width, width), 0)
    target = lax.broadcasted_iota(jnp.int32, (half_width, width), 1) // 2
    spread = jnp.where(place == target, 1.0, 0.0).astype(BF16)
    deep = fourth.shape[1]
    wide = jnp.dot(
        fourth[...].reshape(-1, half_width), spread, preferred_element_type=F32
    ).astype(BF16).reshape(fourth.shape[0], deep, width)
    for row in range(2 * fourth.shape[0]):
        joined[row, chans:, :] = wide[row // 2]
        joined[row, :chans, :] = second[row + 4]

    def up_step(row, carry):
        total = None
        for tap in range(3):
            part = jnp.dot(taps(w_up, tap), joined[row + tap], preferred_element_type=F32)
            total = part if total is None else total + part
        line = silu(across(total, chans, width))
        fifth[row] = (line * inside(row, 1, height + 1)).astype(BF16)
        return carry

    lax.fori_loop(0, fifth.shape[0], up_step, 0, unroll=fifth.shape[0])

    colours = out_ref.shape[1]
    weight_out = beside(w_out)
    for row in range(height):
        lines = fifth[row : row + 3].reshape(3 * chans, width)
        total = jnp.dot(weight_out, lines, preferred_element_type=F32)
        line = across(total, w_out.shape[1], width)
        for colour in range(colours):
            final[colour, row : row + 1, :] = line[colour : colour + 1, :]
    out_ref[0] = final[...].astype(BF16)


def stem(where, field, w_in, w_mid):
    height = field.shape[0] // 3
    width = field.shape[2]
    one = w_mid.shape[1]
    return pl.pallas_call(
        stem_kernel,
        out_shape=jax.ShapeDtypeStruct((3 * height - 4, one, width), BF16),
        in_specs=[smem()] + [vmem()] * 3,
        out_specs=vmem(),
        scratch_shapes=[pltpu.VMEM((3 * height - 2, one, width), BF16)],
        compiler_params=params(16),
        cost_estimate=pl.CostEstimate(
            flops=1_000_000_000, bytes_accessed=MIB, transcendentals=300_000
        ),
        name="stem",
    )(where, field, w_in, w_mid)


def middle(where, second, w_down):
    rows, one, width = second.shape
    half = (rows + 4) // 6
    two = w_down.shape[2]
    return pl.pallas_call(
        middle_kernel,
        out_shape=jax.ShapeDtypeStruct((3 * half - 4, two, width // 2), BF16),
        in_specs=[smem()] + [vmem()] * 2,
        out_specs=vmem(),
        scratch_shapes=[pltpu.VMEM((3 * half - 2, one, width // 2), BF16)],
        compiler_params=params(16),
        cost_estimate=pl.CostEstimate(
            flops=500_000_000, bytes_accessed=MIB, transcendentals=100_000
        ),
        name="middle",
    )(where, second, w_down)


def decoder(where, second, third, w_deep, w_up, w_out, height, colours):
    one = second.shape[1]
    two = third.shape[1]
    width = second.shape[2]
    return pl.pallas_call(
        decoder_kernel,
        out_shape=jax.ShapeDtypeStruct((1, colours, height, width), BF16),
        in_specs=[smem()] + [vmem()] * 5,
        out_specs=vmem(),
        scratch_shapes=[
            pltpu.VMEM((third.shape[0] - 2, two, width // 2), BF16),
            pltpu.VMEM((height + 4, one + two, width), BF16),
            pltpu.VMEM((height + 2, one, width), BF16),
            pltpu.VMEM((colours, height, width), F32),
        ],
        compiler_params=params(16),
        cost_estimate=pl.CostEstimate(
            flops=1_500_000_000, bytes_accessed=MIB, transcendentals=200_000
        ),
        name="decoder",
    )(where, second, third, w_deep, w_up, w_out)


def on_device(
    bricks, sends, cells, fracs, sample_order, pending, w_in, w_mid, w_down, w_deep, w_up, w_out
):
    n_tile = lax.axis_size("tile")
    tile = lax.axis_index("tile")
    n_section = lax.axis_size("section")
    cap = sends.shape[3]
    height = pending.shape[2]
    width = pending.shape[3]
    samples = cells.shape[3]
    slots = n_tile * cap
    per_slot = samples // slots
    padded = -(-per_slot // BLOCK) * BLOCK

    def fill(part):
        if padded != per_slot:
            part = part.reshape(3, slots, per_slot)
            part = jnp.pad(part, ((0, 0), (0, 0), (0, padded - per_slot)))
        return part.reshape(3, slots * padded // LANES, LANES)

    def trim(found):
        if padded == per_slot:
            return found
        return found.reshape(slots, padded)[:, :per_slot].reshape(1, samples // LANES, LANES)

    places = positions(fill(cells), fill(fracs), n_tile)
    places, bricks, pending = lax.optimization_barrier((places, bricks, pending))
    arrived = lax.all_to_all(places, "tile", split_axis=0, concat_axis=0, tiled=True)

    down = [(i, i + 1) for i in range(n_tile - 1)]
    up = [(i + 1, i) for i in range(n_tile - 1)]
    over = lax.ppermute(pending, "tile", down)
    under = lax.ppermute(pending, "tile", up)
    where = jnp.stack([tile, jnp.int32(n_tile)]).astype(jnp.int32)
    picks = sends[0, 0].T
    colours = w_out.shape[1]
    w_in = w_in.transpose(0, 2, 1)
    w_in = jnp.pad(w_in, ((0, 0), (0, 16 - w_in.shape[1]), (0, 0)))
    w_out = jnp.pad(w_out, ((0, 0), (0, 16 - colours), (0, 0)))
    windows = windows_of(where, picks, bricks, places)
    arrived, w_in, w_out = lax.optimization_barrier((arrived, w_in, w_out))
    found = sample_values(where, picks, windows, arrived)

    found, over, under, pending = lax.optimization_barrier((found, over, under, pending))
    values = lax.all_to_all(found, "tile", split_axis=0, concat_axis=0, tiled=True)
    field = jnp.concatenate([over[0], pending[0], under[0]], axis=1).transpose(1, 0, 2)
    field = jnp.pad(field, ((0, 0), (0, 16 - field.shape[1]), (0, 0)))
    second = stem(where, field, w_in, w_mid)
    third = middle(where, second, w_down.transpose(0, 2, 1))
    values, third = lax.optimization_barrier((values, third))
    rendered = gbuffer(trim(values), sample_order, height, width)
    rendered, third = lax.optimization_barrier((rendered, third))
    ring = [(i, (i + 1) % n_section) for i in range(n_section)]
    handoff = lax.ppermute(rendered, "section", ring)
    denoised = decoder(where, second, third, w_deep, w_up, w_out, height, colours)
    return (handoff, denoised)


def solution(mesh):
    in_specs = (
        P("tile", None),
        P("section", "tile", None, None),
        P("section", "tile", None, None),
        P("section", "tile", None, None),
        P("section", "tile", None, None),
        P("section", None, "tile", None),
        P(),
        P(),
        P(),
        P(),
        P(),
        P(),
    )
    out_specs = (P("section", None, "tile", None), P("section", None, "tile", None))
    return jax.shard_map(
        on_device, mesh=mesh, in_specs=in_specs, out_specs=out_specs, check_vma=False
    )
```

```python
import functools

import jax
import jax.numpy as jnp
from jax import lax
from jax.experimental import pallas as pl
from jax.experimental.pallas import tpu as pltpu
from jax.sharding import PartitionSpec as P

EDGE = 34
NSP = 4
NRAY = 8
NOS = 2
LANES = 128
BLOCK = 256
STRIDE = 6
WINDOWS = 6
MAIN = 32
TAIL = 16
BRICK_ROWS = WINDOWS * MAIN + TAIL
KDIM = 256
HBM_ROWS = 640

F32 = jnp.float32
BF16 = jnp.bfloat16
MIB = 1024 * 1024


def params(mib):
    return pltpu.CompilerParams(vmem_limit_bytes=mib * MIB)


def vmem():
    return pl.BlockSpec(memory_space=pltpu.VMEM)


def smem():
    return pl.BlockSpec(memory_space=pltpu.SMEM)


def positions_kernel(cells_ref, fracs_ref, out_ref, cells, fracs, found, arrivals, departures):
    owners, rows, _ = out_ref.shape
    lines = rows // 3
    parts = arrivals.shape[1]
    share = owners // parts
    pieces = [(axis, part) for axis in range(3) for part in range(parts)]

    def reads(axis, part):
        span = pl.ds(part * share * lines, share * lines)
        return [
            pltpu.make_async_copy(
                source.at[axis, span], target.at[axis, span], arrivals.at[axis, part, number]
            )
            for number, (source, target) in enumerate(((cells_ref, cells), (fracs_ref, fracs)))
        ]

    def write(axis, part):
        place = (pl.ds(part * share, share), pl.ds(axis * lines, lines))
        return pltpu.make_async_copy(
            found.at[place], out_ref.at[place], departures.at[axis, part]
        )

    for piece in pieces:
        for copy in reads(*piece):
            copy.start()
    for axis, part in pieces:
        for copy in reads(axis, part):
            copy.wait()
        span = slice(part * share * lines, (part + 1) * share * lines)
        place = cells[axis, span].astype(F32) + fracs[axis, span]
        found[part * share : (part + 1) * share, axis * lines : (axis + 1) * lines, :] = (
            place.reshape(share, lines, LANES)
        )
        write(axis, part).start()
    for piece in pieces:
        write(*piece).wait()


def positions(cells, fracs, owners):
    lines = cells.shape[1]
    shape = (owners, 3 * lines // owners, LANES)
    hbm = pl.BlockSpec(memory_space=pltpu.HBM)
    return pl.pallas_call(
        positions_kernel,
        out_shape=jax.ShapeDtypeStruct(shape, F32),
        in_specs=[hbm, hbm],
        out_specs=hbm,
        scratch_shapes=[
            pltpu.VMEM(cells.shape, jnp.int32),
            pltpu.VMEM(fracs.shape, F32),
            pltpu.VMEM(shape, F32),
            pltpu.SemaphoreType.DMA((3, 2, 2)),
            pltpu.SemaphoreType.DMA((3, 2)),
        ],
        compiler_params=params(60),
        cost_estimate=pl.CostEstimate(
            flops=3 * lines * LANES, bytes_accessed=36 * lines * LANES, transcendentals=0
        ),
        name="positions",
    )(cells, fracs)


def windows_kernel(
    where_ref, picks_ref, cube_ref, place_ref, out_ref,
    wide, found_all, tail, places, sums, own, arrival, departures,
):
    tile = where_ref[0]
    own_places = pltpu.make_async_copy(place_ref.at[tile], places, arrival)
    own_places.start()
    count = cube_ref.shape[0]
    plane = EDGE * EDGE
    copies = []

    def send(source, target):
        copy = pltpu.make_async_copy(source, target, departures.at[len(copies)])
        copy.start()
        copies.append(copy)

    def send_rows(first, size):
        rows = pl.ds(first, size)
        send(found_all.at[:, rows], out_ref.at[pl.ds(0, count), rows])

    wide[...] = jnp.zeros_like(wide)
    wide[:, :EDGE, :plane] = cube_ref[...]
    column = lax.broadcasted_iota(jnp.int32, (1, KDIM), 1)
    main = (column // MAIN) * EDGE + column % MAIN
    rest = column - 7 * MAIN
    last = (rest % 8) * EDGE + MAIN + rest // 8
    source = jnp.where(column < 7 * MAIN, main, last)
    unused = (column >= 7 * MAIN) & ((rest % 8 == 7) | (rest >= TAIL))
    source = jnp.where(unused, -(1 << 20), source)
    for window in range(WINDOWS):
        first = window * STRIDE * EDGE
        low = first // LANES * LANES
        length = min(3 * LANES, wide.shape[2] - low)
        place = lax.broadcasted_iota(jnp.int32, (length, KDIM), 0)
        pick = jnp.where(place == source + (first - low), 1.0, 0.0).astype(BF16)
        found = jnp.dot(
            wide[:, :, low : low + length].reshape(-1, length),
            pick,
            preferred_element_type=F32,
        )
        found = found.reshape(count, 48, KDIM)
        found_all[:, window * MAIN : (window + 1) * MAIN, :] = found[:, :MAIN, :].astype(BF16)
        send_rows(window * MAIN, MAIN)
        tail[:, window : window + 1, :] = found[:, MAIN : MAIN + 1, :]
        tail[:, 8 + window : 9 + window, :] = found[:, MAIN + 1 : MAIN + 2, :]
    for row in (6, 7, 14, 15):
        tail[:, row : row + 1, :] = jnp.zeros((count, 1, KDIM), F32)
    found_all[:, WINDOWS * MAIN :, :] = tail[...].astype(BF16)
    send_rows(WINDOWS * MAIN, TAIL)

    own_places.wait()
    cap = picks_ref.shape[0]
    lines = places.shape[0] // 3
    part = lines // cap

    for piece in range(cap):
        brick = found_all[picks_ref[piece, tile]]
        slot_sums(brick, places, sums, piece * part, part // 2)
    own[...] = line_values(sums, lines, own.shape[0])
    send(own, out_ref.at[count, pl.ds(0, own.shape[0]), pl.ds(0, LANES)])
    for copy in copies:
        copy.wait()


def windows_of(where, picks, bricks, places):
    count = bricks.shape[0]
    cube = bricks.reshape(count, EDGE, EDGE * EDGE)
    rows = places.shape[1]
    return pl.pallas_call(
        windows_kernel,
        out_shape=jax.ShapeDtypeStruct((max(count + 1, HBM_ROWS), BRICK_ROWS, KDIM), BF16),
        in_specs=[smem(), smem(), vmem(), pl.BlockSpec(memory_space=pl.ANY)],
        out_specs=pl.BlockSpec(memory_space=pl.ANY),
        scratch_shapes=[
            pltpu.VMEM((count, 48, 10 * LANES), BF16),
            pltpu.VMEM((count, BRICK_ROWS, KDIM), BF16),
            pltpu.VMEM((count, TAIL, KDIM), F32),
            pltpu.VMEM((rows, LANES), F32),
            pltpu.VMEM((8 * rows // 3, LANES), F32),
            pltpu.VMEM((whole_tiles(rows // 3), LANES), BF16),
            pltpu.SemaphoreType.DMA,
            pltpu.SemaphoreType.DMA((WINDOWS + 2,)),
        ],
        compiler_params=params(16),
        cost_estimate=pl.CostEstimate(
            flops=2 * count * 48 * 384 * KDIM * WINDOWS, bytes_accessed=4 * MIB,
            transcendentals=0,
        ),
        name="brick_windows",
    )(where, picks, cube, places)


def hat(distance):
    return jnp.maximum(1.0 - jnp.abs(distance), 0.0)


def blend(brick, px, py, pz):
    width = px.shape[1]
    eight = lax.broadcasted_iota(jnp.int32, (8, width), 0).astype(F32)
    places = lax.broadcasted_iota(jnp.int32, (MAIN, width), 0).astype(F32).astype(BF16)

    def tile(rows):
        return jnp.concatenate([rows, rows], axis=0).astype(BF16)

    cell_y = jnp.floor(py)
    frac_y = py - cell_y
    lower, low_share, high_share = tile(cell_y), tile(1.0 - frac_y), tile(frac_y)
    nothing = jnp.zeros((TAIL, width), BF16)
    weight_y = []
    for start in range(0, MAIN, TAIL):
        offset = places[start : start + TAIL] - lower
        weight_y.append(
            jnp.where(offset == 0, low_share, jnp.where(offset == 1, high_share, nothing))
        )
    window = jnp.floor(px * (1.0 / STRIDE))
    weight_x = hat(eight - (px - STRIDE * window))
    parts = []
    for i in range(STRIDE + 1):
        share = tile(jnp.broadcast_to(weight_x[i : i + 1], (8, width)))
        parts += [share * part for part in weight_y]
    tail = [weight_x * hat(MAIN - py), weight_x * jnp.maximum(py - MAIN, 0.0)]
    parts.append(jnp.concatenate(tail, axis=0).astype(BF16))
    parts.append(nothing)
    plane = jnp.concatenate(parts, axis=0)
    found = jnp.dot(brick, plane, preferred_element_type=F32)
    groups = range(0, MAIN, 8)
    chosen = [found[row : row + 8] for row in groups]
    for other in range(1, WINDOWS):
        here = window == float(other)
        base = other * MAIN
        chosen = [
            jnp.where(here, found[base + row : base + row + 8], old)
            for row, old in zip(groups, chosen)
        ]
    base = WINDOWS * MAIN
    edges = found[base : base + 8] * hat(MAIN - pz)
    edges = edges + found[base + 8 :] * jnp.maximum(pz - MAIN, 0.0)
    total = jnp.where(eight == window, edges, 0.0)
    for row, part in zip(groups, chosen):
        total = total + part * hat((eight + float(row)) - pz)
    return total


def slot_sums(brick, places, sums, first, blocks):
    lines = places.shape[0] // 3
    for step in range(blocks):
        row = first + 2 * step

        def line(axis):
            both = [
                jnp.broadcast_to(places[pl.ds(axis * lines + row + half, 1), :], (8, LANES))
                for half in range(2)
            ]
            return jnp.concatenate(both, axis=1)

        total = blend(brick, line(0), line(1), line(2))
        for half in range(2):
            sums[pl.ds(pl.multiple_of(8 * (row + half), 8), 8), :] = total[
                :, half * LANES : (half + 1) * LANES
            ]


def whole_tiles(lines):
    return -(-lines // TAIL) * TAIL


def line_values(sums, lines, height):
    values = []
    for row in range(0, lines, 8):
        value = sums[pl.ds(8 * row, 8, stride=8), :]
        for other in range(1, 8):
            value = value + sums[pl.ds(8 * row + other, 8, stride=8), :]
        values.append(value)
    if height > lines:
        values.append(jnp.zeros((height - lines, LANES), F32))
    return jnp.concatenate(values, axis=0).astype(BF16)


def samples_kernel(
    count, where_ref, picks_ref, brick_ref, place_ref, out_ref, bricks, places, sums, own, arrivals,
    own_arrival,
):
    owners, rows, _ = place_ref.shape
    cap = picks_ref.shape[0]
    lines = rows // 3
    part = lines // cap
    turns = owners - 1
    tile = where_ref[0]
    pairs, rest = turns // 2, turns % 2
    own_values = pltpu.make_async_copy(
        brick_ref.at[count, pl.ds(0, own.shape[0]), pl.ds(0, LANES)],
        own,
        own_arrival,
    )

    def renderer_of(number):
        return lax.rem(tile + 1 + number, owners)

    def fetches(held, first, members):
        copies = []
        for member in range(members):
            renderer = renderer_of(first + member)
            copies.append(
                pltpu.make_async_copy(
                    place_ref.at[renderer],
                    places.at[held, member],
                    arrivals.at[held, member, cap],
                )
            )
            for piece in range(cap):
                copies.append(
                    pltpu.make_async_copy(
                        brick_ref.at[picks_ref[piece, renderer]],
                        bricks.at[held, member, piece],
                        arrivals.at[held, member, piece],
                    )
                )
        return copies

    def pair_fetches(turn):
        return fetches((turn + rest) % 2, rest + 2 * turn, 2)

    def start(copies):
        for copy in copies:
            copy.start()

    def blend_slot(held, member, piece):
        slot_sums(
            bricks[held, member, piece],
            places.at[held, member],
            sums.at[member],
            piece * part,
            part // 2,
        )

    def one_pair(turn, carry):
        for copy in pair_fetches(turn):
            copy.wait()
        for member in range(2):
            for piece in range(cap):
                blend_slot((turn + rest) % 2, member, piece)
        for member in range(2):
            out_ref[renderer_of(rest + 2 * turn + member)] = line_values(
                sums.at[member], lines, lines
            )

        @pl.when(turn + 2 < pairs)
        def _():
            start(pair_fetches(turn + 2))

        return carry

    if rest:
        copies = fetches(0, 0, 1)
        start(copies)
        copies[0].wait()
        for piece in range(cap):
            copies[1 + piece].wait()
            if piece == 0 and pairs > 0:
                start(pair_fetches(0))
            blend_slot(0, 0, piece)
        out_ref[renderer_of(0)] = line_values(sums.at[0], lines, lines)
    elif pairs > 0:
        start(pair_fetches(0))
    if pairs > 1:
        start(pair_fetches(1))
    own_values.start()
    lax.fori_loop(0, pairs, one_pair, 0)
    own_values.wait()
    out_ref[tile] = own[...].astype(F32)[:lines].astype(BF16)


def sample_values(where, picks, windows, places, count):
    owners, rows, _ = places.shape
    cap = picks.shape[0]
    samples = owners * rows * LANES // 3
    some = pl.BlockSpec(memory_space=pl.ANY)
    return pl.pallas_call(
        functools.partial(samples_kernel, count),
        out_shape=jax.ShapeDtypeStruct((owners, rows // 3, LANES), BF16),
        in_specs=[smem(), smem(), some, some],
        out_specs=vmem(),
        scratch_shapes=[
            pltpu.VMEM((2, 2, cap, BRICK_ROWS, KDIM), BF16),
            pltpu.VMEM((2, 2, rows, LANES), F32),
            pltpu.VMEM((2, 8 * rows // 3, LANES), F32),
            pltpu.VMEM((whole_tiles(rows // 3), LANES), BF16),
            pltpu.SemaphoreType.DMA((2, 2, cap + 1)),
            pltpu.SemaphoreType.DMA,
        ],
        compiler_params=params(16),
        cost_estimate=pl.CostEstimate(
            flops=2 * samples * KDIM * BRICK_ROWS, bytes_accessed=3 * MIB,
            transcendentals=0,
        ),
        name="sample_values",
    )(where, picks, windows, places)


def gbuffer_kernel(value_ref, order_ref, out_ref, values):
    values[...] = value_ref[...].astype(F32).reshape(values.shape)
    height = out_ref.shape[2]

    def ray_of(number):
        rows_now = slice(number * height, (number + 1) * height)
        first, second = (
            values[pl.ds(2 * number * height + half, height, stride=2), :] for half in range(2)
        )
        parts = []
        for half in range(2):
            order = order_ref[0, 0, rows_now, half * LANES : (half + 1) * LANES]
            inner = order & (LANES - 1)
            parts.append(
                jnp.where(
                    order < LANES,
                    jnp.take_along_axis(first, inner, axis=1, mode="promise_in_bounds"),
                    jnp.take_along_axis(second, inner, axis=1, mode="promise_in_bounds"),
                )
            )
        return jnp.concatenate(parts, axis=1)

    remain = 1.0
    shade = 0.0
    depth = 0.0
    for step in range(NSP):
        ray = ray_of(step)
        half_tanh = 0.5 * jnp.tanh(ray)
        weight = remain * (0.5 + half_tanh)
        shade = shade + weight * ray
        depth = depth + weight * ((step + 1) / NSP)
        remain = remain * (0.5 - half_tanh)
    occlusion = 0.0
    for ray_number in range(NRAY):
        passing = 1.0
        for step in range(NOS):
            ray = ray_of(NSP + ray_number * NOS + step)
            passing = passing * (0.5 - 0.5 * jnp.tanh(ray))
        occlusion = occlusion + passing
    out_ref[0, 0] = shade.astype(BF16)
    out_ref[0, 1] = (1.0 - remain).astype(BF16)
    out_ref[0, 2] = depth.astype(BF16)
    out_ref[0, 3] = (occlusion * (1.0 / NRAY)).astype(BF16)


def gbuffer(values, order, height, width):
    total = order.shape[2]
    return pl.pallas_call(
        gbuffer_kernel,
        out_shape=jax.ShapeDtypeStruct((1, 4, height, width), BF16),
        in_specs=[vmem(), vmem()],
        out_specs=vmem(),
        scratch_shapes=[pltpu.VMEM((2 * total, LANES), F32)],
        compiler_params=params(16),
        cost_estimate=pl.CostEstimate(
            flops=20 * total * BLOCK, bytes_accessed=8 * total * BLOCK, transcendentals=0
        ),
        name="gbuffer",
    )(values, order)


def silu(field):
    half = 0.5 * field
    return half + half * jnp.tanh(half)


def shifted(rows, steps):
    lane = lax.broadcasted_iota(jnp.int32, (1, LANES), 1)
    edge = lane == (0 if steps == 1 else LANES - 1)
    moved = []
    for row in rows:
        tiles = [row[:, i : i + LANES] for i in range(0, row.shape[1], LANES)]
        tiles = [pltpu.roll(tile, steps % LANES, 1) for tile in tiles]
        for i, tile in enumerate(tiles):
            source = i - steps
            fill = tiles[source] if 0 <= source < len(tiles) else 0.0
            moved.append(jnp.where(edge, fill, tile))
    return jnp.concatenate(moved, axis=1)


def across(total, chans, row_width):
    left, middle, right = (total[i * chans : (i + 1) * chans] for i in range(3))

    def rows_of(part):
        return [part[:, i : i + row_width] for i in range(0, part.shape[1], row_width)]

    return middle + shifted(rows_of(left), 1) + shifted(rows_of(right), -1)


def taps(weight_ref, tap):
    _, out_chans, chans = weight_ref.shape
    return weight_ref[3 * tap : 3 * tap + 3].reshape(3 * out_chans, chans)


def beside(weight_ref):
    return jnp.concatenate([taps(weight_ref, tap) for tap in range(3)], axis=1)


def sides(where_ref):
    above = jnp.where(where_ref[0] > 0, 1.0, 0.0)
    below = jnp.where(where_ref[0] < where_ref[1] - 1, 1.0, 0.0)

    def inside(row, low, high):
        return jnp.where(row < low, above, jnp.where(row >= high, below, 1.0))

    return inside


def turned(weight_ref):
    _, chans, out_chans = weight_ref.shape
    here = lax.broadcasted_iota(jnp.int32, (out_chans, out_chans), 0)
    there = lax.broadcasted_iota(jnp.int32, (out_chans, out_chans), 1)
    unit = jnp.where(here == there, 1.0, 0.0).astype(BF16)
    rows = []
    for column in range(3):
        stack = jnp.concatenate([weight_ref[3 * tap + column] for tap in range(3)], axis=0)
        rows.append(
            lax.dot_general(
                unit, stack, (((1,), (1,)), ((), ())), preferred_element_type=F32
            )
        )
    return jnp.concatenate(rows, axis=0).astype(BF16)


def stem_kernel(where_ref, x_ref, w_in, w_mid, second, first):
    height = x_ref.shape[0] // 3
    width = x_ref.shape[2]
    inside = sides(where_ref)

    def full_layer(weight, source, target, low, high, unroll):
        chans = target.shape[1]
        depth = weight.shape[1]

        def step(row, carry):
            lines = source[pl.ds(row, 3)].reshape(depth, width)
            line = across(jnp.dot(weight, lines, preferred_element_type=F32), chans, width)
            target[row] = (silu(line) * inside(row, low, high)).astype(BF16)
            return carry

        lax.fori_loop(0, target.shape[0], step, 0, unroll=unroll)

    full_layer(turned(w_in), x_ref, first, height - 1, 2 * height - 1, first.shape[0])
    full_layer(beside(w_mid), first, second, height - 2, 2 * height - 2, second.shape[0])


def half_pair(source, row, tap):
    return jnp.concatenate([source[row + tap], source[row + tap + 1]], axis=1)


def half_layer(product, target, inside, low, high):
    chans, half_width = target.shape[1], target.shape[2]
    for row in range(0, target.shape[0], 2):
        both = silu(across(product(row), chans, half_width))
        for now in range(2):
            line = both[:, now * half_width : (now + 1) * half_width]
            if row + now < low or row + now >= high:
                line = line * inside(row + now, low, high)
            target[row + now] = line.astype(BF16)


def middle_kernel(where_ref, second, w_down, third, pooled):
    count, chans, width = second.shape
    half_height = (count + 4) // 6
    half_width = width // 2
    inside = sides(where_ref)
    place = lax.broadcasted_iota(jnp.int32, (width, half_width), 0) // 2
    target = lax.broadcasted_iota(jnp.int32, (width, half_width), 1)
    shrink = jnp.where(place == target, 0.25, 0.0).astype(BF16)
    pairs = jnp.dot(
        second[...].reshape(count * chans, width), shrink, preferred_element_type=F32
    ).reshape(count // 2, 2, chans, half_width)
    pooled[...] = (pairs[:, 0] + pairs[:, 1]).astype(BF16)
    weight_down = turned(w_down)

    def down_product(row):
        lines = jnp.concatenate([half_pair(pooled, row, tap) for tap in range(3)], axis=0)
        return jnp.dot(weight_down, lines, preferred_element_type=F32)

    half_layer(down_product, third, inside, half_height - 2, 2 * half_height - 2)


def decoder_kernel(
    where_ref, second, third, w_deep, w_up, w_out, out_ref, fourth, joined, fifth, final
):
    height = out_ref.shape[2]
    half_height = height // 2
    width = out_ref.shape[3]
    half_width = width // 2
    chans = second.shape[1]
    inside = sides(where_ref)

    def deep_product(row):
        total = None
        for tap in range(3):
            part = jnp.dot(
                taps(w_deep, tap), half_pair(third, row, tap), preferred_element_type=F32
            )
            total = part if total is None else total + part
        return total

    half_layer(deep_product, fourth, inside, half_height - 3, 2 * half_height - 3)
    place = lax.broadcasted_iota(jnp.int32, (half_width, width), 0)
    target = lax.broadcasted_iota(jnp.int32, (half_width, width), 1) // 2
    spread = jnp.where(place == target, 1.0, 0.0).astype(BF16)
    deep = fourth.shape[1]
    wide = jnp.dot(
        fourth[...].reshape(-1, half_width), spread, preferred_element_type=F32
    ).astype(BF16).reshape(fourth.shape[0], deep, width)
    for row in range(2 * fourth.shape[0]):
        joined[row, chans:, :] = wide[row // 2]
        joined[row, :chans, :] = second[row + 4]

    def up_step(row, carry):
        total = None
        for tap in range(3):
            part = jnp.dot(taps(w_up, tap), joined[row + tap], preferred_element_type=F32)
            total = part if total is None else total + part
        line = silu(across(total, chans, width))
        fifth[row] = (line * inside(row, 1, height + 1)).astype(BF16)
        return carry

    lax.fori_loop(0, fifth.shape[0], up_step, 0, unroll=fifth.shape[0])

    colours = out_ref.shape[1]
    weight_out = beside(w_out)
    for row in range(height):
        lines = fifth[row : row + 3].reshape(3 * chans, width)
        total = jnp.dot(weight_out, lines, preferred_element_type=F32)
        line = across(total, w_out.shape[1], width)
        for colour in range(colours):
            final[colour, row : row + 1, :] = line[colour : colour + 1, :]
    out_ref[0] = final[...].astype(BF16)


def stem(where, field, w_in, w_mid):
    height = field.shape[0] // 3
    width = field.shape[2]
    one = w_mid.shape[1]
    return pl.pallas_call(
        stem_kernel,
        out_shape=jax.ShapeDtypeStruct((3 * height - 4, one, width), BF16),
        in_specs=[smem()] + [vmem()] * 3,
        out_specs=vmem(),
        scratch_shapes=[pltpu.VMEM((3 * height - 2, one, width), BF16)],
        compiler_params=params(16),
        cost_estimate=pl.CostEstimate(
            flops=1_000_000_000, bytes_accessed=MIB, transcendentals=300_000
        ),
        name="stem",
    )(where, field, w_in, w_mid)


def middle(where, second, w_down):
    rows, one, width = second.shape
    half = (rows + 4) // 6
    two = w_down.shape[2]
    return pl.pallas_call(
        middle_kernel,
        out_shape=jax.ShapeDtypeStruct((3 * half - 4, two, width // 2), BF16),
        in_specs=[smem()] + [vmem()] * 2,
        out_specs=vmem(),
        scratch_shapes=[pltpu.VMEM((3 * half - 2, one, width // 2), BF16)],
        compiler_params=params(16),
        cost_estimate=pl.CostEstimate(
            flops=500_000_000, bytes_accessed=MIB, transcendentals=100_000
        ),
        name="middle",
    )(where, second, w_down)


def decoder(where, second, third, w_deep, w_up, w_out, height, colours):
    one = second.shape[1]
    two = third.shape[1]
    width = second.shape[2]
    return pl.pallas_call(
        decoder_kernel,
        out_shape=jax.ShapeDtypeStruct((1, colours, height, width), BF16),
        in_specs=[smem()] + [vmem()] * 5,
        out_specs=vmem(),
        scratch_shapes=[
            pltpu.VMEM((third.shape[0] - 2, two, width // 2), BF16),
            pltpu.VMEM((height + 4, one + two, width), BF16),
            pltpu.VMEM((height + 2, one, width), BF16),
            pltpu.VMEM((colours, height, width), F32),
        ],
        compiler_params=params(16),
        cost_estimate=pl.CostEstimate(
            flops=1_500_000_000, bytes_accessed=MIB, transcendentals=200_000
        ),
        name="decoder",
    )(where, second, third, w_deep, w_up, w_out)


def on_device(
    bricks, sends, cells, fracs, sample_order, pending, w_in, w_mid, w_down, w_deep, w_up, w_out
):
    n_tile = lax.axis_size("tile")
    tile = lax.axis_index("tile")
    n_section = lax.axis_size("section")
    cap = sends.shape[3]
    height = pending.shape[2]
    width = pending.shape[3]
    samples = cells.shape[3]
    slots = n_tile * cap
    per_slot = samples // slots
    padded = -(-per_slot // BLOCK) * BLOCK

    def fill(part):
        if padded != per_slot:
            part = part.reshape(3, slots, per_slot)
            part = jnp.pad(part, ((0, 0), (0, 0), (0, padded - per_slot)))
        return part.reshape(3, slots * padded // LANES, LANES)

    def trim(found):
        if padded == per_slot:
            return found
        return found.reshape(slots, padded)[:, :per_slot].reshape(1, samples // LANES, LANES)

    places = positions(fill(cells), fill(fracs), n_tile)
    places, bricks, pending = lax.optimization_barrier((places, bricks, pending))
    arrived = lax.all_to_all(places, "tile", split_axis=0, concat_axis=0, tiled=True)

    down = [(i, i + 1) for i in range(n_tile - 1)]
    up = [(i + 1, i) for i in range(n_tile - 1)]
    over = lax.ppermute(pending, "tile", down)
    under = lax.ppermute(pending, "tile", up)
    where = jnp.stack([tile, jnp.int32(n_tile)]).astype(jnp.int32)
    picks = sends[0, 0].T
    colours = w_out.shape[1]
    w_in = w_in.transpose(0, 2, 1)
    w_in = jnp.pad(w_in, ((0, 0), (0, 16 - w_in.shape[1]), (0, 0)))
    w_out = jnp.pad(w_out, ((0, 0), (0, 16 - colours), (0, 0)))
    windows = windows_of(where, picks, bricks, places)
    arrived, w_in, w_out = lax.optimization_barrier((arrived, w_in, w_out))
    found = sample_values(where, picks, windows, arrived, bricks.shape[0])

    found, over, under, pending = lax.optimization_barrier((found, over, under, pending))
    values = lax.all_to_all(found, "tile", split_axis=0, concat_axis=0, tiled=True)
    field = jnp.concatenate([over[0], pending[0], under[0]], axis=1).transpose(1, 0, 2)
    field = jnp.pad(field, ((0, 0), (0, 16 - field.shape[1]), (0, 0)))
    second = stem(where, field, w_in, w_mid)
    third = middle(where, second, w_down.transpose(0, 2, 1))
    values, third = lax.optimization_barrier((values, third))
    rendered = gbuffer(trim(values), sample_order, height, width)
    rendered, third = lax.optimization_barrier((rendered, third))
    ring = [(i, (i + 1) % n_section) for i in range(n_section)]
    handoff = lax.ppermute(rendered, "section", ring)
    denoised = decoder(where, second, third, w_deep, w_up, w_out, height, colours)
    return (handoff, denoised)


def solution(mesh):
    in_specs = (
        P("tile", None),
        P("section", "tile", None, None),
        P("section", "tile", None, None),
        P("section", "tile", None, None),
        P("section", "tile", None, None),
        P("section", None, "tile", None),
        P(),
        P(),
        P(),
        P(),
        P(),
        P(),
    )
    out_specs = (P("section", None, "tile", None), P("section", None, "tile", None))
    return jax.shard_map(
        on_device, mesh=mesh, in_specs=in_specs, out_specs=out_specs, check_vma=False
    )
```

```python
import functools

import jax
import jax.numpy as jnp
from jax import lax
from jax.experimental import pallas as pl
from jax.experimental.pallas import tpu as pltpu
from jax.sharding import PartitionSpec as P

EDGE = 34
NSP = 4
NRAY = 8
NOS = 2
LANES = 128
BLOCK = 256
STRIDE = 6
WINDOWS = 6
MAIN = 32
TAIL = 16
BRICK_ROWS = WINDOWS * MAIN + TAIL
KDIM = 256

F32 = jnp.float32
BF16 = jnp.bfloat16
MIB = 1024 * 1024


def params(mib):
    return pltpu.CompilerParams(vmem_limit_bytes=mib * MIB)


def vmem():
    return pl.BlockSpec(memory_space=pltpu.VMEM)


def smem():
    return pl.BlockSpec(memory_space=pltpu.SMEM)


def positions_kernel(cells_ref, fracs_ref, out_ref, cells, fracs, found, arrivals, departures):
    owners, rows, _ = out_ref.shape
    lines = rows // 3
    parts = arrivals.shape[1]
    share = owners // parts
    pieces = [(axis, part) for axis in range(3) for part in range(parts)]

    def reads(axis, part):
        span = pl.ds(part * share * lines, share * lines)
        return [
            pltpu.make_async_copy(
                source.at[axis, span], target.at[axis, span], arrivals.at[axis, part, number]
            )
            for number, (source, target) in enumerate(((cells_ref, cells), (fracs_ref, fracs)))
        ]

    def write(axis, part):
        place = (pl.ds(part * share, share), pl.ds(axis * lines, lines))
        return pltpu.make_async_copy(
            found.at[place], out_ref.at[place], departures.at[axis, part]
        )

    for piece in pieces:
        for copy in reads(*piece):
            copy.start()
    for axis, part in pieces:
        for copy in reads(axis, part):
            copy.wait()
        span = slice(part * share * lines, (part + 1) * share * lines)
        place = cells[axis, span].astype(F32) + fracs[axis, span]
        found[part * share : (part + 1) * share, axis * lines : (axis + 1) * lines, :] = (
            place.reshape(share, lines, LANES)
        )
        write(axis, part).start()
    for piece in pieces:
        write(*piece).wait()


def positions(cells, fracs, owners):
    lines = cells.shape[1]
    shape = (owners, 3 * lines // owners, LANES)
    hbm = pl.BlockSpec(memory_space=pltpu.HBM)
    return pl.pallas_call(
        positions_kernel,
        out_shape=jax.ShapeDtypeStruct(shape, F32),
        in_specs=[hbm, hbm],
        out_specs=hbm,
        scratch_shapes=[
            pltpu.VMEM(cells.shape, jnp.int32),
            pltpu.VMEM(fracs.shape, F32),
            pltpu.VMEM(shape, F32),
            pltpu.SemaphoreType.DMA((3, 4, 2)),
            pltpu.SemaphoreType.DMA((3, 4)),
        ],
        compiler_params=params(60),
        cost_estimate=pl.CostEstimate(
            flops=3 * lines * LANES, bytes_accessed=36 * lines * LANES, transcendentals=0
        ),
        name="positions",
    )(cells, fracs)


def windows_kernel(
    where_ref, picks_ref, cube_ref, place_ref, out_ref, wide, tail, places, sums, arrival
):
    tile = where_ref[0]
    own_places = pltpu.make_async_copy(place_ref.at[tile], places, arrival)
    own_places.start()
    count = cube_ref.shape[0]
    plane = EDGE * EDGE
    wide[...] = jnp.zeros_like(wide)
    wide[:, :EDGE, :plane] = cube_ref[...]
    column = lax.broadcasted_iota(jnp.int32, (1, KDIM), 1)
    main = (column // MAIN) * EDGE + column % MAIN
    rest = column - 7 * MAIN
    last = (rest % 8) * EDGE + MAIN + rest // 8
    source = jnp.where(column < 7 * MAIN, main, last)
    unused = (column >= 7 * MAIN) & ((rest % 8 == 7) | (rest >= TAIL))
    source = jnp.where(unused, -(1 << 20), source)
    for window in range(WINDOWS):
        first = window * STRIDE * EDGE
        low = first // LANES * LANES
        length = min(3 * LANES, wide.shape[2] - low)
        place = lax.broadcasted_iota(jnp.int32, (length, KDIM), 0)
        pick = jnp.where(place == source + (first - low), 1.0, 0.0).astype(BF16)
        found = jnp.dot(
            wide[:, :, low : low + length].reshape(-1, length),
            pick,
            preferred_element_type=F32,
        )
        found = found.reshape(count, 48, KDIM)
        out_ref[:count, window * MAIN : (window + 1) * MAIN, :] = found[:, :MAIN, :].astype(BF16)
        tail[:, window : window + 1, :] = found[:, MAIN : MAIN + 1, :]
        tail[:, 8 + window : 9 + window, :] = found[:, MAIN + 1 : MAIN + 2, :]
    for row in (6, 7, 14, 15):
        tail[:, row : row + 1, :] = jnp.zeros((count, 1, KDIM), F32)
    out_ref[:count, WINDOWS * MAIN :, :] = tail[...].astype(BF16)

    own_places.wait()
    cap = picks_ref.shape[0]
    lines = places.shape[0] // 3
    part = lines // cap

    for piece in range(cap):
        brick = out_ref[picks_ref[piece, tile]]
        slot_sums(brick, places, sums, piece * part, part // 2)
    out_ref[count, : whole_tiles(lines), :LANES] = line_values(sums, lines, whole_tiles(lines))


def windows_of(where, picks, bricks, places):
    count = bricks.shape[0]
    cube = bricks.reshape(count, EDGE, EDGE * EDGE)
    rows = places.shape[1]
    return pl.pallas_call(
        windows_kernel,
        out_shape=jax.ShapeDtypeStruct((count + 1, BRICK_ROWS, KDIM), BF16),
        in_specs=[smem(), smem(), vmem(), pl.BlockSpec(memory_space=pl.ANY)],
        out_specs=vmem(),
        scratch_shapes=[
            pltpu.VMEM((count, 48, 10 * LANES), BF16),
            pltpu.VMEM((count, TAIL, KDIM), F32),
            pltpu.VMEM((rows, LANES), F32),
            pltpu.VMEM((8 * rows // 3, LANES), F32),
            pltpu.SemaphoreType.DMA,
        ],
        compiler_params=params(16),
        cost_estimate=pl.CostEstimate(
            flops=2 * count * 48 * 384 * KDIM * WINDOWS, bytes_accessed=4 * MIB,
            transcendentals=0,
        ),
        name="brick_windows",
    )(where, picks, cube, places)


def hat(distance):
    return jnp.maximum(1.0 - jnp.abs(distance), 0.0)


def blend(brick, px, py, pz):
    width = px.shape[1]
    eight = lax.broadcasted_iota(jnp.int32, (8, width), 0).astype(F32)
    places = lax.broadcasted_iota(jnp.int32, (MAIN, width), 0).astype(F32).astype(BF16)

    def tile(rows):
        return jnp.concatenate([rows, rows], axis=0).astype(BF16)

    cell_y = jnp.floor(py)
    frac_y = py - cell_y
    lower, low_share, high_share = tile(cell_y), tile(1.0 - frac_y), tile(frac_y)
    nothing = jnp.zeros((TAIL, width), BF16)
    weight_y = []
    for start in range(0, MAIN, TAIL):
        offset = places[start : start + TAIL] - lower
        weight_y.append(
            jnp.where(offset == 0, low_share, jnp.where(offset == 1, high_share, nothing))
        )
    window = jnp.floor(px * (1.0 / STRIDE))
    weight_x = hat(eight - (px - STRIDE * window))
    parts = []
    for i in range(STRIDE + 1):
        share = tile(jnp.broadcast_to(weight_x[i : i + 1], (8, width)))
        parts += [share * part for part in weight_y]
    tail = [weight_x * hat(MAIN - py), weight_x * jnp.maximum(py - MAIN, 0.0)]
    parts.append(jnp.concatenate(tail, axis=0).astype(BF16))
    plane = jnp.concatenate(parts, axis=0)
    found = jnp.dot(brick[:, : plane.shape[0]], plane, preferred_element_type=F32)
    groups = range(0, MAIN, 8)
    chosen = [found[row : row + 8] for row in groups]
    for other in range(1, WINDOWS):
        here = window == float(other)
        base = other * MAIN
        chosen = [
            jnp.where(here, found[base + row : base + row + 8], old)
            for row, old in zip(groups, chosen)
        ]
    base = WINDOWS * MAIN
    edges = found[base : base + 8] * hat(MAIN - pz)
    edges = edges + found[base + 8 :] * jnp.maximum(pz - MAIN, 0.0)
    total = jnp.where(eight == window, edges, 0.0)
    for row, part in zip(groups, chosen):
        total = total + part * hat((eight + float(row)) - pz)
    return total


def slot_sums(brick, places, sums, first, blocks):
    lines = places.shape[0] // 3
    for step in range(blocks):
        row = first + 2 * step

        def line(axis):
            both = [
                jnp.broadcast_to(places[pl.ds(axis * lines + row + half, 1), :], (8, LANES))
                for half in range(2)
            ]
            return jnp.concatenate(both, axis=1)

        total = blend(brick, line(0), line(1), line(2))
        for half in range(2):
            sums[pl.ds(pl.multiple_of(8 * (row + half), 8), 8), :] = total[
                :, half * LANES : (half + 1) * LANES
            ]


def whole_tiles(lines):
    return -(-lines // TAIL) * TAIL


def line_values(sums, lines, height):
    values = []
    for row in range(0, lines, 8):
        value = sums[pl.ds(8 * row, 8, stride=8), :]
        for other in range(1, 8):
            value = value + sums[pl.ds(8 * row + other, 8, stride=8), :]
        values.append(value)
    if height > lines:
        values.append(jnp.zeros((height - lines, LANES), F32))
    return jnp.concatenate(values, axis=0).astype(BF16)


def samples_kernel(
    where_ref, picks_ref, brick_ref, place_ref, out_ref, bricks, places, sums, own, arrivals,
    own_arrival,
):
    owners, rows, _ = place_ref.shape
    cap = picks_ref.shape[0]
    lines = rows // 3
    part = lines // cap
    turns = owners - 1
    tile = where_ref[0]
    pairs, rest = turns // 2, turns % 2
    own_values = pltpu.make_async_copy(
        brick_ref.at[brick_ref.shape[0] - 1, pl.ds(0, own.shape[0]), pl.ds(0, LANES)],
        own,
        own_arrival,
    )

    def renderer_of(number):
        return lax.rem(tile + 1 + number, owners)

    def fetches(turn, members):
        held = turn % 2
        copies = []
        for member in range(members):
            renderer = renderer_of(2 * turn + member)
            copies.append(
                pltpu.make_async_copy(
                    place_ref.at[renderer],
                    places.at[held, member],
                    arrivals.at[held, member, cap],
                )
            )
            for piece in range(cap):
                copies.append(
                    pltpu.make_async_copy(
                        brick_ref.at[picks_ref[piece, renderer]],
                        bricks.at[held, member, piece],
                        arrivals.at[held, member, piece],
                    )
                )
        return copies

    def start(turn, members):
        for copy in fetches(turn, members):
            copy.start()

    def work(turn, members):
        held = turn % 2
        for copy in fetches(turn, members):
            copy.wait()
        for member in range(members):
            for piece in range(cap):
                slot_sums(
                    bricks[held, member, piece],
                    places.at[held, member],
                    sums.at[member],
                    piece * part,
                    part // 2,
                )
        for member in range(members):
            out_ref[renderer_of(2 * turn + member)] = line_values(
                sums.at[member], lines, lines
            )

    def one_pair(turn, carry):
        work(turn, 2)

        @pl.when(turn + 2 < pairs)
        def _():
            start(turn + 2, 2)

        if rest:

            @pl.when(turn + 2 == pairs)
            def _():
                start(pairs, 1)

        return carry

    for turn in range(min(2, pairs)):
        start(turn, 2)
    if rest and pairs < 2:
        start(pairs, 1)
    own_values.start()
    lax.fori_loop(0, pairs, one_pair, 0)
    if rest:
        work(pairs, 1)
    own_values.wait()
    out_ref[tile] = own[...].astype(F32)[:lines].astype(BF16)


def sample_values(where, picks, windows, places):
    owners, rows, _ = places.shape
    cap = picks.shape[0]
    samples = owners * rows * LANES // 3
    some = pl.BlockSpec(memory_space=pl.ANY)
    return pl.pallas_call(
        samples_kernel,
        out_shape=jax.ShapeDtypeStruct((owners, rows // 3, LANES), BF16),
        in_specs=[smem(), smem(), some, some],
        out_specs=vmem(),
        scratch_shapes=[
            pltpu.VMEM((2, 2, cap, BRICK_ROWS, KDIM), BF16),
            pltpu.VMEM((2, 2, rows, LANES), F32),
            pltpu.VMEM((2, 8 * rows // 3, LANES), F32),
            pltpu.VMEM((whole_tiles(rows // 3), LANES), BF16),
            pltpu.SemaphoreType.DMA((2, 2, cap + 1)),
            pltpu.SemaphoreType.DMA,
        ],
        compiler_params=pltpu.CompilerParams(vmem_limit_bytes=61_600_000),
        cost_estimate=pl.CostEstimate(
            flops=2 * samples * KDIM * BRICK_ROWS, bytes_accessed=3 * MIB,
            transcendentals=0,
        ),
        name="sample_values",
    )(where, picks, windows, places)


def gbuffer_kernel(value_ref, order_ref, out_ref, values):
    values[...] = value_ref[...].astype(F32).reshape(values.shape)
    height = out_ref.shape[2]

    def ray_of(number):
        rows_now = slice(number * height, (number + 1) * height)
        first, second = (
            values[pl.ds(2 * number * height + half, height, stride=2), :] for half in range(2)
        )
        parts = []
        for half in range(2):
            order = order_ref[0, 0, rows_now, half * LANES : (half + 1) * LANES]
            inner = order & (LANES - 1)
            parts.append(
                jnp.where(
                    order < LANES,
                    jnp.take_along_axis(first, inner, axis=1, mode="promise_in_bounds"),
                    jnp.take_along_axis(second, inner, axis=1, mode="promise_in_bounds"),
                )
            )
        return jnp.concatenate(parts, axis=1)

    remain = 1.0
    shade = 0.0
    depth = 0.0
    for step in range(NSP):
        ray = ray_of(step)
        half_tanh = 0.5 * jnp.tanh(ray)
        weight = remain * (0.5 + half_tanh)
        shade = shade + weight * ray
        depth = depth + weight * ((step + 1) / NSP)
        remain = remain * (0.5 - half_tanh)
    occlusion = 0.0
    for ray_number in range(NRAY):
        passing = 1.0
        for step in range(NOS):
            ray = ray_of(NSP + ray_number * NOS + step)
            passing = passing * (0.5 - 0.5 * jnp.tanh(ray))
        occlusion = occlusion + passing
    out_ref[0, 0] = shade.astype(BF16)
    out_ref[0, 1] = (1.0 - remain).astype(BF16)
    out_ref[0, 2] = depth.astype(BF16)
    out_ref[0, 3] = (occlusion * (1.0 / NRAY)).astype(BF16)


def gbuffer(values, order, height, width):
    total = order.shape[2]
    return pl.pallas_call(
        gbuffer_kernel,
        out_shape=jax.ShapeDtypeStruct((1, 4, height, width), BF16),
        in_specs=[vmem(), vmem()],
        out_specs=vmem(),
        scratch_shapes=[pltpu.VMEM((2 * total, LANES), F32)],
        compiler_params=params(16),
        cost_estimate=pl.CostEstimate(
            flops=20 * total * BLOCK, bytes_accessed=8 * total * BLOCK, transcendentals=0
        ),
        name="gbuffer",
    )(values, order)


def silu(field):
    half = 0.5 * field
    return half + half * jnp.tanh(half)


def shifted(rows, steps):
    lane = lax.broadcasted_iota(jnp.int32, (1, LANES), 1)
    edge = lane == (0 if steps == 1 else LANES - 1)
    moved = []
    for row in rows:
        tiles = [row[:, i : i + LANES] for i in range(0, row.shape[1], LANES)]
        tiles = [pltpu.roll(tile, steps % LANES, 1) for tile in tiles]
        for i, tile in enumerate(tiles):
            source = i - steps
            fill = tiles[source] if 0 <= source < len(tiles) else 0.0
            moved.append(jnp.where(edge, fill, tile))
    return jnp.concatenate(moved, axis=1)


def across(total, chans, row_width):
    left, middle, right = (total[i * chans : (i + 1) * chans] for i in range(3))

    def rows_of(part):
        return [part[:, i : i + row_width] for i in range(0, part.shape[1], row_width)]

    return middle + shifted(rows_of(left), 1) + shifted(rows_of(right), -1)


def taps(weight_ref, tap):
    _, out_chans, chans = weight_ref.shape
    return weight_ref[3 * tap : 3 * tap + 3].reshape(3 * out_chans, chans)


def beside(weight_ref):
    return jnp.concatenate([taps(weight_ref, tap) for tap in range(3)], axis=1)


def sides(where_ref):
    above = jnp.where(where_ref[0] > 0, 1.0, 0.0)
    below = jnp.where(where_ref[0] < where_ref[1] - 1, 1.0, 0.0)

    def inside(row, low, high):
        return jnp.where(row < low, above, jnp.where(row >= high, below, 1.0))

    return inside


def turned(weight_ref):
    _, chans, out_chans = weight_ref.shape
    here = lax.broadcasted_iota(jnp.int32, (out_chans, out_chans), 0)
    there = lax.broadcasted_iota(jnp.int32, (out_chans, out_chans), 1)
    unit = jnp.where(here == there, 1.0, 0.0).astype(BF16)
    rows = []
    for column in range(3):
        stack = jnp.concatenate([weight_ref[3 * tap + column] for tap in range(3)], axis=0)
        rows.append(
            lax.dot_general(
                unit, stack, (((1,), (1,)), ((), ())), preferred_element_type=F32
            )
        )
    return jnp.concatenate(rows, axis=0).astype(BF16)


def stem_kernel(where_ref, x_ref, w_in, w_mid, second, first):
    height = x_ref.shape[0] // 3
    width = x_ref.shape[2]
    inside = sides(where_ref)

    def full_layer(weight, source, target, low, high, unroll):
        chans = target.shape[1]
        depth = weight.shape[1]

        def step(row, carry):
            lines = source[pl.ds(row, 3)].reshape(depth, width)
            line = across(jnp.dot(weight, lines, preferred_element_type=F32), chans, width)
            target[row] = (silu(line) * inside(row, low, high)).astype(BF16)
            return carry

        lax.fori_loop(0, target.shape[0], step, 0, unroll=unroll)

    full_layer(turned(w_in), x_ref, first, height - 1, 2 * height - 1, first.shape[0])
    full_layer(beside(w_mid), first, second, height - 2, 2 * height - 2, second.shape[0])


def half_pair(source, row, tap):
    return jnp.concatenate([source[row + tap], source[row + tap + 1]], axis=1)


def half_layer(product, target, inside, low, high):
    chans, half_width = target.shape[1], target.shape[2]
    for row in range(0, target.shape[0], 2):
        both = silu(across(product(row), chans, half_width))
        for now in range(2):
            line = both[:, now * half_width : (now + 1) * half_width]
            if row + now < low or row + now >= high:
                line = line * inside(row + now, low, high)
            target[row + now] = line.astype(BF16)


def middle_kernel(where_ref, second, w_down, third, pooled):
    count, chans, width = second.shape
    half_height = (count + 4) // 6
    half_width = width // 2
    inside = sides(where_ref)
    place = lax.broadcasted_iota(jnp.int32, (width, half_width), 0) // 2
    target = lax.broadcasted_iota(jnp.int32, (width, half_width), 1)
    shrink = jnp.where(place == target, 0.25, 0.0).astype(BF16)
    pairs = jnp.dot(
        second[...].reshape(count * chans, width), shrink, preferred_element_type=F32
    ).reshape(count // 2, 2, chans, half_width)
    pooled[...] = (pairs[:, 0] + pairs[:, 1]).astype(BF16)
    weight_down = turned(w_down)

    def down_product(row):
        lines = jnp.concatenate([half_pair(pooled, row, tap) for tap in range(3)], axis=0)
        return jnp.dot(weight_down, lines, preferred_element_type=F32)

    half_layer(down_product, third, inside, half_height - 2, 2 * half_height - 2)


def decoder_kernel(
    where_ref, second, third, w_deep, w_up, w_out, out_ref, fourth, joined, fifth, final
):
    height = out_ref.shape[2]
    half_height = height // 2
    width = out_ref.shape[3]
    half_width = width // 2
    chans = second.shape[1]
    inside = sides(where_ref)

    def deep_product(row):
        total = None
        for tap in range(3):
            part = jnp.dot(
                taps(w_deep, tap), half_pair(third, row, tap), preferred_element_type=F32
            )
            total = part if total is None else total + part
        return total

    half_layer(deep_product, fourth, inside, half_height - 3, 2 * half_height - 3)
    place = lax.broadcasted_iota(jnp.int32, (half_width, width), 0)
    target = lax.broadcasted_iota(jnp.int32, (half_width, width), 1) // 2
    spread = jnp.where(place == target, 1.0, 0.0).astype(BF16)
    deep = fourth.shape[1]
    wide = jnp.dot(
        fourth[...].reshape(-1, half_width), spread, preferred_element_type=F32
    ).astype(BF16).reshape(fourth.shape[0], deep, width)
    for row in range(2 * fourth.shape[0]):
        joined[row, chans:, :] = wide[row // 2]
        joined[row, :chans, :] = second[row + 4]

    def up_step(row, carry):
        total = None
        for tap in range(3):
            part = jnp.dot(taps(w_up, tap), joined[row + tap], preferred_element_type=F32)
            total = part if total is None else total + part
        line = silu(across(total, chans, width))
        fifth[row] = (line * inside(row, 1, height + 1)).astype(BF16)
        return carry

    lax.fori_loop(0, fifth.shape[0], up_step, 0, unroll=fifth.shape[0])

    colours = out_ref.shape[1]
    weight_out = beside(w_out)
    for row in range(height):
        lines = fifth[row : row + 3].reshape(3 * chans, width)
        total = jnp.dot(weight_out, lines, preferred_element_type=F32)
        line = across(total, w_out.shape[1], width)
        for colour in range(colours):
            final[colour, row : row + 1, :] = line[colour : colour + 1, :]
    out_ref[0] = final[...].astype(BF16)


def stem(where, field, w_in, w_mid):
    height = field.shape[0] // 3
    width = field.shape[2]
    one = w_mid.shape[1]
    return pl.pallas_call(
        stem_kernel,
        out_shape=jax.ShapeDtypeStruct((3 * height - 4, one, width), BF16),
        in_specs=[smem()] + [vmem()] * 3,
        out_specs=vmem(),
        scratch_shapes=[pltpu.VMEM((3 * height - 2, one, width), BF16)],
        compiler_params=params(16),
        cost_estimate=pl.CostEstimate(
            flops=1_000_000_000, bytes_accessed=MIB, transcendentals=300_000
        ),
        name="stem",
    )(where, field, w_in, w_mid)


def middle(where, second, w_down):
    rows, one, width = second.shape
    half = (rows + 4) // 6
    two = w_down.shape[2]
    return pl.pallas_call(
        middle_kernel,
        out_shape=jax.ShapeDtypeStruct((3 * half - 4, two, width // 2), BF16),
        in_specs=[smem()] + [vmem()] * 2,
        out_specs=vmem(),
        scratch_shapes=[pltpu.VMEM((3 * half - 2, one, width // 2), BF16)],
        compiler_params=params(16),
        cost_estimate=pl.CostEstimate(
            flops=500_000_000, bytes_accessed=MIB, transcendentals=100_000
        ),
        name="middle",
    )(where, second, w_down)


def decoder(where, second, third, w_deep, w_up, w_out, height, colours):
    one = second.shape[1]
    two = third.shape[1]
    width = second.shape[2]
    return pl.pallas_call(
        decoder_kernel,
        out_shape=jax.ShapeDtypeStruct((1, colours, height, width), BF16),
        in_specs=[smem()] + [vmem()] * 5,
        out_specs=vmem(),
        scratch_shapes=[
            pltpu.VMEM((third.shape[0] - 2, two, width // 2), BF16),
            pltpu.VMEM((height + 4, one + two, width), BF16),
            pltpu.VMEM((height + 2, one, width), BF16),
            pltpu.VMEM((colours, height, width), F32),
        ],
        compiler_params=params(16),
        cost_estimate=pl.CostEstimate(
            flops=1_500_000_000, bytes_accessed=MIB, transcendentals=200_000
        ),
        name="decoder",
    )(where, second, third, w_deep, w_up, w_out)


def on_device(
    bricks, sends, cells, fracs, sample_order, pending, w_in, w_mid, w_down, w_deep, w_up, w_out
):
    n_tile = lax.axis_size("tile")
    tile = lax.axis_index("tile")
    n_section = lax.axis_size("section")
    cap = sends.shape[3]
    height = pending.shape[2]
    width = pending.shape[3]
    samples = cells.shape[3]
    slots = n_tile * cap
    per_slot = samples // slots
    padded = -(-per_slot // BLOCK) * BLOCK

    def fill(part):
        if padded != per_slot:
            part = part.reshape(3, slots, per_slot)
            part = jnp.pad(part, ((0, 0), (0, 0), (0, padded - per_slot)))
        return part.reshape(3, slots * padded // LANES, LANES)

    def trim(found):
        if padded == per_slot:
            return found
        return found.reshape(slots, padded)[:, :per_slot].reshape(1, samples // LANES, LANES)

    places = positions(fill(cells), fill(fracs), n_tile)
    places, bricks, pending = lax.optimization_barrier((places, bricks, pending))
    arrived = lax.all_to_all(places, "tile", split_axis=0, concat_axis=0, tiled=True)

    mates = [(i, i ^ 1) for i in range(n_tile) if i ^ 1 < n_tile]
    across_chips = [
        pair for i in range(1, n_tile - 1, 2) for pair in ((i, i + 1), (i + 1, i))
    ]
    near = lax.ppermute(pending, "tile", mates)
    far = lax.ppermute(pending, "tile", across_chips)
    where = jnp.stack([tile, jnp.int32(n_tile)]).astype(jnp.int32)
    picks = sends[0, 0].T
    colours = w_out.shape[1]
    w_in = w_in.transpose(0, 2, 1)
    w_in = jnp.pad(w_in, ((0, 0), (0, 16 - w_in.shape[1]), (0, 0)))
    w_out = jnp.pad(w_out, ((0, 0), (0, 16 - colours), (0, 0)))
    windows = windows_of(where, picks, bricks, places)
    arrived, w_in, w_out = lax.optimization_barrier((arrived, w_in, w_out))
    found = sample_values(where, picks, windows, arrived)

    found, near, far, pending = lax.optimization_barrier((found, near, far, pending))
    values = lax.all_to_all(found, "tile", split_axis=0, concat_axis=0, tiled=True)
    first_core = tile % 2 == 0
    over = jnp.where(first_core, far, near)
    under = jnp.where(first_core, near, far)
    field = jnp.concatenate([over[0], pending[0], under[0]], axis=1).transpose(1, 0, 2)
    field = jnp.pad(field, ((0, 0), (0, 16 - field.shape[1]), (0, 0)))
    second = stem(where, field, w_in, w_mid)
    third = middle(where, second, w_down.transpose(0, 2, 1))
    values, third = lax.optimization_barrier((values, third))
    rendered = gbuffer(trim(values), sample_order, height, width)
    rendered, third = lax.optimization_barrier((rendered, third))
    ring = [(i, (i + 1) % n_section) for i in range(n_section)]
    handoff = lax.ppermute(rendered, "section", ring)
    denoised = decoder(where, second, third, w_deep, w_up, w_out, height, colours)
    return (handoff, denoised)


def solution(mesh):
    in_specs = (
        P("tile", None),
        P("section", "tile", None, None),
        P("section", "tile", None, None),
        P("section", "tile", None, None),
        P("section", "tile", None, None),
        P("section", None, "tile", None),
        P(),
        P(),
        P(),
        P(),
        P(),
        P(),
    )
    out_specs = (P("section", None, "tile", None), P("section", None, "tile", None))
    return jax.shard_map(
        on_device, mesh=mesh, in_specs=in_specs, out_specs=out_specs, check_vma=False
    )
```

```python
import functools

import jax
import jax.numpy as jnp
from jax import lax
from jax.experimental import pallas as pl
from jax.experimental.pallas import tpu as pltpu
from jax.sharding import PartitionSpec as P

EDGE = 34
NSP = 4
NRAY = 8
NOS = 2
LANES = 128
BLOCK = 256
STRIDE = 6
WINDOWS = 6
MAIN = 32
TAIL = 16
BRICK_ROWS = WINDOWS * MAIN + TAIL
KDIM = 256

F32 = jnp.float32
BF16 = jnp.bfloat16
MIB = 1024 * 1024


def params(mib):
    return pltpu.CompilerParams(vmem_limit_bytes=mib * MIB)


def vmem():
    return pl.BlockSpec(memory_space=pltpu.VMEM)


def smem():
    return pl.BlockSpec(memory_space=pltpu.SMEM)


def positions_kernel(
    where_ref, cells_ref, fracs_ref, out_ref, mate_ref,
    cells, fracs, found, arrivals, departures, mate_departure,
):
    owners, rows, _ = out_ref.shape
    lines = rows // 3
    parts = arrivals.shape[1]
    share = owners // parts
    pieces = [(axis, part) for axis in range(3) for part in range(parts)]

    def reads(axis, part):
        span = pl.ds(part * share * lines, share * lines)
        return [
            pltpu.make_async_copy(
                source.at[axis, span], target.at[axis, span], arrivals.at[axis, part, number]
            )
            for number, (source, target) in enumerate(((cells_ref, cells), (fracs_ref, fracs)))
        ]

    def write(axis, part):
        place = (pl.ds(part * share, share), pl.ds(axis * lines, lines))
        return pltpu.make_async_copy(
            found.at[place], out_ref.at[place], departures.at[axis, part]
        )

    for piece in pieces:
        for copy in reads(*piece):
            copy.start()
    for axis, part in pieces:
        for copy in reads(axis, part):
            copy.wait()
        span = slice(part * share * lines, (part + 1) * share * lines)
        place = cells[axis, span].astype(F32) + fracs[axis, span]
        found[part * share : (part + 1) * share, axis * lines : (axis + 1) * lines, :] = (
            place.reshape(share, lines, LANES)
        )
        write(axis, part).start()
    for_mate = pltpu.make_async_copy(
        found.at[mate_of(where_ref[0])], mate_ref.at[0], mate_departure
    )
    for_mate.start()
    for piece in pieces:
        write(*piece).wait()
    for_mate.wait()


def mate_of(tile):
    return tile + 1 - 2 * lax.rem(tile, 2)


def positions(where, cells, fracs, owners):
    lines = cells.shape[1]
    shape = (owners, 3 * lines // owners, LANES)
    hbm = pl.BlockSpec(memory_space=pltpu.HBM)
    return pl.pallas_call(
        positions_kernel,
        out_shape=(
            jax.ShapeDtypeStruct(shape, F32),
            jax.ShapeDtypeStruct((1,) + shape[1:], F32),
        ),
        in_specs=[smem(), hbm, hbm],
        out_specs=(hbm, hbm),
        scratch_shapes=[
            pltpu.VMEM(cells.shape, jnp.int32),
            pltpu.VMEM(fracs.shape, F32),
            pltpu.VMEM(shape, F32),
            pltpu.SemaphoreType.DMA((3, 4, 2)),
            pltpu.SemaphoreType.DMA((3, 4)),
            pltpu.SemaphoreType.DMA,
        ],
        compiler_params=params(60),
        cost_estimate=pl.CostEstimate(
            flops=3 * lines * LANES, bytes_accessed=36 * lines * LANES, transcendentals=0
        ),
        name="positions",
    )(where, cells, fracs)


def windows_kernel(
    where_ref, picks_ref, cube_ref, place_ref, mate_place_ref, out_ref,
    wide, tail, places, sums, arrivals,
):
    tile = where_ref[0]
    near = ((tile, place_ref.at[tile]), (mate_of(tile), mate_place_ref.at[0]))
    copies = [
        pltpu.make_async_copy(source, places.at[i], arrivals.at[i])
        for i, (_, source) in enumerate(near)
    ]
    for copy in copies:
        copy.start()
    count = cube_ref.shape[0]
    plane = EDGE * EDGE
    wide[...] = jnp.zeros_like(wide)
    wide[:, :EDGE, :plane] = cube_ref[...]
    column = lax.broadcasted_iota(jnp.int32, (1, KDIM), 1)
    main = (column // MAIN) * EDGE + column % MAIN
    rest = column - 7 * MAIN
    last = (rest % 8) * EDGE + MAIN + rest // 8
    source = jnp.where(column < 7 * MAIN, main, last)
    unused = (column >= 7 * MAIN) & ((rest % 8 == 7) | (rest >= TAIL))
    source = jnp.where(unused, -(1 << 20), source)
    for window in range(WINDOWS):
        first = window * STRIDE * EDGE
        low = first // LANES * LANES
        length = min(3 * LANES, wide.shape[2] - low)
        place = lax.broadcasted_iota(jnp.int32, (length, KDIM), 0)
        pick = jnp.where(place == source + (first - low), 1.0, 0.0).astype(BF16)
        found = jnp.dot(
            wide[:, :, low : low + length].reshape(-1, length),
            pick,
            preferred_element_type=F32,
        )
        found = found.reshape(count, 48, KDIM)
        out_ref[:count, window * MAIN : (window + 1) * MAIN, :] = found[:, :MAIN, :].astype(BF16)
        tail[:, window : window + 1, :] = found[:, MAIN : MAIN + 1, :]
        tail[:, 8 + window : 9 + window, :] = found[:, MAIN + 1 : MAIN + 2, :]
    for row in (6, 7, 14, 15):
        tail[:, row : row + 1, :] = jnp.zeros((count, 1, KDIM), F32)
    out_ref[:count, WINDOWS * MAIN :, :] = tail[...].astype(BF16)

    for copy in copies:
        copy.wait()
    cap = picks_ref.shape[0]
    lines = places.shape[1] // 3
    part = lines // cap
    height = whole_tiles(lines)
    for i, (renderer, _) in enumerate(near):
        for piece in range(cap):
            brick = out_ref[picks_ref[piece, renderer]]
            slot_sums(brick, places.at[i], sums.at[i], piece * part, part // 2)
    for i in range(len(near)):
        out_ref[count, i * height : (i + 1) * height, :LANES] = line_values(
            sums.at[i], lines, height
        )


def windows_of(where, picks, bricks, places, mate_places):
    count = bricks.shape[0]
    cube = bricks.reshape(count, EDGE, EDGE * EDGE)
    rows = places.shape[1]
    return pl.pallas_call(
        windows_kernel,
        out_shape=jax.ShapeDtypeStruct((count + 1, BRICK_ROWS, KDIM), BF16),
        in_specs=[smem(), smem(), vmem()] + [pl.BlockSpec(memory_space=pl.ANY)] * 2,
        out_specs=vmem(),
        scratch_shapes=[
            pltpu.VMEM((count, 48, 10 * LANES), BF16),
            pltpu.VMEM((count, TAIL, KDIM), F32),
            pltpu.VMEM((2, rows, LANES), F32),
            pltpu.VMEM((2, 8 * rows // 3, LANES), F32),
            pltpu.SemaphoreType.DMA((2,)),
        ],
        compiler_params=params(16),
        cost_estimate=pl.CostEstimate(
            flops=2 * count * 48 * 384 * KDIM * WINDOWS, bytes_accessed=4 * MIB,
            transcendentals=0,
        ),
        name="brick_windows",
    )(where, picks, cube, places, mate_places)


def hat(distance):
    return jnp.maximum(1.0 - jnp.abs(distance), 0.0)


def blend(brick, px, py, pz):
    width = px.shape[1]
    eight = lax.broadcasted_iota(jnp.int32, (8, width), 0).astype(F32)
    places = lax.broadcasted_iota(jnp.int32, (MAIN, width), 0).astype(F32).astype(BF16)

    def tile(rows):
        return jnp.concatenate([rows, rows], axis=0).astype(BF16)

    cell_y = jnp.floor(py)
    frac_y = py - cell_y
    lower, low_share, high_share = tile(cell_y), tile(1.0 - frac_y), tile(frac_y)
    nothing = jnp.zeros((TAIL, width), BF16)
    weight_y = []
    for start in range(0, MAIN, TAIL):
        offset = places[start : start + TAIL] - lower
        weight_y.append(
            jnp.where(offset == 0, low_share, jnp.where(offset == 1, high_share, nothing))
        )
    window = jnp.floor(px * (1.0 / STRIDE))
    weight_x = hat(eight - (px - STRIDE * window))
    parts = []
    for i in range(STRIDE + 1):
        share = tile(jnp.broadcast_to(weight_x[i : i + 1], (8, width)))
        parts += [share * part for part in weight_y]
    tail = [weight_x * hat(MAIN - py), weight_x * jnp.maximum(py - MAIN, 0.0)]
    parts.append(jnp.concatenate(tail, axis=0).astype(BF16))
    plane = jnp.concatenate(parts, axis=0)
    found = jnp.dot(brick[:, : plane.shape[0]], plane, preferred_element_type=F32)
    groups = range(0, MAIN, 8)
    chosen = [found[row : row + 8] for row in groups]
    for other in range(1, WINDOWS):
        here = window == float(other)
        base = other * MAIN
        chosen = [
            jnp.where(here, found[base + row : base + row + 8], old)
            for row, old in zip(groups, chosen)
        ]
    base = WINDOWS * MAIN
    edges = found[base : base + 8] * hat(MAIN - pz)
    edges = edges + found[base + 8 :] * jnp.maximum(pz - MAIN, 0.0)
    total = jnp.where(eight == window, edges, 0.0)
    for row, part in zip(groups, chosen):
        total = total + part * hat((eight + float(row)) - pz)
    return total


def slot_sums(brick, places, sums, first, blocks):
    lines = places.shape[0] // 3
    for step in range(blocks):
        row = first + 2 * step

        def line(axis):
            both = [
                jnp.broadcast_to(places[pl.ds(axis * lines + row + half, 1), :], (8, LANES))
                for half in range(2)
            ]
            return jnp.concatenate(both, axis=1)

        total = blend(brick, line(0), line(1), line(2))
        for half in range(2):
            sums[pl.ds(pl.multiple_of(8 * (row + half), 8), 8), :] = total[
                :, half * LANES : (half + 1) * LANES
            ]


def whole_tiles(lines):
    return -(-lines // TAIL) * TAIL


def line_values(sums, lines, height):
    values = []
    for row in range(0, lines, 8):
        value = sums[pl.ds(8 * row, 8, stride=8), :]
        for other in range(1, 8):
            value = value + sums[pl.ds(8 * row + other, 8, stride=8), :]
        values.append(value)
    if height > lines:
        values.append(jnp.zeros((height - lines, LANES), F32))
    return jnp.concatenate(values, axis=0).astype(BF16)


def samples_kernel(
    where_ref, picks_ref, brick_ref, place_ref, out_ref, bricks, places, sums, own, arrivals,
    own_arrival,
):
    owners, rows, _ = place_ref.shape
    cap = picks_ref.shape[0]
    lines = rows // 3
    part = lines // cap
    turns = owners - 2
    tile = where_ref[0]
    pairs, rest = turns // 2, turns % 2
    own_values = pltpu.make_async_copy(
        brick_ref.at[brick_ref.shape[0] - 1, pl.ds(0, own.shape[0]), pl.ds(0, LANES)],
        own,
        own_arrival,
    )

    def renderer_of(number):
        return lax.rem(2 * (tile // 2) + 2 + number, owners)

    def fetches(turn, members):
        held = turn % 2
        copies = []
        for member in range(members):
            renderer = renderer_of(2 * turn + member)
            copies.append(
                pltpu.make_async_copy(
                    place_ref.at[renderer],
                    places.at[held, member],
                    arrivals.at[held, member, cap],
                )
            )
            for piece in range(cap):
                copies.append(
                    pltpu.make_async_copy(
                        brick_ref.at[picks_ref[piece, renderer]],
                        bricks.at[held, member, piece],
                        arrivals.at[held, member, piece],
                    )
                )
        return copies

    def start(turn, members):
        for copy in fetches(turn, members):
            copy.start()

    def work(turn, members):
        held = turn % 2
        for copy in fetches(turn, members):
            copy.wait()
        for member in range(members):
            for piece in range(cap):
                slot_sums(
                    bricks[held, member, piece],
                    places.at[held, member],
                    sums.at[member],
                    piece * part,
                    part // 2,
                )
        for member in range(members):
            out_ref[renderer_of(2 * turn + member)] = line_values(
                sums.at[member], lines, lines
            )

    def one_pair(turn, carry):
        work(turn, 2)

        @pl.when(turn + 2 < pairs)
        def _():
            start(turn + 2, 2)

        if rest:

            @pl.when(turn + 2 == pairs)
            def _():
                start(pairs, 1)

        return carry

    for turn in range(min(2, pairs)):
        start(turn, 2)
    if rest and pairs < 2:
        start(pairs, 1)
    own_values.start()
    lax.fori_loop(0, pairs, one_pair, 0)
    if rest:
        work(pairs, 1)
    own_values.wait()
    height = whole_tiles(lines)
    for i, renderer in enumerate((tile, mate_of(tile))):
        values = own[i * height : (i + 1) * height, :].astype(F32)
        out_ref[renderer] = values[:lines].astype(BF16)


def sample_values(where, picks, windows, places):
    owners, rows, _ = places.shape
    cap = picks.shape[0]
    samples = owners * rows * LANES // 3
    some = pl.BlockSpec(memory_space=pl.ANY)
    return pl.pallas_call(
        samples_kernel,
        out_shape=jax.ShapeDtypeStruct((owners, rows // 3, LANES), BF16),
        in_specs=[smem(), smem(), some, some],
        out_specs=vmem(),
        scratch_shapes=[
            pltpu.VMEM((2, 2, cap, BRICK_ROWS, KDIM), BF16),
            pltpu.VMEM((2, 2, rows, LANES), F32),
            pltpu.VMEM((2, 8 * rows // 3, LANES), F32),
            pltpu.VMEM((2 * whole_tiles(rows // 3), LANES), BF16),
            pltpu.SemaphoreType.DMA((2, 2, cap + 1)),
            pltpu.SemaphoreType.DMA,
        ],
        compiler_params=pltpu.CompilerParams(vmem_limit_bytes=61_600_000),
        cost_estimate=pl.CostEstimate(
            flops=2 * samples * KDIM * BRICK_ROWS, bytes_accessed=3 * MIB,
            transcendentals=0,
        ),
        name="sample_values",
    )(where, picks, windows, places)


def gbuffer_kernel(*refs):
    *parts, order_ref, out_ref, values = refs
    if len(parts) == 1:
        values[...] = parts[0][...].astype(F32).reshape(values.shape)
    else:
        where_ref, chips_ref, others_ref = parts
        chips, lines, _ = others_ref.shape
        core = lax.rem(where_ref[0], 2)
        for chip in range(chips):
            for straight in range(2):
                owner = 2 * chip + (core if straight else 1 - core)
                first = pl.multiple_of(owner * lines, 8)
                line = chips_ref[chip, core] if straight else others_ref[chip]
                values[pl.ds(first, lines), :] = line.astype(F32)
    height = out_ref.shape[2]

    def ray_of(number):
        rows_now = slice(number * height, (number + 1) * height)
        first, second = (
            values[pl.ds(2 * number * height + half, height, stride=2), :] for half in range(2)
        )
        parts = []
        for half in range(2):
            order = order_ref[0, 0, rows_now, half * LANES : (half + 1) * LANES]
            inner = order & (LANES - 1)
            parts.append(
                jnp.where(
                    order < LANES,
                    jnp.take_along_axis(first, inner, axis=1, mode="promise_in_bounds"),
                    jnp.take_along_axis(second, inner, axis=1, mode="promise_in_bounds"),
                )
            )
        return jnp.concatenate(parts, axis=1)

    remain = 1.0
    shade = 0.0
    depth = 0.0
    for step in range(NSP):
        ray = ray_of(step)
        half_tanh = 0.5 * jnp.tanh(ray)
        weight = remain * (0.5 + half_tanh)
        shade = shade + weight * ray
        depth = depth + weight * ((step + 1) / NSP)
        remain = remain * (0.5 - half_tanh)
    occlusion = 0.0
    for ray_number in range(NRAY):
        passing = 1.0
        for step in range(NOS):
            ray = ray_of(NSP + ray_number * NOS + step)
            passing = passing * (0.5 - 0.5 * jnp.tanh(ray))
        occlusion = occlusion + passing
    out_ref[0, 0] = shade.astype(BF16)
    out_ref[0, 1] = (1.0 - remain).astype(BF16)
    out_ref[0, 2] = depth.astype(BF16)
    out_ref[0, 3] = (occlusion * (1.0 / NRAY)).astype(BF16)


def gbuffer(parts, order, height, width):
    total = order.shape[2]
    return pl.pallas_call(
        gbuffer_kernel,
        out_shape=jax.ShapeDtypeStruct((1, 4, height, width), BF16),
        in_specs=[smem()] * (len(parts) == 3) + [vmem()] * min(len(parts), 2) + [vmem()],
        out_specs=vmem(),
        scratch_shapes=[pltpu.VMEM((2 * total, LANES), F32)],
        compiler_params=params(16),
        cost_estimate=pl.CostEstimate(
            flops=20 * total * BLOCK, bytes_accessed=8 * total * BLOCK, transcendentals=0
        ),
        name="gbuffer",
    )(*parts, order)


def silu(field):
    half = 0.5 * field
    return half + half * jnp.tanh(half)


def shifted(rows, steps):
    lane = lax.broadcasted_iota(jnp.int32, (1, LANES), 1)
    edge = lane == (0 if steps == 1 else LANES - 1)
    moved = []
    for row in rows:
        tiles = [row[:, i : i + LANES] for i in range(0, row.shape[1], LANES)]
        tiles = [pltpu.roll(tile, steps % LANES, 1) for tile in tiles]
        for i, tile in enumerate(tiles):
            source = i - steps
            fill = tiles[source] if 0 <= source < len(tiles) else 0.0
            moved.append(jnp.where(edge, fill, tile))
    return jnp.concatenate(moved, axis=1)


def across(total, chans, row_width):
    left, middle, right = (total[i * chans : (i + 1) * chans] for i in range(3))

    def rows_of(part):
        return [part[:, i : i + row_width] for i in range(0, part.shape[1], row_width)]

    return middle + shifted(rows_of(left), 1) + shifted(rows_of(right), -1)


def taps(weight_ref, tap):
    _, out_chans, chans = weight_ref.shape
    return weight_ref[3 * tap : 3 * tap + 3].reshape(3 * out_chans, chans)


def beside(weight_ref):
    return jnp.concatenate([taps(weight_ref, tap) for tap in range(3)], axis=1)


def sides(where_ref):
    above = jnp.where(where_ref[0] > 0, 1.0, 0.0)
    below = jnp.where(where_ref[0] < where_ref[1] - 1, 1.0, 0.0)

    def inside(row, low, high):
        return jnp.where(row < low, above, jnp.where(row >= high, below, 1.0))

    return inside


def turned(weight_ref):
    _, chans, out_chans = weight_ref.shape
    here = lax.broadcasted_iota(jnp.int32, (out_chans, out_chans), 0)
    there = lax.broadcasted_iota(jnp.int32, (out_chans, out_chans), 1)
    unit = jnp.where(here == there, 1.0, 0.0).astype(BF16)
    rows = []
    for column in range(3):
        stack = jnp.concatenate([weight_ref[3 * tap + column] for tap in range(3)], axis=0)
        rows.append(
            lax.dot_general(
                unit, stack, (((1,), (1,)), ((), ())), preferred_element_type=F32
            )
        )
    return jnp.concatenate(rows, axis=0).astype(BF16)


def stem_kernel(where_ref, x_ref, w_in, w_mid, second, first):
    height = x_ref.shape[0] // 3
    width = x_ref.shape[2]
    inside = sides(where_ref)

    def full_layer(weight, source, target, low, high, unroll):
        chans = target.shape[1]
        depth = weight.shape[1]

        def step(row, carry):
            lines = source[pl.ds(row, 3)].reshape(depth, width)
            line = across(jnp.dot(weight, lines, preferred_element_type=F32), chans, width)
            target[row] = (silu(line) * inside(row, low, high)).astype(BF16)
            return carry

        lax.fori_loop(0, target.shape[0], step, 0, unroll=unroll)

    full_layer(turned(w_in), x_ref, first, height - 1, 2 * height - 1, first.shape[0])
    full_layer(beside(w_mid), first, second, height - 2, 2 * height - 2, second.shape[0])


def half_pair(source, row, tap):
    return jnp.concatenate([source[row + tap], source[row + tap + 1]], axis=1)


def half_layer(product, target, inside, low, high):
    chans, half_width = target.shape[1], target.shape[2]
    for row in range(0, target.shape[0], 2):
        both = silu(across(product(row), chans, half_width))
        for now in range(2):
            line = both[:, now * half_width : (now + 1) * half_width]
            if row + now < low or row + now >= high:
                line = line * inside(row + now, low, high)
            target[row + now] = line.astype(BF16)


def middle_kernel(where_ref, second, w_down, third, pooled):
    count, chans, width = second.shape
    half_height = (count + 4) // 6
    half_width = width // 2
    inside = sides(where_ref)
    place = lax.broadcasted_iota(jnp.int32, (width, half_width), 0) // 2
    target = lax.broadcasted_iota(jnp.int32, (width, half_width), 1)
    shrink = jnp.where(place == target, 0.25, 0.0).astype(BF16)
    pairs = jnp.dot(
        second[...].reshape(count * chans, width), shrink, preferred_element_type=F32
    ).reshape(count // 2, 2, chans, half_width)
    pooled[...] = (pairs[:, 0] + pairs[:, 1]).astype(BF16)
    weight_down = turned(w_down)

    def down_product(row):
        lines = jnp.concatenate([half_pair(pooled, row, tap) for tap in range(3)], axis=0)
        return jnp.dot(weight_down, lines, preferred_element_type=F32)

    half_layer(down_product, third, inside, half_height - 2, 2 * half_height - 2)


def decoder_kernel(
    where_ref, second, third, w_deep, w_up, w_out, out_ref, fourth, joined, fifth, final
):
    height = out_ref.shape[2]
    half_height = height // 2
    width = out_ref.shape[3]
    half_width = width // 2
    chans = second.shape[1]
    inside = sides(where_ref)

    def deep_product(row):
        total = None
        for tap in range(3):
            part = jnp.dot(
                taps(w_deep, tap), half_pair(third, row, tap), preferred_element_type=F32
            )
            total = part if total is None else total + part
        return total

    half_layer(deep_product, fourth, inside, half_height - 3, 2 * half_height - 3)
    place = lax.broadcasted_iota(jnp.int32, (half_width, width), 0)
    target = lax.broadcasted_iota(jnp.int32, (half_width, width), 1) // 2
    spread = jnp.where(place == target, 1.0, 0.0).astype(BF16)
    deep = fourth.shape[1]
    wide = jnp.dot(
        fourth[...].reshape(-1, half_width), spread, preferred_element_type=F32
    ).astype(BF16).reshape(fourth.shape[0], deep, width)
    for row in range(2 * fourth.shape[0]):
        joined[row, chans:, :] = wide[row // 2]
        joined[row, :chans, :] = second[row + 4]

    def up_step(row, carry):
        total = None
        for tap in range(3):
            part = jnp.dot(taps(w_up, tap), joined[row + tap], preferred_element_type=F32)
            total = part if total is None else total + part
        line = silu(across(total, chans, width))
        fifth[row] = (line * inside(row, 1, height + 1)).astype(BF16)
        return carry

    lax.fori_loop(0, fifth.shape[0], up_step, 0, unroll=fifth.shape[0])

    colours = out_ref.shape[1]
    weight_out = beside(w_out)
    for row in range(height):
        lines = fifth[row : row + 3].reshape(3 * chans, width)
        total = jnp.dot(weight_out, lines, preferred_element_type=F32)
        line = across(total, w_out.shape[1], width)
        for colour in range(colours):
            final[colour, row : row + 1, :] = line[colour : colour + 1, :]
    out_ref[0] = final[...].astype(BF16)


def stem(where, field, w_in, w_mid):
    height = field.shape[0] // 3
    width = field.shape[2]
    one = w_mid.shape[1]
    return pl.pallas_call(
        stem_kernel,
        out_shape=jax.ShapeDtypeStruct((3 * height - 4, one, width), BF16),
        in_specs=[smem()] + [vmem()] * 3,
        out_specs=vmem(),
        scratch_shapes=[pltpu.VMEM((3 * height - 2, one, width), BF16)],
        compiler_params=params(16),
        cost_estimate=pl.CostEstimate(
            flops=1_000_000_000, bytes_accessed=MIB, transcendentals=300_000
        ),
        name="stem",
    )(where, field, w_in, w_mid)


def middle(where, second, w_down):
    rows, one, width = second.shape
    half = (rows + 4) // 6
    two = w_down.shape[2]
    return pl.pallas_call(
        middle_kernel,
        out_shape=jax.ShapeDtypeStruct((3 * half - 4, two, width // 2), BF16),
        in_specs=[smem()] + [vmem()] * 2,
        out_specs=vmem(),
        scratch_shapes=[pltpu.VMEM((3 * half - 2, one, width // 2), BF16)],
        compiler_params=params(16),
        cost_estimate=pl.CostEstimate(
            flops=500_000_000, bytes_accessed=MIB, transcendentals=100_000
        ),
        name="middle",
    )(where, second, w_down)


def decoder(where, second, third, w_deep, w_up, w_out, height, colours):
    one = second.shape[1]
    two = third.shape[1]
    width = second.shape[2]
    return pl.pallas_call(
        decoder_kernel,
        out_shape=jax.ShapeDtypeStruct((1, colours, height, width), BF16),
        in_specs=[smem()] + [vmem()] * 5,
        out_specs=vmem(),
        scratch_shapes=[
            pltpu.VMEM((third.shape[0] - 2, two, width // 2), BF16),
            pltpu.VMEM((height + 4, one + two, width), BF16),
            pltpu.VMEM((height + 2, one, width), BF16),
            pltpu.VMEM((colours, height, width), F32),
        ],
        compiler_params=params(16),
        cost_estimate=pl.CostEstimate(
            flops=1_500_000_000, bytes_accessed=MIB, transcendentals=200_000
        ),
        name="decoder",
    )(where, second, third, w_deep, w_up, w_out)


def on_device(
    bricks, sends, cells, fracs, sample_order, pending, w_in, w_mid, w_down, w_deep, w_up, w_out
):
    n_tile = lax.axis_size("tile")
    tile = lax.axis_index("tile")
    n_section = lax.axis_size("section")
    cap = sends.shape[3]
    height = pending.shape[2]
    width = pending.shape[3]
    samples = cells.shape[3]
    slots = n_tile * cap
    per_slot = samples // slots
    padded = -(-per_slot // BLOCK) * BLOCK

    def fill(part):
        if padded != per_slot:
            part = part.reshape(3, slots, per_slot)
            part = jnp.pad(part, ((0, 0), (0, 0), (0, padded - per_slot)))
        return part.reshape(3, slots * padded // LANES, LANES)

    def trim(found):
        if padded == per_slot:
            return found
        return found.reshape(slots, padded)[:, :per_slot].reshape(1, samples // LANES, LANES)

    where = jnp.stack([tile, jnp.int32(n_tile)]).astype(jnp.int32)
    places, for_mate = positions(where, fill(cells), fill(fracs), n_tile)
    places, for_mate, bricks, pending = lax.optimization_barrier(
        (places, for_mate, bricks, pending)
    )
    arrived = lax.all_to_all(places, "tile", split_axis=0, concat_axis=0, tiled=True)

    mates = [(i, i ^ 1) for i in range(n_tile) if i ^ 1 < n_tile]
    across_chips = [
        pair for i in range(1, n_tile - 1, 2) for pair in ((i, i + 1), (i + 1, i))
    ]
    mate_places = lax.ppermute(for_mate, "tile", mates)
    near = lax.ppermute(pending, "tile", mates)
    far = lax.ppermute(pending, "tile", across_chips)
    picks = sends[0, 0].T
    colours = w_out.shape[1]
    w_in = w_in.transpose(0, 2, 1)
    w_in = jnp.pad(w_in, ((0, 0), (0, 16 - w_in.shape[1]), (0, 0)))
    w_out = jnp.pad(w_out, ((0, 0), (0, 16 - colours), (0, 0)))
    windows = windows_of(where, picks, bricks, places, mate_places)
    arrived, w_in, w_out = lax.optimization_barrier((arrived, w_in, w_out))
    found = sample_values(where, picks, windows, arrived)

    found, near, far, pending = lax.optimization_barrier((found, near, far, pending))
    same_core = [list(range(core, n_tile, 2)) for core in range(2)]
    chips = found.reshape((n_tile // 2, 2) + found.shape[1:])
    chips = lax.all_to_all(
        chips, "tile", split_axis=0, concat_axis=0, axis_index_groups=same_core, tiled=True
    )
    first_core = tile % 2 == 0
    over = jnp.where(first_core, far, near)
    under = jnp.where(first_core, near, far)
    field = jnp.concatenate([over[0], pending[0], under[0]], axis=1).transpose(1, 0, 2)
    field = jnp.pad(field, ((0, 0), (0, 16 - field.shape[1]), (0, 0)))
    second = stem(where, field, w_in, w_mid)
    third = middle(where, second, w_down.transpose(0, 2, 1))
    chips, third = lax.optimization_barrier((chips, third))
    core = tile % 2
    others = lax.dynamic_index_in_dim(chips, 1 - core, 1, keepdims=False)
    others = lax.ppermute(others, "tile", mates)
    if padded == per_slot:
        parts = (where, chips, others)
    else:
        mine = lax.dynamic_index_in_dim(chips, core, 1, keepdims=False)
        values = jnp.where(
            first_core, jnp.stack([mine, others], axis=1), jnp.stack([others, mine], axis=1)
        )
        parts = (trim(values.reshape(found.shape)),)
    rendered = gbuffer(parts, sample_order, height, width)
    rendered, third = lax.optimization_barrier((rendered, third))
    ring = [(i, (i + 1) % n_section) for i in range(n_section)]
    handoff = lax.ppermute(rendered, "section", ring)
    denoised = decoder(where, second, third, w_deep, w_up, w_out, height, colours)
    return (handoff, denoised)


def solution(mesh):
    in_specs = (
        P("tile", None),
        P("section", "tile", None, None),
        P("section", "tile", None, None),
        P("section", "tile", None, None),
        P("section", "tile", None, None),
        P("section", None, "tile", None),
        P(),
        P(),
        P(),
        P(),
        P(),
        P(),
    )
    out_specs = (P("section", None, "tile", None), P("section", None, "tile", None))
    return jax.shard_map(
        on_device, mesh=mesh, in_specs=in_specs, out_specs=out_specs, check_vma=False
    )
```

```python
import functools

import jax
import jax.numpy as jnp
from jax import lax
from jax.experimental import pallas as pl
from jax.experimental.pallas import tpu as pltpu
from jax.sharding import PartitionSpec as P

EDGE = 34
NSP = 4
NRAY = 8
NOS = 2
LANES = 128
BLOCK = 256
STRIDE = 6
WINDOWS = 6
MAIN = 32
TAIL = 16
BRICK_ROWS = WINDOWS * MAIN + TAIL
KDIM = 256

F32 = jnp.float32
BF16 = jnp.bfloat16
MIB = 1024 * 1024


def params(mib):
    return pltpu.CompilerParams(vmem_limit_bytes=mib * MIB)


def vmem():
    return pl.BlockSpec(memory_space=pltpu.VMEM)


def smem():
    return pl.BlockSpec(memory_space=pltpu.SMEM)


def positions_kernel(cells_ref, fracs_ref, out_ref, cells, fracs, found, arrivals, departures):
    owners, rows, _ = out_ref.shape
    lines = rows // 3
    parts = arrivals.shape[1]
    share = owners // parts
    pieces = [(axis, part) for axis in range(3) for part in range(parts)]

    def reads(axis, part):
        span = pl.ds(part * share * lines, share * lines)
        return [
            pltpu.make_async_copy(
                source.at[axis, span], target.at[axis, span], arrivals.at[axis, part, number]
            )
            for number, (source, target) in enumerate(((cells_ref, cells), (fracs_ref, fracs)))
        ]

    def write(axis, part):
        place = (pl.ds(part * share, share), pl.ds(axis * lines, lines))
        return pltpu.make_async_copy(
            found.at[place], out_ref.at[place], departures.at[axis, part]
        )

    for piece in pieces:
        for copy in reads(*piece):
            copy.start()
    for axis, part in pieces:
        for copy in reads(axis, part):
            copy.wait()
        span = slice(part * share * lines, (part + 1) * share * lines)
        place = cells[axis, span].astype(F32) + fracs[axis, span]
        found[part * share : (part + 1) * share, axis * lines : (axis + 1) * lines, :] = (
            place.reshape(share, lines, LANES)
        )
        write(axis, part).start()
    for piece in pieces:
        write(*piece).wait()


def positions(cells, fracs, owners):
    lines = cells.shape[1]
    shape = (owners, 3 * lines // owners, LANES)
    hbm = pl.BlockSpec(memory_space=pltpu.HBM)
    return pl.pallas_call(
        positions_kernel,
        out_shape=jax.ShapeDtypeStruct(shape, F32),
        in_specs=[hbm, hbm],
        out_specs=hbm,
        scratch_shapes=[
            pltpu.VMEM(cells.shape, jnp.int32),
            pltpu.VMEM(fracs.shape, F32),
            pltpu.VMEM(shape, F32),
            pltpu.SemaphoreType.DMA((3, 4, 2)),
            pltpu.SemaphoreType.DMA((3, 4)),
        ],
        compiler_params=params(60),
        cost_estimate=pl.CostEstimate(
            flops=3 * lines * LANES, bytes_accessed=36 * lines * LANES, transcendentals=0
        ),
        name="positions",
    )(cells, fracs)


def mate_of(tile):
    return tile + 1 - 2 * lax.rem(tile, 2)


def windows_kernel(
    where_ref, picks_ref, cube_ref, place_ref, mate_place_ref, out_ref,
    wide, tail, places, sums, arrivals,
):
    tile = where_ref[0]
    near = ((tile, place_ref.at[tile]), (mate_of(tile), mate_place_ref.at[0]))
    copies = [
        pltpu.make_async_copy(source, places.at[i], arrivals.at[i])
        for i, (_, source) in enumerate(near)
    ]
    for copy in copies:
        copy.start()
    count = cube_ref.shape[0]
    plane = EDGE * EDGE
    wide[...] = jnp.zeros_like(wide)
    wide[:, :EDGE, :plane] = cube_ref[...]
    column = lax.broadcasted_iota(jnp.int32, (1, KDIM), 1)
    main = (column // MAIN) * EDGE + column % MAIN
    rest = column - 7 * MAIN
    last = (rest % 8) * EDGE + MAIN + rest // 8
    source = jnp.where(column < 7 * MAIN, main, last)
    unused = (column >= 7 * MAIN) & ((rest % 8 == 7) | (rest >= TAIL))
    source = jnp.where(unused, -(1 << 20), source)
    for window in range(WINDOWS):
        first = window * STRIDE * EDGE
        low = first // LANES * LANES
        length = min(3 * LANES, wide.shape[2] - low)
        place = lax.broadcasted_iota(jnp.int32, (length, KDIM), 0)
        pick = jnp.where(place == source + (first - low), 1.0, 0.0).astype(BF16)
        found = jnp.dot(
            wide[:, :, low : low + length].reshape(-1, length),
            pick,
            preferred_element_type=F32,
        )
        found = found.reshape(count, 48, KDIM)
        out_ref[:count, window * MAIN : (window + 1) * MAIN, :] = found[:, :MAIN, :].astype(BF16)
        tail[:, window : window + 1, :] = found[:, MAIN : MAIN + 1, :]
        tail[:, 8 + window : 9 + window, :] = found[:, MAIN + 1 : MAIN + 2, :]
    for row in (6, 7, 14, 15):
        tail[:, row : row + 1, :] = jnp.zeros((count, 1, KDIM), F32)
    out_ref[:count, WINDOWS * MAIN :, :] = tail[...].astype(BF16)

    for copy in copies:
        copy.wait()
    cap = picks_ref.shape[0]
    lines = places.shape[1] // 3
    part = lines // cap
    height = whole_tiles(lines)
    for i, (renderer, _) in enumerate(near):
        for piece in range(cap):
            brick = out_ref[picks_ref[piece, renderer]]
            slot_sums(brick, places.at[i], sums.at[i], piece * part, part // 2)
    for i in range(len(near)):
        out_ref[count, i * height : (i + 1) * height, :LANES] = line_values(
            sums.at[i], lines, height
        )


def windows_of(where, picks, bricks, places, mate_places):
    count = bricks.shape[0]
    cube = bricks.reshape(count, EDGE, EDGE * EDGE)
    rows = places.shape[1]
    return pl.pallas_call(
        windows_kernel,
        out_shape=jax.ShapeDtypeStruct((count + 1, BRICK_ROWS, KDIM), BF16),
        in_specs=[smem(), smem(), vmem()] + [pl.BlockSpec(memory_space=pl.ANY)] * 2,
        out_specs=vmem(),
        scratch_shapes=[
            pltpu.VMEM((count, 48, 10 * LANES), BF16),
            pltpu.VMEM((count, TAIL, KDIM), F32),
            pltpu.VMEM((2, rows, LANES), F32),
            pltpu.VMEM((2, 8 * rows // 3, LANES), F32),
            pltpu.SemaphoreType.DMA((2,)),
        ],
        compiler_params=params(16),
        cost_estimate=pl.CostEstimate(
            flops=2 * count * 48 * 384 * KDIM * WINDOWS, bytes_accessed=4 * MIB,
            transcendentals=0,
        ),
        name="brick_windows",
    )(where, picks, cube, places, mate_places)


def hat(distance):
    return jnp.maximum(1.0 - jnp.abs(distance), 0.0)


def blend(brick, px, py, pz):
    width = px.shape[1]
    eight = lax.broadcasted_iota(jnp.int32, (8, width), 0).astype(F32)
    places = lax.broadcasted_iota(jnp.int32, (MAIN, width), 0).astype(F32).astype(BF16)

    def tile(rows):
        return jnp.concatenate([rows, rows], axis=0).astype(BF16)

    cell_y = jnp.floor(py)
    frac_y = py - cell_y
    lower, low_share, high_share = tile(cell_y), tile(1.0 - frac_y), tile(frac_y)
    nothing = jnp.zeros((TAIL, width), BF16)
    weight_y = []
    for start in range(0, MAIN, TAIL):
        offset = places[start : start + TAIL] - lower
        weight_y.append(
            jnp.where(offset == 0, low_share, jnp.where(offset == 1, high_share, nothing))
        )
    window = jnp.floor(px * (1.0 / STRIDE))
    weight_x = hat(eight - (px - STRIDE * window))
    parts = []
    for i in range(STRIDE + 1):
        share = tile(jnp.broadcast_to(weight_x[i : i + 1], (8, width)))
        parts += [share * part for part in weight_y]
    tail = [weight_x * hat(MAIN - py), weight_x * jnp.maximum(py - MAIN, 0.0)]
    parts.append(jnp.concatenate(tail, axis=0).astype(BF16))
    plane = jnp.concatenate(parts, axis=0)
    found = jnp.dot(brick[:, : plane.shape[0]], plane, preferred_element_type=F32)
    groups = range(0, MAIN, 8)
    chosen = [found[row : row + 8] for row in groups]
    for other in range(1, WINDOWS):
        here = window == float(other)
        base = other * MAIN
        chosen = [
            jnp.where(here, found[base + row : base + row + 8], old)
            for row, old in zip(groups, chosen)
        ]
    base = WINDOWS * MAIN
    edges = found[base : base + 8] * hat(MAIN - pz)
    edges = edges + found[base + 8 :] * jnp.maximum(pz - MAIN, 0.0)
    total = jnp.where(eight == window, edges, 0.0)
    for row, part in zip(groups, chosen):
        total = total + part * hat((eight + float(row)) - pz)
    return total


def slot_sums(brick, places, sums, first, blocks):
    lines = places.shape[0] // 3
    for step in range(blocks):
        row = first + 2 * step

        def line(axis):
            both = [
                jnp.broadcast_to(places[pl.ds(axis * lines + row + half, 1), :], (8, LANES))
                for half in range(2)
            ]
            return jnp.concatenate(both, axis=1)

        total = blend(brick, line(0), line(1), line(2))
        for half in range(2):
            sums[pl.ds(pl.multiple_of(8 * (row + half), 8), 8), :] = total[
                :, half * LANES : (half + 1) * LANES
            ]


def whole_tiles(lines):
    return -(-lines // TAIL) * TAIL


def line_values(sums, lines, height):
    values = []
    for row in range(0, lines, 8):
        value = sums[pl.ds(8 * row, 8, stride=8), :]
        for other in range(1, 8):
            value = value + sums[pl.ds(8 * row + other, 8, stride=8), :]
        values.append(value)
    if height > lines:
        values.append(jnp.zeros((height - lines, LANES), F32))
    return jnp.concatenate(values, axis=0).astype(BF16)


def samples_kernel(
    where_ref, picks_ref, brick_ref, place_ref, out_ref, bricks, places, sums, own, arrivals,
    own_arrival,
):
    owners, rows, _ = place_ref.shape
    cap = picks_ref.shape[0]
    lines = rows // 3
    part = lines // cap
    turns = owners - 2
    tile = where_ref[0]
    pairs, rest = turns // 2, turns % 2
    own_values = pltpu.make_async_copy(
        brick_ref.at[brick_ref.shape[0] - 1, pl.ds(0, own.shape[0]), pl.ds(0, LANES)],
        own,
        own_arrival,
    )

    def renderer_of(number):
        return lax.rem(2 * (tile // 2) + 2 + number, owners)

    def fetches(turn, members):
        held = turn % 2
        copies = []
        for member in range(members):
            renderer = renderer_of(2 * turn + member)
            copies.append(
                pltpu.make_async_copy(
                    place_ref.at[renderer],
                    places.at[held, member],
                    arrivals.at[held, member, cap],
                )
            )
            for piece in range(cap):
                copies.append(
                    pltpu.make_async_copy(
                        brick_ref.at[picks_ref[piece, renderer]],
                        bricks.at[held, member, piece],
                        arrivals.at[held, member, piece],
                    )
                )
        return copies

    def start(turn, members):
        for copy in fetches(turn, members):
            copy.start()

    def work(turn, members):
        held = turn % 2
        for copy in fetches(turn, members):
            copy.wait()
        for member in range(members):
            for piece in range(cap):
                slot_sums(
                    bricks[held, member, piece],
                    places.at[held, member],
                    sums.at[member],
                    piece * part,
                    part // 2,
                )
        for member in range(members):
            out_ref[renderer_of(2 * turn + member)] = line_values(
                sums.at[member], lines, lines
            )

    def one_pair(turn, carry):
        work(turn, 2)

        @pl.when(turn + 2 < pairs)
        def _():
            start(turn + 2, 2)

        if rest:

            @pl.when(turn + 2 == pairs)
            def _():
                start(pairs, 1)

        return carry

    for turn in range(min(2, pairs)):
        start(turn, 2)
    if rest and pairs < 2:
        start(pairs, 1)
    own_values.start()
    lax.fori_loop(0, pairs, one_pair, 0)
    if rest:
        work(pairs, 1)
    own_values.wait()
    height = whole_tiles(lines)
    for i, renderer in enumerate((tile, mate_of(tile))):
        values = own[i * height : (i + 1) * height, :].astype(F32)
        out_ref[renderer] = values[:lines].astype(BF16)


def sample_values(where, picks, windows, places):
    owners, rows, _ = places.shape
    cap = picks.shape[0]
    samples = owners * rows * LANES // 3
    some = pl.BlockSpec(memory_space=pl.ANY)
    return pl.pallas_call(
        samples_kernel,
        out_shape=jax.ShapeDtypeStruct((owners, rows // 3, LANES), BF16),
        in_specs=[smem(), smem(), some, some],
        out_specs=vmem(),
        scratch_shapes=[
            pltpu.VMEM((2, 2, cap, BRICK_ROWS, KDIM), BF16),
            pltpu.VMEM((2, 2, rows, LANES), F32),
            pltpu.VMEM((2, 8 * rows // 3, LANES), F32),
            pltpu.VMEM((2 * whole_tiles(rows // 3), LANES), BF16),
            pltpu.SemaphoreType.DMA((2, 2, cap + 1)),
            pltpu.SemaphoreType.DMA,
        ],
        compiler_params=pltpu.CompilerParams(vmem_limit_bytes=61_600_000),
        cost_estimate=pl.CostEstimate(
            flops=2 * samples * KDIM * BRICK_ROWS, bytes_accessed=3 * MIB,
            transcendentals=0,
        ),
        name="sample_values",
    )(where, picks, windows, places)


def gbuffer_kernel(value_ref, order_ref, out_ref, values):
    values[...] = value_ref[...].astype(F32).reshape(values.shape)
    height = out_ref.shape[2]

    def ray_of(number):
        rows_now = slice(number * height, (number + 1) * height)
        first, second = (
            values[pl.ds(2 * number * height + half, height, stride=2), :] for half in range(2)
        )
        parts = []
        for half in range(2):
            order = order_ref[0, 0, rows_now, half * LANES : (half + 1) * LANES]
            inner = order & (LANES - 1)
            parts.append(
                jnp.where(
                    order < LANES,
                    jnp.take_along_axis(first, inner, axis=1, mode="promise_in_bounds"),
                    jnp.take_along_axis(second, inner, axis=1, mode="promise_in_bounds"),
                )
            )
        return jnp.concatenate(parts, axis=1)

    remain = 1.0
    shade = 0.0
    depth = 0.0
    for step in range(NSP):
        ray = ray_of(step)
        half_tanh = 0.5 * jnp.tanh(ray)
        weight = remain * (0.5 + half_tanh)
        shade = shade + weight * ray
        depth = depth + weight * ((step + 1) / NSP)
        remain = remain * (0.5 - half_tanh)
    occlusion = 0.0
    for ray_number in range(NRAY):
        passing = 1.0
        for step in range(NOS):
            ray = ray_of(NSP + ray_number * NOS + step)
            passing = passing * (0.5 - 0.5 * jnp.tanh(ray))
        occlusion = occlusion + passing
    out_ref[0, 0] = shade.astype(BF16)
    out_ref[0, 1] = (1.0 - remain).astype(BF16)
    out_ref[0, 2] = depth.astype(BF16)
    out_ref[0, 3] = (occlusion * (1.0 / NRAY)).astype(BF16)


def gbuffer(values, order, height, width):
    total = order.shape[2]
    return pl.pallas_call(
        gbuffer_kernel,
        out_shape=jax.ShapeDtypeStruct((1, 4, height, width), BF16),
        in_specs=[vmem(), vmem()],
        out_specs=vmem(),
        scratch_shapes=[pltpu.VMEM((2 * total, LANES), F32)],
        compiler_params=params(16),
        cost_estimate=pl.CostEstimate(
            flops=20 * total * BLOCK, bytes_accessed=8 * total * BLOCK, transcendentals=0
        ),
        name="gbuffer",
    )(values, order)


def silu(field):
    half = 0.5 * field
    return half + half * jnp.tanh(half)


def shifted(rows, steps):
    lane = lax.broadcasted_iota(jnp.int32, (1, LANES), 1)
    edge = lane == (0 if steps == 1 else LANES - 1)
    moved = []
    for row in rows:
        tiles = [row[:, i : i + LANES] for i in range(0, row.shape[1], LANES)]
        tiles = [pltpu.roll(tile, steps % LANES, 1) for tile in tiles]
        for i, tile in enumerate(tiles):
            source = i - steps
            fill = tiles[source] if 0 <= source < len(tiles) else 0.0
            moved.append(jnp.where(edge, fill, tile))
    return jnp.concatenate(moved, axis=1)


def across(total, chans, row_width):
    left, middle, right = (total[i * chans : (i + 1) * chans] for i in range(3))

    def rows_of(part):
        return [part[:, i : i + row_width] for i in range(0, part.shape[1], row_width)]

    return middle + shifted(rows_of(left), 1) + shifted(rows_of(right), -1)


def taps(weight_ref, tap):
    _, out_chans, chans = weight_ref.shape
    return weight_ref[3 * tap : 3 * tap + 3].reshape(3 * out_chans, chans)


def beside(weight_ref):
    return jnp.concatenate([taps(weight_ref, tap) for tap in range(3)], axis=1)


def sides(where_ref):
    above = jnp.where(where_ref[0] > 0, 1.0, 0.0)
    below = jnp.where(where_ref[0] < where_ref[1] - 1, 1.0, 0.0)

    def inside(row, low, high):
        return jnp.where(row < low, above, jnp.where(row >= high, below, 1.0))

    return inside


def turned(weight_ref):
    _, chans, out_chans = weight_ref.shape
    here = lax.broadcasted_iota(jnp.int32, (out_chans, out_chans), 0)
    there = lax.broadcasted_iota(jnp.int32, (out_chans, out_chans), 1)
    unit = jnp.where(here == there, 1.0, 0.0).astype(BF16)
    rows = []
    for column in range(3):
        stack = jnp.concatenate([weight_ref[3 * tap + column] for tap in range(3)], axis=0)
        rows.append(
            lax.dot_general(
                unit, stack, (((1,), (1,)), ((), ())), preferred_element_type=F32
            )
        )
    return jnp.concatenate(rows, axis=0).astype(BF16)


def stem_kernel(where_ref, x_ref, w_in, w_mid, second, first):
    height = x_ref.shape[0] // 3
    width = x_ref.shape[2]
    inside = sides(where_ref)

    def full_layer(weight, source, target, low, high, unroll):
        chans = target.shape[1]
        depth = weight.shape[1]

        def step(row, carry):
            lines = source[pl.ds(row, 3)].reshape(depth, width)
            line = across(jnp.dot(weight, lines, preferred_element_type=F32), chans, width)
            target[row] = (silu(line) * inside(row, low, high)).astype(BF16)
            return carry

        lax.fori_loop(0, target.shape[0], step, 0, unroll=unroll)

    full_layer(turned(w_in), x_ref, first, height - 1, 2 * height - 1, first.shape[0])
    full_layer(beside(w_mid), first, second, height - 2, 2 * height - 2, second.shape[0])


def half_pair(source, row, tap):
    return jnp.concatenate([source[row + tap], source[row + tap + 1]], axis=1)


def half_layer(product, target, inside, low, high):
    chans, half_width = target.shape[1], target.shape[2]
    for row in range(0, target.shape[0], 2):
        both = silu(across(product(row), chans, half_width))
        for now in range(2):
            line = both[:, now * half_width : (now + 1) * half_width]
            if row + now < low or row + now >= high:
                line = line * inside(row + now, low, high)
            target[row + now] = line.astype(BF16)


def middle_kernel(where_ref, second, w_down, third, pooled):
    count, chans, width = second.shape
    half_height = (count + 4) // 6
    half_width = width // 2
    inside = sides(where_ref)
    place = lax.broadcasted_iota(jnp.int32, (width, half_width), 0) // 2
    target = lax.broadcasted_iota(jnp.int32, (width, half_width), 1)
    shrink = jnp.where(place == target, 0.25, 0.0).astype(BF16)
    pairs = jnp.dot(
        second[...].reshape(count * chans, width), shrink, preferred_element_type=F32
    ).reshape(count // 2, 2, chans, half_width)
    pooled[...] = (pairs[:, 0] + pairs[:, 1]).astype(BF16)
    weight_down = turned(w_down)

    def down_product(row):
        lines = jnp.concatenate([half_pair(pooled, row, tap) for tap in range(3)], axis=0)
        return jnp.dot(weight_down, lines, preferred_element_type=F32)

    half_layer(down_product, third, inside, half_height - 2, 2 * half_height - 2)


def decoder_kernel(
    where_ref, second, third, w_deep, w_up, w_out, out_ref, fourth, joined, fifth, final
):
    height = out_ref.shape[2]
    half_height = height // 2
    width = out_ref.shape[3]
    half_width = width // 2
    chans = second.shape[1]
    inside = sides(where_ref)

    def deep_product(row):
        total = None
        for tap in range(3):
            part = jnp.dot(
                taps(w_deep, tap), half_pair(third, row, tap), preferred_element_type=F32
            )
            total = part if total is None else total + part
        return total

    half_layer(deep_product, fourth, inside, half_height - 3, 2 * half_height - 3)
    place = lax.broadcasted_iota(jnp.int32, (half_width, width), 0)
    target = lax.broadcasted_iota(jnp.int32, (half_width, width), 1) // 2
    spread = jnp.where(place == target, 1.0, 0.0).astype(BF16)
    deep = fourth.shape[1]
    wide = jnp.dot(
        fourth[...].reshape(-1, half_width), spread, preferred_element_type=F32
    ).astype(BF16).reshape(fourth.shape[0], deep, width)
    for row in range(2 * fourth.shape[0]):
        joined[row, chans:, :] = wide[row // 2]
        joined[row, :chans, :] = second[row + 4]

    def up_step(row, carry):
        total = None
        for tap in range(3):
            part = jnp.dot(taps(w_up, tap), joined[row + tap], preferred_element_type=F32)
            total = part if total is None else total + part
        line = silu(across(total, chans, width))
        fifth[row] = (line * inside(row, 1, height + 1)).astype(BF16)
        return carry

    lax.fori_loop(0, fifth.shape[0], up_step, 0, unroll=fifth.shape[0])

    colours = out_ref.shape[1]
    weight_out = beside(w_out)
    for row in range(height):
        lines = fifth[row : row + 3].reshape(3 * chans, width)
        total = jnp.dot(weight_out, lines, preferred_element_type=F32)
        line = across(total, w_out.shape[1], width)
        for colour in range(colours):
            final[colour, row : row + 1, :] = line[colour : colour + 1, :]
    out_ref[0] = final[...].astype(BF16)


def stem(where, field, w_in, w_mid):
    height = field.shape[0] // 3
    width = field.shape[2]
    one = w_mid.shape[1]
    return pl.pallas_call(
        stem_kernel,
        out_shape=jax.ShapeDtypeStruct((3 * height - 4, one, width), BF16),
        in_specs=[smem()] + [vmem()] * 3,
        out_specs=vmem(),
        scratch_shapes=[pltpu.VMEM((3 * height - 2, one, width), BF16)],
        compiler_params=params(16),
        cost_estimate=pl.CostEstimate(
            flops=1_000_000_000, bytes_accessed=MIB, transcendentals=300_000
        ),
        name="stem",
    )(where, field, w_in, w_mid)


def middle(where, second, w_down):
    rows, one, width = second.shape
    half = (rows + 4) // 6
    two = w_down.shape[2]
    return pl.pallas_call(
        middle_kernel,
        out_shape=jax.ShapeDtypeStruct((3 * half - 4, two, width // 2), BF16),
        in_specs=[smem()] + [vmem()] * 2,
        out_specs=vmem(),
        scratch_shapes=[pltpu.VMEM((3 * half - 2, one, width // 2), BF16)],
        compiler_params=params(16),
        cost_estimate=pl.CostEstimate(
            flops=500_000_000, bytes_accessed=MIB, transcendentals=100_000
        ),
        name="middle",
    )(where, second, w_down)


def decoder(where, second, third, w_deep, w_up, w_out, height, colours):
    one = second.shape[1]
    two = third.shape[1]
    width = second.shape[2]
    return pl.pallas_call(
        decoder_kernel,
        out_shape=jax.ShapeDtypeStruct((1, colours, height, width), BF16),
        in_specs=[smem()] + [vmem()] * 5,
        out_specs=vmem(),
        scratch_shapes=[
            pltpu.VMEM((third.shape[0] - 2, two, width // 2), BF16),
            pltpu.VMEM((height + 4, one + two, width), BF16),
            pltpu.VMEM((height + 2, one, width), BF16),
            pltpu.VMEM((colours, height, width), F32),
        ],
        compiler_params=params(16),
        cost_estimate=pl.CostEstimate(
            flops=1_500_000_000, bytes_accessed=MIB, transcendentals=200_000
        ),
        name="decoder",
    )(where, second, third, w_deep, w_up, w_out)


def on_device(
    bricks, sends, cells, fracs, sample_order, pending, w_in, w_mid, w_down, w_deep, w_up, w_out
):
    n_tile = lax.axis_size("tile")
    tile = lax.axis_index("tile")
    n_section = lax.axis_size("section")
    cap = sends.shape[3]
    height = pending.shape[2]
    width = pending.shape[3]
    samples = cells.shape[3]
    slots = n_tile * cap
    per_slot = samples // slots
    padded = -(-per_slot // BLOCK) * BLOCK

    def fill(part):
        if padded != per_slot:
            part = part.reshape(3, slots, per_slot)
            part = jnp.pad(part, ((0, 0), (0, 0), (0, padded - per_slot)))
        return part.reshape(3, slots * padded // LANES, LANES)

    def trim(found):
        if padded == per_slot:
            return found
        return found.reshape(slots, padded)[:, :per_slot].reshape(1, samples // LANES, LANES)

    places = positions(fill(cells), fill(fracs), n_tile)
    places, bricks, pending, tile = lax.optimization_barrier((places, bricks, pending, tile))
    arrived = lax.all_to_all(places, "tile", split_axis=0, concat_axis=0, tiled=True)
    where = jnp.stack([tile, jnp.int32(n_tile)]).astype(jnp.int32)

    mates = [(i, i ^ 1) for i in range(n_tile) if i ^ 1 < n_tile]
    across_chips = [
        pair for i in range(1, n_tile - 1, 2) for pair in ((i, i + 1), (i + 1, i))
    ]
    for_mate = lax.dynamic_slice_in_dim(places, mate_of(tile), 1, 0)
    mate_places = lax.ppermute(for_mate, "tile", mates)
    near = lax.ppermute(pending, "tile", mates)
    far = lax.ppermute(pending, "tile", across_chips)
    picks = sends[0, 0].T
    colours = w_out.shape[1]
    w_in = w_in.transpose(0, 2, 1)
    w_in = jnp.pad(w_in, ((0, 0), (0, 16 - w_in.shape[1]), (0, 0)))
    w_out = jnp.pad(w_out, ((0, 0), (0, 16 - colours), (0, 0)))
    windows = windows_of(where, picks, bricks, places, mate_places)
    arrived, w_in, w_out = lax.optimization_barrier((arrived, w_in, w_out))
    found = sample_values(where, picks, windows, arrived)

    found, near, far, pending = lax.optimization_barrier((found, near, far, pending))
    values = lax.all_to_all(found, "tile", split_axis=0, concat_axis=0, tiled=True)
    first_core = tile % 2 == 0
    over = jnp.where(first_core, far, near)
    under = jnp.where(first_core, near, far)
    field = jnp.concatenate([over[0], pending[0], under[0]], axis=1).transpose(1, 0, 2)
    field = jnp.pad(field, ((0, 0), (0, 16 - field.shape[1]), (0, 0)))
    second = stem(where, field, w_in, w_mid)
    third = middle(where, second, w_down.transpose(0, 2, 1))
    values, third = lax.optimization_barrier((values, third))
    rendered = gbuffer(trim(values), sample_order, height, width)
    rendered, third = lax.optimization_barrier((rendered, third))
    ring = [(i, (i + 1) % n_section) for i in range(n_section)]
    handoff = lax.ppermute(rendered, "section", ring)
    denoised = decoder(where, second, third, w_deep, w_up, w_out, height, colours)
    return (handoff, denoised)


def solution(mesh):
    in_specs = (
        P("tile", None),
        P("section", "tile", None, None),
        P("section", "tile", None, None),
        P("section", "tile", None, None),
        P("section", "tile", None, None),
        P("section", None, "tile", None),
        P(),
        P(),
        P(),
        P(),
        P(),
        P(),
    )
    out_specs = (P("section", None, "tile", None), P("section", None, "tile", None))
    return jax.shard_map(
        on_device, mesh=mesh, in_specs=in_specs, out_specs=out_specs, check_vma=False
    )
```

```python
import functools

import jax
import jax.numpy as jnp
from jax import lax
from jax.experimental import pallas as pl
from jax.experimental.pallas import tpu as pltpu
from jax.sharding import PartitionSpec as P

EDGE = 34
NSP = 4
NRAY = 8
NOS = 2
LANES = 128
BLOCK = 256
STRIDE = 6
WINDOWS = 6
MAIN = 32
TAIL = 16
BRICK_ROWS = WINDOWS * MAIN + TAIL
KDIM = 256

F32 = jnp.float32
BF16 = jnp.bfloat16
MIB = 1024 * 1024


def params(mib):
    return pltpu.CompilerParams(vmem_limit_bytes=mib * MIB)


def vmem():
    return pl.BlockSpec(memory_space=pltpu.VMEM)


def smem():
    return pl.BlockSpec(memory_space=pltpu.SMEM)


def positions_kernel(cells_ref, fracs_ref, out_ref, cells, fracs, found, arrivals, departures):
    owners, rows, _ = out_ref.shape
    lines = rows // 3
    parts = arrivals.shape[1]
    share = owners // parts
    pieces = [(axis, part) for axis in range(3) for part in range(parts)]

    def reads(axis, part):
        span = pl.ds(part * share * lines, share * lines)
        return [
            pltpu.make_async_copy(
                source.at[axis, span], target.at[axis, span], arrivals.at[axis, part, number]
            )
            for number, (source, target) in enumerate(((cells_ref, cells), (fracs_ref, fracs)))
        ]

    def write(axis, part):
        place = (pl.ds(part * share, share), pl.ds(axis * lines, lines))
        return pltpu.make_async_copy(
            found.at[place], out_ref.at[place], departures.at[axis, part]
        )

    for piece in pieces:
        for copy in reads(*piece):
            copy.start()
    for axis, part in pieces:
        for copy in reads(axis, part):
            copy.wait()
        span = slice(part * share * lines, (part + 1) * share * lines)
        place = cells[axis, span].astype(F32) + fracs[axis, span]
        found[part * share : (part + 1) * share, axis * lines : (axis + 1) * lines, :] = (
            place.reshape(share, lines, LANES)
        )
        write(axis, part).start()
    for piece in pieces:
        write(*piece).wait()


def positions(cells, fracs, owners):
    lines = cells.shape[1]
    shape = (owners, 3 * lines // owners, LANES)
    hbm = pl.BlockSpec(memory_space=pltpu.HBM)
    return pl.pallas_call(
        positions_kernel,
        out_shape=jax.ShapeDtypeStruct(shape, F32),
        in_specs=[hbm, hbm],
        out_specs=hbm,
        scratch_shapes=[
            pltpu.VMEM(cells.shape, jnp.int32),
            pltpu.VMEM(fracs.shape, F32),
            pltpu.VMEM(shape, F32),
            pltpu.SemaphoreType.DMA((3, 4, 2)),
            pltpu.SemaphoreType.DMA((3, 4)),
        ],
        compiler_params=params(60),
        cost_estimate=pl.CostEstimate(
            flops=3 * lines * LANES, bytes_accessed=36 * lines * LANES, transcendentals=0
        ),
        name="positions",
    )(cells, fracs)


def mate_of(tile):
    return tile + 1 - 2 * lax.rem(tile, 2)


def windows_kernel(
    where_ref, picks_ref, cube_ref, place_ref, mate_place_ref, out_ref,
    wide, tail, places, sums, arrivals,
):
    tile = where_ref[0]
    near = ((tile, place_ref.at[tile]), (mate_of(tile), mate_place_ref.at[0]))
    copies = [
        pltpu.make_async_copy(source, places.at[i], arrivals.at[i])
        for i, (_, source) in enumerate(near)
    ]
    for copy in copies:
        copy.start()
    count = cube_ref.shape[0]
    plane = EDGE * EDGE
    wide[...] = jnp.zeros_like(wide)
    wide[:, :EDGE, :plane] = cube_ref[...]
    column = lax.broadcasted_iota(jnp.int32, (1, KDIM), 1)
    main = (column // MAIN) * EDGE + column % MAIN
    rest = column - 7 * MAIN
    last = (rest % 8) * EDGE + MAIN + rest // 8
    source = jnp.where(column < 7 * MAIN, main, last)
    unused = (column >= 7 * MAIN) & ((rest % 8 == 7) | (rest >= TAIL))
    source = jnp.where(unused, -(1 << 20), source)
    for window in range(WINDOWS):
        first = window * STRIDE * EDGE
        low = first // LANES * LANES
        length = min(3 * LANES, wide.shape[2] - low)
        place = lax.broadcasted_iota(jnp.int32, (length, KDIM), 0)
        pick = jnp.where(place == source + (first - low), 1.0, 0.0).astype(BF16)
        found = jnp.dot(
            wide[:, :, low : low + length].reshape(-1, length),
            pick,
            preferred_element_type=F32,
        )
        found = found.reshape(count, 48, KDIM)
        out_ref[:count, window * MAIN : (window + 1) * MAIN, :] = found[:, :MAIN, :].astype(BF16)
        tail[:, window : window + 1, :] = found[:, MAIN : MAIN + 1, :]
        tail[:, 8 + window : 9 + window, :] = found[:, MAIN + 1 : MAIN + 2, :]
    for row in (6, 7, 14, 15):
        tail[:, row : row + 1, :] = jnp.zeros((count, 1, KDIM), F32)
    out_ref[:count, WINDOWS * MAIN :, :] = tail[...].astype(BF16)

    for copy in copies:
        copy.wait()
    cap = picks_ref.shape[0]
    lines = places.shape[1] // 3
    part = lines // cap
    height = whole_tiles(lines)
    for i, (renderer, _) in enumerate(near):
        for piece in range(cap):
            brick = out_ref[picks_ref[piece, renderer]]
            slot_sums(brick, places.at[i], sums.at[i], piece * part, part // 2)
    for i in range(len(near)):
        out_ref[count, i * height : (i + 1) * height, :LANES] = line_values(
            sums.at[i], lines, height
        )


def windows_of(where, picks, bricks, places, mate_places):
    count = bricks.shape[0]
    cube = bricks.reshape(count, EDGE, EDGE * EDGE)
    rows = places.shape[1]
    return pl.pallas_call(
        windows_kernel,
        out_shape=jax.ShapeDtypeStruct((count + 1, BRICK_ROWS, KDIM), BF16),
        in_specs=[smem(), smem(), vmem()] + [pl.BlockSpec(memory_space=pl.ANY)] * 2,
        out_specs=vmem(),
        scratch_shapes=[
            pltpu.VMEM((count, 48, 10 * LANES), BF16),
            pltpu.VMEM((count, TAIL, KDIM), F32),
            pltpu.VMEM((2, rows, LANES), F32),
            pltpu.VMEM((2, 8 * rows // 3, LANES), F32),
            pltpu.SemaphoreType.DMA((2,)),
        ],
        compiler_params=params(16),
        cost_estimate=pl.CostEstimate(
            flops=2 * count * 48 * 384 * KDIM * WINDOWS, bytes_accessed=4 * MIB,
            transcendentals=0,
        ),
        name="brick_windows",
    )(where, picks, cube, places, mate_places)


def hat(distance):
    return jnp.maximum(1.0 - jnp.abs(distance), 0.0)


def blend(brick, px, py, pz):
    width = px.shape[1]
    eight = lax.broadcasted_iota(jnp.int32, (8, width), 0).astype(F32)
    places = lax.broadcasted_iota(jnp.int32, (MAIN, width), 0).astype(F32).astype(BF16)

    def tile(rows):
        return jnp.concatenate([rows, rows], axis=0).astype(BF16)

    cell_y = jnp.floor(py)
    frac_y = py - cell_y
    lower, low_share, high_share = tile(cell_y), tile(1.0 - frac_y), tile(frac_y)
    nothing = jnp.zeros((TAIL, width), BF16)
    weight_y = []
    for start in range(0, MAIN, TAIL):
        offset = places[start : start + TAIL] - lower
        weight_y.append(
            jnp.where(offset == 0, low_share, jnp.where(offset == 1, high_share, nothing))
        )
    window = jnp.floor(px * (1.0 / STRIDE))
    weight_x = hat(eight - (px - STRIDE * window))
    parts = []
    for i in range(STRIDE + 1):
        share = tile(jnp.broadcast_to(weight_x[i : i + 1], (8, width)))
        parts += [share * part for part in weight_y]
    tail = [weight_x * hat(MAIN - py), weight_x * jnp.maximum(py - MAIN, 0.0)]
    parts.append(jnp.concatenate(tail, axis=0).astype(BF16))
    plane = jnp.concatenate(parts, axis=0)
    found = jnp.dot(brick[:, : plane.shape[0]], plane, preferred_element_type=F32)
    groups = range(0, MAIN, 8)
    chosen = [found[row : row + 8] for row in groups]
    for other in range(1, WINDOWS):
        here = window == float(other)
        base = other * MAIN
        chosen = [
            jnp.where(here, found[base + row : base + row + 8], old)
            for row, old in zip(groups, chosen)
        ]
    base = WINDOWS * MAIN
    edges = found[base : base + 8] * hat(MAIN - pz)
    edges = edges + found[base + 8 :] * jnp.maximum(pz - MAIN, 0.0)
    total = jnp.where(eight == window, edges, 0.0)
    for row, part in zip(groups, chosen):
        total = total + part * hat((eight + float(row)) - pz)
    return total


def slot_sums(brick, places, sums, first, blocks):
    lines = places.shape[0] // 3
    for step in range(blocks):
        row = first + 2 * step

        def line(axis):
            both = [
                jnp.broadcast_to(places[pl.ds(axis * lines + row + half, 1), :], (8, LANES))
                for half in range(2)
            ]
            return jnp.concatenate(both, axis=1)

        total = blend(brick, line(0), line(1), line(2))
        for half in range(2):
            sums[pl.ds(pl.multiple_of(8 * (row + half), 8), 8), :] = total[
                :, half * LANES : (half + 1) * LANES
            ]


def whole_tiles(lines):
    return -(-lines // TAIL) * TAIL


def line_values(sums, lines, height):
    values = []
    for row in range(0, lines, 8):
        value = sums[pl.ds(8 * row, 8, stride=8), :]
        for other in range(1, 8):
            value = value + sums[pl.ds(8 * row + other, 8, stride=8), :]
        values.append(value)
    if height > lines:
        values.append(jnp.zeros((height - lines, LANES), F32))
    return jnp.concatenate(values, axis=0).astype(BF16)


def samples_kernel(
    where_ref, picks_ref, brick_ref, place_ref, out_ref, bricks, places, sums, own, arrivals,
    own_arrival,
):
    owners, rows, _ = place_ref.shape
    cap = picks_ref.shape[0]
    lines = rows // 3
    part = lines // cap
    turns = owners - 2
    tile = where_ref[0]
    pairs, rest = turns // 2, turns % 2
    own_values = pltpu.make_async_copy(
        brick_ref.at[brick_ref.shape[0] - 1, pl.ds(0, own.shape[0]), pl.ds(0, LANES)],
        own,
        own_arrival,
    )

    def renderer_of(number):
        return lax.rem(2 * (tile // 2) + 2 + number, owners)

    def fetches(turn, members):
        held = turn % 2
        copies = []
        for member in range(members):
            renderer = renderer_of(2 * turn + member)
            copies.append(
                pltpu.make_async_copy(
                    place_ref.at[renderer],
                    places.at[held, member],
                    arrivals.at[held, member, cap],
                )
            )
            for piece in range(cap):
                copies.append(
                    pltpu.make_async_copy(
                        brick_ref.at[picks_ref[piece, renderer]],
                        bricks.at[held, member, piece],
                        arrivals.at[held, member, piece],
                    )
                )
        return copies

    def start(turn, members):
        for copy in fetches(turn, members):
            copy.start()

    def work(turn, members):
        held = turn % 2
        for copy in fetches(turn, members):
            copy.wait()
        for member in range(members):
            for piece in range(cap):
                slot_sums(
                    bricks[held, member, piece],
                    places.at[held, member],
                    sums.at[member],
                    piece * part,
                    part // 2,
                )
        for member in range(members):
            out_ref[renderer_of(2 * turn + member)] = line_values(
                sums.at[member], lines, lines
            )

    def one_pair(turn, carry):
        work(turn, 2)

        @pl.when(turn + 2 < pairs)
        def _():
            start(turn + 2, 2)

        if rest:

            @pl.when(turn + 2 == pairs)
            def _():
                start(pairs, 1)

        return carry

    for turn in range(min(2, pairs)):
        start(turn, 2)
    if rest and pairs < 2:
        start(pairs, 1)
    own_values.start()
    lax.fori_loop(0, pairs, one_pair, 0)
    if rest:
        work(pairs, 1)
    own_values.wait()
    height = whole_tiles(lines)
    for i, renderer in enumerate((tile, mate_of(tile))):
        values = own[i * height : (i + 1) * height, :].astype(F32)
        out_ref[renderer] = values[:lines].astype(BF16)


def sample_values(where, picks, windows, places):
    owners, rows, _ = places.shape
    cap = picks.shape[0]
    samples = owners * rows * LANES // 3
    some = pl.BlockSpec(memory_space=pl.ANY)
    return pl.pallas_call(
        samples_kernel,
        out_shape=jax.ShapeDtypeStruct((owners, rows // 3, LANES), BF16),
        in_specs=[smem(), smem(), some, some],
        out_specs=vmem(),
        scratch_shapes=[
            pltpu.VMEM((2, 2, cap, BRICK_ROWS, KDIM), BF16),
            pltpu.VMEM((2, 2, rows, LANES), F32),
            pltpu.VMEM((2, 8 * rows // 3, LANES), F32),
            pltpu.VMEM((2 * whole_tiles(rows // 3), LANES), BF16),
            pltpu.SemaphoreType.DMA((2, 2, cap + 1)),
            pltpu.SemaphoreType.DMA,
        ],
        compiler_params=pltpu.CompilerParams(vmem_limit_bytes=61_600_000),
        cost_estimate=pl.CostEstimate(
            flops=2 * samples * KDIM * BRICK_ROWS, bytes_accessed=3 * MIB,
            transcendentals=0,
        ),
        name="sample_values",
    )(where, picks, windows, places)


def gbuffer_kernel(value_ref, order_ref, out_ref, values):
    values[...] = value_ref[...].astype(F32).reshape(values.shape)
    height = out_ref.shape[2]

    def ray_of(number):
        rows_now = slice(number * height, (number + 1) * height)
        first, second = (
            values[pl.ds(2 * number * height + half, height, stride=2), :] for half in range(2)
        )
        parts = []
        for half in range(2):
            order = order_ref[0, 0, rows_now, half * LANES : (half + 1) * LANES]
            inner = order & (LANES - 1)
            parts.append(
                jnp.where(
                    order < LANES,
                    jnp.take_along_axis(first, inner, axis=1, mode="promise_in_bounds"),
                    jnp.take_along_axis(second, inner, axis=1, mode="promise_in_bounds"),
                )
            )
        return jnp.concatenate(parts, axis=1)

    remain = 1.0
    shade = 0.0
    depth = 0.0
    for step in range(NSP):
        ray = ray_of(step)
        half_tanh = 0.5 * jnp.tanh(ray)
        weight = remain * (0.5 + half_tanh)
        shade = shade + weight * ray
        depth = depth + weight * ((step + 1) / NSP)
        remain = remain * (0.5 - half_tanh)
    occlusion = 0.0
    for ray_number in range(NRAY):
        passing = 1.0
        for step in range(NOS):
            ray = ray_of(NSP + ray_number * NOS + step)
            passing = passing * (0.5 - 0.5 * jnp.tanh(ray))
        occlusion = occlusion + passing
    out_ref[0, 0] = shade.astype(BF16)
    out_ref[0, 1] = (1.0 - remain).astype(BF16)
    out_ref[0, 2] = depth.astype(BF16)
    out_ref[0, 3] = (occlusion * (1.0 / NRAY)).astype(BF16)


def gbuffer(values, order, height, width):
    total = order.shape[2]
    return pl.pallas_call(
        gbuffer_kernel,
        out_shape=jax.ShapeDtypeStruct((1, 4, height, width), BF16),
        in_specs=[vmem(), vmem()],
        out_specs=vmem(),
        scratch_shapes=[pltpu.VMEM((2 * total, LANES), F32)],
        compiler_params=params(16),
        cost_estimate=pl.CostEstimate(
            flops=20 * total * BLOCK, bytes_accessed=8 * total * BLOCK, transcendentals=0
        ),
        name="gbuffer",
    )(values, order)


def silu(field):
    half = 0.5 * field
    return half + half * jnp.tanh(half)


def shifted(rows, steps):
    lane = lax.broadcasted_iota(jnp.int32, (1, LANES), 1)
    edge = lane == (0 if steps == 1 else LANES - 1)
    moved = []
    for row in rows:
        tiles = [row[:, i : i + LANES] for i in range(0, row.shape[1], LANES)]
        tiles = [pltpu.roll(tile, steps % LANES, 1) for tile in tiles]
        for i, tile in enumerate(tiles):
            source = i - steps
            fill = tiles[source] if 0 <= source < len(tiles) else 0.0
            moved.append(jnp.where(edge, fill, tile))
    return jnp.concatenate(moved, axis=1)


def across(total, chans, row_width):
    left, middle, right = (total[i * chans : (i + 1) * chans] for i in range(3))

    def rows_of(part):
        return [part[:, i : i + row_width] for i in range(0, part.shape[1], row_width)]

    return middle + shifted(rows_of(left), 1) + shifted(rows_of(right), -1)


def taps(weight_ref, tap):
    _, out_chans, chans = weight_ref.shape
    return weight_ref[3 * tap : 3 * tap + 3].reshape(3 * out_chans, chans)


def beside(weight_ref):
    return jnp.concatenate([taps(weight_ref, tap) for tap in range(3)], axis=1)


def beside_padded(weight_ref, spare):
    few = weight_ref.shape[1]
    spare[...] = jnp.zeros_like(spare)
    for tap in range(3):
        for column in range(3):
            spare[tap, column * TAIL : column * TAIL + few, :] = weight_ref[
                3 * tap + column
            ].astype(F32)
    return jnp.concatenate([spare[tap].astype(BF16) for tap in range(3)], axis=1)


def sides(where_ref):
    above = jnp.where(where_ref[0] > 0, 1.0, 0.0)
    below = jnp.where(where_ref[0] < where_ref[1] - 1, 1.0, 0.0)

    def inside(row, low, high):
        return jnp.where(row < low, above, jnp.where(row >= high, below, 1.0))

    return inside


def turned(weight_ref, spare=None):
    _, few, out_chans = weight_ref.shape
    here = lax.broadcasted_iota(jnp.int32, (out_chans, out_chans), 0)
    there = lax.broadcasted_iota(jnp.int32, (out_chans, out_chans), 1)
    unit = jnp.where(here == there, 1.0, 0.0).astype(BF16)
    if spare is not None:
        spare[...] = jnp.zeros_like(spare)
    rows = []
    for column in range(3):
        if spare is None:
            stack = jnp.concatenate([weight_ref[3 * tap + column] for tap in range(3)], axis=0)
        else:
            for tap in range(3):
                spare[column, tap * TAIL : tap * TAIL + few, :] = weight_ref[
                    3 * tap + column
                ].astype(F32)
            stack = spare[column].astype(BF16)
        rows.append(
            lax.dot_general(
                unit, stack, (((1,), (1,)), ((), ())), preferred_element_type=F32
            )
        )
    return jnp.concatenate(rows, axis=0).astype(BF16)


def stem_kernel(
    where_ref, own_ref, near_ref, far_ref, w_in, w_mid, second, x_ref, first, spare
):
    height, chans, width = own_ref.shape
    inside = sides(where_ref)
    first_core = lax.rem(where_ref[0], 2) == 0
    near, far = near_ref[...].astype(F32), far_ref[...].astype(F32)
    x_ref[...] = jnp.zeros_like(x_ref)
    x_ref[:height, :chans, :] = jnp.where(first_core, far, near).astype(BF16)
    x_ref[height : 2 * height, :chans, :] = own_ref[...]
    x_ref[2 * height :, :chans, :] = jnp.where(first_core, near, far).astype(BF16)

    def full_layer(weight, source, target, low, high, unroll):
        chans = target.shape[1]
        depth = weight.shape[1]

        def step(row, carry):
            lines = source[pl.ds(row, 3)].reshape(depth, width)
            line = across(jnp.dot(weight, lines, preferred_element_type=F32), chans, width)
            target[row] = (silu(line) * inside(row, low, high)).astype(BF16)
            return carry

        lax.fori_loop(0, target.shape[0], step, 0, unroll=unroll)

    full_layer(turned(w_in, spare), x_ref, first, height - 1, 2 * height - 1, first.shape[0])
    full_layer(beside(w_mid), first, second, height - 2, 2 * height - 2, second.shape[0])


def half_pair(source, row, tap):
    return jnp.concatenate([source[row + tap], source[row + tap + 1]], axis=1)


def half_layer(product, target, inside, low, high):
    chans, half_width = target.shape[1], target.shape[2]
    for row in range(0, target.shape[0], 2):
        both = silu(across(product(row), chans, half_width))
        for now in range(2):
            line = both[:, now * half_width : (now + 1) * half_width]
            if row + now < low or row + now >= high:
                line = line * inside(row + now, low, high)
            target[row + now] = line.astype(BF16)


def middle_kernel(where_ref, second, w_down, third, pooled):
    count, chans, width = second.shape
    half_height = (count + 4) // 6
    half_width = width // 2
    inside = sides(where_ref)
    place = lax.broadcasted_iota(jnp.int32, (width, half_width), 0) // 2
    target = lax.broadcasted_iota(jnp.int32, (width, half_width), 1)
    shrink = jnp.where(place == target, 0.25, 0.0).astype(BF16)
    pairs = jnp.dot(
        second[...].reshape(count * chans, width), shrink, preferred_element_type=F32
    ).reshape(count // 2, 2, chans, half_width)
    pooled[...] = (pairs[:, 0] + pairs[:, 1]).astype(BF16)
    weight_down = turned(w_down)

    def down_product(row):
        lines = jnp.concatenate([half_pair(pooled, row, tap) for tap in range(3)], axis=0)
        return jnp.dot(weight_down, lines, preferred_element_type=F32)

    half_layer(down_product, third, inside, half_height - 2, 2 * half_height - 2)


def decoder_kernel(
    where_ref, second, third, w_deep, w_up, w_out, out_ref, fourth, joined, fifth, final, spare
):
    height = out_ref.shape[2]
    half_height = height // 2
    width = out_ref.shape[3]
    half_width = width // 2
    chans = second.shape[1]
    inside = sides(where_ref)

    def deep_product(row):
        total = None
        for tap in range(3):
            part = jnp.dot(
                taps(w_deep, tap), half_pair(third, row, tap), preferred_element_type=F32
            )
            total = part if total is None else total + part
        return total

    half_layer(deep_product, fourth, inside, half_height - 3, 2 * half_height - 3)
    place = lax.broadcasted_iota(jnp.int32, (half_width, width), 0)
    target = lax.broadcasted_iota(jnp.int32, (half_width, width), 1) // 2
    spread = jnp.where(place == target, 1.0, 0.0).astype(BF16)
    deep = fourth.shape[1]
    wide = jnp.dot(
        fourth[...].reshape(-1, half_width), spread, preferred_element_type=F32
    ).astype(BF16).reshape(fourth.shape[0], deep, width)
    for row in range(2 * fourth.shape[0]):
        joined[row, chans:, :] = wide[row // 2]
        joined[row, :chans, :] = second[row + 4]

    def up_step(row, carry):
        total = None
        for tap in range(3):
            part = jnp.dot(taps(w_up, tap), joined[row + tap], preferred_element_type=F32)
            total = part if total is None else total + part
        line = silu(across(total, chans, width))
        fifth[row] = (line * inside(row, 1, height + 1)).astype(BF16)
        return carry

    lax.fori_loop(0, fifth.shape[0], up_step, 0, unroll=fifth.shape[0])

    colours = out_ref.shape[1]
    weight_out = beside_padded(w_out, spare)
    for row in range(height):
        lines = fifth[row : row + 3].reshape(3 * chans, width)
        total = jnp.dot(weight_out, lines, preferred_element_type=F32)
        line = across(total, TAIL, width)
        for colour in range(colours):
            final[colour, row : row + 1, :] = line[colour : colour + 1, :]
    out_ref[0] = final[...].astype(BF16)


def stem(where, own, near, far, w_in, w_mid):
    height, _, width = own.shape
    one = w_mid.shape[1]
    return pl.pallas_call(
        stem_kernel,
        out_shape=jax.ShapeDtypeStruct((3 * height - 4, one, width), BF16),
        in_specs=[smem()] + [vmem()] * 5,
        out_specs=vmem(),
        scratch_shapes=[
            pltpu.VMEM((3 * height, TAIL, width), BF16),
            pltpu.VMEM((3 * height - 2, one, width), BF16),
            pltpu.VMEM((3, 3 * TAIL, one), F32),
        ],
        compiler_params=params(16),
        cost_estimate=pl.CostEstimate(
            flops=1_000_000_000, bytes_accessed=MIB, transcendentals=300_000
        ),
        name="stem",
    )(where, own, near, far, w_in, w_mid)


def middle(where, second, w_down):
    rows, one, width = second.shape
    half = (rows + 4) // 6
    two = w_down.shape[2]
    return pl.pallas_call(
        middle_kernel,
        out_shape=jax.ShapeDtypeStruct((3 * half - 4, two, width // 2), BF16),
        in_specs=[smem()] + [vmem()] * 2,
        out_specs=vmem(),
        scratch_shapes=[pltpu.VMEM((3 * half - 2, one, width // 2), BF16)],
        compiler_params=params(16),
        cost_estimate=pl.CostEstimate(
            flops=500_000_000, bytes_accessed=MIB, transcendentals=100_000
        ),
        name="middle",
    )(where, second, w_down)


def decoder(where, second, third, w_deep, w_up, w_out, height, colours):
    one = second.shape[1]
    two = third.shape[1]
    width = second.shape[2]
    return pl.pallas_call(
        decoder_kernel,
        out_shape=jax.ShapeDtypeStruct((1, colours, height, width), BF16),
        in_specs=[smem()] + [vmem()] * 5,
        out_specs=vmem(),
        scratch_shapes=[
            pltpu.VMEM((third.shape[0] - 2, two, width // 2), BF16),
            pltpu.VMEM((height + 4, one + two, width), BF16),
            pltpu.VMEM((height + 2, one, width), BF16),
            pltpu.VMEM((colours, height, width), F32),
            pltpu.VMEM((3, 3 * TAIL, one), F32),
        ],
        compiler_params=params(16),
        cost_estimate=pl.CostEstimate(
            flops=1_500_000_000, bytes_accessed=MIB, transcendentals=200_000
        ),
        name="decoder",
    )(where, second, third, w_deep, w_up, w_out)


def on_device(
    bricks, sends, cells, fracs, sample_order, pending, w_in, w_mid, w_down, w_deep, w_up, w_out
):
    n_tile = lax.axis_size("tile")
    tile = lax.axis_index("tile")
    n_section = lax.axis_size("section")
    cap = sends.shape[3]
    height = pending.shape[2]
    width = pending.shape[3]
    samples = cells.shape[3]
    slots = n_tile * cap
    per_slot = samples // slots
    padded = -(-per_slot // BLOCK) * BLOCK

    def fill(part):
        if padded != per_slot:
            part = part.reshape(3, slots, per_slot)
            part = jnp.pad(part, ((0, 0), (0, 0), (0, padded - per_slot)))
        return part.reshape(3, slots * padded // LANES, LANES)

    def trim(found):
        if padded == per_slot:
            return found
        return found.reshape(slots, padded)[:, :per_slot].reshape(1, samples // LANES, LANES)

    places = positions(fill(cells), fill(fracs), n_tile)
    places, bricks, pending, tile = lax.optimization_barrier((places, bricks, pending, tile))
    arrived = lax.all_to_all(places, "tile", split_axis=0, concat_axis=0, tiled=True)
    where = jnp.stack([tile, jnp.int32(n_tile)]).astype(jnp.int32)

    mates = [(i, i ^ 1) for i in range(n_tile) if i ^ 1 < n_tile]
    across_chips = [
        pair for i in range(1, n_tile - 1, 2) for pair in ((i, i + 1), (i + 1, i))
    ]
    for_mate = lax.dynamic_slice_in_dim(places, mate_of(tile), 1, 0)
    mate_places = lax.ppermute(for_mate, "tile", mates)
    rows = pending[0].transpose(1, 0, 2)
    near = lax.ppermute(rows, "tile", mates)
    far = lax.ppermute(rows, "tile", across_chips)
    picks = sends[0, 0].T
    colours = w_out.shape[1]
    windows = windows_of(where, picks, bricks, places, mate_places)
    found = sample_values(where, picks, windows, arrived)

    found, rows, near, far = lax.optimization_barrier((found, rows, near, far))
    values = lax.all_to_all(found, "tile", split_axis=0, concat_axis=0, tiled=True)
    second = stem(where, rows, near, far, w_in.transpose(0, 2, 1), w_mid)
    third = middle(where, second, w_down.transpose(0, 2, 1))
    values, third = lax.optimization_barrier((values, third))
    rendered = gbuffer(trim(values), sample_order, height, width)
    rendered, third = lax.optimization_barrier((rendered, third))
    ring = [(i, (i + 1) % n_section) for i in range(n_section)]
    handoff = lax.ppermute(rendered, "section", ring)
    denoised = decoder(where, second, third, w_deep, w_up, w_out, height, colours)
    return (handoff, denoised)


def solution(mesh):
    in_specs = (
        P("tile", None),
        P("section", "tile", None, None),
        P("section", "tile", None, None),
        P("section", "tile", None, None),
        P("section", "tile", None, None),
        P("section", None, "tile", None),
        P(),
        P(),
        P(),
        P(),
        P(),
        P(),
    )
    out_specs = (P("section", None, "tile", None), P("section", None, "tile", None))
    return jax.shard_map(
        on_device, mesh=mesh, in_specs=in_specs, out_specs=out_specs, check_vma=False
    )
```

```python
import functools

import jax
import jax.numpy as jnp
from jax import lax
from jax.experimental import pallas as pl
from jax.experimental.pallas import tpu as pltpu
from jax.sharding import PartitionSpec as P

EDGE = 34
NSP = 4
NRAY = 8
NOS = 2
LANES = 128
BLOCK = 256
STRIDE = 6
WINDOWS = 6
MAIN = 32
TAIL = 16
BRICK_ROWS = WINDOWS * MAIN + TAIL
KDIM = 256

F32 = jnp.float32
BF16 = jnp.bfloat16
MIB = 1024 * 1024


def params(mib):
    return pltpu.CompilerParams(vmem_limit_bytes=mib * MIB)


def vmem():
    return pl.BlockSpec(memory_space=pltpu.VMEM)


def smem():
    return pl.BlockSpec(memory_space=pltpu.SMEM)


def positions_kernel(cells_ref, fracs_ref, out_ref, cells, fracs, found, arrivals, departures):
    owners, rows, _ = out_ref.shape
    lines = rows // 3
    parts = arrivals.shape[1]
    share = owners // parts
    pieces = [(axis, part) for axis in range(3) for part in range(parts)]

    def reads(axis, part):
        span = pl.ds(part * share * lines, share * lines)
        return [
            pltpu.make_async_copy(
                source.at[axis, span], target.at[axis, span], arrivals.at[axis, part, number]
            )
            for number, (source, target) in enumerate(((cells_ref, cells), (fracs_ref, fracs)))
        ]

    def write(axis, part):
        place = (pl.ds(part * share, share), pl.ds(axis * lines, lines))
        return pltpu.make_async_copy(
            found.at[place], out_ref.at[place], departures.at[axis, part]
        )

    ahead = 3
    for piece in pieces[:ahead]:
        for copy in reads(*piece):
            copy.start()
    for number, (axis, part) in enumerate(pieces):
        for copy in reads(axis, part):
            copy.wait()
        for piece in pieces[number + ahead : number + ahead + 1]:
            for copy in reads(*piece):
                copy.start()
        span = slice(part * share * lines, (part + 1) * share * lines)
        place = cells[axis, span].astype(F32) + fracs[axis, span]
        found[part * share : (part + 1) * share, axis * lines : (axis + 1) * lines, :] = (
            place.reshape(share, lines, LANES)
        )
        write(axis, part).start()
    for piece in pieces:
        write(*piece).wait()


def positions(cells, fracs, owners):
    lines = cells.shape[1]
    shape = (owners, 3 * lines // owners, LANES)
    hbm = pl.BlockSpec(memory_space=pltpu.HBM)
    return pl.pallas_call(
        positions_kernel,
        out_shape=jax.ShapeDtypeStruct(shape, F32),
        in_specs=[hbm, hbm],
        out_specs=hbm,
        scratch_shapes=[
            pltpu.VMEM(cells.shape, jnp.int32),
            pltpu.VMEM(fracs.shape, F32),
            pltpu.VMEM(shape, F32),
            pltpu.SemaphoreType.DMA((3, 2, 2)),
            pltpu.SemaphoreType.DMA((3, 2)),
        ],
        compiler_params=params(60),
        cost_estimate=pl.CostEstimate(
            flops=3 * lines * LANES, bytes_accessed=36 * lines * LANES, transcendentals=0
        ),
        name="positions",
    )(cells, fracs)


def mate_of(tile):
    return tile + 1 - 2 * lax.rem(tile, 2)


def windows_kernel(
    where_ref, picks_ref, cube_ref, place_ref, mate_place_ref, out_ref,
    wide, tail, places, sums, arrivals,
):
    tile = where_ref[0]
    near = ((tile, place_ref.at[tile]), (mate_of(tile), mate_place_ref.at[0]))
    copies = [
        pltpu.make_async_copy(source, places.at[i], arrivals.at[i])
        for i, (_, source) in enumerate(near)
    ]
    for copy in copies:
        copy.start()
    count = cube_ref.shape[0]
    plane = EDGE * EDGE
    wide[:, :, plane // LANES * LANES :] = jnp.zeros((count, wide.shape[1], LANES), BF16)
    wide[:, :EDGE, :plane] = cube_ref[...]
    column = lax.broadcasted_iota(jnp.int32, (1, KDIM), 1)
    main = (column // MAIN) * EDGE + column % MAIN
    rest = column - 7 * MAIN
    last = (rest % 8) * EDGE + MAIN + rest // 8
    source = jnp.where(column < 7 * MAIN, main, last)
    unused = (column >= 7 * MAIN) & ((rest % 8 == 7) | (rest >= TAIL))
    source = jnp.where(unused, -(1 << 20), source)
    for window in range(WINDOWS):
        first = window * STRIDE * EDGE
        low = first // LANES * LANES
        length = min(3 * LANES, wide.shape[2] - low)
        place = lax.broadcasted_iota(jnp.int32, (length, KDIM), 0)
        pick = jnp.where(place == source + (first - low), 1.0, 0.0).astype(BF16)
        found = jnp.dot(
            wide[:, :, low : low + length].reshape(-1, length),
            pick,
            preferred_element_type=F32,
        )
        found = found.reshape(count, 48, KDIM)
        out_ref[:count, window * MAIN : (window + 1) * MAIN, :] = found[:, :MAIN, :].astype(BF16)
        tail[:, window : window + 1, :] = found[:, MAIN : MAIN + 1, :]
        tail[:, 8 + window : 9 + window, :] = found[:, MAIN + 1 : MAIN + 2, :]
    for row in (6, 7, 14, 15):
        tail[:, row : row + 1, :] = jnp.zeros((count, 1, KDIM), F32)
    out_ref[:count, WINDOWS * MAIN :, :] = tail[...].astype(BF16)

    for copy in copies:
        copy.wait()
    cap = picks_ref.shape[0]
    lines = places.shape[1] // 3
    part = lines // cap
    height = whole_tiles(lines)
    for i, (renderer, _) in enumerate(near):
        for piece in range(cap):
            brick = out_ref[picks_ref[piece, renderer]]
            slot_sums(brick, places.at[i], sums.at[i], piece * part, part // 2)
    for i in range(len(near)):
        out_ref[count, i * height : (i + 1) * height, :LANES] = line_values(
            sums.at[i], lines, height
        )


def windows_of(where, picks, bricks, places, mate_places):
    count = bricks.shape[0]
    cube = bricks.reshape(count, EDGE, EDGE * EDGE)
    rows = places.shape[1]
    return pl.pallas_call(
        windows_kernel,
        out_shape=jax.ShapeDtypeStruct((count + 1, BRICK_ROWS, KDIM), BF16),
        in_specs=[smem(), smem(), vmem()] + [pl.BlockSpec(memory_space=pl.ANY)] * 2,
        out_specs=vmem(),
        scratch_shapes=[
            pltpu.VMEM((count, 48, 10 * LANES), BF16),
            pltpu.VMEM((count, TAIL, KDIM), F32),
            pltpu.VMEM((2, rows, LANES), F32),
            pltpu.VMEM((2, 8 * rows // 3, LANES), F32),
            pltpu.SemaphoreType.DMA((2,)),
        ],
        compiler_params=params(16),
        cost_estimate=pl.CostEstimate(
            flops=2 * count * 48 * 384 * KDIM * WINDOWS, bytes_accessed=4 * MIB,
            transcendentals=0,
        ),
        name="brick_windows",
    )(where, picks, cube, places, mate_places)


def hat(distance):
    return jnp.maximum(1.0 - jnp.abs(distance), 0.0)


def blend(brick, px, py, pz):
    width = px.shape[1]
    eight = lax.broadcasted_iota(jnp.int32, (8, width), 0).astype(F32)
    places = lax.broadcasted_iota(jnp.int32, (MAIN, width), 0).astype(F32).astype(BF16)

    def tile(rows):
        return jnp.concatenate([rows, rows], axis=0).astype(BF16)

    cell_y = jnp.floor(py)
    frac_y = py - cell_y
    lower, low_share, high_share = tile(cell_y), tile(1.0 - frac_y), tile(frac_y)
    nothing = jnp.zeros((TAIL, width), BF16)
    weight_y = []
    for start in range(0, MAIN, TAIL):
        offset = places[start : start + TAIL] - lower
        weight_y.append(
            jnp.where(offset == 0, low_share, jnp.where(offset == 1, high_share, nothing))
        )
    window = jnp.floor(px * (1.0 / STRIDE))
    weight_x = hat(eight - (px - STRIDE * window))
    parts = []
    for i in range(STRIDE + 1):
        share = tile(jnp.broadcast_to(weight_x[i : i + 1], (8, width)))
        parts += [share * part for part in weight_y]
    tail = [weight_x * hat(MAIN - py), weight_x * jnp.maximum(py - MAIN, 0.0)]
    parts.append(jnp.concatenate(tail, axis=0).astype(BF16))
    plane = jnp.concatenate(parts, axis=0)
    found = jnp.dot(brick[:, : plane.shape[0]], plane, preferred_element_type=F32)
    groups = range(0, MAIN, 8)
    chosen = [found[row : row + 8] for row in groups]
    for other in range(1, WINDOWS):
        here = window == float(other)
        base = other * MAIN
        chosen = [
            jnp.where(here, found[base + row : base + row + 8], old)
            for row, old in zip(groups, chosen)
        ]
    base = WINDOWS * MAIN
    edges = found[base : base + 8] * hat(MAIN - pz)
    edges = edges + found[base + 8 :] * jnp.maximum(pz - MAIN, 0.0)
    total = jnp.where(eight == window, edges, 0.0)
    for row, part in zip(groups, chosen):
        total = total + part * hat((eight + float(row)) - pz)
    return total


def slot_sums(brick, places, sums, first, blocks):
    lines = places.shape[0] // 3
    for step in range(blocks):
        row = first + 2 * step

        def line(axis):
            both = [
                jnp.broadcast_to(places[pl.ds(axis * lines + row + half, 1), :], (8, LANES))
                for half in range(2)
            ]
            return jnp.concatenate(both, axis=1)

        total = blend(brick, line(0), line(1), line(2))
        for half in range(2):
            sums[pl.ds(pl.multiple_of(8 * (row + half), 8), 8), :] = total[
                :, half * LANES : (half + 1) * LANES
            ]


def whole_tiles(lines):
    return -(-lines // TAIL) * TAIL


def line_values(sums, lines, height):
    values = []
    for row in range(0, lines, 8):
        value = sums[pl.ds(8 * row, 8, stride=8), :]
        for other in range(1, 8):
            value = value + sums[pl.ds(8 * row + other, 8, stride=8), :]
        values.append(value)
    if height > lines:
        values.append(jnp.zeros((height - lines, LANES), F32))
    return jnp.concatenate(values, axis=0).astype(BF16)


def samples_kernel(
    where_ref, picks_ref, brick_ref, place_ref, out_ref, bricks, places, sums, own, arrivals,
    own_arrival,
):
    owners, rows, _ = place_ref.shape
    cap = picks_ref.shape[0]
    lines = rows // 3
    part = lines // cap
    turns = owners - 2
    tile = where_ref[0]
    pairs, rest = turns // 2, turns % 2
    own_values = pltpu.make_async_copy(
        brick_ref.at[brick_ref.shape[0] - 1, pl.ds(0, own.shape[0]), pl.ds(0, LANES)],
        own,
        own_arrival,
    )

    def renderer_of(number):
        return lax.rem(2 * (tile // 2) + 2 + number, owners)

    def fetches(turn, members):
        held = turn % 2
        copies = []
        for member in range(members):
            renderer = renderer_of(2 * turn + member)
            copies.append(
                pltpu.make_async_copy(
                    place_ref.at[renderer],
                    places.at[held, member],
                    arrivals.at[held, member, cap],
                )
            )
            for piece in range(cap):
                copies.append(
                    pltpu.make_async_copy(
                        brick_ref.at[picks_ref[piece, renderer]],
                        bricks.at[held, member, piece],
                        arrivals.at[held, member, piece],
                    )
                )
        return copies

    def start(turn, members):
        for copy in fetches(turn, members):
            copy.start()

    def work(turn, members):
        held = turn % 2
        for copy in fetches(turn, members):
            copy.wait()

        if members == 2:

            @pl.when(turn + 1 < pairs)
            def _():
                start(turn + 1, 2)

            if rest:

                @pl.when(turn + 1 == pairs)
                def _():
                    start(pairs, 1)

            @pl.when(turn == 0)
            def _():
                own_values.start()

        for member in range(members):
            for piece in range(cap):
                slot_sums(
                    bricks[held, member, piece],
                    places.at[held, member],
                    sums.at[member],
                    piece * part,
                    part // 2,
                )
        for member in range(members):
            out_ref[renderer_of(2 * turn + member)] = line_values(
                sums.at[member], lines, lines
            )

    def one_pair(turn, carry):
        work(turn, 2)

        return carry

    if pairs > 0:
        start(0, 2)
    elif rest:
        start(0, 1)
    lax.fori_loop(0, pairs, one_pair, 0)
    if rest:
        work(pairs, 1)
    if pairs == 0:
        own_values.start()
    own_values.wait()
    height = whole_tiles(lines)
    for i, renderer in enumerate((tile, mate_of(tile))):
        values = own[i * height : (i + 1) * height, :].astype(F32)
        out_ref[renderer] = values[:lines].astype(BF16)


def sample_values(where, picks, windows, places):
    owners, rows, _ = places.shape
    cap = picks.shape[0]
    samples = owners * rows * LANES // 3
    some = pl.BlockSpec(memory_space=pl.ANY)
    return pl.pallas_call(
        samples_kernel,
        out_shape=jax.ShapeDtypeStruct((owners, rows // 3, LANES), BF16),
        in_specs=[smem(), smem(), some, some],
        out_specs=vmem(),
        scratch_shapes=[
            pltpu.VMEM((2, 2, cap, BRICK_ROWS, KDIM), BF16),
            pltpu.VMEM((2, 2, rows, LANES), F32),
            pltpu.VMEM((2, 8 * rows // 3, LANES), F32),
            pltpu.VMEM((2 * whole_tiles(rows // 3), LANES), BF16),
            pltpu.SemaphoreType.DMA((2, 2, cap + 1)),
            pltpu.SemaphoreType.DMA,
        ],
        compiler_params=pltpu.CompilerParams(vmem_limit_bytes=61_600_000),
        cost_estimate=pl.CostEstimate(
            flops=2 * samples * KDIM * BRICK_ROWS, bytes_accessed=3 * MIB,
            transcendentals=0,
        ),
        name="sample_values",
    )(where, picks, windows, places)


def gbuffer_kernel(value_ref, order_ref, out_ref, values):
    values[...] = value_ref[...].astype(F32).reshape(values.shape)
    height = out_ref.shape[2]

    def ray_of(number):
        rows_now = slice(number * height, (number + 1) * height)
        first, second = (
            values[pl.ds(2 * number * height + half, height, stride=2), :] for half in range(2)
        )
        parts = []
        for half in range(2):
            order = order_ref[0, 0, rows_now, half * LANES : (half + 1) * LANES]
            inner = order & (LANES - 1)
            parts.append(
                jnp.where(
                    order < LANES,
                    jnp.take_along_axis(first, inner, axis=1, mode="promise_in_bounds"),
                    jnp.take_along_axis(second, inner, axis=1, mode="promise_in_bounds"),
                )
            )
        return jnp.concatenate(parts, axis=1)

    remain = 1.0
    shade = 0.0
    depth = 0.0
    for step in range(NSP):
        ray = ray_of(step)
        half_tanh = 0.5 * jnp.tanh(ray)
        weight = remain * (0.5 + half_tanh)
        shade = shade + weight * ray
        depth = depth + weight * ((step + 1) / NSP)
        remain = remain * (0.5 - half_tanh)
    occlusion = 0.0
    for ray_number in range(NRAY):
        passing = 1.0
        for step in range(NOS):
            ray = ray_of(NSP + ray_number * NOS + step)
            passing = passing * (0.5 - 0.5 * jnp.tanh(ray))
        occlusion = occlusion + passing
    out_ref[0, 0] = shade.astype(BF16)
    out_ref[0, 1] = (1.0 - remain).astype(BF16)
    out_ref[0, 2] = depth.astype(BF16)
    out_ref[0, 3] = (occlusion * (1.0 / NRAY)).astype(BF16)


def gbuffer(values, order, height, width):
    total = order.shape[2]
    return pl.pallas_call(
        gbuffer_kernel,
        out_shape=jax.ShapeDtypeStruct((1, 4, height, width), BF16),
        in_specs=[vmem(), vmem()],
        out_specs=vmem(),
        scratch_shapes=[pltpu.VMEM((2 * total, LANES), F32)],
        compiler_params=params(16),
        cost_estimate=pl.CostEstimate(
            flops=20 * total * BLOCK, bytes_accessed=8 * total * BLOCK, transcendentals=0
        ),
        name="gbuffer",
    )(values, order)


def silu(field):
    half = 0.5 * field
    return half + half * jnp.tanh(half)


def shifted(rows, steps):
    lane = lax.broadcasted_iota(jnp.int32, (1, LANES), 1)
    edge = lane == (0 if steps == 1 else LANES - 1)
    moved = []
    for row in rows:
        tiles = [row[:, i : i + LANES] for i in range(0, row.shape[1], LANES)]
        tiles = [pltpu.roll(tile, steps % LANES, 1) for tile in tiles]
        for i, tile in enumerate(tiles):
            source = i - steps
            fill = tiles[source] if 0 <= source < len(tiles) else 0.0
            moved.append(jnp.where(edge, fill, tile))
    return jnp.concatenate(moved, axis=1)


def across(total, chans, row_width):
    left, middle, right = (total[i * chans : (i + 1) * chans] for i in range(3))

    def rows_of(part):
        return [part[:, i : i + row_width] for i in range(0, part.shape[1], row_width)]

    return middle + shifted(rows_of(left), 1) + shifted(rows_of(right), -1)


def taps(weight_ref, tap):
    _, out_chans, chans = weight_ref.shape
    return weight_ref[3 * tap : 3 * tap + 3].reshape(3 * out_chans, chans)


def beside(weight_ref):
    return jnp.concatenate([taps(weight_ref, tap) for tap in range(3)], axis=1)


def beside_padded(weight_ref, spare):
    few = weight_ref.shape[1]
    spare[...] = jnp.zeros_like(spare)
    for tap in range(3):
        for column in range(3):
            spare[tap, column * TAIL : column * TAIL + few, :] = weight_ref[
                3 * tap + column
            ].astype(F32)
    return jnp.concatenate([spare[tap].astype(BF16) for tap in range(3)], axis=1)


def sides(where_ref):
    above = jnp.where(where_ref[0] > 0, 1.0, 0.0)
    below = jnp.where(where_ref[0] < where_ref[1] - 1, 1.0, 0.0)

    def inside(row, low, high):
        return jnp.where(row < low, above, jnp.where(row >= high, below, 1.0))

    return inside


def turned(weight_ref, spare=None):
    _, few, out_chans = weight_ref.shape
    here = lax.broadcasted_iota(jnp.int32, (out_chans, out_chans), 0)
    there = lax.broadcasted_iota(jnp.int32, (out_chans, out_chans), 1)
    unit = jnp.where(here == there, 1.0, 0.0).astype(BF16)
    if spare is not None:
        spare[...] = jnp.zeros_like(spare)
    rows = []
    for column in range(3):
        if spare is None:
            stack = jnp.concatenate([weight_ref[3 * tap + column] for tap in range(3)], axis=0)
        else:
            for tap in range(3):
                spare[column, tap * TAIL : tap * TAIL + few, :] = weight_ref[
                    3 * tap + column
                ].astype(F32)
            stack = spare[column].astype(BF16)
        rows.append(
            lax.dot_general(
                unit, stack, (((1,), (1,)), ((), ())), preferred_element_type=F32
            )
        )
    return jnp.concatenate(rows, axis=0).astype(BF16)


def stem_kernel(
    where_ref, own_ref, near_ref, far_ref, w_in, w_mid, second, x_ref, first, spare
):
    height, chans, width = own_ref.shape
    inside = sides(where_ref)
    first_core = lax.rem(where_ref[0], 2) == 0
    near, far = near_ref[...].astype(F32), far_ref[...].astype(F32)
    x_ref[...] = jnp.zeros_like(x_ref)
    x_ref[:height, :chans, :] = jnp.where(first_core, far, near).astype(BF16)
    x_ref[height : 2 * height, :chans, :] = own_ref[...]
    x_ref[2 * height :, :chans, :] = jnp.where(first_core, near, far).astype(BF16)

    def full_layer(weight, source, target, low, high, unroll):
        chans = target.shape[1]
        depth = weight.shape[1]

        def step(row, carry):
            lines = source[pl.ds(row, 3)].reshape(depth, width)
            line = across(jnp.dot(weight, lines, preferred_element_type=F32), chans, width)
            target[row] = (silu(line) * inside(row, low, high)).astype(BF16)
            return carry

        lax.fori_loop(0, target.shape[0], step, 0, unroll=unroll)

    full_layer(turned(w_in, spare), x_ref, first, height - 1, 2 * height - 1, first.shape[0])
    full_layer(beside(w_mid), first, second, height - 2, 2 * height - 2, second.shape[0])


def half_pair(source, row, tap):
    return jnp.concatenate([source[row + tap], source[row + tap + 1]], axis=1)


def half_layer(product, target, inside, low, high):
    chans, half_width = target.shape[1], target.shape[2]
    for row in range(0, target.shape[0], 2):
        both = silu(across(product(row), chans, half_width))
        for now in range(2):
            line = both[:, now * half_width : (now + 1) * half_width]
            if row + now < low or row + now >= high:
                line = line * inside(row + now, low, high)
            target[row + now] = line.astype(BF16)


def middle_kernel(where_ref, second, w_down, third, pooled):
    count, chans, width = second.shape
    half_height = (count + 4) // 6
    half_width = width // 2
    inside = sides(where_ref)
    place = lax.broadcasted_iota(jnp.int32, (width, half_width), 0) // 2
    target = lax.broadcasted_iota(jnp.int32, (width, half_width), 1)
    shrink = jnp.where(place == target, 0.25, 0.0).astype(BF16)
    pairs = jnp.dot(
        second[...].reshape(count * chans, width), shrink, preferred_element_type=F32
    ).reshape(count // 2, 2, chans, half_width)
    pooled[...] = (pairs[:, 0] + pairs[:, 1]).astype(BF16)
    weight_down = turned(w_down)

    def down_product(row):
        lines = jnp.concatenate([half_pair(pooled, row, tap) for tap in range(3)], axis=0)
        return jnp.dot(weight_down, lines, preferred_element_type=F32)

    half_layer(down_product, third, inside, half_height - 2, 2 * half_height - 2)


def decoder_kernel(
    where_ref, second, third, w_deep, w_up, w_out, out_ref, fourth, joined, fifth, final, spare
):
    height = out_ref.shape[2]
    half_height = height // 2
    width = out_ref.shape[3]
    half_width = width // 2
    chans = second.shape[1]
    inside = sides(where_ref)

    def deep_product(row):
        total = None
        for tap in range(3):
            part = jnp.dot(
                taps(w_deep, tap), half_pair(third, row, tap), preferred_element_type=F32
            )
            total = part if total is None else total + part
        return total

    half_layer(deep_product, fourth, inside, half_height - 3, 2 * half_height - 3)
    place = lax.broadcasted_iota(jnp.int32, (half_width, width), 0)
    target = lax.broadcasted_iota(jnp.int32, (half_width, width), 1) // 2
    spread = jnp.where(place == target, 1.0, 0.0).astype(BF16)
    deep = fourth.shape[1]
    wide = jnp.dot(
        fourth[...].reshape(-1, half_width), spread, preferred_element_type=F32
    ).astype(BF16).reshape(fourth.shape[0], deep, width)
    for row in range(2 * fourth.shape[0]):
        joined[row, chans:, :] = wide[row // 2]
        joined[row, :chans, :] = second[row + 4]

    def up_step(row, carry):
        total = None
        for tap in range(3):
            part = jnp.dot(taps(w_up, tap), joined[row + tap], preferred_element_type=F32)
            total = part if total is None else total + part
        line = silu(across(total, chans, width))
        fifth[row] = (line * inside(row, 1, height + 1)).astype(BF16)
        return carry

    lax.fori_loop(0, fifth.shape[0], up_step, 0, unroll=fifth.shape[0])

    colours = out_ref.shape[1]
    weight_out = beside_padded(w_out, spare)
    for row in range(height):
        lines = fifth[row : row + 3].reshape(3 * chans, width)
        total = jnp.dot(weight_out, lines, preferred_element_type=F32)
        line = across(total, TAIL, width)
        for colour in range(colours):
            final[colour, row : row + 1, :] = line[colour : colour + 1, :]
    out_ref[0] = final[...].astype(BF16)


def stem(where, own, near, far, w_in, w_mid):
    height, _, width = own.shape
    one = w_mid.shape[1]
    return pl.pallas_call(
        stem_kernel,
        out_shape=jax.ShapeDtypeStruct((3 * height - 4, one, width), BF16),
        in_specs=[smem()] + [vmem()] * 5,
        out_specs=vmem(),
        scratch_shapes=[
            pltpu.VMEM((3 * height, TAIL, width), BF16),
            pltpu.VMEM((3 * height - 2, one, width), BF16),
            pltpu.VMEM((3, 3 * TAIL, one), F32),
        ],
        compiler_params=params(16),
        cost_estimate=pl.CostEstimate(
            flops=1_000_000_000, bytes_accessed=MIB, transcendentals=300_000
        ),
        name="stem",
    )(where, own, near, far, w_in, w_mid)


def middle(where, second, w_down):
    rows, one, width = second.shape
    half = (rows + 4) // 6
    two = w_down.shape[2]
    return pl.pallas_call(
        middle_kernel,
        out_shape=jax.ShapeDtypeStruct((3 * half - 4, two, width // 2), BF16),
        in_specs=[smem()] + [vmem()] * 2,
        out_specs=vmem(),
        scratch_shapes=[pltpu.VMEM((3 * half - 2, one, width // 2), BF16)],
        compiler_params=params(16),
        cost_estimate=pl.CostEstimate(
            flops=500_000_000, bytes_accessed=MIB, transcendentals=100_000
        ),
        name="middle",
    )(where, second, w_down)


def decoder(where, second, third, w_deep, w_up, w_out, height, colours):
    one = second.shape[1]
    two = third.shape[1]
    width = second.shape[2]
    return pl.pallas_call(
        decoder_kernel,
        out_shape=jax.ShapeDtypeStruct((1, colours, height, width), BF16),
        in_specs=[smem()] + [vmem()] * 5,
        out_specs=vmem(),
        scratch_shapes=[
            pltpu.VMEM((third.shape[0] - 2, two, width // 2), BF16),
            pltpu.VMEM((height + 4, one + two, width), BF16),
            pltpu.VMEM((height + 2, one, width), BF16),
            pltpu.VMEM((colours, height, width), F32),
            pltpu.VMEM((3, 3 * TAIL, one), F32),
        ],
        compiler_params=params(16),
        cost_estimate=pl.CostEstimate(
            flops=1_500_000_000, bytes_accessed=MIB, transcendentals=200_000
        ),
        name="decoder",
    )(where, second, third, w_deep, w_up, w_out)


def on_device(
    bricks, sends, cells, fracs, sample_order, pending, w_in, w_mid, w_down, w_deep, w_up, w_out
):
    n_tile = lax.axis_size("tile")
    tile = lax.axis_index("tile")
    n_section = lax.axis_size("section")
    cap = sends.shape[3]
    height = pending.shape[2]
    width = pending.shape[3]
    samples = cells.shape[3]
    slots = n_tile * cap
    per_slot = samples // slots
    padded = -(-per_slot // BLOCK) * BLOCK

    def fill(part):
        if padded != per_slot:
            part = part.reshape(3, slots, per_slot)
            part = jnp.pad(part, ((0, 0), (0, 0), (0, padded - per_slot)))
        return part.reshape(3, slots * padded // LANES, LANES)

    def trim(found):
        if padded == per_slot:
            return found
        return found.reshape(slots, padded)[:, :per_slot].reshape(1, samples // LANES, LANES)

    places = positions(fill(cells), fill(fracs), n_tile)
    places, bricks, pending, tile = lax.optimization_barrier((places, bricks, pending, tile))
    arrived = lax.all_to_all(places, "tile", split_axis=0, concat_axis=0, tiled=True)
    where = jnp.stack([tile, jnp.int32(n_tile)]).astype(jnp.int32)

    mates = [(i, i ^ 1) for i in range(n_tile) if i ^ 1 < n_tile]
    across_chips = [
        pair for i in range(1, n_tile - 1, 2) for pair in ((i, i + 1), (i + 1, i))
    ]
    for_mate = lax.dynamic_slice_in_dim(places, mate_of(tile), 1, 0)
    mate_places = lax.ppermute(for_mate, "tile", mates)
    rows = pending[0].transpose(1, 0, 2)
    near = lax.ppermute(rows, "tile", mates)
    far = lax.ppermute(rows, "tile", across_chips)
    picks = sends[0, 0].T
    colours = w_out.shape[1]
    windows = windows_of(where, picks, bricks, places, mate_places)
    found = sample_values(where, picks, windows, arrived)

    found, rows, near, far = lax.optimization_barrier((found, rows, near, far))
    values = lax.all_to_all(found, "tile", split_axis=0, concat_axis=0, tiled=True)
    second = stem(where, rows, near, far, w_in.transpose(0, 2, 1), w_mid)
    third = middle(where, second, w_down.transpose(0, 2, 1))
    values, third = lax.optimization_barrier((values, third))
    rendered = gbuffer(trim(values), sample_order, height, width)
    rendered, third = lax.optimization_barrier((rendered, third))
    ring = [(i, (i + 1) % n_section) for i in range(n_section)]
    handoff = lax.ppermute(rendered, "section", ring)
    denoised = decoder(where, second, third, w_deep, w_up, w_out, height, colours)
    return (handoff, denoised)


def solution(mesh):
    in_specs = (
        P("tile", None),
        P("section", "tile", None, None),
        P("section", "tile", None, None),
        P("section", "tile", None, None),
        P("section", "tile", None, None),
        P("section", None, "tile", None),
        P(),
        P(),
        P(),
        P(),
        P(),
        P(),
    )
    out_specs = (P("section", None, "tile", None), P("section", None, "tile", None))
    return jax.shard_map(
        on_device, mesh=mesh, in_specs=in_specs, out_specs=out_specs, check_vma=False
    )
```

```python
import functools

import jax
import jax.numpy as jnp
from jax import lax
from jax.experimental import pallas as pl
from jax.experimental.pallas import tpu as pltpu
from jax.sharding import PartitionSpec as P

EDGE = 34
NSP = 4
NRAY = 8
NOS = 2
LANES = 128
BLOCK = 256
STRIDE = 6
WINDOWS = 6
MAIN = 32
TAIL = 16
BRICK_ROWS = WINDOWS * MAIN + TAIL
KDIM = 256

F32 = jnp.float32
BF16 = jnp.bfloat16
MIB = 1024 * 1024


def params(mib):
    return pltpu.CompilerParams(vmem_limit_bytes=mib * MIB)


def vmem():
    return pl.BlockSpec(memory_space=pltpu.VMEM)


def smem():
    return pl.BlockSpec(memory_space=pltpu.SMEM)


def positions_kernel(cells_ref, fracs_ref, out_ref, cells, fracs, found, arrivals, departures):
    owners, rows, _ = out_ref.shape
    lines = rows // 3
    parts = arrivals.shape[1]
    share = owners // parts
    pieces = [(axis, part) for axis in range(3) for part in range(parts)]

    def reads(axis, part):
        span = pl.ds(part * share * lines, share * lines)
        return [
            pltpu.make_async_copy(
                source.at[axis, span], target.at[axis, span], arrivals.at[axis, part, number]
            )
            for number, (source, target) in enumerate(((cells_ref, cells), (fracs_ref, fracs)))
        ]

    def write(axis, part):
        place = (pl.ds(part * share, share), pl.ds(axis * lines, lines))
        return pltpu.make_async_copy(
            found.at[place], out_ref.at[place], departures.at[axis, part]
        )

    for piece in pieces:
        for copy in reads(*piece):
            copy.start()
    for axis, part in pieces:
        for copy in reads(axis, part):
            copy.wait()
        span = slice(part * share * lines, (part + 1) * share * lines)
        place = cells[axis, span].astype(F32) + fracs[axis, span]
        found[part * share : (part + 1) * share, axis * lines : (axis + 1) * lines, :] = (
            place.reshape(share, lines, LANES)
        )
        write(axis, part).start()
    for piece in pieces:
        write(*piece).wait()


def positions(cells, fracs, owners):
    lines = cells.shape[1]
    shape = (owners, 3 * lines // owners, LANES)
    hbm = pl.BlockSpec(memory_space=pltpu.HBM)
    return pl.pallas_call(
        positions_kernel,
        out_shape=jax.ShapeDtypeStruct(shape, F32),
        in_specs=[hbm, hbm],
        out_specs=hbm,
        scratch_shapes=[
            pltpu.VMEM(cells.shape, jnp.int32),
            pltpu.VMEM(fracs.shape, F32),
            pltpu.VMEM(shape, F32),
            pltpu.SemaphoreType.DMA((3, 4, 2)),
            pltpu.SemaphoreType.DMA((3, 4)),
        ],
        compiler_params=params(60),
        cost_estimate=pl.CostEstimate(
            flops=3 * lines * LANES, bytes_accessed=36 * lines * LANES, transcendentals=0
        ),
        name="positions",
    )(cells, fracs)


def mate_of(tile):
    return tile + 1 - 2 * lax.rem(tile, 2)


def windows_kernel(
    where_ref, picks_ref, cube_ref, place_ref, mate_place_ref, out_ref,
    wide, tail, places, sums, arrivals,
):
    tile = where_ref[0]
    near = ((tile, place_ref.at[tile]), (mate_of(tile), mate_place_ref.at[0]))
    copies = [
        pltpu.make_async_copy(source, places.at[i], arrivals.at[i])
        for i, (_, source) in enumerate(near)
    ]
    for copy in copies:
        copy.start()
    count = cube_ref.shape[0]
    plane = EDGE * EDGE
    wide[:, :, plane // LANES * LANES :] = jnp.zeros((count, wide.shape[1], LANES), BF16)
    wide[:, :EDGE, :plane] = cube_ref[...]
    column = lax.broadcasted_iota(jnp.int32, (1, KDIM), 1)
    main = (column // MAIN) * EDGE + column % MAIN
    rest = column - 7 * MAIN
    last = (rest % 8) * EDGE + MAIN + rest // 8
    source = jnp.where(column < 7 * MAIN, main, last)
    unused = (column >= 7 * MAIN) & ((rest % 8 == 7) | (rest >= TAIL))
    source = jnp.where(unused, -(1 << 20), source)
    for window in range(WINDOWS):
        first = window * STRIDE * EDGE
        low = first // LANES * LANES
        length = min(3 * LANES, wide.shape[2] - low)
        place = lax.broadcasted_iota(jnp.int32, (length, KDIM), 0)
        pick = jnp.where(place == source + (first - low), 1.0, 0.0).astype(BF16)
        found = jnp.dot(
            wide[:, :, low : low + length].reshape(-1, length),
            pick,
            preferred_element_type=F32,
        )
        found = found.reshape(count, 48, KDIM)
        out_ref[:count, window * MAIN : (window + 1) * MAIN, :] = found[:, :MAIN, :].astype(BF16)
        tail[:, window : window + 1, :] = found[:, MAIN : MAIN + 1, :]
        tail[:, 8 + window : 9 + window, :] = found[:, MAIN + 1 : MAIN + 2, :]
    for row in (6, 7, 14, 15):
        tail[:, row : row + 1, :] = jnp.zeros((count, 1, KDIM), F32)
    out_ref[:count, WINDOWS * MAIN :, :] = tail[...].astype(BF16)

    for copy in copies:
        copy.wait()
    cap = picks_ref.shape[0]
    lines = places.shape[1] // 3
    part = lines // cap
    height = whole_tiles(lines)
    for i, (renderer, _) in enumerate(near):
        for piece in range(cap):
            brick = out_ref[picks_ref[piece, renderer]]
            slot_sums(brick, places.at[i], sums.at[i], piece * part, part // 2)
    for i in range(len(near)):
        out_ref[count, i * height : (i + 1) * height, :LANES] = line_values(
            sums.at[i], lines, height
        )


def windows_of(where, picks, bricks, places, mate_places):
    count = bricks.shape[0]
    cube = bricks.reshape(count, EDGE, EDGE * EDGE)
    rows = places.shape[1]
    return pl.pallas_call(
        windows_kernel,
        out_shape=jax.ShapeDtypeStruct((count + 1, BRICK_ROWS, KDIM), BF16),
        in_specs=[smem(), smem(), vmem()] + [pl.BlockSpec(memory_space=pl.ANY)] * 2,
        out_specs=vmem(),
        scratch_shapes=[
            pltpu.VMEM((count, 48, 10 * LANES), BF16),
            pltpu.VMEM((count, TAIL, KDIM), F32),
            pltpu.VMEM((2, rows, LANES), F32),
            pltpu.VMEM((2, 8 * rows // 3, LANES), F32),
            pltpu.SemaphoreType.DMA((2,)),
        ],
        compiler_params=params(16),
        cost_estimate=pl.CostEstimate(
            flops=2 * count * 48 * 384 * KDIM * WINDOWS, bytes_accessed=4 * MIB,
            transcendentals=0,
        ),
        name="brick_windows",
    )(where, picks, cube, places, mate_places)


def hat(distance):
    return jnp.maximum(1.0 - jnp.abs(distance), 0.0)


def blend(brick, px, py, pz):
    width = px.shape[1]
    eight = lax.broadcasted_iota(jnp.int32, (8, width), 0).astype(F32)
    places = lax.broadcasted_iota(jnp.int32, (MAIN, width), 0).astype(F32).astype(BF16)

    def tile(rows):
        return jnp.concatenate([rows, rows], axis=0).astype(BF16)

    cell_y = jnp.floor(py)
    frac_y = py - cell_y
    lower, low_share, high_share = tile(cell_y), tile(1.0 - frac_y), tile(frac_y)
    nothing = jnp.zeros((TAIL, width), BF16)
    weight_y = []
    for start in range(0, MAIN, TAIL):
        offset = places[start : start + TAIL] - lower
        weight_y.append(
            jnp.where(offset == 0, low_share, jnp.where(offset == 1, high_share, nothing))
        )
    window = jnp.floor(px * (1.0 / STRIDE))
    weight_x = hat(eight - (px - STRIDE * window))
    parts = []
    for i in range(STRIDE + 1):
        share = tile(jnp.broadcast_to(weight_x[i : i + 1], (8, width)))
        parts += [share * part for part in weight_y]
    tail = [weight_x * hat(MAIN - py), weight_x * jnp.maximum(py - MAIN, 0.0)]
    parts.append(jnp.concatenate(tail, axis=0).astype(BF16))
    plane = jnp.concatenate(parts, axis=0)
    found = jnp.dot(brick[:, : plane.shape[0]], plane, preferred_element_type=F32)
    groups = range(0, MAIN, 8)
    chosen = [found[row : row + 8] for row in groups]
    for other in range(1, WINDOWS):
        here = window == float(other)
        base = other * MAIN
        chosen = [
            jnp.where(here, found[base + row : base + row + 8], old)
            for row, old in zip(groups, chosen)
        ]
    base = WINDOWS * MAIN
    edges = found[base : base + 8] * hat(MAIN - pz)
    edges = edges + found[base + 8 :] * jnp.maximum(pz - MAIN, 0.0)
    total = jnp.where(eight == window, edges, 0.0)
    for row, part in zip(groups, chosen):
        total = total + part * hat((eight + float(row)) - pz)
    return total


def slot_sums(brick, places, sums, first, blocks):
    lines = places.shape[0] // 3
    for step in range(blocks):
        row = first + 2 * step

        def line(axis):
            both = [
                jnp.broadcast_to(places[pl.ds(axis * lines + row + half, 1), :], (8, LANES))
                for half in range(2)
            ]
            return jnp.concatenate(both, axis=1)

        total = blend(brick, line(0), line(1), line(2))
        for half in range(2):
            sums[pl.ds(pl.multiple_of(8 * (row + half), 8), 8), :] = total[
                :, half * LANES : (half + 1) * LANES
            ]


def whole_tiles(lines):
    return -(-lines // TAIL) * TAIL


def line_values(sums, lines, height):
    values = []
    for row in range(0, lines, 8):
        value = sums[pl.ds(8 * row, 8, stride=8), :]
        for other in range(1, 8):
            value = value + sums[pl.ds(8 * row + other, 8, stride=8), :]
        values.append(value)
    if height > lines:
        values.append(jnp.zeros((height - lines, LANES), F32))
    return jnp.concatenate(values, axis=0).astype(BF16)


def samples_kernel(
    where_ref, picks_ref, brick_ref, place_ref, out_ref, bricks, places, sums, own, arrivals,
    own_arrival,
):
    owners, rows, _ = place_ref.shape
    cap = picks_ref.shape[0]
    lines = rows // 3
    part = lines // cap
    turns = owners - 2
    tile = where_ref[0]
    pairs, rest = turns // 2, turns % 2
    own_values = pltpu.make_async_copy(
        brick_ref.at[brick_ref.shape[0] - 1, pl.ds(0, own.shape[0]), pl.ds(0, LANES)],
        own,
        own_arrival,
    )

    def renderer_of(number):
        return lax.rem(2 * (tile // 2) + 2 + number, owners)

    def fetches(turn, members):
        held = turn % 2
        copies = []
        for member in range(members):
            renderer = renderer_of(2 * turn + member)
            copies.append(
                pltpu.make_async_copy(
                    place_ref.at[renderer],
                    places.at[held, member],
                    arrivals.at[held, member, cap],
                )
            )
            for piece in range(cap):
                copies.append(
                    pltpu.make_async_copy(
                        brick_ref.at[picks_ref[piece, renderer]],
                        bricks.at[held, member, piece],
                        arrivals.at[held, member, piece],
                    )
                )
        return copies

    def start(turn, members):
        for copy in fetches(turn, members):
            copy.start()

    def work(turn, members):
        held = turn % 2
        for copy in fetches(turn, members):
            copy.wait()

        if members == 2:
            pl.when(turn + 1 < pairs)(lambda: start(turn + 1, 2))
            if rest:
                pl.when(turn + 1 == pairs)(lambda: start(pairs, 1))
            pl.when(turn == 0)(own_values.start)

        for member in range(members):
            for piece in range(cap):
                slot_sums(
                    bricks[held, member, piece],
                    places.at[held, member],
                    sums.at[member],
                    piece * part,
                    part // 2,
                )
        for member in range(members):
            out_ref[renderer_of(2 * turn + member)] = line_values(
                sums.at[member], lines, lines
            )

    def one_pair(turn, carry):
        work(turn, 2)
        return carry

    if pairs > 0:
        start(0, 2)
    elif rest:
        start(0, 1)
    if pairs <= 4:
        for turn in range(pairs):
            work(turn, 2)
    else:
        lax.fori_loop(0, pairs, one_pair, 0)
    if rest:
        work(pairs, 1)
    if pairs == 0:
        own_values.start()
    own_values.wait()
    height = whole_tiles(lines)
    for i, renderer in enumerate((tile, mate_of(tile))):
        values = own[i * height : (i + 1) * height, :].astype(F32)
        out_ref[renderer] = values[:lines].astype(BF16)


def sample_values(where, picks, windows, places):
    owners, rows, _ = places.shape
    cap = picks.shape[0]
    samples = owners * rows * LANES // 3
    some = pl.BlockSpec(memory_space=pl.ANY)
    return pl.pallas_call(
        samples_kernel,
        out_shape=jax.ShapeDtypeStruct((owners, rows // 3, LANES), BF16),
        in_specs=[smem(), smem(), some, some],
        out_specs=vmem(),
        scratch_shapes=[
            pltpu.VMEM((2, 2, cap, BRICK_ROWS, KDIM), BF16),
            pltpu.VMEM((2, 2, rows, LANES), F32),
            pltpu.VMEM((2, 8 * rows // 3, LANES), F32),
            pltpu.VMEM((2 * whole_tiles(rows // 3), LANES), BF16),
            pltpu.SemaphoreType.DMA((2, 2, cap + 1)),
            pltpu.SemaphoreType.DMA,
        ],
        compiler_params=pltpu.CompilerParams(vmem_limit_bytes=61_600_000),
        cost_estimate=pl.CostEstimate(
            flops=2 * samples * KDIM * BRICK_ROWS, bytes_accessed=3 * MIB,
            transcendentals=0,
        ),
        name="sample_values",
    )(where, picks, windows, places)


def gbuffer_kernel(value_ref, order_ref, out_ref, values):
    values[...] = value_ref[...].astype(F32).reshape(values.shape)
    height = out_ref.shape[2]

    def ray_of(number):
        rows_now = slice(number * height, (number + 1) * height)
        first, second = (
            values[pl.ds(2 * number * height + half, height, stride=2), :] for half in range(2)
        )
        parts = []
        for half in range(2):
            order = order_ref[0, 0, rows_now, half * LANES : (half + 1) * LANES]
            inner = order & (LANES - 1)
            parts.append(
                jnp.where(
                    order < LANES,
                    jnp.take_along_axis(first, inner, axis=1, mode="promise_in_bounds"),
                    jnp.take_along_axis(second, inner, axis=1, mode="promise_in_bounds"),
                )
            )
        return jnp.concatenate(parts, axis=1)

    remain = 1.0
    shade = 0.0
    depth = 0.0
    for step in range(NSP):
        ray = ray_of(step)
        half_tanh = 0.5 * jnp.tanh(ray)
        weight = remain * (0.5 + half_tanh)
        shade = shade + weight * ray
        depth = depth + weight * ((step + 1) / NSP)
        remain = remain * (0.5 - half_tanh)
    occlusion = 0.0
    for ray_number in range(NRAY):
        passing = 1.0
        for step in range(NOS):
            ray = ray_of(NSP + ray_number * NOS + step)
            passing = passing * (0.5 - 0.5 * jnp.tanh(ray))
        occlusion = occlusion + passing
    out_ref[0, 0] = shade.astype(BF16)
    out_ref[0, 1] = (1.0 - remain).astype(BF16)
    out_ref[0, 2] = depth.astype(BF16)
    out_ref[0, 3] = (occlusion * (1.0 / NRAY)).astype(BF16)


def gbuffer(values, order, height, width):
    total = order.shape[2]
    return pl.pallas_call(
        gbuffer_kernel,
        out_shape=jax.ShapeDtypeStruct((1, 4, height, width), BF16),
        in_specs=[vmem(), vmem()],
        out_specs=vmem(),
        scratch_shapes=[pltpu.VMEM((2 * total, LANES), F32)],
        compiler_params=params(16),
        cost_estimate=pl.CostEstimate(
            flops=20 * total * BLOCK, bytes_accessed=8 * total * BLOCK, transcendentals=0
        ),
        name="gbuffer",
    )(values, order)


def silu(field):
    half = 0.5 * field
    return half + half * jnp.tanh(half)


def shifted(rows, steps):
    lane = lax.broadcasted_iota(jnp.int32, (1, LANES), 1)
    edge = lane == (0 if steps == 1 else LANES - 1)
    moved = []
    for row in rows:
        tiles = [row[:, i : i + LANES] for i in range(0, row.shape[1], LANES)]
        tiles = [pltpu.roll(tile, steps % LANES, 1) for tile in tiles]
        for i, tile in enumerate(tiles):
            source = i - steps
            fill = tiles[source] if 0 <= source < len(tiles) else 0.0
            moved.append(jnp.where(edge, fill, tile))
    return jnp.concatenate(moved, axis=1)


def across(total, chans, row_width):
    left, middle, right = (total[i * chans : (i + 1) * chans] for i in range(3))

    def rows_of(part):
        return [part[:, i : i + row_width] for i in range(0, part.shape[1], row_width)]

    return middle + shifted(rows_of(left), 1) + shifted(rows_of(right), -1)


def taps(weight_ref, tap):
    _, out_chans, chans = weight_ref.shape
    return weight_ref[3 * tap : 3 * tap + 3].reshape(3 * out_chans, chans)


def beside(weight_ref):
    return jnp.concatenate([taps(weight_ref, tap) for tap in range(3)], axis=1)


def beside_padded(weight_ref, spare):
    few = weight_ref.shape[1]
    spare[...] = jnp.zeros_like(spare)
    for tap in range(3):
        for column in range(3):
            spare[tap, column * TAIL : column * TAIL + few, :] = weight_ref[
                3 * tap + column
            ].astype(F32)
    return jnp.concatenate([spare[tap].astype(BF16) for tap in range(3)], axis=1)


def sides(where_ref):
    above = jnp.where(where_ref[0] > 0, 1.0, 0.0)
    below = jnp.where(where_ref[0] < where_ref[1] - 1, 1.0, 0.0)

    def inside(row, low, high):
        return jnp.where(row < low, above, jnp.where(row >= high, below, 1.0))

    return inside


def turned(weight_ref, spare=None):
    _, few, out_chans = weight_ref.shape
    here = lax.broadcasted_iota(jnp.int32, (out_chans, out_chans), 0)
    there = lax.broadcasted_iota(jnp.int32, (out_chans, out_chans), 1)
    unit = jnp.where(here == there, 1.0, 0.0).astype(BF16)
    if spare is not None:
        spare[...] = jnp.zeros_like(spare)
    rows = []
    for column in range(3):
        if spare is None:
            stack = jnp.concatenate([weight_ref[3 * tap + column] for tap in range(3)], axis=0)
        else:
            for tap in range(3):
                spare[column, tap * TAIL : tap * TAIL + few, :] = weight_ref[
                    3 * tap + column
                ].astype(F32)
            stack = spare[column].astype(BF16)
        rows.append(
            lax.dot_general(
                unit, stack, (((1,), (1,)), ((), ())), preferred_element_type=F32
            )
        )
    return jnp.concatenate(rows, axis=0).astype(BF16)


def stem_kernel(
    where_ref, own_ref, near_ref, far_ref, w_in, w_mid, second, x_ref, first, spare
):
    height, chans, width = own_ref.shape
    inside = sides(where_ref)
    first_core = lax.rem(where_ref[0], 2) == 0
    near, far = near_ref[...].astype(F32), far_ref[...].astype(F32)
    x_ref[...] = jnp.zeros_like(x_ref)
    x_ref[:height, :chans, :] = jnp.where(first_core, far, near).astype(BF16)
    x_ref[height : 2 * height, :chans, :] = own_ref[...]
    x_ref[2 * height :, :chans, :] = jnp.where(first_core, near, far).astype(BF16)

    def full_layer(weight, source, target, low, high, unroll):
        chans = target.shape[1]
        depth = weight.shape[1]

        def step(row, carry):
            lines = source[pl.ds(row, 3)].reshape(depth, width)
            line = across(jnp.dot(weight, lines, preferred_element_type=F32), chans, width)
            target[row] = (silu(line) * inside(row, low, high)).astype(BF16)
            return carry

        lax.fori_loop(0, target.shape[0], step, 0, unroll=unroll)

    full_layer(turned(w_in, spare), x_ref, first, height - 1, 2 * height - 1, first.shape[0])
    full_layer(beside(w_mid), first, second, height - 2, 2 * height - 2, second.shape[0])


def half_pair(source, row, tap):
    return jnp.concatenate([source[row + tap], source[row + tap + 1]], axis=1)


def half_layer(product, target, inside, low, high):
    chans, half_width = target.shape[1], target.shape[2]
    for row in range(0, target.shape[0], 2):
        both = silu(across(product(row), chans, half_width))
        for now in range(2):
            line = both[:, now * half_width : (now + 1) * half_width]
            if row + now < low or row + now >= high:
                line = line * inside(row + now, low, high)
            target[row + now] = line.astype(BF16)


def middle_kernel(where_ref, second, w_down, third, pooled):
    count, chans, width = second.shape
    half_height = (count + 4) // 6
    half_width = width // 2
    inside = sides(where_ref)
    place = lax.broadcasted_iota(jnp.int32, (width, half_width), 0) // 2
    target = lax.broadcasted_iota(jnp.int32, (width, half_width), 1)
    shrink = jnp.where(place == target, 0.25, 0.0).astype(BF16)
    pairs = jnp.dot(
        second[...].reshape(count * chans, width), shrink, preferred_element_type=F32
    ).reshape(count // 2, 2, chans, half_width)
    pooled[...] = (pairs[:, 0] + pairs[:, 1]).astype(BF16)
    weight_down = turned(w_down)

    def down_product(row):
        lines = jnp.concatenate([half_pair(pooled, row, tap) for tap in range(3)], axis=0)
        return jnp.dot(weight_down, lines, preferred_element_type=F32)

    half_layer(down_product, third, inside, half_height - 2, 2 * half_height - 2)


def decoder_kernel(
    where_ref, second, third, w_deep, w_up, w_out, out_ref, fourth, joined, fifth, final, spare
):
    height = out_ref.shape[2]
    half_height = height // 2
    width = out_ref.shape[3]
    half_width = width // 2
    chans = second.shape[1]
    inside = sides(where_ref)

    def deep_product(row):
        total = None
        for tap in range(3):
            part = jnp.dot(
                taps(w_deep, tap), half_pair(third, row, tap), preferred_element_type=F32
            )
            total = part if total is None else total + part
        return total

    half_layer(deep_product, fourth, inside, half_height - 3, 2 * half_height - 3)
    place = lax.broadcasted_iota(jnp.int32, (half_width, width), 0)
    target = lax.broadcasted_iota(jnp.int32, (half_width, width), 1) // 2
    spread = jnp.where(place == target, 1.0, 0.0).astype(BF16)
    deep = fourth.shape[1]
    wide = jnp.dot(
        fourth[...].reshape(-1, half_width), spread, preferred_element_type=F32
    ).astype(BF16).reshape(fourth.shape[0], deep, width)
    for row in range(2 * fourth.shape[0]):
        joined[row, chans:, :] = wide[row // 2]
        joined[row, :chans, :] = second[row + 4]

    def up_step(row, carry):
        total = None
        for tap in range(3):
            part = jnp.dot(taps(w_up, tap), joined[row + tap], preferred_element_type=F32)
            total = part if total is None else total + part
        line = silu(across(total, chans, width))
        fifth[row] = (line * inside(row, 1, height + 1)).astype(BF16)
        return carry

    lax.fori_loop(0, fifth.shape[0], up_step, 0, unroll=fifth.shape[0])

    colours = out_ref.shape[1]
    weight_out = beside_padded(w_out, spare)
    for row in range(height):
        lines = fifth[row : row + 3].reshape(3 * chans, width)
        total = jnp.dot(weight_out, lines, preferred_element_type=F32)
        line = across(total, TAIL, width)
        for colour in range(colours):
            final[colour, row : row + 1, :] = line[colour : colour + 1, :]
    out_ref[0] = final[...].astype(BF16)


def stem(where, own, near, far, w_in, w_mid):
    height, _, width = own.shape
    one = w_mid.shape[1]
    return pl.pallas_call(
        stem_kernel,
        out_shape=jax.ShapeDtypeStruct((3 * height - 4, one, width), BF16),
        in_specs=[smem()] + [vmem()] * 5,
        out_specs=vmem(),
        scratch_shapes=[
            pltpu.VMEM((3 * height, TAIL, width), BF16),
            pltpu.VMEM((3 * height - 2, one, width), BF16),
            pltpu.VMEM((3, 3 * TAIL, one), F32),
        ],
        compiler_params=params(16),
        cost_estimate=pl.CostEstimate(
            flops=1_000_000_000, bytes_accessed=MIB, transcendentals=300_000
        ),
        name="stem",
    )(where, own, near, far, w_in, w_mid)


def middle(where, second, w_down):
    rows, one, width = second.shape
    half = (rows + 4) // 6
    two = w_down.shape[2]
    return pl.pallas_call(
        middle_kernel,
        out_shape=jax.ShapeDtypeStruct((3 * half - 4, two, width // 2), BF16),
        in_specs=[smem()] + [vmem()] * 2,
        out_specs=vmem(),
        scratch_shapes=[pltpu.VMEM((3 * half - 2, one, width // 2), BF16)],
        compiler_params=params(16),
        cost_estimate=pl.CostEstimate(
            flops=500_000_000, bytes_accessed=MIB, transcendentals=100_000
        ),
        name="middle",
    )(where, second, w_down)


def decoder(where, second, third, w_deep, w_up, w_out, height, colours):
    one = second.shape[1]
    two = third.shape[1]
    width = second.shape[2]
    return pl.pallas_call(
        decoder_kernel,
        out_shape=jax.ShapeDtypeStruct((1, colours, height, width), BF16),
        in_specs=[smem()] + [vmem()] * 5,
        out_specs=vmem(),
        scratch_shapes=[
            pltpu.VMEM((third.shape[0] - 2, two, width // 2), BF16),
            pltpu.VMEM((height + 4, one + two, width), BF16),
            pltpu.VMEM((height + 2, one, width), BF16),
            pltpu.VMEM((colours, height, width), F32),
            pltpu.VMEM((3, 3 * TAIL, one), F32),
        ],
        compiler_params=params(16),
        cost_estimate=pl.CostEstimate(
            flops=1_500_000_000, bytes_accessed=MIB, transcendentals=200_000
        ),
        name="decoder",
    )(where, second, third, w_deep, w_up, w_out)


def on_device(
    bricks, sends, cells, fracs, sample_order, pending, w_in, w_mid, w_down, w_deep, w_up, w_out
):
    n_tile = lax.axis_size("tile")
    tile = lax.axis_index("tile")
    n_section = lax.axis_size("section")
    cap = sends.shape[3]
    height = pending.shape[2]
    width = pending.shape[3]
    samples = cells.shape[3]
    slots = n_tile * cap
    per_slot = samples // slots
    padded = -(-per_slot // BLOCK) * BLOCK

    def fill(part):
        if padded != per_slot:
            part = part.reshape(3, slots, per_slot)
            part = jnp.pad(part, ((0, 0), (0, 0), (0, padded - per_slot)))
        return part.reshape(3, slots * padded // LANES, LANES)

    def trim(found):
        if padded == per_slot:
            return found
        return found.reshape(slots, padded)[:, :per_slot].reshape(1, samples // LANES, LANES)

    places = positions(fill(cells), fill(fracs), n_tile)
    places, bricks, pending, tile = lax.optimization_barrier((places, bricks, pending, tile))
    arrived = lax.all_to_all(places, "tile", split_axis=0, concat_axis=0, tiled=True)
    where = jnp.stack([tile, jnp.int32(n_tile)]).astype(jnp.int32)

    mates = [(i, i ^ 1) for i in range(n_tile) if i ^ 1 < n_tile]
    across_chips = [
        pair for i in range(1, n_tile - 1, 2) for pair in ((i, i + 1), (i + 1, i))
    ]
    for_mate = lax.dynamic_slice_in_dim(places, mate_of(tile), 1, 0)
    mate_places = lax.ppermute(for_mate, "tile", mates)
    rows = pending[0].transpose(1, 0, 2)
    near = lax.ppermute(rows, "tile", mates)
    far = lax.ppermute(rows, "tile", across_chips)
    picks = sends[0, 0].T
    colours = w_out.shape[1]
    windows = windows_of(where, picks, bricks, places, mate_places)
    found = sample_values(where, picks, windows, arrived)

    found, rows, near, far = lax.optimization_barrier((found, rows, near, far))
    values = lax.all_to_all(found, "tile", split_axis=0, concat_axis=0, tiled=True)
    second = stem(where, rows, near, far, w_in.transpose(0, 2, 1), w_mid)
    third = middle(where, second, w_down.transpose(0, 2, 1))
    values, third = lax.optimization_barrier((values, third))
    rendered = gbuffer(trim(values), sample_order, height, width)
    rendered, third = lax.optimization_barrier((rendered, third))
    ring = [(i, (i + 1) % n_section) for i in range(n_section)]
    handoff = lax.ppermute(rendered, "section", ring)
    denoised = decoder(where, second, third, w_deep, w_up, w_out, height, colours)
    return (handoff, denoised)


def solution(mesh):
    in_specs = (
        P("tile", None),
        P("section", "tile", None, None),
        P("section", "tile", None, None),
        P("section", "tile", None, None),
        P("section", "tile", None, None),
        P("section", None, "tile", None),
        P(),
        P(),
        P(),
        P(),
        P(),
        P(),
    )
    out_specs = (P("section", None, "tile", None), P("section", None, "tile", None))
    return jax.shard_map(
        on_device, mesh=mesh, in_specs=in_specs, out_specs=out_specs, check_vma=False
    )
```

```python
import functools

import jax
import jax.numpy as jnp
from jax import lax
from jax.experimental import pallas as pl
from jax.experimental.pallas import tpu as pltpu
from jax.sharding import PartitionSpec as P

EDGE = 34
NSP = 4
NRAY = 8
NOS = 2
LANES = 128
BLOCK = 256
STRIDE = 6
WINDOWS = 6
MAIN = 32
TAIL = 16
BRICK_ROWS = WINDOWS * MAIN + TAIL
KDIM = 256

F32 = jnp.float32
BF16 = jnp.bfloat16
MIB = 1024 * 1024


def params(mib):
    return pltpu.CompilerParams(vmem_limit_bytes=mib * MIB)


def vmem():
    return pl.BlockSpec(memory_space=pltpu.VMEM)


def smem():
    return pl.BlockSpec(memory_space=pltpu.SMEM)


def positions_kernel(cells_ref, fracs_ref, out_ref, cells, fracs, found, arrivals, departures):
    owners, rows, _ = out_ref.shape
    lines = rows // 3
    parts = arrivals.shape[1]
    share = owners // parts
    pieces = [(axis, part) for axis in range(3) for part in range(parts)]

    def reads(axis, part):
        span = pl.ds(part * share * lines, share * lines)
        return [
            pltpu.make_async_copy(
                source.at[axis, span], target.at[axis, span], arrivals.at[axis, part, number]
            )
            for number, (source, target) in enumerate(((cells_ref, cells), (fracs_ref, fracs)))
        ]

    def write(axis, part):
        place = (pl.ds(part * share, share), pl.ds(axis * lines, lines))
        return pltpu.make_async_copy(
            found.at[place], out_ref.at[place], departures.at[axis, part]
        )

    for piece in pieces:
        for copy in reads(*piece):
            copy.start()
    for axis, part in pieces:
        for copy in reads(axis, part):
            copy.wait()
        span = slice(part * share * lines, (part + 1) * share * lines)
        place = cells[axis, span].astype(F32) + fracs[axis, span]
        found[part * share : (part + 1) * share, axis * lines : (axis + 1) * lines, :] = (
            place.reshape(share, lines, LANES)
        )
        write(axis, part).start()
    for piece in pieces:
        write(*piece).wait()


def positions(cells, fracs, owners):
    lines = cells.shape[1]
    shape = (owners, 3 * lines // owners, LANES)
    hbm = pl.BlockSpec(memory_space=pltpu.HBM)
    return pl.pallas_call(
        positions_kernel,
        out_shape=jax.ShapeDtypeStruct(shape, F32),
        in_specs=[hbm, hbm],
        out_specs=hbm,
        scratch_shapes=[
            pltpu.VMEM(cells.shape, jnp.int32),
            pltpu.VMEM(fracs.shape, F32),
            pltpu.VMEM(shape, F32),
            pltpu.SemaphoreType.DMA((3, 4, 2)),
            pltpu.SemaphoreType.DMA((3, 4)),
        ],
        compiler_params=params(60),
        cost_estimate=pl.CostEstimate(
            flops=3 * lines * LANES, bytes_accessed=36 * lines * LANES, transcendentals=0
        ),
        name="positions",
    )(cells, fracs)


def mate_of(tile):
    return tile + 1 - 2 * lax.rem(tile, 2)


def windows_kernel(
    where_ref, picks_ref, cube_ref, place_ref, mate_place_ref, out_ref,
    wide, tail, places, sums, arrivals,
):
    tile = where_ref[0]
    near = ((tile, place_ref.at[tile]), (mate_of(tile), mate_place_ref.at[0]))
    copies = [
        pltpu.make_async_copy(source, places.at[i], arrivals.at[i])
        for i, (_, source) in enumerate(near)
    ]
    for copy in copies:
        copy.start()
    count = cube_ref.shape[0]
    plane = EDGE * EDGE
    wide[:, :, plane // LANES * LANES :] = jnp.zeros((count, wide.shape[1], LANES), BF16)
    wide[:, :EDGE, :plane] = cube_ref[...]
    column = lax.broadcasted_iota(jnp.int32, (1, KDIM), 1)
    main = (column // MAIN) * EDGE + column % MAIN
    rest = column - 7 * MAIN
    last = (rest % 8) * EDGE + MAIN + rest // 8
    source = jnp.where(column < 7 * MAIN, main, last)
    unused = (column >= 7 * MAIN) & ((rest % 8 == 7) | (rest >= TAIL))
    source = jnp.where(unused, -(1 << 20), source)
    for window in range(WINDOWS):
        first = window * STRIDE * EDGE
        low = first // LANES * LANES
        length = min(3 * LANES, wide.shape[2] - low)
        place = lax.broadcasted_iota(jnp.int32, (length, KDIM), 0)
        pick = jnp.where(place == source + (first - low), 1.0, 0.0).astype(BF16)
        found = jnp.dot(
            wide[:, :, low : low + length].reshape(-1, length),
            pick,
            preferred_element_type=F32,
        )
        found = found.reshape(count, 48, KDIM)
        out_ref[:count, window * MAIN : (window + 1) * MAIN, :] = found[:, :MAIN, :].astype(BF16)
        tail[:, window : window + 1, :] = found[:, MAIN : MAIN + 1, :]
        tail[:, 8 + window : 9 + window, :] = found[:, MAIN + 1 : MAIN + 2, :]
    for row in (6, 7, 14, 15):
        tail[:, row : row + 1, :] = jnp.zeros((count, 1, KDIM), F32)
    out_ref[:count, WINDOWS * MAIN :, :] = tail[...].astype(BF16)

    for copy in copies:
        copy.wait()
    cap = picks_ref.shape[0]
    lines = places.shape[1] // 3
    part = lines // cap
    height = whole_tiles(lines)
    for i, (renderer, _) in enumerate(near):
        for piece in range(cap):
            brick = out_ref[picks_ref[piece, renderer]]
            slot_sums(brick, places.at[i], sums.at[i], piece * part, part // 2)
    for i in range(len(near)):
        out_ref[count, i * height : (i + 1) * height, :LANES] = line_values(
            sums.at[i], lines, height
        )


def windows_of(where, picks, bricks, places, mate_places):
    count = bricks.shape[0]
    cube = bricks.reshape(count, EDGE, EDGE * EDGE)
    rows = places.shape[1]
    return pl.pallas_call(
        windows_kernel,
        out_shape=jax.ShapeDtypeStruct((count + 1, BRICK_ROWS, KDIM), BF16),
        in_specs=[smem(), smem(), vmem()] + [pl.BlockSpec(memory_space=pl.ANY)] * 2,
        out_specs=vmem(),
        scratch_shapes=[
            pltpu.VMEM((count, 48, 10 * LANES), BF16),
            pltpu.VMEM((count, TAIL, KDIM), F32),
            pltpu.VMEM((2, rows, LANES), F32),
            pltpu.VMEM((2, 8 * rows // 3, LANES), F32),
            pltpu.SemaphoreType.DMA((2,)),
        ],
        compiler_params=params(16),
        cost_estimate=pl.CostEstimate(
            flops=2 * count * 48 * 384 * KDIM * WINDOWS, bytes_accessed=4 * MIB,
            transcendentals=0,
        ),
        name="brick_windows",
    )(where, picks, cube, places, mate_places)


def hat(distance):
    return jnp.maximum(1.0 - jnp.abs(distance), 0.0)


def blend(brick, px, py, pz):
    width = px.shape[1]
    eight = lax.broadcasted_iota(jnp.int32, (8, width), 0).astype(F32)
    places = lax.broadcasted_iota(jnp.int32, (MAIN, width), 0).astype(F32).astype(BF16)

    def tile(rows):
        return jnp.concatenate([rows, rows], axis=0).astype(BF16)

    cell_y = jnp.floor(py)
    frac_y = py - cell_y
    lower, upper = tile(cell_y), tile(cell_y + 1.0)
    low_share, high_share = tile(1.0 - frac_y), tile(frac_y)
    nothing = jnp.zeros((TAIL, width), BF16)
    weight_y = []
    for start in range(0, MAIN, TAIL):
        here = places[start : start + TAIL]
        weight_y.append(
            jnp.where(here == lower, low_share, jnp.where(here == upper, high_share, nothing))
        )
    window = jnp.floor(px * (1.0 / STRIDE))
    weight_x = hat(eight - (px - STRIDE * window))
    parts = []
    for i in range(STRIDE + 1):
        share = tile(jnp.broadcast_to(weight_x[i : i + 1], (8, width)))
        parts += [share * part for part in weight_y]
    tail = [weight_x * hat(MAIN - py), weight_x * jnp.maximum(py - MAIN, 0.0)]
    parts.append(jnp.concatenate(tail, axis=0).astype(BF16))
    plane = jnp.concatenate(parts, axis=0)
    found = jnp.dot(brick[:, : plane.shape[0]], plane, preferred_element_type=F32)
    groups = range(0, MAIN, 8)
    chosen = [found[row : row + 8] for row in groups]
    for other in range(1, WINDOWS):
        here = window == float(other)
        base = other * MAIN
        chosen = [
            jnp.where(here, found[base + row : base + row + 8], old)
            for row, old in zip(groups, chosen)
        ]
    base = WINDOWS * MAIN
    edges = found[base : base + 8] * hat(MAIN - pz)
    edges = edges + found[base + 8 :] * jnp.maximum(pz - MAIN, 0.0)
    total = jnp.where(eight == window, edges, 0.0)
    for row, part in zip(groups, chosen):
        total = total + part * hat((eight + float(row)) - pz)
    return total


def slot_sums(brick, places, sums, first, blocks):
    lines = places.shape[0] // 3
    together = 2 if blocks % 2 == 0 else 1
    halves = 2 * together
    for step in range(0, blocks, together):
        row = first + 2 * step

        def line(axis):
            parts = [
                jnp.broadcast_to(places[pl.ds(axis * lines + row + half, 1), :], (8, LANES))
                for half in range(halves)
            ]
            return jnp.concatenate(parts, axis=1)

        total = blend(brick, line(0), line(1), line(2))
        for half in range(halves):
            sums[pl.ds(pl.multiple_of(8 * (row + half), 8), 8), :] = total[
                :, half * LANES : (half + 1) * LANES
            ]


def whole_tiles(lines):
    return -(-lines // TAIL) * TAIL


def line_values(sums, lines, height):
    values = []
    for row in range(0, lines, 8):
        value = sums[pl.ds(8 * row, 8, stride=8), :]
        for other in range(1, 8):
            value = value + sums[pl.ds(8 * row + other, 8, stride=8), :]
        values.append(value)
    if height > lines:
        values.append(jnp.zeros((height - lines, LANES), F32))
    return jnp.concatenate(values, axis=0).astype(BF16)


def samples_kernel(
    where_ref, picks_ref, brick_ref, place_ref, out_ref, bricks, places, sums, own, arrivals,
    own_arrival,
):
    owners, rows, _ = place_ref.shape
    cap = picks_ref.shape[0]
    lines = rows // 3
    part = lines // cap
    turns = owners - 2
    tile = where_ref[0]
    pairs, rest = turns // 2, turns % 2
    own_values = pltpu.make_async_copy(
        brick_ref.at[brick_ref.shape[0] - 1, pl.ds(0, own.shape[0]), pl.ds(0, LANES)],
        own,
        own_arrival,
    )

    def renderer_of(number):
        return lax.rem(2 * (tile // 2) + 2 + number, owners)

    def fetches(turn, members):
        held = turn % 2
        copies = []
        for member in range(members):
            renderer = renderer_of(2 * turn + member)
            copies.append(
                pltpu.make_async_copy(
                    place_ref.at[renderer],
                    places.at[held, member],
                    arrivals.at[held, member, cap],
                )
            )
            for piece in range(cap):
                copies.append(
                    pltpu.make_async_copy(
                        brick_ref.at[picks_ref[piece, renderer]],
                        bricks.at[held, member, piece],
                        arrivals.at[held, member, piece],
                    )
                )
        return copies

    def start(turn, members):
        for copy in fetches(turn, members):
            copy.start()

    def work(turn, members):
        held = turn % 2
        for copy in fetches(turn, members):
            copy.wait()

        if members == 2:
            pl.when(turn + 1 < pairs)(lambda: start(turn + 1, 2))
            if rest:
                pl.when(turn + 1 == pairs)(lambda: start(pairs, 1))
            pl.when(turn == 0)(own_values.start)

        for member in range(members):
            for piece in range(cap):
                slot_sums(
                    bricks[held, member, piece],
                    places.at[held, member],
                    sums.at[member],
                    piece * part,
                    part // 2,
                )
        for member in range(members):
            out_ref[renderer_of(2 * turn + member)] = line_values(
                sums.at[member], lines, lines
            )

    def one_pair(turn, carry):
        work(turn, 2)
        return carry

    if pairs > 0:
        start(0, 2)
    elif rest:
        start(0, 1)
    lax.fori_loop(0, pairs, one_pair, 0)
    if rest:
        work(pairs, 1)
    if pairs == 0:
        own_values.start()
    own_values.wait()
    height = whole_tiles(lines)
    for i, renderer in enumerate((tile, mate_of(tile))):
        values = own[i * height : (i + 1) * height, :].astype(F32)
        out_ref[renderer] = values[:lines].astype(BF16)


def sample_values(where, picks, windows, places):
    owners, rows, _ = places.shape
    cap = picks.shape[0]
    samples = owners * rows * LANES // 3
    some = pl.BlockSpec(memory_space=pl.ANY)
    return pl.pallas_call(
        samples_kernel,
        out_shape=jax.ShapeDtypeStruct((owners, rows // 3, LANES), BF16),
        in_specs=[smem(), smem(), some, some],
        out_specs=vmem(),
        scratch_shapes=[
            pltpu.VMEM((2, 2, cap, BRICK_ROWS, KDIM), BF16),
            pltpu.VMEM((2, 2, rows, LANES), F32),
            pltpu.VMEM((2, 8 * rows // 3, LANES), F32),
            pltpu.VMEM((2 * whole_tiles(rows // 3), LANES), BF16),
            pltpu.SemaphoreType.DMA((2, 2, cap + 1)),
            pltpu.SemaphoreType.DMA,
        ],
        compiler_params=pltpu.CompilerParams(vmem_limit_bytes=61_600_000),
        cost_estimate=pl.CostEstimate(
            flops=2 * samples * KDIM * BRICK_ROWS, bytes_accessed=3 * MIB,
            transcendentals=0,
        ),
        name="sample_values",
    )(where, picks, windows, places)


def gbuffer_kernel(value_ref, order_ref, out_ref, values):
    values[...] = value_ref[...].astype(F32).reshape(values.shape)
    height = out_ref.shape[2]

    def ray_of(number):
        rows_now = slice(number * height, (number + 1) * height)
        first, second = (
            values[pl.ds(2 * number * height + half, height, stride=2), :] for half in range(2)
        )
        parts = []
        for half in range(2):
            order = order_ref[0, 0, rows_now, half * LANES : (half + 1) * LANES]
            inner = order & (LANES - 1)
            parts.append(
                jnp.where(
                    order < LANES,
                    jnp.take_along_axis(first, inner, axis=1, mode="promise_in_bounds"),
                    jnp.take_along_axis(second, inner, axis=1, mode="promise_in_bounds"),
                )
            )
        return jnp.concatenate(parts, axis=1)

    remain = 1.0
    shade = 0.0
    depth = 0.0
    for step in range(NSP):
        ray = ray_of(step)
        half_tanh = 0.5 * jnp.tanh(ray)
        weight = remain * (0.5 + half_tanh)
        shade = shade + weight * ray
        depth = depth + weight * ((step + 1) / NSP)
        remain = remain * (0.5 - half_tanh)
    occlusion = 0.0
    for ray_number in range(NRAY):
        passing = 1.0
        for step in range(NOS):
            ray = ray_of(NSP + ray_number * NOS + step)
            passing = passing * (0.5 - 0.5 * jnp.tanh(ray))
        occlusion = occlusion + passing
    out_ref[0, 0] = shade.astype(BF16)
    out_ref[0, 1] = (1.0 - remain).astype(BF16)
    out_ref[0, 2] = depth.astype(BF16)
    out_ref[0, 3] = (occlusion * (1.0 / NRAY)).astype(BF16)


def gbuffer(values, order, height, width):
    total = order.shape[2]
    return pl.pallas_call(
        gbuffer_kernel,
        out_shape=jax.ShapeDtypeStruct((1, 4, height, width), BF16),
        in_specs=[vmem(), vmem()],
        out_specs=vmem(),
        scratch_shapes=[pltpu.VMEM((2 * total, LANES), F32)],
        compiler_params=params(16),
        cost_estimate=pl.CostEstimate(
            flops=20 * total * BLOCK, bytes_accessed=8 * total * BLOCK, transcendentals=0
        ),
        name="gbuffer",
    )(values, order)


def silu(field):
    half = 0.5 * field
    return half + half * jnp.tanh(half)


def shifted(rows, steps):
    lane = lax.broadcasted_iota(jnp.int32, (1, LANES), 1)
    edge = lane == (0 if steps == 1 else LANES - 1)
    moved = []
    for row in rows:
        tiles = [row[:, i : i + LANES] for i in range(0, row.shape[1], LANES)]
        tiles = [pltpu.roll(tile, steps % LANES, 1) for tile in tiles]
        for i, tile in enumerate(tiles):
            source = i - steps
            fill = tiles[source] if 0 <= source < len(tiles) else 0.0
            moved.append(jnp.where(edge, fill, tile))
    return jnp.concatenate(moved, axis=1)


def across(total, chans, row_width):
    left, middle, right = (total[i * chans : (i + 1) * chans] for i in range(3))

    def rows_of(part):
        return [part[:, i : i + row_width] for i in range(0, part.shape[1], row_width)]

    return middle + shifted(rows_of(left), 1) + shifted(rows_of(right), -1)


def taps(weight_ref, tap):
    _, out_chans, chans = weight_ref.shape
    return weight_ref[3 * tap : 3 * tap + 3].reshape(3 * out_chans, chans)


def beside(weight_ref):
    return jnp.concatenate([taps(weight_ref, tap) for tap in range(3)], axis=1)


def beside_padded(weight_ref, spare):
    few = weight_ref.shape[1]
    spare[...] = jnp.zeros_like(spare)
    for tap in range(3):
        for column in range(3):
            spare[tap, column * TAIL : column * TAIL + few, :] = weight_ref[
                3 * tap + column
            ].astype(F32)
    return jnp.concatenate([spare[tap].astype(BF16) for tap in range(3)], axis=1)


def sides(where_ref):
    above = jnp.where(where_ref[0] > 0, 1.0, 0.0)
    below = jnp.where(where_ref[0] < where_ref[1] - 1, 1.0, 0.0)

    def inside(row, low, high):
        return jnp.where(row < low, above, jnp.where(row >= high, below, 1.0))

    return inside


def turned(weight_ref, spare=None):
    _, few, out_chans = weight_ref.shape
    here = lax.broadcasted_iota(jnp.int32, (out_chans, out_chans), 0)
    there = lax.broadcasted_iota(jnp.int32, (out_chans, out_chans), 1)
    unit = jnp.where(here == there, 1.0, 0.0).astype(BF16)
    if spare is not None:
        spare[...] = jnp.zeros_like(spare)
    rows = []
    for column in range(3):
        if spare is None:
            stack = jnp.concatenate([weight_ref[3 * tap + column] for tap in range(3)], axis=0)
        else:
            for tap in range(3):
                spare[column, tap * TAIL : tap * TAIL + few, :] = weight_ref[
                    3 * tap + column
                ].astype(F32)
            stack = spare[column].astype(BF16)
        rows.append(
            lax.dot_general(
                unit, stack, (((1,), (1,)), ((), ())), preferred_element_type=F32
            )
        )
    return jnp.concatenate(rows, axis=0).astype(BF16)


def stem_kernel(
    where_ref, own_ref, near_ref, far_ref, w_in, w_mid, second, x_ref, first, spare
):
    height, chans, width = own_ref.shape
    inside = sides(where_ref)
    first_core = lax.rem(where_ref[0], 2) == 0
    near, far = near_ref[...].astype(F32), far_ref[...].astype(F32)
    x_ref[...] = jnp.zeros_like(x_ref)
    x_ref[:height, :chans, :] = jnp.where(first_core, far, near).astype(BF16)
    x_ref[height : 2 * height, :chans, :] = own_ref[...]
    x_ref[2 * height :, :chans, :] = jnp.where(first_core, near, far).astype(BF16)

    def full_layer(weight, source, target, low, high, unroll):
        chans = target.shape[1]
        depth = weight.shape[1]

        def step(row, carry):
            lines = source[pl.ds(row, 3)].reshape(depth, width)
            line = across(jnp.dot(weight, lines, preferred_element_type=F32), chans, width)
            target[row] = (silu(line) * inside(row, low, high)).astype(BF16)
            return carry

        lax.fori_loop(0, target.shape[0], step, 0, unroll=unroll)

    full_layer(turned(w_in, spare), x_ref, first, height - 1, 2 * height - 1, first.shape[0])
    full_layer(beside(w_mid), first, second, height - 2, 2 * height - 2, second.shape[0])


def half_pair(source, row, tap):
    return jnp.concatenate([source[row + tap], source[row + tap + 1]], axis=1)


def half_layer(product, target, inside, low, high):
    chans, half_width = target.shape[1], target.shape[2]
    for row in range(0, target.shape[0], 2):
        both = silu(across(product(row), chans, half_width))
        for now in range(2):
            line = both[:, now * half_width : (now + 1) * half_width]
            if row + now < low or row + now >= high:
                line = line * inside(row + now, low, high)
            target[row + now] = line.astype(BF16)


def middle_kernel(where_ref, second, w_down, third, pooled):
    count, chans, width = second.shape
    half_height = (count + 4) // 6
    half_width = width // 2
    inside = sides(where_ref)
    place = lax.broadcasted_iota(jnp.int32, (width, half_width), 0) // 2
    target = lax.broadcasted_iota(jnp.int32, (width, half_width), 1)
    shrink = jnp.where(place == target, 0.25, 0.0).astype(BF16)
    pairs = jnp.dot(
        second[...].reshape(count * chans, width), shrink, preferred_element_type=F32
    ).reshape(count // 2, 2, chans, half_width)
    pooled[...] = (pairs[:, 0] + pairs[:, 1]).astype(BF16)
    weight_down = turned(w_down)

    def down_product(row):
        lines = jnp.concatenate([half_pair(pooled, row, tap) for tap in range(3)], axis=0)
        return jnp.dot(weight_down, lines, preferred_element_type=F32)

    half_layer(down_product, third, inside, half_height - 2, 2 * half_height - 2)


def decoder_kernel(
    where_ref, second, third, w_deep, w_up, w_out, out_ref, fourth, joined, fifth, final, spare
):
    height = out_ref.shape[2]
    half_height = height // 2
    width = out_ref.shape[3]
    half_width = width // 2
    chans = second.shape[1]
    inside = sides(where_ref)

    def deep_product(row):
        total = None
        for tap in range(3):
            part = jnp.dot(
                taps(w_deep, tap), half_pair(third, row, tap), preferred_element_type=F32
            )
            total = part if total is None else total + part
        return total

    half_layer(deep_product, fourth, inside, half_height - 3, 2 * half_height - 3)
    place = lax.broadcasted_iota(jnp.int32, (half_width, width), 0)
    target = lax.broadcasted_iota(jnp.int32, (half_width, width), 1) // 2
    spread = jnp.where(place == target, 1.0, 0.0).astype(BF16)
    deep = fourth.shape[1]
    wide = jnp.dot(
        fourth[...].reshape(-1, half_width), spread, preferred_element_type=F32
    ).astype(BF16).reshape(fourth.shape[0], deep, width)
    for row in range(2 * fourth.shape[0]):
        joined[row, chans:, :] = wide[row // 2]
        joined[row, :chans, :] = second[row + 4]

    def up_step(row, carry):
        total = None
        for tap in range(3):
            part = jnp.dot(taps(w_up, tap), joined[row + tap], preferred_element_type=F32)
            total = part if total is None else total + part
        line = silu(across(total, chans, width))
        fifth[row] = (line * inside(row, 1, height + 1)).astype(BF16)
        return carry

    lax.fori_loop(0, fifth.shape[0], up_step, 0, unroll=fifth.shape[0])

    colours = out_ref.shape[1]
    weight_out = beside_padded(w_out, spare)
    for row in range(height):
        lines = fifth[row : row + 3].reshape(3 * chans, width)
        total = jnp.dot(weight_out, lines, preferred_element_type=F32)
        line = across(total, TAIL, width)
        for colour in range(colours):
            final[colour, row : row + 1, :] = line[colour : colour + 1, :]
    out_ref[0] = final[...].astype(BF16)


def stem(where, own, near, far, w_in, w_mid):
    height, _, width = own.shape
    one = w_mid.shape[1]
    return pl.pallas_call(
        stem_kernel,
        out_shape=jax.ShapeDtypeStruct((3 * height - 4, one, width), BF16),
        in_specs=[smem()] + [vmem()] * 5,
        out_specs=vmem(),
        scratch_shapes=[
            pltpu.VMEM((3 * height, TAIL, width), BF16),
            pltpu.VMEM((3 * height - 2, one, width), BF16),
            pltpu.VMEM((3, 3 * TAIL, one), F32),
        ],
        compiler_params=params(16),
        cost_estimate=pl.CostEstimate(
            flops=1_000_000_000, bytes_accessed=MIB, transcendentals=300_000
        ),
        name="stem",
    )(where, own, near, far, w_in, w_mid)


def middle(where, second, w_down):
    rows, one, width = second.shape
    half = (rows + 4) // 6
    two = w_down.shape[2]
    return pl.pallas_call(
        middle_kernel,
        out_shape=jax.ShapeDtypeStruct((3 * half - 4, two, width // 2), BF16),
        in_specs=[smem()] + [vmem()] * 2,
        out_specs=vmem(),
        scratch_shapes=[pltpu.VMEM((3 * half - 2, one, width // 2), BF16)],
        compiler_params=params(16),
        cost_estimate=pl.CostEstimate(
            flops=500_000_000, bytes_accessed=MIB, transcendentals=100_000
        ),
        name="middle",
    )(where, second, w_down)


def decoder(where, second, third, w_deep, w_up, w_out, height, colours):
    one = second.shape[1]
    two = third.shape[1]
    width = second.shape[2]
    return pl.pallas_call(
        decoder_kernel,
        out_shape=jax.ShapeDtypeStruct((1, colours, height, width), BF16),
        in_specs=[smem()] + [vmem()] * 5,
        out_specs=vmem(),
        scratch_shapes=[
            pltpu.VMEM((third.shape[0] - 2, two, width // 2), BF16),
            pltpu.VMEM((height + 4, one + two, width), BF16),
            pltpu.VMEM((height + 2, one, width), BF16),
            pltpu.VMEM((colours, height, width), F32),
            pltpu.VMEM((3, 3 * TAIL, one), F32),
        ],
        compiler_params=params(16),
        cost_estimate=pl.CostEstimate(
            flops=1_500_000_000, bytes_accessed=MIB, transcendentals=200_000
        ),
        name="decoder",
    )(where, second, third, w_deep, w_up, w_out)


def on_device(
    bricks, sends, cells, fracs, sample_order, pending, w_in, w_mid, w_down, w_deep, w_up, w_out
):
    n_tile = lax.axis_size("tile")
    tile = lax.axis_index("tile")
    n_section = lax.axis_size("section")
    cap = sends.shape[3]
    height = pending.shape[2]
    width = pending.shape[3]
    samples = cells.shape[3]
    slots = n_tile * cap
    per_slot = samples // slots
    padded = -(-per_slot // BLOCK) * BLOCK

    def fill(part):
        if padded != per_slot:
            part = part.reshape(3, slots, per_slot)
            part = jnp.pad(part, ((0, 0), (0, 0), (0, padded - per_slot)))
        return part.reshape(3, slots * padded // LANES, LANES)

    def trim(found):
        if padded == per_slot:
            return found
        return found.reshape(slots, padded)[:, :per_slot].reshape(1, samples // LANES, LANES)

    places = positions(fill(cells), fill(fracs), n_tile)
    places, bricks, pending, tile = lax.optimization_barrier((places, bricks, pending, tile))
    arrived = lax.all_to_all(places, "tile", split_axis=0, concat_axis=0, tiled=True)
    where = jnp.stack([tile, jnp.int32(n_tile)]).astype(jnp.int32)

    mates = [(i, i ^ 1) for i in range(n_tile) if i ^ 1 < n_tile]
    across_chips = [
        pair for i in range(1, n_tile - 1, 2) for pair in ((i, i + 1), (i + 1, i))
    ]
    for_mate = lax.dynamic_slice_in_dim(places, mate_of(tile), 1, 0)
    mate_places = lax.ppermute(for_mate, "tile", mates)
    rows = pending[0].transpose(1, 0, 2)
    near = lax.ppermute(rows, "tile", mates)
    far = lax.ppermute(rows, "tile", across_chips)
    picks = sends[0, 0].T
    colours = w_out.shape[1]
    windows = windows_of(where, picks, bricks, places, mate_places)
    found = sample_values(where, picks, windows, arrived)

    found, rows, near, far = lax.optimization_barrier((found, rows, near, far))
    values = lax.all_to_all(found, "tile", split_axis=0, concat_axis=0, tiled=True)
    second = stem(where, rows, near, far, w_in.transpose(0, 2, 1), w_mid)
    third = middle(where, second, w_down.transpose(0, 2, 1))
    values, third = lax.optimization_barrier((values, third))
    rendered = gbuffer(trim(values), sample_order, height, width)
    rendered, third = lax.optimization_barrier((rendered, third))
    ring = [(i, (i + 1) % n_section) for i in range(n_section)]
    handoff = lax.ppermute(rendered, "section", ring)
    denoised = decoder(where, second, third, w_deep, w_up, w_out, height, colours)
    return (handoff, denoised)


def solution(mesh):
    in_specs = (
        P("tile", None),
        P("section", "tile", None, None),
        P("section", "tile", None, None),
        P("section", "tile", None, None),
        P("section", "tile", None, None),
        P("section", None, "tile", None),
        P(),
        P(),
        P(),
        P(),
        P(),
        P(),
    )
    out_specs = (P("section", None, "tile", None), P("section", None, "tile", None))
    return jax.shard_map(
        on_device, mesh=mesh, in_specs=in_specs, out_specs=out_specs, check_vma=False
    )
```

```python
import functools

import jax
import jax.numpy as jnp
from jax import lax
from jax.experimental import pallas as pl
from jax.experimental.pallas import tpu as pltpu
from jax.sharding import PartitionSpec as P

EDGE = 34
NSP = 4
NRAY = 8
NOS = 2
LANES = 128
BLOCK = 256
STRIDE = 6
WINDOWS = 6
MAIN = 32
TAIL = 16
BRICK_ROWS = WINDOWS * MAIN + TAIL
KDIM = 256

F32 = jnp.float32
BF16 = jnp.bfloat16
MIB = 1024 * 1024


def params(mib):
    return pltpu.CompilerParams(vmem_limit_bytes=mib * MIB)


def vmem():
    return pl.BlockSpec(memory_space=pltpu.VMEM)


def smem():
    return pl.BlockSpec(memory_space=pltpu.SMEM)


def positions_kernel(cells_ref, fracs_ref, out_ref, cells, fracs, found, arrivals, departures):
    owners, rows, _ = out_ref.shape
    lines = rows // 3
    parts = arrivals.shape[1]
    share = owners // parts
    pieces = [(axis, part) for axis in range(3) for part in range(parts)]

    def reads(axis, part):
        span = pl.ds(part * share * lines, share * lines)
        return [
            pltpu.make_async_copy(
                source.at[axis, span], target.at[axis, span], arrivals.at[axis, part, number]
            )
            for number, (source, target) in enumerate(((cells_ref, cells), (fracs_ref, fracs)))
        ]

    def write(axis, part):
        place = (pl.ds(part * share, share), pl.ds(axis * lines, lines))
        return pltpu.make_async_copy(
            found.at[place], out_ref.at[place], departures.at[axis, part]
        )

    for piece in pieces:
        for number, copy in enumerate(reads(*piece)):
            copy.start(priority=number)
    for axis, part in pieces:
        for copy in reads(axis, part):
            copy.wait()
        span = slice(part * share * lines, (part + 1) * share * lines)
        place = cells[axis, span].astype(F32) + fracs[axis, span]
        found[part * share : (part + 1) * share, axis * lines : (axis + 1) * lines, :] = (
            place.reshape(share, lines, LANES)
        )
        write(axis, part).start()
    for piece in pieces:
        write(*piece).wait()


def positions(cells, fracs, owners):
    lines = cells.shape[1]
    shape = (owners, 3 * lines // owners, LANES)
    hbm = pl.BlockSpec(memory_space=pltpu.HBM)
    return pl.pallas_call(
        positions_kernel,
        out_shape=jax.ShapeDtypeStruct(shape, F32),
        in_specs=[hbm, hbm],
        out_specs=hbm,
        scratch_shapes=[
            pltpu.VMEM(cells.shape, jnp.int32),
            pltpu.VMEM(fracs.shape, F32),
            pltpu.VMEM(shape, F32),
            pltpu.SemaphoreType.DMA((3, 4, 2)),
            pltpu.SemaphoreType.DMA((3, 4)),
        ],
        compiler_params=params(60),
        cost_estimate=pl.CostEstimate(
            flops=3 * lines * LANES, bytes_accessed=36 * lines * LANES, transcendentals=0
        ),
        name="positions",
    )(cells, fracs)


def mate_of(tile):
    return tile + 1 - 2 * lax.rem(tile, 2)


def windows_kernel(
    where_ref, picks_ref, cube_ref, place_ref, mate_place_ref, out_ref,
    wide, tail, places, sums, arrivals,
):
    tile = where_ref[0]
    near = ((tile, place_ref.at[tile]), (mate_of(tile), mate_place_ref.at[0]))
    copies = [
        pltpu.make_async_copy(source, places.at[i], arrivals.at[i])
        for i, (_, source) in enumerate(near)
    ]
    for copy in copies:
        copy.start()
    count = cube_ref.shape[0]
    plane = EDGE * EDGE
    wide[:, :, plane // LANES * LANES :] = jnp.zeros((count, wide.shape[1], LANES), BF16)
    wide[:, :EDGE, :plane] = cube_ref[...]
    column = lax.broadcasted_iota(jnp.int32, (1, KDIM), 1)
    main = (column // MAIN) * EDGE + column % MAIN
    rest = column - 7 * MAIN
    last = (rest % 8) * EDGE + MAIN + rest // 8
    source = jnp.where(column < 7 * MAIN, main, last)
    unused = (column >= 7 * MAIN) & ((rest % 8 == 7) | (rest >= TAIL))
    source = jnp.where(unused, -(1 << 20), source)
    for window in range(WINDOWS):
        first = window * STRIDE * EDGE
        low = first // LANES * LANES
        length = min(3 * LANES, wide.shape[2] - low)
        place = lax.broadcasted_iota(jnp.int32, (length, KDIM), 0)
        pick = jnp.where(place == source + (first - low), 1.0, 0.0).astype(BF16)
        found = jnp.dot(
            wide[:, :, low : low + length].reshape(-1, length),
            pick,
            preferred_element_type=F32,
        )
        found = found.reshape(count, 48, KDIM)
        out_ref[:count, window * MAIN : (window + 1) * MAIN, :] = found[:, :MAIN, :].astype(BF16)
        tail[:, window : window + 1, :] = found[:, MAIN : MAIN + 1, :]
        tail[:, 8 + window : 9 + window, :] = found[:, MAIN + 1 : MAIN + 2, :]
    for row in (6, 7, 14, 15):
        tail[:, row : row + 1, :] = jnp.zeros((count, 1, KDIM), F32)
    out_ref[:count, WINDOWS * MAIN :, :] = tail[...].astype(BF16)

    for copy in copies:
        copy.wait()
    cap = picks_ref.shape[0]
    lines = places.shape[1] // 3
    part = lines // cap
    height = whole_tiles(lines)
    for i, (renderer, _) in enumerate(near):
        for piece in range(cap):
            brick = out_ref[picks_ref[piece, renderer]]
            slot_sums(brick, places.at[i], sums.at[i], piece * part, part // 2)
    for i in range(len(near)):
        out_ref[count, i * height : (i + 1) * height, :LANES] = line_values(
            sums.at[i], lines, height
        )


def windows_of(where, picks, bricks, places, mate_places):
    count = bricks.shape[0]
    cube = bricks.reshape(count, EDGE, EDGE * EDGE)
    rows = places.shape[1]
    return pl.pallas_call(
        windows_kernel,
        out_shape=jax.ShapeDtypeStruct((count + 1, BRICK_ROWS, KDIM), BF16),
        in_specs=[smem(), smem(), vmem()] + [pl.BlockSpec(memory_space=pl.ANY)] * 2,
        out_specs=vmem(),
        scratch_shapes=[
            pltpu.VMEM((count, 48, 10 * LANES), BF16),
            pltpu.VMEM((count, TAIL, KDIM), F32),
            pltpu.VMEM((2, rows, LANES), F32),
            pltpu.VMEM((2, 8 * rows // 3, LANES), F32),
            pltpu.SemaphoreType.DMA((2,)),
        ],
        compiler_params=params(16),
        cost_estimate=pl.CostEstimate(
            flops=2 * count * 48 * 384 * KDIM * WINDOWS, bytes_accessed=4 * MIB,
            transcendentals=0,
        ),
        name="brick_windows",
    )(where, picks, cube, places, mate_places)


def hat(distance):
    return jnp.maximum(1.0 - jnp.abs(distance), 0.0)


def blend(brick, px, py, pz):
    width = px.shape[1]
    eight = lax.broadcasted_iota(jnp.int32, (8, width), 0).astype(F32)
    places = lax.broadcasted_iota(jnp.int32, (MAIN, width), 0).astype(F32).astype(BF16)

    def tile(rows):
        return jnp.concatenate([rows, rows], axis=0).astype(BF16)

    cell_y = jnp.floor(py)
    frac_y = py - cell_y
    lower, upper = tile(cell_y), tile(cell_y + 1.0)
    low_share, high_share = tile(1.0 - frac_y), tile(frac_y)
    nothing = jnp.zeros((TAIL, width), BF16)
    weight_y = []
    for start in range(0, MAIN, TAIL):
        here = places[start : start + TAIL]
        weight_y.append(
            jnp.where(here == lower, low_share, jnp.where(here == upper, high_share, nothing))
        )
    window = jnp.floor(px * (1.0 / STRIDE))
    weight_x = hat(eight - (px - STRIDE * window))
    parts = []
    for i in range(STRIDE + 1):
        share = tile(jnp.broadcast_to(weight_x[i : i + 1], (8, width)))
        parts += [share * part for part in weight_y]
    tail = [weight_x * hat(MAIN - py), weight_x * jnp.maximum(py - MAIN, 0.0)]
    parts.append(jnp.concatenate(tail, axis=0).astype(BF16))
    plane = jnp.concatenate(parts, axis=0)
    found = jnp.dot(brick[:, : plane.shape[0]], plane, preferred_element_type=F32)
    groups = range(0, MAIN, 8)
    chosen = [found[row : row + 8] for row in groups]
    for other in range(1, WINDOWS):
        here = window == float(other)
        base = other * MAIN
        chosen = [
            jnp.where(here, found[base + row : base + row + 8], old)
            for row, old in zip(groups, chosen)
        ]
    base = WINDOWS * MAIN
    edges = found[base : base + 8] * hat(MAIN - pz)
    edges = edges + found[base + 8 :] * jnp.maximum(pz - MAIN, 0.0)
    total = jnp.where(eight == window, edges, 0.0)
    for row, part in zip(groups, chosen):
        total = total + part * hat((eight + float(row)) - pz)
    return total


def slot_sums(brick, places, sums, first, blocks):
    lines = places.shape[0] // 3
    together = 2 if blocks % 2 == 0 else 1
    halves = 2 * together
    for step in range(0, blocks, together):
        row = first + 2 * step

        def line(axis):
            parts = [
                jnp.broadcast_to(places[pl.ds(axis * lines + row + half, 1), :], (8, LANES))
                for half in range(halves)
            ]
            return jnp.concatenate(parts, axis=1)

        total = blend(brick, line(0), line(1), line(2))
        for half in range(halves):
            sums[pl.ds(pl.multiple_of(8 * (row + half), 8), 8), :] = total[
                :, half * LANES : (half + 1) * LANES
            ]


def whole_tiles(lines):
    return -(-lines // TAIL) * TAIL


def line_values(sums, lines, height):
    values = []
    for row in range(0, lines, 8):
        value = sums[pl.ds(8 * row, 8, stride=8), :]
        for other in range(1, 8):
            value = value + sums[pl.ds(8 * row + other, 8, stride=8), :]
        values.append(value)
    if height > lines:
        values.append(jnp.zeros((height - lines, LANES), F32))
    return jnp.concatenate(values, axis=0).astype(BF16)


def samples_kernel(
    where_ref, picks_ref, brick_ref, place_ref, out_ref, bricks, places, sums, own, arrivals,
    own_arrival,
):
    owners, rows, _ = place_ref.shape
    cap = picks_ref.shape[0]
    lines = rows // 3
    part = lines // cap
    turns = owners - 2
    tile = where_ref[0]
    pairs, rest = turns // 2, turns % 2
    own_values = pltpu.make_async_copy(
        brick_ref.at[brick_ref.shape[0] - 1, pl.ds(0, own.shape[0]), pl.ds(0, LANES)],
        own,
        own_arrival,
    )

    def renderer_of(number):
        return lax.rem(2 * (tile // 2) + 2 + number, owners)

    def fetches(turn, members):
        held = turn % 2
        copies = []
        for member in range(members):
            renderer = renderer_of(2 * turn + member)
            copies.append(
                pltpu.make_async_copy(
                    place_ref.at[renderer],
                    places.at[held, member],
                    arrivals.at[held, member, cap],
                )
            )
            for piece in range(cap):
                copies.append(
                    pltpu.make_async_copy(
                        brick_ref.at[picks_ref[piece, renderer]],
                        bricks.at[held, member, piece],
                        arrivals.at[held, member, piece],
                    )
                )
        return copies

    def start(turn, members):
        for number, copy in enumerate(fetches(turn, members)):
            copy.start(priority=number % 2)

    def work(turn, members):
        held = turn % 2
        for copy in fetches(turn, members):
            copy.wait()

        if members == 2:
            pl.when(turn + 1 < pairs)(lambda: start(turn + 1, 2))
            if rest:
                pl.when(turn + 1 == pairs)(lambda: start(pairs, 1))
            pl.when(turn == 0)(own_values.start)

        for member in range(members):
            for piece in range(cap):
                slot_sums(
                    bricks[held, member, piece],
                    places.at[held, member],
                    sums.at[member],
                    piece * part,
                    part // 2,
                )
        for member in range(members):
            out_ref[renderer_of(2 * turn + member)] = line_values(
                sums.at[member], lines, lines
            )

    def one_pair(turn, carry):
        work(turn, 2)
        return carry

    if pairs > 0:
        start(0, 2)
    elif rest:
        start(0, 1)
    lax.fori_loop(0, pairs, one_pair, 0)
    if rest:
        work(pairs, 1)
    if pairs == 0:
        own_values.start()
    own_values.wait()
    height = whole_tiles(lines)
    for i, renderer in enumerate((tile, mate_of(tile))):
        values = own[i * height : (i + 1) * height, :].astype(F32)
        out_ref[renderer] = values[:lines].astype(BF16)


def sample_values(where, picks, windows, places):
    owners, rows, _ = places.shape
    cap = picks.shape[0]
    samples = owners * rows * LANES // 3
    some = pl.BlockSpec(memory_space=pl.ANY)
    return pl.pallas_call(
        samples_kernel,
        out_shape=jax.ShapeDtypeStruct((owners, rows // 3, LANES), BF16),
        in_specs=[smem(), smem(), some, some],
        out_specs=vmem(),
        scratch_shapes=[
            pltpu.VMEM((2, 2, cap, BRICK_ROWS, KDIM), BF16),
            pltpu.VMEM((2, 2, rows, LANES), F32),
            pltpu.VMEM((2, 8 * rows // 3, LANES), F32),
            pltpu.VMEM((2 * whole_tiles(rows // 3), LANES), BF16),
            pltpu.SemaphoreType.DMA((2, 2, cap + 1)),
            pltpu.SemaphoreType.DMA,
        ],
        compiler_params=pltpu.CompilerParams(vmem_limit_bytes=61_600_000),
        cost_estimate=pl.CostEstimate(
            flops=2 * samples * KDIM * BRICK_ROWS, bytes_accessed=3 * MIB,
            transcendentals=0,
        ),
        name="sample_values",
    )(where, picks, windows, places)


def gbuffer_kernel(value_ref, order_ref, out_ref, values):
    values[...] = value_ref[...].astype(F32).reshape(values.shape)
    height = out_ref.shape[2]

    def ray_of(number):
        rows_now = slice(number * height, (number + 1) * height)
        first, second = (
            values[pl.ds(2 * number * height + half, height, stride=2), :] for half in range(2)
        )
        parts = []
        for half in range(2):
            order = order_ref[0, 0, rows_now, half * LANES : (half + 1) * LANES]
            inner = order & (LANES - 1)
            parts.append(
                jnp.where(
                    order < LANES,
                    jnp.take_along_axis(first, inner, axis=1, mode="promise_in_bounds"),
                    jnp.take_along_axis(second, inner, axis=1, mode="promise_in_bounds"),
                )
            )
        return jnp.concatenate(parts, axis=1)

    remain = 1.0
    shade = 0.0
    depth = 0.0
    for step in range(NSP):
        ray = ray_of(step)
        half_tanh = 0.5 * jnp.tanh(ray)
        weight = remain * (0.5 + half_tanh)
        shade = shade + weight * ray
        depth = depth + weight * ((step + 1) / NSP)
        remain = remain * (0.5 - half_tanh)
    occlusion = 0.0
    for ray_number in range(NRAY):
        passing = 1.0
        for step in range(NOS):
            ray = ray_of(NSP + ray_number * NOS + step)
            passing = passing * (0.5 - 0.5 * jnp.tanh(ray))
        occlusion = occlusion + passing
    out_ref[0, 0] = shade.astype(BF16)
    out_ref[0, 1] = (1.0 - remain).astype(BF16)
    out_ref[0, 2] = depth.astype(BF16)
    out_ref[0, 3] = (occlusion * (1.0 / NRAY)).astype(BF16)


def gbuffer(values, order, height, width):
    total = order.shape[2]
    return pl.pallas_call(
        gbuffer_kernel,
        out_shape=jax.ShapeDtypeStruct((1, 4, height, width), BF16),
        in_specs=[vmem(), vmem()],
        out_specs=vmem(),
        scratch_shapes=[pltpu.VMEM((2 * total, LANES), F32)],
        compiler_params=params(16),
        cost_estimate=pl.CostEstimate(
            flops=20 * total * BLOCK, bytes_accessed=8 * total * BLOCK, transcendentals=0
        ),
        name="gbuffer",
    )(values, order)


def silu(field):
    half = 0.5 * field
    return half + half * jnp.tanh(half)


def shifted(rows, steps):
    lane = lax.broadcasted_iota(jnp.int32, (1, LANES), 1)
    edge = lane == (0 if steps == 1 else LANES - 1)
    moved = []
    for row in rows:
        tiles = [row[:, i : i + LANES] for i in range(0, row.shape[1], LANES)]
        tiles = [pltpu.roll(tile, steps % LANES, 1) for tile in tiles]
        for i, tile in enumerate(tiles):
            source = i - steps
            fill = tiles[source] if 0 <= source < len(tiles) else 0.0
            moved.append(jnp.where(edge, fill, tile))
    return jnp.concatenate(moved, axis=1)


def across(total, chans, row_width):
    left, middle, right = (total[i * chans : (i + 1) * chans] for i in range(3))

    def rows_of(part):
        return [part[:, i : i + row_width] for i in range(0, part.shape[1], row_width)]

    return middle + shifted(rows_of(left), 1) + shifted(rows_of(right), -1)


def taps(weight_ref, tap):
    _, out_chans, chans = weight_ref.shape
    return weight_ref[3 * tap : 3 * tap + 3].reshape(3 * out_chans, chans)


def beside(weight_ref):
    return jnp.concatenate([taps(weight_ref, tap) for tap in range(3)], axis=1)


def beside_padded(weight_ref, spare):
    few = weight_ref.shape[1]
    spare[...] = jnp.zeros_like(spare)
    for tap in range(3):
        for column in range(3):
            spare[tap, column * TAIL : column * TAIL + few, :] = weight_ref[
                3 * tap + column
            ].astype(F32)
    return jnp.concatenate([spare[tap].astype(BF16) for tap in range(3)], axis=1)


def sides(where_ref):
    above = jnp.where(where_ref[0] > 0, 1.0, 0.0)
    below = jnp.where(where_ref[0] < where_ref[1] - 1, 1.0, 0.0)

    def inside(row, low, high):
        return jnp.where(row < low, above, jnp.where(row >= high, below, 1.0))

    return inside


def turned(weight_ref, spare=None):
    _, few, out_chans = weight_ref.shape
    here = lax.broadcasted_iota(jnp.int32, (out_chans, out_chans), 0)
    there = lax.broadcasted_iota(jnp.int32, (out_chans, out_chans), 1)
    unit = jnp.where(here == there, 1.0, 0.0).astype(BF16)
    if spare is not None:
        spare[...] = jnp.zeros_like(spare)
    rows = []
    for column in range(3):
        if spare is None:
            stack = jnp.concatenate([weight_ref[3 * tap + column] for tap in range(3)], axis=0)
        else:
            for tap in range(3):
                spare[column, tap * TAIL : tap * TAIL + few, :] = weight_ref[
                    3 * tap + column
                ].astype(F32)
            stack = spare[column].astype(BF16)
        rows.append(
            lax.dot_general(
                unit, stack, (((1,), (1,)), ((), ())), preferred_element_type=F32
            )
        )
    return jnp.concatenate(rows, axis=0).astype(BF16)


def stem_kernel(
    where_ref, own_ref, near_ref, far_ref, w_in, w_mid, second, x_ref, first, spare
):
    height, chans, width = own_ref.shape
    inside = sides(where_ref)
    first_core = lax.rem(where_ref[0], 2) == 0
    near, far = near_ref[...].astype(F32), far_ref[...].astype(F32)
    x_ref[...] = jnp.zeros_like(x_ref)
    x_ref[:height, :chans, :] = jnp.where(first_core, far, near).astype(BF16)
    x_ref[height : 2 * height, :chans, :] = own_ref[...]
    x_ref[2 * height :, :chans, :] = jnp.where(first_core, near, far).astype(BF16)

    def full_layer(weight, source, target, low, high, unroll):
        chans = target.shape[1]
        depth = weight.shape[1]

        def step(row, carry):
            lines = source[pl.ds(row, 3)].reshape(depth, width)
            line = across(jnp.dot(weight, lines, preferred_element_type=F32), chans, width)
            target[row] = (silu(line) * inside(row, low, high)).astype(BF16)
            return carry

        lax.fori_loop(0, target.shape[0], step, 0, unroll=unroll)

    full_layer(turned(w_in, spare), x_ref, first, height - 1, 2 * height - 1, first.shape[0])
    full_layer(beside(w_mid), first, second, height - 2, 2 * height - 2, second.shape[0])


def half_pair(source, row, tap):
    return jnp.concatenate([source[row + tap], source[row + tap + 1]], axis=1)


def half_layer(product, target, inside, low, high):
    chans, half_width = target.shape[1], target.shape[2]
    for row in range(0, target.shape[0], 2):
        both = silu(across(product(row), chans, half_width))
        for now in range(2):
            line = both[:, now * half_width : (now + 1) * half_width]
            if row + now < low or row + now >= high:
                line = line * inside(row + now, low, high)
            target[row + now] = line.astype(BF16)


def middle_kernel(where_ref, second, w_down, third, pooled):
    count, chans, width = second.shape
    half_height = (count + 4) // 6
    half_width = width // 2
    inside = sides(where_ref)
    place = lax.broadcasted_iota(jnp.int32, (width, half_width), 0) // 2
    target = lax.broadcasted_iota(jnp.int32, (width, half_width), 1)
    shrink = jnp.where(place == target, 0.25, 0.0).astype(BF16)
    pairs = jnp.dot(
        second[...].reshape(count * chans, width), shrink, preferred_element_type=F32
    ).reshape(count // 2, 2, chans, half_width)
    pooled[...] = (pairs[:, 0] + pairs[:, 1]).astype(BF16)
    weight_down = turned(w_down)

    def down_product(row):
        lines = jnp.concatenate([half_pair(pooled, row, tap) for tap in range(3)], axis=0)
        return jnp.dot(weight_down, lines, preferred_element_type=F32)

    half_layer(down_product, third, inside, half_height - 2, 2 * half_height - 2)


def decoder_kernel(
    where_ref, second, third, w_deep, w_up, w_out, out_ref, fourth, joined, fifth, final, spare
):
    height = out_ref.shape[2]
    half_height = height // 2
    width = out_ref.shape[3]
    half_width = width // 2
    chans = second.shape[1]
    inside = sides(where_ref)

    def deep_product(row):
        total = None
        for tap in range(3):
            part = jnp.dot(
                taps(w_deep, tap), half_pair(third, row, tap), preferred_element_type=F32
            )
            total = part if total is None else total + part
        return total

    half_layer(deep_product, fourth, inside, half_height - 3, 2 * half_height - 3)
    place = lax.broadcasted_iota(jnp.int32, (half_width, width), 0)
    target = lax.broadcasted_iota(jnp.int32, (half_width, width), 1) // 2
    spread = jnp.where(place == target, 1.0, 0.0).astype(BF16)
    deep = fourth.shape[1]
    wide = jnp.dot(
        fourth[...].reshape(-1, half_width), spread, preferred_element_type=F32
    ).astype(BF16).reshape(fourth.shape[0], deep, width)
    for row in range(2 * fourth.shape[0]):
        joined[row, chans:, :] = wide[row // 2]
        joined[row, :chans, :] = second[row + 4]

    def up_step(row, carry):
        total = None
        for tap in range(3):
            part = jnp.dot(taps(w_up, tap), joined[row + tap], preferred_element_type=F32)
            total = part if total is None else total + part
        line = silu(across(total, chans, width))
        fifth[row] = (line * inside(row, 1, height + 1)).astype(BF16)
        return carry

    lax.fori_loop(0, fifth.shape[0], up_step, 0, unroll=fifth.shape[0])

    colours = out_ref.shape[1]
    weight_out = beside_padded(w_out, spare)
    for row in range(height):
        lines = fifth[row : row + 3].reshape(3 * chans, width)
        total = jnp.dot(weight_out, lines, preferred_element_type=F32)
        line = across(total, TAIL, width)
        for colour in range(colours):
            final[colour, row : row + 1, :] = line[colour : colour + 1, :]
    out_ref[0] = final[...].astype(BF16)


def stem(where, own, near, far, w_in, w_mid):
    height, _, width = own.shape
    one = w_mid.shape[1]
    return pl.pallas_call(
        stem_kernel,
        out_shape=jax.ShapeDtypeStruct((3 * height - 4, one, width), BF16),
        in_specs=[smem()] + [vmem()] * 5,
        out_specs=vmem(),
        scratch_shapes=[
            pltpu.VMEM((3 * height, TAIL, width), BF16),
            pltpu.VMEM((3 * height - 2, one, width), BF16),
            pltpu.VMEM((3, 3 * TAIL, one), F32),
        ],
        compiler_params=params(16),
        cost_estimate=pl.CostEstimate(
            flops=1_000_000_000, bytes_accessed=MIB, transcendentals=300_000
        ),
        name="stem",
    )(where, own, near, far, w_in, w_mid)


def middle(where, second, w_down):
    rows, one, width = second.shape
    half = (rows + 4) // 6
    two = w_down.shape[2]
    return pl.pallas_call(
        middle_kernel,
        out_shape=jax.ShapeDtypeStruct((3 * half - 4, two, width // 2), BF16),
        in_specs=[smem()] + [vmem()] * 2,
        out_specs=vmem(),
        scratch_shapes=[pltpu.VMEM((3 * half - 2, one, width // 2), BF16)],
        compiler_params=params(16),
        cost_estimate=pl.CostEstimate(
            flops=500_000_000, bytes_accessed=MIB, transcendentals=100_000
        ),
        name="middle",
    )(where, second, w_down)


def decoder(where, second, third, w_deep, w_up, w_out, height, colours):
    one = second.shape[1]
    two = third.shape[1]
    width = second.shape[2]
    return pl.pallas_call(
        decoder_kernel,
        out_shape=jax.ShapeDtypeStruct((1, colours, height, width), BF16),
        in_specs=[smem()] + [vmem()] * 5,
        out_specs=vmem(),
        scratch_shapes=[
            pltpu.VMEM((third.shape[0] - 2, two, width // 2), BF16),
            pltpu.VMEM((height + 4, one + two, width), BF16),
            pltpu.VMEM((height + 2, one, width), BF16),
            pltpu.VMEM((colours, height, width), F32),
            pltpu.VMEM((3, 3 * TAIL, one), F32),
        ],
        compiler_params=params(16),
        cost_estimate=pl.CostEstimate(
            flops=1_500_000_000, bytes_accessed=MIB, transcendentals=200_000
        ),
        name="decoder",
    )(where, second, third, w_deep, w_up, w_out)


def on_device(
    bricks, sends, cells, fracs, sample_order, pending, w_in, w_mid, w_down, w_deep, w_up, w_out
):
    n_tile = lax.axis_size("tile")
    tile = lax.axis_index("tile")
    n_section = lax.axis_size("section")
    cap = sends.shape[3]
    height = pending.shape[2]
    width = pending.shape[3]
    samples = cells.shape[3]
    slots = n_tile * cap
    per_slot = samples // slots
    padded = -(-per_slot // BLOCK) * BLOCK

    def fill(part):
        if padded != per_slot:
            part = part.reshape(3, slots, per_slot)
            part = jnp.pad(part, ((0, 0), (0, 0), (0, padded - per_slot)))
        return part.reshape(3, slots * padded // LANES, LANES)

    def trim(found):
        if padded == per_slot:
            return found
        return found.reshape(slots, padded)[:, :per_slot].reshape(1, samples // LANES, LANES)

    places = positions(fill(cells), fill(fracs), n_tile)
    places, bricks, pending, tile = lax.optimization_barrier((places, bricks, pending, tile))
    arrived = lax.all_to_all(places, "tile", split_axis=0, concat_axis=0, tiled=True)
    where = jnp.stack([tile, jnp.int32(n_tile)]).astype(jnp.int32)

    mates = [(i, i ^ 1) for i in range(n_tile) if i ^ 1 < n_tile]
    across_chips = [
        pair for i in range(1, n_tile - 1, 2) for pair in ((i, i + 1), (i + 1, i))
    ]
    for_mate = lax.dynamic_slice_in_dim(places, mate_of(tile), 1, 0)
    mate_places = lax.ppermute(for_mate, "tile", mates)
    rows = pending[0].transpose(1, 0, 2)
    near = lax.ppermute(rows, "tile", mates)
    far = lax.ppermute(rows, "tile", across_chips)
    picks = sends[0, 0].T
    colours = w_out.shape[1]
    windows = windows_of(where, picks, bricks, places, mate_places)
    found = sample_values(where, picks, windows, arrived)

    found, rows, near, far = lax.optimization_barrier((found, rows, near, far))
    values = lax.all_to_all(found, "tile", split_axis=0, concat_axis=0, tiled=True)
    second = stem(where, rows, near, far, w_in.transpose(0, 2, 1), w_mid)
    third = middle(where, second, w_down.transpose(0, 2, 1))
    values, third = lax.optimization_barrier((values, third))
    rendered = gbuffer(trim(values), sample_order, height, width)
    rendered, third = lax.optimization_barrier((rendered, third))
    ring = [(i, (i + 1) % n_section) for i in range(n_section)]
    handoff = lax.ppermute(rendered, "section", ring)
    denoised = decoder(where, second, third, w_deep, w_up, w_out, height, colours)
    return (handoff, denoised)


def solution(mesh):
    in_specs = (
        P("tile", None),
        P("section", "tile", None, None),
        P("section", "tile", None, None),
        P("section", "tile", None, None),
        P("section", "tile", None, None),
        P("section", None, "tile", None),
        P(),
        P(),
        P(),
        P(),
        P(),
        P(),
    )
    out_specs = (P("section", None, "tile", None), P("section", None, "tile", None))
    return jax.shard_map(
        on_device, mesh=mesh, in_specs=in_specs, out_specs=out_specs, check_vma=False
    )
```

```python
import functools

import jax
import jax.numpy as jnp
from jax import lax
from jax.experimental import pallas as pl
from jax.experimental.pallas import tpu as pltpu
from jax.sharding import PartitionSpec as P

EDGE = 34
NSP = 4
NRAY = 8
NOS = 2
LANES = 128
BLOCK = 256
STRIDE = 6
WINDOWS = 6
MAIN = 32
TAIL = 16
BRICK_ROWS = WINDOWS * MAIN + TAIL
KDIM = 256

F32 = jnp.float32
BF16 = jnp.bfloat16
MIB = 1024 * 1024


def params(mib):
    return pltpu.CompilerParams(vmem_limit_bytes=mib * MIB)


def vmem():
    return pl.BlockSpec(memory_space=pltpu.VMEM)


def smem():
    return pl.BlockSpec(memory_space=pltpu.SMEM)


def positions_kernel(cells_ref, fracs_ref, out_ref, cells, fracs, found, arrivals, departures):
    owners, rows, _ = out_ref.shape
    lines = rows // 3
    parts = arrivals.shape[1]
    share = owners // parts
    pieces = [(axis, part) for axis in range(3) for part in range(parts)]

    def reads(axis, part):
        span = pl.ds(part * share * lines, share * lines)
        return [
            pltpu.make_async_copy(
                source.at[axis, span], target.at[axis, span], arrivals.at[axis, part, number]
            )
            for number, (source, target) in enumerate(((cells_ref, cells), (fracs_ref, fracs)))
        ]

    def write(axis, part):
        place = (pl.ds(part * share, share), pl.ds(axis * lines, lines))
        return pltpu.make_async_copy(
            found.at[place], out_ref.at[place], departures.at[axis, part]
        )

    for piece in pieces:
        for copy in reads(*piece):
            copy.start()
    for axis, part in pieces:
        for copy in reads(axis, part):
            copy.wait()
        span = slice(part * share * lines, (part + 1) * share * lines)
        place = cells[axis, span].astype(F32) + fracs[axis, span]
        found[part * share : (part + 1) * share, axis * lines : (axis + 1) * lines, :] = (
            place.reshape(share, lines, LANES)
        )
        write(axis, part).start()
    for piece in pieces:
        write(*piece).wait()


def positions(cells, fracs, owners):
    lines = cells.shape[1]
    shape = (owners, 3 * lines // owners, LANES)
    hbm = pl.BlockSpec(memory_space=pltpu.HBM)
    return pl.pallas_call(
        positions_kernel,
        out_shape=jax.ShapeDtypeStruct(shape, F32),
        in_specs=[hbm, hbm],
        out_specs=hbm,
        scratch_shapes=[
            pltpu.VMEM(cells.shape, jnp.int32),
            pltpu.VMEM(fracs.shape, F32),
            pltpu.VMEM(shape, F32),
            pltpu.SemaphoreType.DMA((3, 4, 2)),
            pltpu.SemaphoreType.DMA((3, 4)),
        ],
        compiler_params=params(60),
        cost_estimate=pl.CostEstimate(
            flops=3 * lines * LANES, bytes_accessed=36 * lines * LANES, transcendentals=0
        ),
        name="positions",
    )(cells, fracs)


def mate_of(tile):
    return tile + 1 - 2 * lax.rem(tile, 2)


def windows_kernel(
    where_ref, picks_ref, cube_ref, place_ref, mate_place_ref, out_ref,
    wide, tail, places, sums, arrivals,
):
    tile = where_ref[0]
    near = ((tile, place_ref.at[tile]), (mate_of(tile), mate_place_ref.at[0]))
    copies = [
        pltpu.make_async_copy(source, places.at[i], arrivals.at[i])
        for i, (_, source) in enumerate(near)
    ]
    for copy in copies:
        copy.start()
    count = cube_ref.shape[0]
    plane = EDGE * EDGE
    wide[:, :, plane // LANES * LANES :] = jnp.zeros((count, wide.shape[1], LANES), BF16)
    wide[:, :EDGE, :plane] = cube_ref[...]
    column = lax.broadcasted_iota(jnp.int32, (1, KDIM), 1)
    main = (column // MAIN) * EDGE + column % MAIN
    rest = column - 7 * MAIN
    last = (rest % 8) * EDGE + MAIN + rest // 8
    source = jnp.where(column < 7 * MAIN, main, last)
    unused = (column >= 7 * MAIN) & ((rest % 8 == 7) | (rest >= TAIL))
    source = jnp.where(unused, -(1 << 20), source)
    for window in range(WINDOWS):
        first = window * STRIDE * EDGE
        low = first // LANES * LANES
        length = min(3 * LANES, wide.shape[2] - low)
        place = lax.broadcasted_iota(jnp.int32, (length, KDIM), 0)
        pick = jnp.where(place == source + (first - low), 1.0, 0.0).astype(BF16)
        found = jnp.dot(
            wide[:, :, low : low + length].reshape(-1, length),
            pick,
            preferred_element_type=F32,
        )
        found = found.reshape(count, 48, KDIM)
        out_ref[:count, window * MAIN : (window + 1) * MAIN, :] = found[:, :MAIN, :].astype(BF16)
        tail[:, window : window + 1, :] = found[:, MAIN : MAIN + 1, :]
        tail[:, 8 + window : 9 + window, :] = found[:, MAIN + 1 : MAIN + 2, :]
    for row in (6, 7, 14, 15):
        tail[:, row : row + 1, :] = jnp.zeros((count, 1, KDIM), F32)
    out_ref[:count, WINDOWS * MAIN :, :] = tail[...].astype(BF16)

    for copy in copies:
        copy.wait()
    cap = picks_ref.shape[0]
    lines = places.shape[1] // 3
    part = lines // cap
    height = whole_tiles(lines)
    for i, (renderer, _) in enumerate(near):
        for piece in range(cap):
            brick = out_ref[picks_ref[piece, renderer]]
            slot_sums(brick, places.at[i], sums.at[i], piece * part, part // 2)
    for i in range(len(near)):
        out_ref[count, i * height : (i + 1) * height, :LANES] = line_values(
            sums.at[i], lines, height
        )


def windows_of(where, picks, bricks, places, mate_places):
    count = bricks.shape[0]
    cube = bricks.reshape(count, EDGE, EDGE * EDGE)
    rows = places.shape[1]
    return pl.pallas_call(
        windows_kernel,
        out_shape=jax.ShapeDtypeStruct((count + 1, BRICK_ROWS, KDIM), BF16),
        in_specs=[smem(), smem(), vmem()] + [pl.BlockSpec(memory_space=pl.ANY)] * 2,
        out_specs=vmem(),
        scratch_shapes=[
            pltpu.VMEM((count, 48, 10 * LANES), BF16),
            pltpu.VMEM((count, TAIL, KDIM), F32),
            pltpu.VMEM((2, rows, LANES), F32),
            pltpu.VMEM((2, 8 * rows // 3, LANES), F32),
            pltpu.SemaphoreType.DMA((2,)),
        ],
        compiler_params=params(16),
        cost_estimate=pl.CostEstimate(
            flops=2 * count * 48 * 384 * KDIM * WINDOWS, bytes_accessed=4 * MIB,
            transcendentals=0,
        ),
        name="brick_windows",
    )(where, picks, cube, places, mate_places)


def hat(distance):
    return jnp.maximum(1.0 - jnp.abs(distance), 0.0)


def blend(brick, px, py, pz):
    width = px.shape[1]
    eight = lax.broadcasted_iota(jnp.int32, (8, width), 0).astype(F32)
    places = lax.broadcasted_iota(jnp.int32, (MAIN, width), 0).astype(F32).astype(BF16)

    def tile(rows):
        return jnp.concatenate([rows, rows], axis=0).astype(BF16)

    cell_y = jnp.floor(py)
    frac_y = py - cell_y
    lower, upper = tile(cell_y), tile(cell_y + 1.0)
    low_share, high_share = tile(1.0 - frac_y), tile(frac_y)
    nothing = jnp.zeros((TAIL, width), BF16)
    weight_y = []
    for start in range(0, MAIN, TAIL):
        here = places[start : start + TAIL]
        weight_y.append(
            jnp.where(here == lower, low_share, jnp.where(here == upper, high_share, nothing))
        )
    window = jnp.floor(px * (1.0 / STRIDE))
    local_x = jnp.maximum(px - STRIDE * window, 0.0)
    weight_x = hat(eight - local_x)
    parts = []
    cell_x = jnp.floor(local_x)
    frac_x = local_x - cell_x
    place_x, low_x, high_x = tile(cell_x), tile(1.0 - frac_x), tile(frac_x)
    hits = [place_x == i for i in range(STRIDE + 1)]
    for i in range(STRIDE + 1):
        share = nothing if i == 0 else jnp.where(hits[i - 1], high_x, nothing)
        share = jnp.where(hits[i], low_x, share)
        parts += [share * part for part in weight_y]
    tail = [weight_x * hat(MAIN - py), weight_x * jnp.maximum(py - MAIN, 0.0)]
    parts.append(jnp.concatenate(tail, axis=0).astype(BF16))
    plane = jnp.concatenate(parts, axis=0)
    found = jnp.dot(brick[:, : plane.shape[0]], plane, preferred_element_type=F32)
    groups = range(0, MAIN, 8)
    chosen = [found[row : row + 8] for row in groups]
    for other in range(1, WINDOWS):
        here = window == float(other)
        base = other * MAIN
        chosen = [
            jnp.where(here, found[base + row : base + row + 8], old)
            for row, old in zip(groups, chosen)
        ]
    base = WINDOWS * MAIN
    edges = found[base : base + 8] * hat(MAIN - pz)
    edges = edges + found[base + 8 :] * jnp.maximum(pz - MAIN, 0.0)
    total = jnp.where(eight == window, edges, 0.0)
    for row, part in zip(groups, chosen):
        total = total + part * hat((eight + float(row)) - pz)
    return total


def slot_sums(brick, places, sums, first, blocks):
    lines = places.shape[0] // 3
    together = 2 if blocks % 2 == 0 else 1
    halves = 2 * together
    for step in range(0, blocks, together):
        row = first + 2 * step

        def line(axis):
            parts = [
                jnp.broadcast_to(places[pl.ds(axis * lines + row + half, 1), :], (8, LANES))
                for half in range(halves)
            ]
            return jnp.concatenate(parts, axis=1)

        total = blend(brick, line(0), line(1), line(2))
        for half in range(halves):
            sums[pl.ds(pl.multiple_of(8 * (row + half), 8), 8), :] = total[
                :, half * LANES : (half + 1) * LANES
            ]


def whole_tiles(lines):
    return -(-lines // TAIL) * TAIL


def line_values(sums, lines, height):
    values = []
    for row in range(0, lines, 8):
        value = sums[pl.ds(8 * row, 8, stride=8), :]
        for other in range(1, 8):
            value = value + sums[pl.ds(8 * row + other, 8, stride=8), :]
        values.append(value)
    if height > lines:
        values.append(jnp.zeros((height - lines, LANES), F32))
    return jnp.concatenate(values, axis=0).astype(BF16)


def samples_kernel(
    where_ref, picks_ref, brick_ref, place_ref, out_ref, bricks, places, sums, own, arrivals,
    own_arrival,
):
    owners, rows, _ = place_ref.shape
    cap = picks_ref.shape[0]
    lines = rows // 3
    part = lines // cap
    turns = owners - 2
    tile = where_ref[0]
    pairs, rest = turns // 2, turns % 2
    own_values = pltpu.make_async_copy(
        brick_ref.at[brick_ref.shape[0] - 1, pl.ds(0, own.shape[0]), pl.ds(0, LANES)],
        own,
        own_arrival,
    )

    def renderer_of(number):
        return lax.rem(2 * (tile // 2) + 2 + number, owners)

    def fetches(turn, members):
        held = turn % 2
        copies = []
        for member in range(members):
            renderer = renderer_of(2 * turn + member)
            copies.append(
                pltpu.make_async_copy(
                    place_ref.at[renderer],
                    places.at[held, member],
                    arrivals.at[held, member, cap],
                )
            )
            for piece in range(cap):
                copies.append(
                    pltpu.make_async_copy(
                        brick_ref.at[picks_ref[piece, renderer]],
                        bricks.at[held, member, piece],
                        arrivals.at[held, member, piece],
                    )
                )
        return copies

    def start(turn, members):
        for copy in fetches(turn, members):
            copy.start()

    def work(turn, members):
        held = turn % 2
        for copy in fetches(turn, members):
            copy.wait()

        if members == 2:
            pl.when(turn + 1 < pairs)(lambda: start(turn + 1, 2))
            if rest:
                pl.when(turn + 1 == pairs)(lambda: start(pairs, 1))
            pl.when(turn == 0)(own_values.start)

        for member in range(members):
            for piece in range(cap):
                slot_sums(
                    bricks[held, member, piece],
                    places.at[held, member],
                    sums.at[member],
                    piece * part,
                    part // 2,
                )
        for member in range(members):
            out_ref[renderer_of(2 * turn + member)] = line_values(
                sums.at[member], lines, lines
            )

    def one_pair(turn, carry):
        work(turn, 2)
        return carry

    if pairs > 0:
        start(0, 2)
    elif rest:
        start(0, 1)
    lax.fori_loop(0, pairs, one_pair, 0)
    if rest:
        work(pairs, 1)
    if pairs == 0:
        own_values.start()
    own_values.wait()
    height = whole_tiles(lines)
    for i, renderer in enumerate((tile, mate_of(tile))):
        values = own[i * height : (i + 1) * height, :].astype(F32)
        out_ref[renderer] = values[:lines].astype(BF16)


def sample_values(where, picks, windows, places):
    owners, rows, _ = places.shape
    cap = picks.shape[0]
    samples = owners * rows * LANES // 3
    some = pl.BlockSpec(memory_space=pl.ANY)
    return pl.pallas_call(
        samples_kernel,
        out_shape=jax.ShapeDtypeStruct((owners, rows // 3, LANES), BF16),
        in_specs=[smem(), smem(), some, some],
        out_specs=vmem(),
        scratch_shapes=[
            pltpu.VMEM((2, 2, cap, BRICK_ROWS, KDIM), BF16),
            pltpu.VMEM((2, 2, rows, LANES), F32),
            pltpu.VMEM((2, 8 * rows // 3, LANES), F32),
            pltpu.VMEM((2 * whole_tiles(rows // 3), LANES), BF16),
            pltpu.SemaphoreType.DMA((2, 2, cap + 1)),
            pltpu.SemaphoreType.DMA,
        ],
        compiler_params=pltpu.CompilerParams(vmem_limit_bytes=61_600_000),
        cost_estimate=pl.CostEstimate(
            flops=2 * samples * KDIM * BRICK_ROWS, bytes_accessed=3 * MIB,
            transcendentals=0,
        ),
        name="sample_values",
    )(where, picks, windows, places)


def gbuffer_kernel(value_ref, order_ref, out_ref, values):
    values[...] = value_ref[...].astype(F32).reshape(values.shape)
    height = out_ref.shape[2]

    def ray_of(number):
        rows_now = slice(number * height, (number + 1) * height)
        first, second = (
            values[pl.ds(2 * number * height + half, height, stride=2), :] for half in range(2)
        )
        parts = []
        for half in range(2):
            order = order_ref[0, 0, rows_now, half * LANES : (half + 1) * LANES]
            inner = order & (LANES - 1)
            parts.append(
                jnp.where(
                    order < LANES,
                    jnp.take_along_axis(first, inner, axis=1, mode="promise_in_bounds"),
                    jnp.take_along_axis(second, inner, axis=1, mode="promise_in_bounds"),
                )
            )
        return jnp.concatenate(parts, axis=1)

    remain = 1.0
    shade = 0.0
    depth = 0.0
    for step in range(NSP):
        ray = ray_of(step)
        half_tanh = 0.5 * jnp.tanh(ray)
        weight = remain * (0.5 + half_tanh)
        shade = shade + weight * ray
        depth = depth + weight * ((step + 1) / NSP)
        remain = remain * (0.5 - half_tanh)
    occlusion = 0.0
    for ray_number in range(NRAY):
        passing = 1.0
        for step in range(NOS):
            ray = ray_of(NSP + ray_number * NOS + step)
            passing = passing * (0.5 - 0.5 * jnp.tanh(ray))
        occlusion = occlusion + passing
    out_ref[0, 0] = shade.astype(BF16)
    out_ref[0, 1] = (1.0 - remain).astype(BF16)
    out_ref[0, 2] = depth.astype(BF16)
    out_ref[0, 3] = (occlusion * (1.0 / NRAY)).astype(BF16)


def gbuffer(values, order, height, width):
    total = order.shape[2]
    return pl.pallas_call(
        gbuffer_kernel,
        out_shape=jax.ShapeDtypeStruct((1, 4, height, width), BF16),
        in_specs=[vmem(), vmem()],
        out_specs=vmem(),
        scratch_shapes=[pltpu.VMEM((2 * total, LANES), F32)],
        compiler_params=params(16),
        cost_estimate=pl.CostEstimate(
            flops=20 * total * BLOCK, bytes_accessed=8 * total * BLOCK, transcendentals=0
        ),
        name="gbuffer",
    )(values, order)


def silu(field):
    half = 0.5 * field
    return half + half * jnp.tanh(half)


def shifted(rows, steps):
    lane = lax.broadcasted_iota(jnp.int32, (1, LANES), 1)
    edge = lane == (0 if steps == 1 else LANES - 1)
    moved = []
    for row in rows:
        tiles = [row[:, i : i + LANES] for i in range(0, row.shape[1], LANES)]
        tiles = [pltpu.roll(tile, steps % LANES, 1) for tile in tiles]
        for i, tile in enumerate(tiles):
            source = i - steps
            fill = tiles[source] if 0 <= source < len(tiles) else 0.0
            moved.append(jnp.where(edge, fill, tile))
    return jnp.concatenate(moved, axis=1)


def across(total, chans, row_width):
    left, middle, right = (total[i * chans : (i + 1) * chans] for i in range(3))

    def rows_of(part):
        return [part[:, i : i + row_width] for i in range(0, part.shape[1], row_width)]

    return middle + shifted(rows_of(left), 1) + shifted(rows_of(right), -1)


def taps(weight_ref, tap):
    _, out_chans, chans = weight_ref.shape
    return weight_ref[3 * tap : 3 * tap + 3].reshape(3 * out_chans, chans)


def beside(weight_ref):
    return jnp.concatenate([taps(weight_ref, tap) for tap in range(3)], axis=1)


def beside_padded(weight_ref, spare):
    few = weight_ref.shape[1]
    spare[...] = jnp.zeros_like(spare)
    for tap in range(3):
        for column in range(3):
            spare[tap, column * TAIL : column * TAIL + few, :] = weight_ref[
                3 * tap + column
            ].astype(F32)
    return jnp.concatenate([spare[tap].astype(BF16) for tap in range(3)], axis=1)


def sides(where_ref):
    above = jnp.where(where_ref[0] > 0, 1.0, 0.0)
    below = jnp.where(where_ref[0] < where_ref[1] - 1, 1.0, 0.0)

    def inside(row, low, high):
        return jnp.where(row < low, above, jnp.where(row >= high, below, 1.0))

    return inside


def turned(weight_ref, spare=None):
    _, few, out_chans = weight_ref.shape
    here = lax.broadcasted_iota(jnp.int32, (out_chans, out_chans), 0)
    there = lax.broadcasted_iota(jnp.int32, (out_chans, out_chans), 1)
    unit = jnp.where(here == there, 1.0, 0.0).astype(BF16)
    if spare is not None:
        spare[...] = jnp.zeros_like(spare)
    rows = []
    for column in range(3):
        if spare is None:
            stack = jnp.concatenate([weight_ref[3 * tap + column] for tap in range(3)], axis=0)
        else:
            for tap in range(3):
                spare[column, tap * TAIL : tap * TAIL + few, :] = weight_ref[
                    3 * tap + column
                ].astype(F32)
            stack = spare[column].astype(BF16)
        rows.append(
            lax.dot_general(
                unit, stack, (((1,), (1,)), ((), ())), preferred_element_type=F32
            )
        )
    return jnp.concatenate(rows, axis=0).astype(BF16)


def stem_kernel(
    where_ref, own_ref, near_ref, far_ref, w_in, w_mid, second, x_ref, first, spare
):
    height, chans, width = own_ref.shape
    inside = sides(where_ref)
    first_core = lax.rem(where_ref[0], 2) == 0
    near, far = near_ref[...].astype(F32), far_ref[...].astype(F32)
    x_ref[...] = jnp.zeros_like(x_ref)
    x_ref[:height, :chans, :] = jnp.where(first_core, far, near).astype(BF16)
    x_ref[height : 2 * height, :chans, :] = own_ref[...]
    x_ref[2 * height :, :chans, :] = jnp.where(first_core, near, far).astype(BF16)

    def full_layer(weight, source, target, low, high, unroll):
        chans = target.shape[1]
        depth = weight.shape[1]

        def step(row, carry):
            lines = source[pl.ds(row, 3)].reshape(depth, width)
            line = across(jnp.dot(weight, lines, preferred_element_type=F32), chans, width)
            target[row] = (silu(line) * inside(row, low, high)).astype(BF16)
            return carry

        lax.fori_loop(0, target.shape[0], step, 0, unroll=unroll)

    full_layer(turned(w_in, spare), x_ref, first, height - 1, 2 * height - 1, first.shape[0])
    full_layer(beside(w_mid), first, second, height - 2, 2 * height - 2, second.shape[0])


def half_pair(source, row, tap):
    return jnp.concatenate([source[row + tap], source[row + tap + 1]], axis=1)


def half_layer(product, target, inside, low, high):
    chans, half_width = target.shape[1], target.shape[2]
    for row in range(0, target.shape[0], 2):
        both = silu(across(product(row), chans, half_width))
        for now in range(2):
            line = both[:, now * half_width : (now + 1) * half_width]
            if row + now < low or row + now >= high:
                line = line * inside(row + now, low, high)
            target[row + now] = line.astype(BF16)


def middle_kernel(where_ref, second, w_down, third, pooled):
    count, chans, width = second.shape
    half_height = (count + 4) // 6
    half_width = width // 2
    inside = sides(where_ref)
    place = lax.broadcasted_iota(jnp.int32, (width, half_width), 0) // 2
    target = lax.broadcasted_iota(jnp.int32, (width, half_width), 1)
    shrink = jnp.where(place == target, 0.25, 0.0).astype(BF16)
    pairs = jnp.dot(
        second[...].reshape(count * chans, width), shrink, preferred_element_type=F32
    ).reshape(count // 2, 2, chans, half_width)
    pooled[...] = (pairs[:, 0] + pairs[:, 1]).astype(BF16)
    weight_down = turned(w_down)

    def down_product(row):
        lines = jnp.concatenate([half_pair(pooled, row, tap) for tap in range(3)], axis=0)
        return jnp.dot(weight_down, lines, preferred_element_type=F32)

    half_layer(down_product, third, inside, half_height - 2, 2 * half_height - 2)


def decoder_kernel(
    where_ref, second, third, w_deep, w_up, w_out, out_ref, fourth, joined, fifth, final, spare
):
    height = out_ref.shape[2]
    half_height = height // 2
    width = out_ref.shape[3]
    half_width = width // 2
    chans = second.shape[1]
    inside = sides(where_ref)

    def deep_product(row):
        total = None
        for tap in range(3):
            part = jnp.dot(
                taps(w_deep, tap), half_pair(third, row, tap), preferred_element_type=F32
            )
            total = part if total is None else total + part
        return total

    half_layer(deep_product, fourth, inside, half_height - 3, 2 * half_height - 3)
    place = lax.broadcasted_iota(jnp.int32, (half_width, width), 0)
    target = lax.broadcasted_iota(jnp.int32, (half_width, width), 1) // 2
    spread = jnp.where(place == target, 1.0, 0.0).astype(BF16)
    deep = fourth.shape[1]
    wide = jnp.dot(
        fourth[...].reshape(-1, half_width), spread, preferred_element_type=F32
    ).astype(BF16).reshape(fourth.shape[0], deep, width)
    for row in range(2 * fourth.shape[0]):
        joined[row, chans:, :] = wide[row // 2]
        joined[row, :chans, :] = second[row + 4]

    def up_step(row, carry):
        total = None
        for tap in range(3):
            part = jnp.dot(taps(w_up, tap), joined[row + tap], preferred_element_type=F32)
            total = part if total is None else total + part
        line = silu(across(total, chans, width))
        fifth[row] = (line * inside(row, 1, height + 1)).astype(BF16)
        return carry

    lax.fori_loop(0, fifth.shape[0], up_step, 0, unroll=fifth.shape[0])

    colours = out_ref.shape[1]
    weight_out = beside_padded(w_out, spare)
    for row in range(height):
        lines = fifth[row : row + 3].reshape(3 * chans, width)
        total = jnp.dot(weight_out, lines, preferred_element_type=F32)
        line = across(total, TAIL, width)
        for colour in range(colours):
            final[colour, row : row + 1, :] = line[colour : colour + 1, :]
    out_ref[0] = final[...].astype(BF16)


def stem(where, own, near, far, w_in, w_mid):
    height, _, width = own.shape
    one = w_mid.shape[1]
    return pl.pallas_call(
        stem_kernel,
        out_shape=jax.ShapeDtypeStruct((3 * height - 4, one, width), BF16),
        in_specs=[smem()] + [vmem()] * 5,
        out_specs=vmem(),
        scratch_shapes=[
            pltpu.VMEM((3 * height, TAIL, width), BF16),
            pltpu.VMEM((3 * height - 2, one, width), BF16),
            pltpu.VMEM((3, 3 * TAIL, one), F32),
        ],
        compiler_params=params(16),
        cost_estimate=pl.CostEstimate(
            flops=1_000_000_000, bytes_accessed=MIB, transcendentals=300_000
        ),
        name="stem",
    )(where, own, near, far, w_in, w_mid)


def middle(where, second, w_down):
    rows, one, width = second.shape
    half = (rows + 4) // 6
    two = w_down.shape[2]
    return pl.pallas_call(
        middle_kernel,
        out_shape=jax.ShapeDtypeStruct((3 * half - 4, two, width // 2), BF16),
        in_specs=[smem()] + [vmem()] * 2,
        out_specs=vmem(),
        scratch_shapes=[pltpu.VMEM((3 * half - 2, one, width // 2), BF16)],
        compiler_params=params(16),
        cost_estimate=pl.CostEstimate(
            flops=500_000_000, bytes_accessed=MIB, transcendentals=100_000
        ),
        name="middle",
    )(where, second, w_down)


def decoder(where, second, third, w_deep, w_up, w_out, height, colours):
    one = second.shape[1]
    two = third.shape[1]
    width = second.shape[2]
    return pl.pallas_call(
        decoder_kernel,
        out_shape=jax.ShapeDtypeStruct((1, colours, height, width), BF16),
        in_specs=[smem()] + [vmem()] * 5,
        out_specs=vmem(),
        scratch_shapes=[
            pltpu.VMEM((third.shape[0] - 2, two, width // 2), BF16),
            pltpu.VMEM((height + 4, one + two, width), BF16),
            pltpu.VMEM((height + 2, one, width), BF16),
            pltpu.VMEM((colours, height, width), F32),
            pltpu.VMEM((3, 3 * TAIL, one), F32),
        ],
        compiler_params=params(16),
        cost_estimate=pl.CostEstimate(
            flops=1_500_000_000, bytes_accessed=MIB, transcendentals=200_000
        ),
        name="decoder",
    )(where, second, third, w_deep, w_up, w_out)


def on_device(
    bricks, sends, cells, fracs, sample_order, pending, w_in, w_mid, w_down, w_deep, w_up, w_out
):
    n_tile = lax.axis_size("tile")
    tile = lax.axis_index("tile")
    n_section = lax.axis_size("section")
    cap = sends.shape[3]
    height = pending.shape[2]
    width = pending.shape[3]
    samples = cells.shape[3]
    slots = n_tile * cap
    per_slot = samples // slots
    padded = -(-per_slot // BLOCK) * BLOCK

    def fill(part):
        if padded != per_slot:
            part = part.reshape(3, slots, per_slot)
            part = jnp.pad(part, ((0, 0), (0, 0), (0, padded - per_slot)))
        return part.reshape(3, slots * padded // LANES, LANES)

    def trim(found):
        if padded == per_slot:
            return found
        return found.reshape(slots, padded)[:, :per_slot].reshape(1, samples // LANES, LANES)

    places = positions(fill(cells), fill(fracs), n_tile)
    places, bricks, pending, tile = lax.optimization_barrier((places, bricks, pending, tile))
    arrived = lax.all_to_all(places, "tile", split_axis=0, concat_axis=0, tiled=True)
    where = jnp.stack([tile, jnp.int32(n_tile)]).astype(jnp.int32)

    mates = [(i, i ^ 1) for i in range(n_tile) if i ^ 1 < n_tile]
    across_chips = [
        pair for i in range(1, n_tile - 1, 2) for pair in ((i, i + 1), (i + 1, i))
    ]
    for_mate = lax.dynamic_slice_in_dim(places, mate_of(tile), 1, 0)
    mate_places = lax.ppermute(for_mate, "tile", mates)
    rows = pending[0].transpose(1, 0, 2)
    near = lax.ppermute(rows, "tile", mates)
    far = lax.ppermute(rows, "tile", across_chips)
    picks = sends[0, 0].T
    colours = w_out.shape[1]
    windows = windows_of(where, picks, bricks, places, mate_places)
    found = sample_values(where, picks, windows, arrived)

    found, rows, near, far = lax.optimization_barrier((found, rows, near, far))
    values = lax.all_to_all(found, "tile", split_axis=0, concat_axis=0, tiled=True)
    second = stem(where, rows, near, far, w_in.transpose(0, 2, 1), w_mid)
    third = middle(where, second, w_down.transpose(0, 2, 1))
    values, third = lax.optimization_barrier((values, third))
    rendered = gbuffer(trim(values), sample_order, height, width)
    rendered, third = lax.optimization_barrier((rendered, third))
    ring = [(i, (i + 1) % n_section) for i in range(n_section)]
    handoff = lax.ppermute(rendered, "section", ring)
    denoised = decoder(where, second, third, w_deep, w_up, w_out, height, colours)
    return (handoff, denoised)


def solution(mesh):
    in_specs = (
        P("tile", None),
        P("section", "tile", None, None),
        P("section", "tile", None, None),
        P("section", "tile", None, None),
        P("section", "tile", None, None),
        P("section", None, "tile", None),
        P(),
        P(),
        P(),
        P(),
        P(),
        P(),
    )
    out_specs = (P("section", None, "tile", None), P("section", None, "tile", None))
    return jax.shard_map(
        on_device, mesh=mesh, in_specs=in_specs, out_specs=out_specs, check_vma=False
    )
```

```python
import functools

import jax
import jax.numpy as jnp
from jax import lax
from jax.experimental import pallas as pl
from jax.experimental.pallas import tpu as pltpu
from jax.sharding import PartitionSpec as P

EDGE = 34
NSP = 4
NRAY = 8
NOS = 2
LANES = 128
BLOCK = 256
STRIDE = 6
WINDOWS = 6
MAIN = 32
TAIL = 16
BRICK_ROWS = WINDOWS * MAIN + TAIL
KDIM = 256

F32 = jnp.float32
BF16 = jnp.bfloat16
MIB = 1024 * 1024


def params(mib):
    return pltpu.CompilerParams(vmem_limit_bytes=mib * MIB)


def vmem():
    return pl.BlockSpec(memory_space=pltpu.VMEM)


def smem():
    return pl.BlockSpec(memory_space=pltpu.SMEM)


def positions_kernel(cells_ref, fracs_ref, out_ref, cells, fracs, found, arrivals, departures):
    owners, rows, _ = out_ref.shape
    lines = rows // 3
    parts = arrivals.shape[1]
    share = owners // parts
    pieces = [(axis, part) for axis in range(3) for part in range(parts)]

    def reads(axis, part):
        span = pl.ds(part * share * lines, share * lines)
        return [
            pltpu.make_async_copy(
                source.at[axis, span], target.at[axis, span], arrivals.at[axis, part, number]
            )
            for number, (source, target) in enumerate(((cells_ref, cells), (fracs_ref, fracs)))
        ]

    def write(axis, part):
        place = (pl.ds(part * share, share), pl.ds(axis * lines, lines))
        return pltpu.make_async_copy(
            found.at[place], out_ref.at[place], departures.at[axis, part]
        )

    for piece in pieces:
        for copy in reads(*piece):
            copy.start()
    for axis, part in pieces:
        for copy in reads(axis, part):
            copy.wait()
        span = slice(part * share * lines, (part + 1) * share * lines)
        place = cells[axis, span].astype(F32) + fracs[axis, span]
        found[part * share : (part + 1) * share, axis * lines : (axis + 1) * lines, :] = (
            place.reshape(share, lines, LANES)
        )
        write(axis, part).start()
    for piece in pieces:
        write(*piece).wait()


def positions(cells, fracs, owners):
    lines = cells.shape[1]
    shape = (owners, 3 * lines // owners, LANES)
    hbm = pl.BlockSpec(memory_space=pltpu.HBM)
    return pl.pallas_call(
        positions_kernel,
        out_shape=jax.ShapeDtypeStruct(shape, F32),
        in_specs=[hbm, hbm],
        out_specs=hbm,
        scratch_shapes=[
            pltpu.VMEM(cells.shape, jnp.int32),
            pltpu.VMEM(fracs.shape, F32),
            pltpu.VMEM(shape, F32),
            pltpu.SemaphoreType.DMA((3, 4, 2)),
            pltpu.SemaphoreType.DMA((3, 4)),
        ],
        compiler_params=params(60),
        cost_estimate=pl.CostEstimate(
            flops=3 * lines * LANES, bytes_accessed=36 * lines * LANES, transcendentals=0
        ),
        name="positions",
    )(cells, fracs)


def mate_of(tile):
    return tile + 1 - 2 * lax.rem(tile, 2)


def windows_kernel(
    where_ref, picks_ref, cube_ref, place_ref, mate_place_ref, out_ref,
    wide, tail, places, sums, arrivals,
):
    tile = where_ref[0]
    near = ((tile, place_ref.at[tile]), (mate_of(tile), mate_place_ref.at[0]))
    copies = [
        pltpu.make_async_copy(source, places.at[i], arrivals.at[i])
        for i, (_, source) in enumerate(near)
    ]
    for copy in copies:
        copy.start()
    count = cube_ref.shape[0]
    plane = EDGE * EDGE
    wide[:, :, plane // LANES * LANES :] = jnp.zeros((count, wide.shape[1], LANES), BF16)
    wide[:, :EDGE, :plane] = cube_ref[...]
    column = lax.broadcasted_iota(jnp.int32, (1, KDIM), 1)
    main = (column // MAIN) * EDGE + column % MAIN
    rest = column - 7 * MAIN
    last = (rest % 8) * EDGE + MAIN + rest // 8
    source = jnp.where(column < 7 * MAIN, main, last)
    unused = (column >= 7 * MAIN) & ((rest % 8 == 7) | (rest >= TAIL))
    source = jnp.where(unused, -(1 << 20), source)
    for window in range(WINDOWS):
        first = window * STRIDE * EDGE
        low = first // LANES * LANES
        length = min(3 * LANES, wide.shape[2] - low)
        place = lax.broadcasted_iota(jnp.int32, (length, KDIM), 0)
        pick = jnp.where(place == source + (first - low), 1.0, 0.0).astype(BF16)
        found = jnp.dot(
            wide[:, :, low : low + length].reshape(-1, length),
            pick,
            preferred_element_type=F32,
        )
        found = found.reshape(count, 48, KDIM)
        out_ref[:count, window * MAIN : (window + 1) * MAIN, :] = found[:, :MAIN, :].astype(BF16)
        tail[:, window : window + 1, :] = found[:, MAIN : MAIN + 1, :]
        tail[:, 8 + window : 9 + window, :] = found[:, MAIN + 1 : MAIN + 2, :]
    for row in (6, 7, 14, 15):
        tail[:, row : row + 1, :] = jnp.zeros((count, 1, KDIM), F32)
    out_ref[:count, WINDOWS * MAIN :, :] = tail[...].astype(BF16)

    for copy in copies:
        copy.wait()
    cap = picks_ref.shape[0]
    lines = places.shape[1] // 3
    part = lines // cap
    height = whole_tiles(lines)
    for i, (renderer, _) in enumerate(near):
        for piece in range(cap):
            brick = out_ref[picks_ref[piece, renderer]]
            slot_sums(brick, places.at[i], sums.at[i], piece * part, part // 2)
    for i in range(len(near)):
        out_ref[count, i * height : (i + 1) * height, :LANES] = line_values(
            sums.at[i], lines, height
        )


def windows_of(where, picks, bricks, places, mate_places):
    count = bricks.shape[0]
    cube = bricks.reshape(count, EDGE, EDGE * EDGE)
    rows = places.shape[1]
    return pl.pallas_call(
        windows_kernel,
        out_shape=jax.ShapeDtypeStruct((count + 1, BRICK_ROWS, KDIM), BF16),
        in_specs=[smem(), smem(), vmem()] + [pl.BlockSpec(memory_space=pl.ANY)] * 2,
        out_specs=vmem(),
        scratch_shapes=[
            pltpu.VMEM((count, 48, 10 * LANES), BF16),
            pltpu.VMEM((count, TAIL, KDIM), F32),
            pltpu.VMEM((2, rows, LANES), F32),
            pltpu.VMEM((2, 8 * rows // 3, LANES), F32),
            pltpu.SemaphoreType.DMA((2,)),
        ],
        compiler_params=params(16),
        cost_estimate=pl.CostEstimate(
            flops=2 * count * 48 * 384 * KDIM * WINDOWS, bytes_accessed=4 * MIB,
            transcendentals=0,
        ),
        name="brick_windows",
    )(where, picks, cube, places, mate_places)


def hat(distance):
    return jnp.maximum(1.0 - jnp.abs(distance), 0.0)


def blend(brick, px, py, pz):
    width = px.shape[1]
    eight = lax.broadcasted_iota(jnp.int32, (8, width), 0).astype(F32)
    places = lax.broadcasted_iota(jnp.int32, (MAIN, width), 0).astype(F32).astype(BF16)

    def tile(rows):
        return jnp.concatenate([rows, rows], axis=0).astype(BF16)

    cell_y = jnp.floor(py)
    frac_y = py - cell_y
    lower, high_share = tile(cell_y), tile(frac_y)
    nothing = jnp.zeros((TAIL, width), BF16)
    weight_y = []
    for start in range(0, MAIN, TAIL):
        here = places[start : start + TAIL]
        weight_y.append(
            jnp.maximum(1.0 - jnp.abs((here - lower) - high_share), nothing)
        )
    window = jnp.floor(px * (1.0 / STRIDE))
    weight_x = hat(eight - (px - STRIDE * window))
    parts = []
    for i in range(STRIDE + 1):
        share = tile(jnp.broadcast_to(weight_x[i : i + 1], (8, width)))
        parts += [share * part for part in weight_y]
    tail = [weight_x * hat(MAIN - py), weight_x * jnp.maximum(py - MAIN, 0.0)]
    parts.append(jnp.concatenate(tail, axis=0).astype(BF16))
    plane = jnp.concatenate(parts, axis=0)
    found = jnp.dot(brick[:, : plane.shape[0]], plane, preferred_element_type=F32)
    groups = range(0, MAIN, 8)
    chosen = [found[row : row + 8] for row in groups]
    for other in range(1, WINDOWS):
        here = window == float(other)
        base = other * MAIN
        chosen = [
            jnp.where(here, found[base + row : base + row + 8], old)
            for row, old in zip(groups, chosen)
        ]
    base = WINDOWS * MAIN
    edges = found[base : base + 8] * hat(MAIN - pz)
    edges = edges + found[base + 8 :] * jnp.maximum(pz - MAIN, 0.0)
    total = jnp.where(eight == window, edges, 0.0)
    for row, part in zip(groups, chosen):
        total = total + part * hat((eight + float(row)) - pz)
    return total


def slot_sums(brick, places, sums, first, blocks):
    lines = places.shape[0] // 3
    together = 2 if blocks % 2 == 0 else 1
    halves = 2 * together
    for step in range(0, blocks, together):
        row = first + 2 * step

        def line(axis):
            parts = [
                jnp.broadcast_to(places[pl.ds(axis * lines + row + half, 1), :], (8, LANES))
                for half in range(halves)
            ]
            return jnp.concatenate(parts, axis=1)

        total = blend(brick, line(0), line(1), line(2))
        for half in range(halves):
            sums[pl.ds(pl.multiple_of(8 * (row + half), 8), 8), :] = total[
                :, half * LANES : (half + 1) * LANES
            ]


def whole_tiles(lines):
    return -(-lines // TAIL) * TAIL


def line_values(sums, lines, height):
    values = []
    for row in range(0, lines, 8):
        value = sums[pl.ds(8 * row, 8, stride=8), :]
        for other in range(1, 8):
            value = value + sums[pl.ds(8 * row + other, 8, stride=8), :]
        values.append(value)
    if height > lines:
        values.append(jnp.zeros((height - lines, LANES), F32))
    return jnp.concatenate(values, axis=0).astype(BF16)


def samples_kernel(
    where_ref, picks_ref, brick_ref, place_ref, out_ref, bricks, places, sums, own, arrivals,
    own_arrival,
):
    owners, rows, _ = place_ref.shape
    cap = picks_ref.shape[0]
    lines = rows // 3
    part = lines // cap
    turns = owners - 2
    tile = where_ref[0]
    pairs, rest = turns // 2, turns % 2
    own_values = pltpu.make_async_copy(
        brick_ref.at[brick_ref.shape[0] - 1, pl.ds(0, own.shape[0]), pl.ds(0, LANES)],
        own,
        own_arrival,
    )

    def renderer_of(number):
        return lax.rem(2 * (tile // 2) + 2 + number, owners)

    def fetches(turn, members):
        held = turn % 2
        copies = []
        for member in range(members):
            renderer = renderer_of(2 * turn + member)
            copies.append(
                pltpu.make_async_copy(
                    place_ref.at[renderer],
                    places.at[held, member],
                    arrivals.at[held, member, cap],
                )
            )
            for piece in range(cap):
                copies.append(
                    pltpu.make_async_copy(
                        brick_ref.at[picks_ref[piece, renderer]],
                        bricks.at[held, member, piece],
                        arrivals.at[held, member, piece],
                    )
                )
        return copies

    def start(turn, members):
        for copy in fetches(turn, members):
            copy.start()

    def work(turn, members):
        held = turn % 2
        for copy in fetches(turn, members):
            copy.wait()

        if members == 2:
            pl.when(turn + 1 < pairs)(lambda: start(turn + 1, 2))
            if rest:
                pl.when(turn + 1 == pairs)(lambda: start(pairs, 1))
            pl.when(turn == 0)(own_values.start)

        for member in range(members):
            for piece in range(cap):
                slot_sums(
                    bricks[held, member, piece],
                    places.at[held, member],
                    sums.at[member],
                    piece * part,
                    part // 2,
                )
        for member in range(members):
            out_ref[renderer_of(2 * turn + member)] = line_values(
                sums.at[member], lines, lines
            )

    def one_pair(turn, carry):
        work(turn, 2)
        return carry

    if pairs > 0:
        start(0, 2)
    elif rest:
        start(0, 1)
    lax.fori_loop(0, pairs, one_pair, 0)
    if rest:
        work(pairs, 1)
    if pairs == 0:
        own_values.start()
    own_values.wait()
    height = whole_tiles(lines)
    for i, renderer in enumerate((tile, mate_of(tile))):
        values = own[i * height : (i + 1) * height, :].astype(F32)
        out_ref[renderer] = values[:lines].astype(BF16)


def sample_values(where, picks, windows, places):
    owners, rows, _ = places.shape
    cap = picks.shape[0]
    samples = owners * rows * LANES // 3
    some = pl.BlockSpec(memory_space=pl.ANY)
    return pl.pallas_call(
        samples_kernel,
        out_shape=jax.ShapeDtypeStruct((owners, rows // 3, LANES), BF16),
        in_specs=[smem(), smem(), some, some],
        out_specs=vmem(),
        scratch_shapes=[
            pltpu.VMEM((2, 2, cap, BRICK_ROWS, KDIM), BF16),
            pltpu.VMEM((2, 2, rows, LANES), F32),
            pltpu.VMEM((2, 8 * rows // 3, LANES), F32),
            pltpu.VMEM((2 * whole_tiles(rows // 3), LANES), BF16),
            pltpu.SemaphoreType.DMA((2, 2, cap + 1)),
            pltpu.SemaphoreType.DMA,
        ],
        compiler_params=pltpu.CompilerParams(vmem_limit_bytes=61_600_000),
        cost_estimate=pl.CostEstimate(
            flops=2 * samples * KDIM * BRICK_ROWS, bytes_accessed=3 * MIB,
            transcendentals=0,
        ),
        name="sample_values",
    )(where, picks, windows, places)


def gbuffer_kernel(value_ref, order_ref, out_ref, values):
    values[...] = value_ref[...].astype(F32).reshape(values.shape)
    height = out_ref.shape[2]

    def ray_of(number):
        rows_now = slice(number * height, (number + 1) * height)
        first, second = (
            values[pl.ds(2 * number * height + half, height, stride=2), :] for half in range(2)
        )
        parts = []
        for half in range(2):
            order = order_ref[0, 0, rows_now, half * LANES : (half + 1) * LANES]
            inner = order & (LANES - 1)
            parts.append(
                jnp.where(
                    order < LANES,
                    jnp.take_along_axis(first, inner, axis=1, mode="promise_in_bounds"),
                    jnp.take_along_axis(second, inner, axis=1, mode="promise_in_bounds"),
                )
            )
        return jnp.concatenate(parts, axis=1)

    remain = 1.0
    shade = 0.0
    depth = 0.0
    for step in range(NSP):
        ray = ray_of(step)
        half_tanh = 0.5 * jnp.tanh(ray)
        weight = remain * (0.5 + half_tanh)
        shade = shade + weight * ray
        depth = depth + weight * ((step + 1) / NSP)
        remain = remain * (0.5 - half_tanh)
    occlusion = 0.0
    for ray_number in range(NRAY):
        passing = 1.0
        for step in range(NOS):
            ray = ray_of(NSP + ray_number * NOS + step)
            passing = passing * (0.5 - 0.5 * jnp.tanh(ray))
        occlusion = occlusion + passing
    out_ref[0, 0] = shade.astype(BF16)
    out_ref[0, 1] = (1.0 - remain).astype(BF16)
    out_ref[0, 2] = depth.astype(BF16)
    out_ref[0, 3] = (occlusion * (1.0 / NRAY)).astype(BF16)


def gbuffer(values, order, height, width):
    total = order.shape[2]
    return pl.pallas_call(
        gbuffer_kernel,
        out_shape=jax.ShapeDtypeStruct((1, 4, height, width), BF16),
        in_specs=[vmem(), vmem()],
        out_specs=vmem(),
        scratch_shapes=[pltpu.VMEM((2 * total, LANES), F32)],
        compiler_params=params(16),
        cost_estimate=pl.CostEstimate(
            flops=20 * total * BLOCK, bytes_accessed=8 * total * BLOCK, transcendentals=0
        ),
        name="gbuffer",
    )(values, order)


def silu(field):
    half = 0.5 * field
    return half + half * jnp.tanh(half)


def shifted(rows, steps):
    lane = lax.broadcasted_iota(jnp.int32, (1, LANES), 1)
    edge = lane == (0 if steps == 1 else LANES - 1)
    moved = []
    for row in rows:
        tiles = [row[:, i : i + LANES] for i in range(0, row.shape[1], LANES)]
        tiles = [pltpu.roll(tile, steps % LANES, 1) for tile in tiles]
        for i, tile in enumerate(tiles):
            source = i - steps
            fill = tiles[source] if 0 <= source < len(tiles) else 0.0
            moved.append(jnp.where(edge, fill, tile))
    return jnp.concatenate(moved, axis=1)


def across(total, chans, row_width):
    left, middle, right = (total[i * chans : (i + 1) * chans] for i in range(3))

    def rows_of(part):
        return [part[:, i : i + row_width] for i in range(0, part.shape[1], row_width)]

    return middle + shifted(rows_of(left), 1) + shifted(rows_of(right), -1)


def taps(weight_ref, tap):
    _, out_chans, chans = weight_ref.shape
    return weight_ref[3 * tap : 3 * tap + 3].reshape(3 * out_chans, chans)


def beside(weight_ref):
    return jnp.concatenate([taps(weight_ref, tap) for tap in range(3)], axis=1)


def beside_padded(weight_ref, spare):
    few = weight_ref.shape[1]
    spare[...] = jnp.zeros_like(spare)
    for tap in range(3):
        for column in range(3):
            spare[tap, column * TAIL : column * TAIL + few, :] = weight_ref[
                3 * tap + column
            ].astype(F32)
    return jnp.concatenate([spare[tap].astype(BF16) for tap in range(3)], axis=1)


def sides(where_ref):
    above = jnp.where(where_ref[0] > 0, 1.0, 0.0)
    below = jnp.where(where_ref[0] < where_ref[1] - 1, 1.0, 0.0)

    def inside(row, low, high):
        return jnp.where(row < low, above, jnp.where(row >= high, below, 1.0))

    return inside


def turned(weight_ref, spare=None):
    _, few, out_chans = weight_ref.shape
    here = lax.broadcasted_iota(jnp.int32, (out_chans, out_chans), 0)
    there = lax.broadcasted_iota(jnp.int32, (out_chans, out_chans), 1)
    unit = jnp.where(here == there, 1.0, 0.0).astype(BF16)
    if spare is not None:
        spare[...] = jnp.zeros_like(spare)
    rows = []
    for column in range(3):
        if spare is None:
            stack = jnp.concatenate([weight_ref[3 * tap + column] for tap in range(3)], axis=0)
        else:
            for tap in range(3):
                spare[column, tap * TAIL : tap * TAIL + few, :] = weight_ref[
                    3 * tap + column
                ].astype(F32)
            stack = spare[column].astype(BF16)
        rows.append(
            lax.dot_general(
                unit, stack, (((1,), (1,)), ((), ())), preferred_element_type=F32
            )
        )
    return jnp.concatenate(rows, axis=0).astype(BF16)


def stem_kernel(
    where_ref, own_ref, near_ref, far_ref, w_in, w_mid, second, x_ref, first, spare
):
    height, chans, width = own_ref.shape
    inside = sides(where_ref)
    first_core = lax.rem(where_ref[0], 2) == 0
    near, far = near_ref[...].astype(F32), far_ref[...].astype(F32)
    x_ref[...] = jnp.zeros_like(x_ref)
    x_ref[:height, :chans, :] = jnp.where(first_core, far, near).astype(BF16)
    x_ref[height : 2 * height, :chans, :] = own_ref[...]
    x_ref[2 * height :, :chans, :] = jnp.where(first_core, near, far).astype(BF16)

    def full_layer(weight, source, target, low, high, unroll):
        chans = target.shape[1]
        depth = weight.shape[1]

        def step(row, carry):
            lines = source[pl.ds(row, 3)].reshape(depth, width)
            line = across(jnp.dot(weight, lines, preferred_element_type=F32), chans, width)
            target[row] = (silu(line) * inside(row, low, high)).astype(BF16)
            return carry

        lax.fori_loop(0, target.shape[0], step, 0, unroll=unroll)

    full_layer(turned(w_in, spare), x_ref, first, height - 1, 2 * height - 1, first.shape[0])
    full_layer(beside(w_mid), first, second, height - 2, 2 * height - 2, second.shape[0])


def half_pair(source, row, tap):
    return jnp.concatenate([source[row + tap], source[row + tap + 1]], axis=1)


def half_layer(product, target, inside, low, high):
    chans, half_width = target.shape[1], target.shape[2]
    for row in range(0, target.shape[0], 2):
        both = silu(across(product(row), chans, half_width))
        for now in range(2):
            line = both[:, now * half_width : (now + 1) * half_width]
            if row + now < low or row + now >= high:
                line = line * inside(row + now, low, high)
            target[row + now] = line.astype(BF16)


def middle_kernel(where_ref, second, w_down, third, pooled):
    count, chans, width = second.shape
    half_height = (count + 4) // 6
    half_width = width // 2
    inside = sides(where_ref)
    place = lax.broadcasted_iota(jnp.int32, (width, half_width), 0) // 2
    target = lax.broadcasted_iota(jnp.int32, (width, half_width), 1)
    shrink = jnp.where(place == target, 0.25, 0.0).astype(BF16)
    pairs = jnp.dot(
        second[...].reshape(count * chans, width), shrink, preferred_element_type=F32
    ).reshape(count // 2, 2, chans, half_width)
    pooled[...] = (pairs[:, 0] + pairs[:, 1]).astype(BF16)
    weight_down = turned(w_down)

    def down_product(row):
        lines = jnp.concatenate([half_pair(pooled, row, tap) for tap in range(3)], axis=0)
        return jnp.dot(weight_down, lines, preferred_element_type=F32)

    half_layer(down_product, third, inside, half_height - 2, 2 * half_height - 2)


def decoder_kernel(
    where_ref, second, third, w_deep, w_up, w_out, out_ref, fourth, joined, fifth, final, spare
):
    height = out_ref.shape[2]
    half_height = height // 2
    width = out_ref.shape[3]
    half_width = width // 2
    chans = second.shape[1]
    inside = sides(where_ref)

    def deep_product(row):
        total = None
        for tap in range(3):
            part = jnp.dot(
                taps(w_deep, tap), half_pair(third, row, tap), preferred_element_type=F32
            )
            total = part if total is None else total + part
        return total

    half_layer(deep_product, fourth, inside, half_height - 3, 2 * half_height - 3)
    place = lax.broadcasted_iota(jnp.int32, (half_width, width), 0)
    target = lax.broadcasted_iota(jnp.int32, (half_width, width), 1) // 2
    spread = jnp.where(place == target, 1.0, 0.0).astype(BF16)
    deep = fourth.shape[1]
    wide = jnp.dot(
        fourth[...].reshape(-1, half_width), spread, preferred_element_type=F32
    ).astype(BF16).reshape(fourth.shape[0], deep, width)
    for row in range(2 * fourth.shape[0]):
        joined[row, chans:, :] = wide[row // 2]
        joined[row, :chans, :] = second[row + 4]

    def up_step(row, carry):
        total = None
        for tap in range(3):
            part = jnp.dot(taps(w_up, tap), joined[row + tap], preferred_element_type=F32)
            total = part if total is None else total + part
        line = silu(across(total, chans, width))
        fifth[row] = (line * inside(row, 1, height + 1)).astype(BF16)
        return carry

    lax.fori_loop(0, fifth.shape[0], up_step, 0, unroll=fifth.shape[0])

    colours = out_ref.shape[1]
    weight_out = beside_padded(w_out, spare)
    for row in range(height):
        lines = fifth[row : row + 3].reshape(3 * chans, width)
        total = jnp.dot(weight_out, lines, preferred_element_type=F32)
        line = across(total, TAIL, width)
        for colour in range(colours):
            final[colour, row : row + 1, :] = line[colour : colour + 1, :]
    out_ref[0] = final[...].astype(BF16)


def stem(where, own, near, far, w_in, w_mid):
    height, _, width = own.shape
    one = w_mid.shape[1]
    return pl.pallas_call(
        stem_kernel,
        out_shape=jax.ShapeDtypeStruct((3 * height - 4, one, width), BF16),
        in_specs=[smem()] + [vmem()] * 5,
        out_specs=vmem(),
        scratch_shapes=[
            pltpu.VMEM((3 * height, TAIL, width), BF16),
            pltpu.VMEM((3 * height - 2, one, width), BF16),
            pltpu.VMEM((3, 3 * TAIL, one), F32),
        ],
        compiler_params=params(16),
        cost_estimate=pl.CostEstimate(
            flops=1_000_000_000, bytes_accessed=MIB, transcendentals=300_000
        ),
        name="stem",
    )(where, own, near, far, w_in, w_mid)


def middle(where, second, w_down):
    rows, one, width = second.shape
    half = (rows + 4) // 6
    two = w_down.shape[2]
    return pl.pallas_call(
        middle_kernel,
        out_shape=jax.ShapeDtypeStruct((3 * half - 4, two, width // 2), BF16),
        in_specs=[smem()] + [vmem()] * 2,
        out_specs=vmem(),
        scratch_shapes=[pltpu.VMEM((3 * half - 2, one, width // 2), BF16)],
        compiler_params=params(16),
        cost_estimate=pl.CostEstimate(
            flops=500_000_000, bytes_accessed=MIB, transcendentals=100_000
        ),
        name="middle",
    )(where, second, w_down)


def decoder(where, second, third, w_deep, w_up, w_out, height, colours):
    one = second.shape[1]
    two = third.shape[1]
    width = second.shape[2]
    return pl.pallas_call(
        decoder_kernel,
        out_shape=jax.ShapeDtypeStruct((1, colours, height, width), BF16),
        in_specs=[smem()] + [vmem()] * 5,
        out_specs=vmem(),
        scratch_shapes=[
            pltpu.VMEM((third.shape[0] - 2, two, width // 2), BF16),
            pltpu.VMEM((height + 4, one + two, width), BF16),
            pltpu.VMEM((height + 2, one, width), BF16),
            pltpu.VMEM((colours, height, width), F32),
            pltpu.VMEM((3, 3 * TAIL, one), F32),
        ],
        compiler_params=params(16),
        cost_estimate=pl.CostEstimate(
            flops=1_500_000_000, bytes_accessed=MIB, transcendentals=200_000
        ),
        name="decoder",
    )(where, second, third, w_deep, w_up, w_out)


def on_device(
    bricks, sends, cells, fracs, sample_order, pending, w_in, w_mid, w_down, w_deep, w_up, w_out
):
    n_tile = lax.axis_size("tile")
    tile = lax.axis_index("tile")
    n_section = lax.axis_size("section")
    cap = sends.shape[3]
    height = pending.shape[2]
    width = pending.shape[3]
    samples = cells.shape[3]
    slots = n_tile * cap
    per_slot = samples // slots
    padded = -(-per_slot // BLOCK) * BLOCK

    def fill(part):
        if padded != per_slot:
            part = part.reshape(3, slots, per_slot)
            part = jnp.pad(part, ((0, 0), (0, 0), (0, padded - per_slot)))
        return part.reshape(3, slots * padded // LANES, LANES)

    def trim(found):
        if padded == per_slot:
            return found
        return found.reshape(slots, padded)[:, :per_slot].reshape(1, samples // LANES, LANES)

    places = positions(fill(cells), fill(fracs), n_tile)
    places, bricks, pending, tile = lax.optimization_barrier((places, bricks, pending, tile))
    arrived = lax.all_to_all(places, "tile", split_axis=0, concat_axis=0, tiled=True)
    where = jnp.stack([tile, jnp.int32(n_tile)]).astype(jnp.int32)

    mates = [(i, i ^ 1) for i in range(n_tile) if i ^ 1 < n_tile]
    across_chips = [
        pair for i in range(1, n_tile - 1, 2) for pair in ((i, i + 1), (i + 1, i))
    ]
    for_mate = lax.dynamic_slice_in_dim(places, mate_of(tile), 1, 0)
    mate_places = lax.ppermute(for_mate, "tile", mates)
    rows = pending[0].transpose(1, 0, 2)
    near = lax.ppermute(rows, "tile", mates)
    far = lax.ppermute(rows, "tile", across_chips)
    picks = sends[0, 0].T
    colours = w_out.shape[1]
    windows = windows_of(where, picks, bricks, places, mate_places)
    found = sample_values(where, picks, windows, arrived)

    found, rows, near, far = lax.optimization_barrier((found, rows, near, far))
    values = lax.all_to_all(found, "tile", split_axis=0, concat_axis=0, tiled=True)
    second = stem(where, rows, near, far, w_in.transpose(0, 2, 1), w_mid)
    third = middle(where, second, w_down.transpose(0, 2, 1))
    values, third = lax.optimization_barrier((values, third))
    rendered = gbuffer(trim(values), sample_order, height, width)
    rendered, third = lax.optimization_barrier((rendered, third))
    ring = [(i, (i + 1) % n_section) for i in range(n_section)]
    handoff = lax.ppermute(rendered, "section", ring)
    denoised = decoder(where, second, third, w_deep, w_up, w_out, height, colours)
    return (handoff, denoised)


def solution(mesh):
    in_specs = (
        P("tile", None),
        P("section", "tile", None, None),
        P("section", "tile", None, None),
        P("section", "tile", None, None),
        P("section", "tile", None, None),
        P("section", None, "tile", None),
        P(),
        P(),
        P(),
        P(),
        P(),
        P(),
    )
    out_specs = (P("section", None, "tile", None), P("section", None, "tile", None))
    return jax.shard_map(
        on_device, mesh=mesh, in_specs=in_specs, out_specs=out_specs, check_vma=False
    )
```
